32 devices in a mesh: dp: 8 (over y, x, core), tensor: 4 (over z).
Axes of the slice: x: 2, y: 2, z: 4, core: 2. Of those that a mesh axis runs over, the one named last changes fastest.
Arguments:
- layer_in: bfloat16 [8192, 2304], P(('dp', 'tensor')), may hold values from -6 to 6
- out_grad: bfloat16 [8192, 2304], P(('dp', 'tensor')), may hold values from -6 to 6
- piece_starts: int32 [8, 2], P('dp'), may hold values from 0 to 768, as said below
- attn_gain: bfloat16 [2304], P('dp'), may hold values from -0.3984375 to 0.3984375
- attn_out_gain: bfloat16 [2304], P('dp'), may hold values from -0.3984375 to 0.3984375
- feed_gain: bfloat16 [2304], P('dp'), may hold values from -0.3984375 to 0.3984375
- feed_out_gain: bfloat16 [2304], P('dp'), may hold values from -0.3984375 to 0.3984375
- query_weight: bfloat16 [2304, 2048], P('dp', 'tensor'), may hold values from -2 to 2
- key_weight: bfloat16 [2304, 1024], P('dp'), may hold values from -2 to 2
- value_weight: bfloat16 [2304, 1024], P('dp'), may hold values from -0.125 to 0.125
- out_weight: bfloat16 [2048, 2304], P('tensor', 'dp'), may hold values from -0.75 to 0.75
- gate_weight: bfloat16 [2304, 9216], P('dp', 'tensor'), may hold values from -0.125 to 0.125
- up_weight: bfloat16 [2304, 9216], P('dp', 'tensor'), may hold values from -0.125 to 0.125
- down_weight: bfloat16 [9216, 2304], P('tensor', 'dp'), may hold values from -0.0625 to 0.0625
Outputs:
- layer_out: bfloat16 [8192, 2304], P(('dp', 'tensor'))
- in_grad: bfloat16 [8192, 2304], P(('dp', 'tensor'))
- grad_query_weight: float32 [2304, 2048], P('dp', 'tensor')
- grad_key_weight: float32 [2304, 1024], P('dp')
- grad_value_weight: float32 [2304, 1024], P('dp')
- grad_out_weight: float32 [2048, 2304], P('tensor', 'dp')
- grad_gate_weight: float32 [2304, 9216], P('dp', 'tensor')
- grad_up_weight: float32 [2304, 9216], P('dp', 'tensor')
- grad_down_weight: float32 [9216, 2304], P('tensor', 'dp')
- grad_attn_gain: float32 [2304], P('dp')
- grad_attn_out_gain: float32 [2304], P('dp')
- grad_feed_gain: float32 [2304], P('dp')
- grad_feed_out_gain: float32 [2304], P('dp')
The draws below stay inside these ranges and needn't reach their ends.
Inputs may be any that keep to these rules, and one draw needn't show every extreme that they name: `piece_starts`: each sequence has 2 picture pieces of 256 tokens: the first starts in the sequence's first half and the second in its second half, so they never intersect and each lies inside the sequence.
All inputs are finite; a program needn't handle non-finite values.
Results may differ from the reference program's by a relative error of at most 0.024.
Values may be sent and summed in bfloat16 or wider, within the bound.
A program may use at most 256 MiB of HBM per device.

```python
import math
import jax
import jax.numpy as jnp
from jax import lax

D = 2304
H = 8
KV = 4
HD = 256
FF = 9216
L = 1024
PIECE = 256
SEQS = 8
TOKENS = 8192


def draw_piece_starts(key, part):
    first_key, second_key, pick_key = jax.random.split(jax.random.fold_in(key, 17), 3)
    half_len = L // 2
    first_start = jax.random.randint(first_key, (SEQS,), 0, half_len - PIECE + 1)
    second_start = jax.random.randint(second_key, (SEQS,), half_len, L - PIECE + 1)
    chosen = jax.random.randint(pick_key, (2,), 0, SEQS)
    seq_index = jnp.arange(SEQS)
    first_start = jnp.where(seq_index == chosen[0], 0, first_start)
    second_start = jnp.where(seq_index == chosen[1], L - PIECE, second_start)
    return jnp.stack([first_start, second_start], axis=1).astype(jnp.int32)


def head_scales(key):
    order = jax.random.permutation(jax.random.fold_in(key, 29), KV)
    levels = jnp.maximum(1.0, 1.7 - 0.25 * jnp.arange(KV).astype(jnp.float32))
    return levels[order]


def unit_noise(key, shape):
    return jnp.clip(jax.random.normal(key, shape, jnp.float32), -4.0, 4.0)


def draw_query_weight(key, part):
    column_scale = jnp.repeat(head_scales(key), H // KV * HD)
    noise = unit_noise(jax.random.fold_in(key, 37), (D, H * HD))
    return jnp.clip(noise * column_scale[None, :] / math.sqrt(D), -2.0, 2.0).astype(jnp.bfloat16)


def draw_key_weight(key, part):
    column_scale = jnp.repeat(head_scales(key), HD)
    noise = unit_noise(jax.random.fold_in(key, 31), (D, KV * HD))
    return jnp.clip(noise * column_scale[None, :] / math.sqrt(D), -2.0, 2.0).astype(jnp.bfloat16)


def level_of(own_key, dims, shards, least, high):
    factor_of = 1.0
    for axis_at, shards_of in shards:
        draws = jax.random.uniform(jax.random.fold_in(jax.random.fold_in(own_key, 6), axis_at), (shards_of,), jnp.float32, least / len(shards), high / len(shards))
        factor_of = factor_of * jnp.repeat(jnp.exp(draws), dims[axis_at] // shards_of).reshape((-1,) + (1,) * (len(dims) - 1 - axis_at))
    return factor_of


def centred(rng, extent, deviation, reach, pieces=(), kind=jnp.bfloat16):
    level = level_of(rng, extent, pieces, -0.22, 0.18) if pieces else 1.0
    drawn = jax.random.normal(rng, extent, jnp.float32) * deviation * level
    return jnp.minimum(jnp.maximum(drawn, -reach), reach).astype(kind)


def setup_inputs(seed: int = 0) -> dict:
    seeds = jax.random.split(jax.random.key(seed), 15)
    return {
        "layer_in": centred(seeds[0], (TOKENS, D), 1.0, 6.0, ((0, 32),)),
        "out_grad": centred(seeds[1], (TOKENS, D), 1.0, 6.0, ((0, 32),)),
        "piece_starts": draw_piece_starts(jax.random.fold_in(seeds[14], 71), 0),
        "attn_gain": jnp.clip(jax.random.uniform(seeds[3], (D,), jnp.float32, -0.3984375, 0.3984375) * level_of(seeds[3], (D,), ((0, 8),), -0.4, 0.0), -0.3984375, 0.3984375).astype(jnp.bfloat16),
        "attn_out_gain": jnp.clip(jax.random.uniform(seeds[4], (D,), jnp.float32, -0.3984375, 0.3984375) * level_of(seeds[4], (D,), ((0, 8),), -0.4, 0.0), -0.3984375, 0.3984375).astype(jnp.bfloat16),
        "feed_gain": jnp.clip(jax.random.uniform(seeds[5], (D,), jnp.float32, -0.3984375, 0.3984375) * level_of(seeds[5], (D,), ((0, 8),), -0.4, 0.0), -0.3984375, 0.3984375).astype(jnp.bfloat16),
        "feed_out_gain": jnp.clip(jax.random.uniform(seeds[6], (D,), jnp.float32, -0.3984375, 0.3984375) * level_of(seeds[6], (D,), ((0, 8),), -0.4, 0.0), -0.3984375, 0.3984375).astype(jnp.bfloat16),
        "query_weight": draw_query_weight(jax.random.fold_in(seeds[14], 71), 0),
        "key_weight": draw_key_weight(jax.random.fold_in(seeds[14], 71), 0),
        "value_weight": centred(seeds[9], (D, KV * HD), D ** -0.5, 0.125, ((0, 8),)),
        "out_weight": centred(seeds[10], (H * HD, D), (H * HD // 32) ** -0.5, 0.75, ((0, 4), (1, 8))),
        "gate_weight": centred(seeds[11], (D, FF), D ** -0.5, 0.125, ((0, 8), (1, 4))),
        "up_weight": centred(seeds[12], (D, FF), D ** -0.5, 0.125, ((0, 8), (1, 4))),
        "down_weight": centred(seeds[13], (FF, D), FF ** -0.5, 0.0625, ((0, 4), (1, 8))),
    }


@jax.custom_vjp
def low(v):
    return lax.optimization_barrier(v.astype(jnp.bfloat16)).astype(jnp.float32)

@jax.custom_vjp
def low_back(v):
    return v

def low_keep(v):
    return (low(v), None)

def low_pass(kept, grad):
    return (grad,)

def back_keep(v):
    return (v, None)

def back_low(kept, grad):
    return (low(grad),)
low.defvjp(low_keep, low_pass)
low_back.defvjp(back_keep, back_low)
norm_epsilon = 1e-06
logit_cap = 50.0

def matmul(left_side, right_side):
    return jnp.dot(left_side, right_side, precision=lax.Precision.HIGHEST, preferred_element_type=jnp.float32)

def rms_scale(values, gain):
    inverse = lax.rsqrt(lax.optimization_barrier(jnp.mean(values * values, axis=-1, keepdims=True)) + norm_epsilon)
    return values * inverse * (1.0 + gain)

def rotate(values, cosine_table, sine_table):
    half_size = values.shape[-1] // 2
    turned = jnp.concatenate([-values[..., half_size:], values[..., :half_size]], axis=-1)
    return values * cosine_table + turned * sine_table

def rope_tables(token_count, seq_len, head_size):
    positions = (jnp.arange(token_count, dtype=jnp.int32) % jnp.int32(seq_len)).astype(jnp.float32)
    exponent = jnp.arange(head_size // 2, dtype=jnp.int32).astype(jnp.float32) * (-2.0 / head_size)
    frequency = jnp.exp(exponent * jnp.log(jnp.float32(10000.0)))
    angles = positions[:, None] * frequency[None, :]
    angles = jnp.concatenate([angles, angles], axis=-1)[:, None, :]
    return (jnp.cos(angles), jnp.sin(angles))

def visible(starts, seq_len):
    query_pos = jnp.arange(seq_len, dtype=jnp.int32)
    key_pos = jnp.arange(seq_len, dtype=jnp.int32)
    starts = starts.astype(jnp.int32)
    allowed = key_pos[None, :] <= query_pos[:, None]
    for piece_index in range(starts.shape[0]):
        begin = starts[piece_index]
        finish = begin + jnp.int32(PIECE)
        inside_query = (query_pos >= begin) & (query_pos < finish)
        inside_key = (key_pos >= begin) & (key_pos < finish)
        allowed = allowed | inside_query[:, None] & inside_key[None, :]
    return allowed

def attend_sequence(seq_items):
    queries, keys_wide, values_wide, starts = seq_items
    scores = low_back(jnp.einsum('qhd,khd->hqk', queries, keys_wide, precision=lax.Precision.HIGHEST))
    capped = logit_cap * jnp.tanh(scores / logit_cap)
    allowed = visible(starts, queries.shape[0])
    capped = jnp.where(allowed[None], capped, jnp.full_like(capped, -1e+30))
    largest = lax.optimization_barrier(jnp.max(capped, axis=-1, keepdims=True))
    weights = jnp.exp(capped - largest)
    softmax_low = low(weights / lax.optimization_barrier(jnp.sum(weights, axis=-1, keepdims=True)))
    result = jnp.einsum('hqk,khd->qhd', softmax_low, values_wide, precision=lax.Precision.HIGHEST)
    return result.astype(jnp.float32)

def layer(inputs, gain_one, gain_two, gain_three, gain_four, query_weight, key_weight, value_weight, out_weight, gate_weight, up_weight, down_weight, starts):
    token_count = inputs.shape[0]
    seq_count = token_count // L
    hidden_one = low(rms_scale(inputs, gain_one))
    cosine_table, sine_table = rope_tables(token_count, L, HD)
    query_pre = low_back(matmul(hidden_one, query_weight)).reshape(token_count, H, HD)
    key_pre = matmul(hidden_one, key_weight).reshape(token_count, KV, HD)
    key_rep = low_back(jnp.repeat(key_pre, H // KV, axis=1))
    value_pre = matmul(hidden_one, value_weight).reshape(token_count, KV, HD)
    values_wide = low_back(low(jnp.repeat(value_pre, H // KV, axis=1)))
    queries = low(rotate(query_pre, cosine_table, sine_table) * HD ** (-0.5))
    keys_wide = low(rotate(key_rep, cosine_table, sine_table))
    mixed_heads = lax.map(jax.checkpoint(attend_sequence), (queries.reshape(seq_count, L, H, HD), keys_wide.reshape(seq_count, L, H, HD), values_wide.reshape(seq_count, L, H, HD), starts))
    mixed_heads = low_back(low(mixed_heads.reshape(token_count, H * HD)))
    attention = low_back(matmul(mixed_heads, out_weight))
    resid = inputs + rms_scale(attention, gain_two)
    hidden_three = low(rms_scale(resid, gain_three))
    gate_value = low_back(matmul(hidden_three, gate_weight))
    upward = low_back(matmul(hidden_three, up_weight))
    product = low(jax.nn.gelu(gate_value, approximate=True) * upward)
    feed = low_back(matmul(product, down_weight))
    return resid + rms_scale(feed, gain_four)

def reference(layer_in, out_grad, piece_starts, attn_gain, attn_out_gain, feed_gain, feed_out_gain, query_weight, key_weight, value_weight, out_weight, gate_weight, up_weight, down_weight):
    seq_total = piece_starts.shape[0]
    group_size = math.gcd(seq_total, max(1, 4096 // L))
    step_count = seq_total // group_size
    parameters = tuple((weight.astype(jnp.float32) for weight in (attn_gain, attn_out_gain, feed_gain, feed_out_gain, query_weight, key_weight, value_weight, out_weight, gate_weight, up_weight, down_weight)))
    inputs = layer_in.astype(jnp.float32).reshape(step_count, group_size * L, layer_in.shape[1])
    cotangents = out_grad.astype(jnp.float32).reshape(step_count, group_size * L, layer_in.shape[1])
    starts = piece_starts.astype(jnp.int32).reshape(step_count, group_size, piece_starts.shape[1])

    def scan_step(running, seq_items):
        block_in, block_cot, block_starts = seq_items

        def forward(block, *weights):
            return layer(block, *weights, block_starts)
        result, pullback = jax.vjp(forward, block_in, *parameters)
        gradients = pullback(block_cot)
        running = tuple(((total + addend).astype(jnp.float32) for total, addend in zip(running, gradients[1:])))
        return (running, (result.astype(jnp.bfloat16), gradients[0].astype(jnp.bfloat16)))
    zero_sums = tuple((jnp.zeros(weight.shape, jnp.float32) for weight in parameters))
    running, (out_blocks, grad_blocks) = lax.scan(scan_step, zero_sums, (inputs, cotangents, starts))
    layer_out = out_blocks.reshape(layer_in.shape)
    in_grad = grad_blocks.reshape(layer_in.shape)
    return (layer_out, in_grad, running[4], running[5], running[6], running[7], running[8], running[9], running[10], running[0], running[1], running[2], running[3])
```

```python
import functools

import jax
import jax.numpy as jnp
from jax import lax
from jax.experimental import pallas as pl
from jax.experimental.pallas import tpu as pltpu
from jax.sharding import PartitionSpec as P

H = 8
KV = 4
HD = 256
L = 1024
PIECE = 256

EPS = 1e-06
CAP = 50.0
F32 = jnp.float32
BF16 = jnp.bfloat16
MESH = pl.DeviceIdType.MESH
ANY = pl.BlockSpec(memory_space=pl.ANY)
VM = pl.BlockSpec(memory_space=pltpu.VMEM)
SM = pl.BlockSpec(memory_space=pltpu.SMEM)
ROWS = 16
TILE = 256


def dot_nn(a, b):
    return lax.dot_general(a, b, (((1,), (0,)), ((), ())), preferred_element_type=F32)


def dot_nt(a, b):
    return lax.dot_general(a, b, (((1,), (1,)), ((), ())), preferred_element_type=F32)


def dot_tn(a, b):
    return lax.dot_general(a, b, (((0,), (0,)), ((), ())), preferred_element_type=F32)


def tile_of(width):
    return next(t for t in (256, 384, 128) if width % t == 0)


def loop(count, body):
    lax.fori_loop(0, count, lambda t, c: (body(t), c)[1], 0)


def block_at(i, n, s):
    m = jnp.minimum(i, n - 1 - i)
    near = i + jnp.where(s % 2 == 1, -((s + 1) // 2), s // 2)
    far = jnp.where(i * 2 < n, i + (s - m), i - (s - m))
    return jnp.where(s <= 2 * m, near, far)


def line_barrier(i, n):
    barrier = pltpu.get_barrier_semaphore()

    @pl.when(i > 0)
    def _():
        pl.semaphore_signal(barrier, 1, device_id={"tensor": i - 1}, device_id_type=MESH)

    @pl.when(i < n - 1)
    def _():
        pl.semaphore_signal(barrier, 1, device_id={"tensor": i + 1}, device_id_type=MESH)

    pl.semaphore_wait(barrier, jnp.minimum(i, 1) + jnp.minimum(n - 1 - i, 1))


def gather_line(i, n, held, send, recv, compute):
    def copy(block, way, s, to):
        return pltpu.make_async_remote_copy(
            held.at[block],
            held.at[block],
            send.at[way, s],
            recv.at[block],
            device_id={"tensor": to},
            device_id_type=MESH,
        )

    up, down = jnp.minimum(i + 1, n - 1), jnp.maximum(i - 1, 0)

    def step(s):
        low, high = i - s, i + s

        @pl.when((s > 0) & (low >= 0))
        def _():
            copy(low, 0, s, up).wait_recv()

        @pl.when((low >= 0) & (i < n - 1))
        def _():
            copy(low, 0, s, up).start()

        @pl.when((s > 0) & (high < n))
        def _():
            copy(high, 1, s, down).wait_recv()

        @pl.when((high < n) & (i > 0))
        def _():
            copy(high, 1, s, down).start()

        compute(s, block_at(i, n, s))

    loop(n, step)

    def finish(s):
        low, high = i - s, i + s

        @pl.when((low >= 0) & (i < n - 1))
        def _():
            copy(low, 0, s, up).wait_send()

        @pl.when((high < n) & (i > 0))
        def _():
            copy(high, 1, s, down).wait_send()

    loop(n, finish)


def scatter_line(i, n, part, landed, send, recv, compute, own):
    rows = part.shape[1]

    def copy(block, way, t, to):
        slot = jnp.where(block == to, n, block) if way else block
        return pltpu.make_async_remote_copy(
            part.at[block],
            landed.at[slot],
            send.at[way, t],
            recv.at[slot],
            device_id={"tensor": to},
            device_id_type=MESH,
        )

    def arrived(slot):
        pltpu.make_async_remote_copy(
            landed.at[slot],
            landed.at[slot],
            send.at[0, 0],
            recv.at[slot],
            device_id={"tensor": i},
            device_id_type=MESH,
        ).wait_recv()

    def add(block):
        def chunk(c):
            r = pl.ds(c * ROWS, ROWS)
            total = part[block, r, :].astype(F32) + landed[block, r, :].astype(F32)
            part[block, r, :] = total.astype(BF16)

        loop(rows // ROWS, chunk)

    up, down = jnp.minimum(i + 1, n - 1), jnp.maximum(i - 1, 0)

    def step(k):
        t = k + 1
        compute(k, block_at(i, n, n - t))
        above, below = i + n - t, i - n + t

        @pl.when((above < n) & (i > 0))
        def _():
            arrived(above)
            add(above)

        @pl.when(above < n)
        def _():
            copy(above, 0, t, up).start()

        @pl.when((below >= 0) & (i < n - 1))
        def _():
            arrived(below)
            add(below)

        @pl.when(below >= 0)
        def _():
            copy(below, 1, t, down).start()

    loop(n - 1, step)
    own(n - 1)

    @pl.when(i > 0)
    def _():
        arrived(i)

    @pl.when(i < n - 1)
    def _():
        arrived(jnp.int32(n))

    def finish(k):
        t = k + 1

        @pl.when(i + n - t < n)
        def _():
            copy(i + n - t, 0, t, up).wait_send()

        @pl.when(i - n + t >= 0)
        def _():
            copy(i - n + t, 1, t, down).wait_send()

    return functools.partial(loop, n - 1, finish)


def summed_rows(i, n, mine, landed, r):
    zero = jnp.zeros((), F32)
    low = jnp.where(i > 0, landed[i, r, :].astype(F32), zero)
    high = jnp.where(i < n - 1, landed[n, r, :].astype(F32), zero)
    return mine[r, :] + low + high


def inverse_rms(v):
    return lax.rsqrt(jnp.mean(v * v, axis=-1, keepdims=True) + EPS)


def norm_back(e, v, r):
    unit = v * r
    return r * (e - unit * jnp.mean(e * unit, axis=-1, keepdims=True))


def fold_rows(v):
    return v.reshape(-1, 8, v.shape[-1]).sum(axis=0)


class Feed:
    def __init__(self, sources, slots, sems, which):
        self.sources, self.slots, self.sems, self.which = sources, slots, sems, which

    def copies(self, s):
        return [
            pltpu.make_async_copy(src.at[self.which(s)], slot.at[s % 2], self.sems.at[k, s % 2])
            for k, (src, slot) in enumerate(zip(self.sources, self.slots))
        ]

    def start(self, s):
        for c in self.copies(s):
            c.start()

    def wait(self, s):
        for c in self.copies(s):
            c.wait()

    def advance(self, s, count):
        self.wait(s)

        @pl.when(s + 1 < count)
        def _():
            self.start(s + 1)


class Drain:
    def __init__(self, targets, slots, sems, which):
        self.targets, self.slots, self.sems, self.which = targets, slots, sems, which

    def copies(self, s):
        return [
            pltpu.make_async_copy(slot.at[s % 2], dst.at[self.which(s)], self.sems.at[k, s % 2])
            for k, (dst, slot) in enumerate(zip(self.targets, self.slots))
        ]

    def free(self, s):
        @pl.when(s >= 2)
        def _():
            for c in self.copies(s - 2):
                c.wait()

    def start(self, s):
        for c in self.copies(s):
            c.start()

    def finish(self, count):
        for s in range(max(0, count - 2), count):
            for c in self.copies(jnp.int32(s)):
                c.wait()


def line_scratch(n):
    return [pltpu.SemaphoreType.DMA((2, n)), pltpu.SemaphoreType.DMA((n + 1,))]


def params(cid, mib):
    return pltpu.CompilerParams(
        collective_id=cid, has_side_effects=True, vmem_limit_bytes=mib << 20
    )


def cost(flops, moved):
    return pl.CostEstimate(flops=flops, bytes_accessed=moved, transcendentals=0)


def gains_kernel(m, mine, out, send, recv):
    me = lax.axis_index("dp")
    barrier = pltpu.get_barrier_semaphore()
    for k in range(1, m):
        pl.semaphore_signal(
            barrier, 1, device_id={"dp": lax.rem(me + k, m)}, device_id_type=MESH
        )
    pl.semaphore_wait(barrier, m - 1)

    def copy(owner, k):
        return pltpu.make_async_remote_copy(
            mine,
            out.at[owner],
            send.at[k],
            recv.at[k],
            device_id={"dp": lax.rem(me + k, m)},
            device_id_type=MESH,
        )

    for k in range(1, m):
        copy(me, k).start()
    out[me] = mine[...]
    for k in range(1, m):
        copy(lax.rem(me + m - k, m), k).wait_recv()
    for k in range(1, m):
        copy(me, k).wait_send()


def gather_gains(m, mine):
    return pl.pallas_call(
        functools.partial(gains_kernel, m),
        out_shape=jax.ShapeDtypeStruct((m,) + mine.shape, mine.dtype),
        in_specs=[VM],
        out_specs=VM,
        scratch_shapes=[pltpu.SemaphoreType.DMA((m,)), pltpu.SemaphoreType.DMA((m,))],
        compiler_params=params(0, 16),
        name="gains",
    )(mine)


def sum_gains_kernel(n, m, mine, out, landed, total, across, send, recv, send_two, recv_two):
    me, i = lax.axis_index("dp"), lax.axis_index("tensor")
    barrier = pltpu.get_barrier_semaphore()
    dp_peer = lambda k: {"dp": lax.rem(me + k, m)}
    line_peer = lambda k: {"tensor": lax.rem(i + k, n)}
    for k in range(1, m):
        pl.semaphore_signal(barrier, 1, device_id=dp_peer(k), device_id_type=MESH)
    for k in range(1, n):
        pl.semaphore_signal(barrier, 1, device_id=line_peer(k), device_id_type=MESH)
    pl.semaphore_wait(barrier, m + n - 2)

    def to_owner(k):
        return pltpu.make_async_remote_copy(
            mine.at[lax.rem(me + k, m)], landed.at[k], send.at[k], recv.at[k],
            device_id=dp_peer(k), device_id_type=MESH,
        )

    def along(k):
        return pltpu.make_async_remote_copy(
            total, across.at[k], send_two.at[k], recv_two.at[k],
            device_id=line_peer(k), device_id_type=MESH,
        )

    for k in range(1, m):
        to_owner(k).start()
    here = mine[me]
    for k in range(1, m):
        to_owner(k).wait_recv()
        here = here + landed[k]
    total[...] = here
    for k in range(1, n):
        along(k).start()
    for k in range(1, n):
        along(k).wait_recv()
        here = here + across[k]
    out[...] = here
    for k in range(1, m):
        to_owner(k).wait_send()
    for k in range(1, n):
        along(k).wait_send()


def sum_gains(n, m, mine):
    shape = mine.shape[1:]
    return pl.pallas_call(
        functools.partial(sum_gains_kernel, n, m),
        out_shape=jax.ShapeDtypeStruct(shape, F32),
        in_specs=[VM],
        out_specs=VM,
        scratch_shapes=[
            pltpu.VMEM((m,) + shape, F32),
            pltpu.VMEM(shape, F32),
            pltpu.VMEM((n,) + shape, F32),
        ]
        + [pltpu.SemaphoreType.DMA((m,))] * 2
        + [pltpu.SemaphoreType.DMA((n,))] * 2,
        compiler_params=params(6, 16),
        name="sum_gains",
    )(mine)


def first_kernel(n, x, gains, full, held, send, recv, out_sem):
    i = lax.axis_index("tensor")
    rows = x.shape[0]
    line_barrier(i, n)
    scale = 1.0 + gains[0:1, :]

    def chunk(c):
        r = pl.ds(c * ROWS, ROWS)
        v = x[r, :].astype(F32)
        held[i, r, :] = (v * inverse_rms(v) * scale).astype(BF16)

    loop(rows // ROWS, chunk)

    def keep(s, block):
        pltpu.make_async_copy(held.at[block], full.at[block], out_sem.at[s]).start()

    gather_line(i, n, held, send, recv, keep)

    def finish(s):
        block = block_at(i, n, s)
        pltpu.make_async_copy(held.at[block], full.at[block], out_sem.at[s]).wait()

    loop(n, finish)


def first(n, x, gains):
    rows, width = x.shape
    return pl.pallas_call(
        functools.partial(first_kernel, n),
        out_shape=jax.ShapeDtypeStruct((n, rows, width), BF16),
        in_specs=[VM, VM],
        out_specs=ANY,
        scratch_shapes=[pltpu.VMEM((n, rows, width), BF16)]
        + line_scratch(n)
        + [pltpu.SemaphoreType.DMA((n,))],
        compiler_params=params(1, 32),
        cost_estimate=cost(0, 300 << 20),
        name="first",
    )(x, gains)


def turn(u, cos, sin):
    half = HD // 2
    a, b = u[:, :half], u[:, half:]
    return jnp.concatenate([a * cos - b * sin, b * cos + a * sin], axis=-1)


def row_limit(starts, seq, first_row, rows):
    pos = first_row + lax.broadcasted_iota(jnp.int32, (rows, 1), 0)
    limit = pos + 1
    for piece in range(2):
        begin = starts[seq, piece]
        inside = (pos >= begin) & (pos < begin + PIECE)
        limit = jnp.maximum(limit, jnp.where(inside, begin + PIECE, 0))
    return limit


def key_span(first_row, rows):
    return min(L, first_row + rows + PIECE)


def weights_of(q, k, limit):
    bent = jnp.tanh(dot_nt(q, k) * (1.0 / CAP))
    seen = lax.broadcasted_iota(jnp.int32, (1, k.shape[0]), 1) < limit
    w = jnp.where(seen, jnp.exp(CAP * bent), 0.0)
    return w * pl.reciprocal(jnp.sum(w, axis=-1, keepdims=True)), bent


def attend_kernel(heads, kvs, starts, h1, w, cos, sin, q_out, k_out, v_out, o_out):
    tokens = h1.shape[0]
    fan = heads // kvs
    block = 256

    def project(b):
        r = pl.ds(pl.multiple_of(b * block, block), block)
        at = pl.ds(pl.multiple_of(lax.rem(b * block, L), block), block)
        c, s = cos[at, :], sin[at, :]
        x = h1[r, :]
        for h in range(heads):
            u = dot_nn(x, w[:, h * HD : (h + 1) * HD])
            q_out[h, r, :] = (turn(u, c, s) * (HD**-0.5)).astype(BF16)
        for g in range(kvs):
            u = dot_nn(x, w[:, (heads + g) * HD : (heads + g + 1) * HD])
            k_out[g, r, :] = turn(u, c, s).astype(BF16)
            u = dot_nn(x, w[:, (heads + kvs + g) * HD : (heads + kvs + g + 1) * HD])
            v_out[g, r, :] = u.astype(BF16)

    loop(tokens // block, project)
    for seq in range(tokens // L):
        base = seq * L
        for row in range(0, L, block):
            span = key_span(row, block)
            limit = row_limit(starts, seq, row, block)
            for h in range(heads):
                q = q_out[h, base + row : base + row + block, :]
                p, _ = weights_of(q, k_out[h // fan, base : base + span, :], limit)
                o = dot_nn(p.astype(BF16), v_out[h // fan, base : base + span, :])
                o_out[base + row : base + row + block, h * HD : (h + 1) * HD] = o.astype(BF16)


def attend(heads, kvs, starts, h1, w, cos, sin):
    tokens = h1.shape[0]
    return pl.pallas_call(
        functools.partial(attend_kernel, heads, kvs),
        out_shape=[
            jax.ShapeDtypeStruct((heads, tokens, HD), BF16),
            jax.ShapeDtypeStruct((kvs, tokens, HD), BF16),
            jax.ShapeDtypeStruct((kvs, tokens, HD), BF16),
            jax.ShapeDtypeStruct((tokens, heads * HD), BF16),
        ],
        in_specs=[SM, VM, VM, VM, VM],
        out_specs=[VM, VM, VM, VM],
        compiler_params=pltpu.CompilerParams(vmem_limit_bytes=48 << 20),
        cost_estimate=cost(20 << 30, 20 << 20),
        name="attend",
    )(starts, h1, w, cos, sin)


def attend_back_kernel(heads, kvs, starts, q_in, k_in, v_in, do_in, cos, sin, out, dk, dv):
    tokens = q_in.shape[1]
    fan = heads // kvs
    block = 256
    for seq in range(tokens // L):
        base = seq * L
        for g in range(kvs):
            dk[...] = jnp.zeros_like(dk)
            dv[...] = jnp.zeros_like(dv)
            for row in range(0, L, block):
                span = key_span(row, block)
                limit = row_limit(starts, seq, row, block)
                k = k_in[g, base : base + span, :]
                v = v_in[g, base : base + span, :]
                at = slice(base + row, base + row + block)
                for h in range(g * fan, (g + 1) * fan):
                    q = q_in[h, at, :]
                    do = do_in[at, h * HD : (h + 1) * HD]
                    p, bent = weights_of(q, k, limit)
                    dp = dot_nt(do, v)
                    delta = jnp.sum(p * dp, axis=-1, keepdims=True)
                    ds = (p * (dp - delta) * (1.0 - bent * bent)).astype(BF16)
                    dq = dot_nn(ds, k)
                    c, s = cos[row : row + block, :], sin[row : row + block, :]
                    out[at, h * HD : (h + 1) * HD] = (turn(dq, c, -s) * (HD**-0.5)).astype(BF16)
                    dk[:span, :] += dot_tn(ds, q)
                    dv[:span, :] += dot_tn(p.astype(BF16), do)

            def close(b, g=g, base=base):
                r = pl.ds(pl.multiple_of(b * block, block), block)
                to = pl.ds(pl.multiple_of(base + b * block, block), block)
                back = turn(dk[r, :], cos[r, :], -sin[r, :])
                out[to, (heads + g) * HD : (heads + g + 1) * HD] = back.astype(BF16)
                left = (heads + kvs + g) * HD
                out[to, left : left + HD] = dv[r, :].astype(BF16)

            loop(L // block, close)


def attend_back(heads, kvs, starts, q, k, v, do, cos, sin):
    tokens = q.shape[1]
    return pl.pallas_call(
        functools.partial(attend_back_kernel, heads, kvs),
        out_shape=jax.ShapeDtypeStruct((tokens, (heads + 2 * kvs) * HD), BF16),
        in_specs=[SM, VM, VM, VM, VM, VM, VM],
        out_specs=VM,
        scratch_shapes=[pltpu.VMEM((L, HD), F32), pltpu.VMEM((L, HD), F32)],
        compiler_params=pltpu.CompilerParams(vmem_limit_bytes=48 << 20),
        cost_estimate=cost(30 << 30, 20 << 20),
        name="attend_back",
    )(starts, q, k, v, do, cos, sin)


def into_feed_kernel(
    n, x, gains, o_hbm, wo_hbm, wg_hbm, wu_hbm,
    attn_out, y_out, h3_full, hid_out, up_out, ge_out,
    o, wo, wg, wu, part, landed, mine, held, hid_s, up_s, ge_s,
    load, rs_send, rs_recv, ag_send, ag_recv, keep_sem, out_sem,
):
    i = lax.axis_index("tensor")
    rows, width = x.shape
    loads = [
        pltpu.make_async_copy(src, dst, load.at[k])
        for k, (src, dst) in enumerate(((o_hbm, o), (wo_hbm, wo), (wg_hbm, wg), (wu_hbm, wu)))
    ]
    for c in loads:
        c.start()
    line_barrier(i, n)
    loads[0].wait()
    loads[1].wait()

    def compute(t, block):
        def tile(k):
            at = pl.ds(pl.multiple_of(k * TILE, TILE), TILE)
            part[block, :, at] = dot_nt(o[block], wo[at, :]).astype(BF16)

        loop(width // TILE, tile)

    def own(t):
        def tile(k):
            at = pl.ds(pl.multiple_of(k * TILE, TILE), TILE)
            mine[:, at] = dot_nt(o[i], wo[at, :])

        loop(width // TILE, tile)

    done = scatter_line(i, n, part, landed, rs_send, rs_recv, compute, own)
    scale_two, scale_three = 1.0 + gains[1:2, :], 1.0 + gains[2:3, :]

    def chunk(c):
        r = pl.ds(c * ROWS, ROWS)
        attn = summed_rows(i, n, mine, landed, r)
        attn_out[r, :] = attn
        y = x[r, :].astype(F32) + attn * inverse_rms(attn) * scale_two
        y_out[r, :] = y
        held[i, r, :] = (y * inverse_rms(y) * scale_three).astype(BF16)

    loop(rows // ROWS, chunk)
    done()
    loads[2].wait()
    loads[3].wait()
    drain = Drain(
        (hid_out, up_out, ge_out), (hid_s, up_s, ge_s), out_sem, lambda s: block_at(i, n, s)
    )

    def forward(s, block):
        pltpu.make_async_copy(held.at[block], h3_full.at[block], keep_sem.at[s]).start()
        drain.free(s)
        slot = s % 2
        span = tile_of(wg.shape[1])

        def tile(k):
            at = pl.ds(pl.multiple_of(k * span, span), span)
            u = dot_nn(held[block], wg[:, at])
            up = dot_nn(held[block], wu[:, at])
            c = 0.7978845608028654
            th = jnp.tanh(c * (u + 0.044715 * (u * u * u)))
            half = 0.5 * (1.0 + th)
            gelu = u * half
            slope = half + 0.5 * u * (1.0 - th * th) * (c * (1.0 + 0.134145 * (u * u)))
            hid_s[slot, :, at] = (gelu * up).astype(BF16)
            up_s[slot, :, at] = (up * slope).astype(BF16)
            ge_s[slot, :, at] = gelu.astype(BF16)

        loop(wg.shape[1] // span, tile)
        drain.start(s)

    gather_line(i, n, held, ag_send, ag_recv, forward)
    drain.finish(n)

    def finish(s):
        block = block_at(i, n, s)
        pltpu.make_async_copy(held.at[block], h3_full.at[block], keep_sem.at[s]).wait()

    loop(n, finish)


def into_feed(n, x, gains, o, wo, wg, wu):
    rows, width = x.shape
    wide = wg.shape[1]
    blocks = lambda w: jax.ShapeDtypeStruct((n, rows, w), BF16)
    mine = jax.ShapeDtypeStruct((rows, width), F32)
    return pl.pallas_call(
        functools.partial(into_feed_kernel, n),
        out_shape=[mine, mine, blocks(width), blocks(wide), blocks(wide), blocks(wide)],
        in_specs=[VM, VM, ANY, ANY, ANY, ANY],
        out_specs=[VM, VM, ANY, ANY, ANY, ANY],
        scratch_shapes=[
            pltpu.VMEM(o.shape, BF16),
            pltpu.VMEM(wo.shape, BF16),
            pltpu.VMEM(wg.shape, BF16),
            pltpu.VMEM(wu.shape, BF16),
            pltpu.VMEM((n, rows, width), BF16),
            pltpu.VMEM((n + 1, rows, width), BF16),
            pltpu.VMEM((rows, width), F32),
            pltpu.VMEM((n, rows, width), BF16),
        ]
        + [pltpu.VMEM((2, rows, wide), BF16)] * 3
        + [pltpu.SemaphoreType.DMA((4,))]
        + line_scratch(n) * 2
        + [pltpu.SemaphoreType.DMA((n,)), pltpu.SemaphoreType.DMA((3, 2))],
        compiler_params=params(2, 62),
        cost_estimate=cost(0, 600 << 20),
        name="into_feed",
    )(x, gains, o, wo, wg, wu)


def turn_feed_kernel(
    n, y, dout, gains, hid_hbm, wd_hbm, up_hbm, ge_hbm,
    layer_out, gain_out, df_full, dgate_out, dup_out,
    wd, hid_s, part, landed, mine, held, up_s, ge_s, dg_s, du_s, fold,
    load, feed_sem, rs_send, rs_recv, ag_send, ag_recv, keep_sem, back_sem, out_sem,
):
    i = lax.axis_index("tensor")
    rows, width = y.shape
    whole = pltpu.make_async_copy(wd_hbm, wd, load.at[0])
    whole.start()
    feed = Feed((hid_hbm,), (hid_s,), feed_sem, lambda s: block_at(i, n, n - 1 - s))
    feed.start(jnp.int32(0))
    line_barrier(i, n)
    whole.wait()

    def compute(t, block):
        feed.advance(t, n)
        slot = t % 2

        def tile(k):
            at = pl.ds(pl.multiple_of(k * TILE, TILE), TILE)
            part[block, :, at] = dot_nt(hid_s[slot], wd[at, :]).astype(BF16)

        loop(width // TILE, tile)

    def own(t):
        t = jnp.int32(t)
        feed.advance(t, n)
        slot = t % 2

        def tile(k):
            at = pl.ds(pl.multiple_of(k * TILE, TILE), TILE)
            mine[:, at] = dot_nt(hid_s[slot], wd[at, :])

        loop(width // TILE, tile)

    done = scatter_line(i, n, part, landed, rs_send, rs_recv, compute, own)
    scale = 1.0 + gains[3:4, :]
    fold[...] = jnp.zeros_like(fold)

    def chunk(c):
        r = pl.ds(c * ROWS, ROWS)
        f = summed_rows(i, n, mine, landed, r)
        g = dout[r, :].astype(F32)
        inv = inverse_rms(f)
        layer_out[r, :] = (y[r, :] + f * inv * scale).astype(BF16)
        held[i, r, :] = norm_back(g * scale, f, inv).astype(BF16)
        fold[...] += fold_rows(g * (f * inv))

    loop(rows // ROWS, chunk)
    gain_out[...] = jnp.sum(fold[...], axis=0, keepdims=True)
    done()
    sides = Feed((up_hbm, ge_hbm), (up_s, ge_s), back_sem, lambda s: block_at(i, n, s))
    drain = Drain((dgate_out, dup_out), (dg_s, du_s), out_sem, lambda s: block_at(i, n, s))
    sides.start(jnp.int32(0))

    def backward(s, block):
        pltpu.make_async_copy(held.at[block], df_full.at[block], keep_sem.at[s]).start()
        sides.advance(s, n)
        drain.free(s)
        slot = s % 2
        span = tile_of(wd.shape[1])

        def tile(k):
            at = pl.ds(pl.multiple_of(k * span, span), span)
            dhid = dot_nn(held[block], wd[:, at])
            dg_s[slot, :, at] = (dhid * up_s[slot, :, at].astype(F32)).astype(BF16)
            du_s[slot, :, at] = (dhid * ge_s[slot, :, at].astype(F32)).astype(BF16)

        loop(wd.shape[1] // span, tile)
        drain.start(s)

    gather_line(i, n, held, ag_send, ag_recv, backward)
    drain.finish(n)

    def finish(s):
        block = block_at(i, n, s)
        pltpu.make_async_copy(held.at[block], df_full.at[block], keep_sem.at[s]).wait()

    loop(n, finish)


def turn_feed(n, y, dout, gains, hid, wd, up, ge):
    rows, width = y.shape
    wide = wd.shape[1]
    blocks = lambda w: jax.ShapeDtypeStruct((n, rows, w), BF16)
    return pl.pallas_call(
        functools.partial(turn_feed_kernel, n),
        out_shape=[
            jax.ShapeDtypeStruct((rows, width), BF16),
            jax.ShapeDtypeStruct((1, width), F32),
            blocks(width),
            blocks(wide),
            blocks(wide),
        ],
        in_specs=[VM, VM, VM, ANY, ANY, ANY, ANY],
        out_specs=[VM, VM, ANY, ANY, ANY],
        scratch_shapes=[
            pltpu.VMEM(wd.shape, BF16),
            pltpu.VMEM((2, rows, wide), BF16),
            pltpu.VMEM((n, rows, width), BF16),
            pltpu.VMEM((n + 1, rows, width), BF16),
            pltpu.VMEM((rows, width), F32),
            pltpu.VMEM((n, rows, width), BF16),
        ]
        + [pltpu.VMEM((2, rows, wide), BF16)] * 4
        + [pltpu.VMEM((8, width), F32)]
        + [pltpu.SemaphoreType.DMA((1,)), pltpu.SemaphoreType.DMA((1, 2))]
        + line_scratch(n) * 2
        + [
            pltpu.SemaphoreType.DMA((n,)),
            pltpu.SemaphoreType.DMA((2, 2)),
            pltpu.SemaphoreType.DMA((2, 2)),
        ],
        compiler_params=params(3, 62),
        cost_estimate=cost(0, 600 << 20),
        name="turn_feed",
    )(y, dout, gains, hid, wd, up, ge)


def out_of_feed_kernel(
    n, y, attn, dout, gains, dgate_hbm, dup_hbm, wg_hbm, wu_hbm, wo_hbm,
    dy_out, gain_out, dattn_full, do_out,
    wg, wu, wo, dg_s, du_s, part, landed, mine, held, do_s, fold,
    load, feed_sem, rs_send, rs_recv, ag_send, ag_recv, keep_sem, out_sem,
):
    i = lax.axis_index("tensor")
    rows, width = y.shape
    loads = [
        pltpu.make_async_copy(src, dst, load.at[k])
        for k, (src, dst) in enumerate(((wg_hbm, wg), (wu_hbm, wu), (wo_hbm, wo)))
    ]
    for c in loads:
        c.start()
    feed = Feed((dgate_hbm, dup_hbm), (dg_s, du_s), feed_sem, lambda s: block_at(i, n, n - 1 - s))
    feed.start(jnp.int32(0))
    line_barrier(i, n)
    loads[0].wait()
    loads[1].wait()

    def product(slot, at):
        return dot_nt(dg_s[slot], wg[at, :]) + dot_nt(du_s[slot], wu[at, :])

    def compute(t, block):
        feed.advance(t, n)
        slot = t % 2

        def tile(k):
            at = pl.ds(pl.multiple_of(k * TILE, TILE), TILE)
            part[block, :, at] = product(slot, at).astype(BF16)

        loop(width // TILE, tile)

    def own(t):
        t = jnp.int32(t)
        feed.advance(t, n)
        slot = t % 2

        def tile(k):
            at = pl.ds(pl.multiple_of(k * TILE, TILE), TILE)
            mine[:, at] = product(slot, at)

        loop(width // TILE, tile)

    done = scatter_line(i, n, part, landed, rs_send, rs_recv, compute, own)
    scale_two, scale_three = 1.0 + gains[1:2, :], 1.0 + gains[2:3, :]
    fold[...] = jnp.zeros_like(fold)

    def chunk(c):
        r = pl.ds(c * ROWS, ROWS)
        dh3 = summed_rows(i, n, mine, landed, r)
        v = y[r, :]
        inv = inverse_rms(v)
        dy = dout[r, :].astype(F32) + norm_back(dh3 * scale_three, v, inv)
        dy_out[r, :] = dy
        fold[1] += fold_rows(dh3 * (v * inv))
        a = attn[r, :]
        inv = inverse_rms(a)
        held[i, r, :] = norm_back(dy * scale_two, a, inv).astype(BF16)
        fold[0] += fold_rows(dy * (a * inv))

    loop(rows // ROWS, chunk)
    gain_out[0:1, :] = jnp.sum(fold[0], axis=0, keepdims=True)
    gain_out[1:2, :] = jnp.sum(fold[1], axis=0, keepdims=True)
    done()
    loads[2].wait()
    drain = Drain((do_out,), (do_s,), out_sem, lambda s: block_at(i, n, s))

    def backward(s, block):
        pltpu.make_async_copy(held.at[block], dattn_full.at[block], keep_sem.at[s]).start()
        drain.free(s)
        do_s[s % 2] = dot_nn(held[block], wo[...]).astype(BF16)
        drain.start(s)

    gather_line(i, n, held, ag_send, ag_recv, backward)
    drain.finish(n)

    def finish(s):
        block = block_at(i, n, s)
        pltpu.make_async_copy(held.at[block], dattn_full.at[block], keep_sem.at[s]).wait()

    loop(n, finish)


def out_of_feed(n, y, attn, dout, gains, dgate, dup, wg, wu, wo):
    rows, width = y.shape
    wide = wg.shape[1]
    narrow = wo.shape[1]
    return pl.pallas_call(
        functools.partial(out_of_feed_kernel, n),
        out_shape=[
            jax.ShapeDtypeStruct((rows, width), F32),
            jax.ShapeDtypeStruct((2, width), F32),
            jax.ShapeDtypeStruct((n, rows, width), BF16),
            jax.ShapeDtypeStruct((n, rows, narrow), BF16),
        ],
        in_specs=[VM, VM, VM, VM, ANY, ANY, ANY, ANY, ANY],
        out_specs=[VM, VM, ANY, ANY],
        scratch_shapes=[
            pltpu.VMEM(wg.shape, BF16),
            pltpu.VMEM(wu.shape, BF16),
            pltpu.VMEM(wo.shape, BF16),
            pltpu.VMEM((2, rows, wide), BF16),
            pltpu.VMEM((2, rows, wide), BF16),
            pltpu.VMEM((n, rows, width), BF16),
            pltpu.VMEM((n + 1, rows, width), BF16),
            pltpu.VMEM((rows, width), F32),
            pltpu.VMEM((n, rows, width), BF16),
            pltpu.VMEM((2, rows, narrow), BF16),
            pltpu.VMEM((2, 8, width), F32),
        ]
        + [pltpu.SemaphoreType.DMA((3,)), pltpu.SemaphoreType.DMA((2, 2))]
        + line_scratch(n) * 2
        + [pltpu.SemaphoreType.DMA((n,)), pltpu.SemaphoreType.DMA((1, 2))],
        compiler_params=params(4, 62),
        cost_estimate=cost(0, 600 << 20),
        name="out_of_feed",
    )(y, attn, dout, gains, dgate, dup, wg, wu, wo)


def last_kernel(
    n, x, dy, gains, d_hbm, w_hbm, in_grad, gain_out,
    d, w, part, landed, mine, fold, load, rs_send, rs_recv,
):
    i = lax.axis_index("tensor")
    rows, width = x.shape
    loads = [
        pltpu.make_async_copy(src, dst, load.at[k])
        for k, (src, dst) in enumerate(((d_hbm, d), (w_hbm, w)))
    ]
    for c in loads:
        c.start()
    line_barrier(i, n)
    for c in loads:
        c.wait()

    def compute(t, block):
        def tile(k):
            at = pl.ds(pl.multiple_of(k * TILE, TILE), TILE)
            part[block, :, at] = dot_nt(d[block], w[at, :]).astype(BF16)

        loop(width // TILE, tile)

    def own(t):
        def tile(k):
            at = pl.ds(pl.multiple_of(k * TILE, TILE), TILE)
            mine[:, at] = dot_nt(d[i], w[at, :])

        loop(width // TILE, tile)

    done = scatter_line(i, n, part, landed, rs_send, rs_recv, compute, own)
    scale = 1.0 + gains[0:1, :]
    fold[...] = jnp.zeros_like(fold)

    def chunk(c):
        r = pl.ds(c * ROWS, ROWS)
        dh1 = summed_rows(i, n, mine, landed, r)
        v = x[r, :].astype(F32)
        inv = inverse_rms(v)
        in_grad[r, :] = (dy[r, :] + norm_back(dh1 * scale, v, inv)).astype(BF16)
        fold[...] += fold_rows(dh1 * (v * inv))

    loop(rows // ROWS, chunk)
    gain_out[...] = jnp.sum(fold[...], axis=0, keepdims=True)
    done()


def last(n, x, dy, gains, d, w):
    rows, width = x.shape
    return pl.pallas_call(
        functools.partial(last_kernel, n),
        out_shape=[
            jax.ShapeDtypeStruct((rows, width), BF16),
            jax.ShapeDtypeStruct((1, width), F32),
        ],
        in_specs=[VM, VM, VM, ANY, ANY],
        out_specs=[VM, VM],
        scratch_shapes=[
            pltpu.VMEM(d.shape, BF16),
            pltpu.VMEM(w.shape, BF16),
            pltpu.VMEM((n, rows, width), BF16),
            pltpu.VMEM((n + 1, rows, width), BF16),
            pltpu.VMEM((rows, width), F32),
            pltpu.VMEM((8, width), F32),
            pltpu.SemaphoreType.DMA((2,)),
        ]
        + line_scratch(n),
        compiler_params=params(5, 48),
        cost_estimate=cost(0, 300 << 20),
        name="last",
    )(x, dy, gains, d, w)


def rope_tables():
    positions = jnp.arange(L, dtype=jnp.int32).astype(F32)
    exponent = jnp.arange(HD // 2, dtype=jnp.int32).astype(F32) * (-2.0 / HD)
    angles = positions[:, None] * jnp.exp(exponent * jnp.log(F32(10000.0)))[None, :]
    return jnp.cos(angles), jnp.sin(angles)


def weight_grad(left, right):
    return dot_tn(left, right).astype(BF16)


def scatter_rows(grad):
    return lax.psum_scatter(grad, "dp", scatter_dimension=0, tiled=True)


def body(
    n,
    m,
    layer_in,
    out_grad,
    piece_starts,
    attn_gain,
    attn_out_gain,
    feed_gain,
    feed_out_gain,
    query_weight,
    key_weight,
    value_weight,
    out_weight,
    gate_weight,
    up_weight,
    down_weight,
):
    heads = query_weight.shape[1] // HD
    fan = H // KV
    kvs = max(1, heads // fan)
    rank = lax.axis_index("tensor")
    kv_at = (rank * heads // fan) * HD
    rows, width = layer_in.shape
    tokens = n * rows

    gathered = gather_gains(m, jnp.stack([attn_gain, attn_out_gain, feed_gain, feed_out_gain]))
    gains = gathered.transpose(1, 0, 2).reshape(4, width).astype(F32)

    def collect(shard):
        return lax.all_gather(shard, "dp", axis=0, tiled=True)

    wqkv = collect(
        jnp.concatenate(
            [
                query_weight,
                lax.dynamic_slice_in_dim(key_weight, kv_at, kvs * HD, 1),
                lax.dynamic_slice_in_dim(value_weight, kv_at, kvs * HD, 1),
            ],
            axis=1,
        )
    )
    wo = collect(out_weight.T)
    wg = collect(gate_weight)
    wu = collect(up_weight)
    wd = collect(down_weight.T)
    cos, sin = rope_tables()

    h1 = first(n, layer_in, gains)
    h1_flat = h1.reshape(tokens, width)
    q, k, v, o = attend(heads, kvs, piece_starts, h1_flat, wqkv, cos, sin)
    attn, y, h3, hid, up, ge = into_feed(
        n, layer_in, gains, o.reshape(n, rows, heads * HD), wo, wg, wu
    )
    layer_out, gain_four, df, dgate, dup = turn_feed(n, y, out_grad, gains, hid, wd, up, ge)
    flat = lambda a: a.reshape(tokens, a.shape[-1])
    tie = lax.optimization_barrier
    down_part = weight_grad(flat(df), flat(hid))
    gate_part = weight_grad(flat(h3), flat(dgate))
    up_part = weight_grad(flat(h3), flat(dup))
    dgate, dup, down_part, gate_part, up_part = tie((dgate, dup, down_part, gate_part, up_part))
    down_sum, gate_sum, up_sum = map(scatter_rows, (down_part, gate_part, up_part))
    dy, gain_mid, dattn, do = out_of_feed(n, y, attn, out_grad, gains, dgate, dup, wg, wu, wo)
    do, dattn, down_sum, gate_sum = tie((do, dattn, down_sum, gate_sum))
    out_part = weight_grad(flat(dattn), o)
    do, out_part = tie((do, out_part))
    d = attend_back(heads, kvs, piece_starts, q, k, v, flat(do), cos, sin)
    qkv_part = weight_grad(h1_flat, d)
    d, qkv_part, up_sum = tie((d, qkv_part, up_sum))
    out_sum, qkv_sum = scatter_rows(out_part), scatter_rows(qkv_part)
    in_grad, gain_one = last(n, layer_in, dy, gains, d.reshape(n, rows, -1), wqkv)

    own_rows = qkv_sum.shape[0]
    split = heads * HD
    kv = qkv_sum[:, split:].reshape(own_rows, 2, kvs * HD).transpose(1, 0, 2)
    if n * kvs == KV:
        kv = lax.all_gather(kv, "tensor", axis=2, tiled=True)
    else:
        kv = lax.dynamic_update_slice_in_dim(jnp.zeros((2, own_rows, KV * HD), BF16), kv, kv_at, 2)
        kv = lax.psum(kv, "tensor")
    kv = kv.astype(F32)

    gain_grads = jnp.concatenate([gain_one, gain_mid, gain_four], axis=0)
    gain_grads = sum_gains(n, m, gain_grads.reshape(4, m, width // m).transpose(1, 0, 2))
    return (
        layer_out,
        in_grad,
        qkv_sum[:, :split].astype(F32),
        kv[0],
        kv[1],
        out_sum.astype(F32).T,
        gate_sum.astype(F32),
        up_sum.astype(F32),
        down_sum.astype(F32).T,
        gain_grads[0],
        gain_grads[1],
        gain_grads[2],
        gain_grads[3],
    )


def solution(mesh):
    in_specs = (
        P(("dp", "tensor"), None),
        P(("dp", "tensor"), None),
        P("dp", None),
        P("dp"),
        P("dp"),
        P("dp"),
        P("dp"),
        P("dp", "tensor"),
        P("dp", None),
        P("dp", None),
        P("tensor", "dp"),
        P("dp", "tensor"),
        P("dp", "tensor"),
        P("tensor", "dp"),
    )
    out_specs = (
        P(("dp", "tensor"), None),
        P(("dp", "tensor"), None),
        P("dp", "tensor"),
        P("dp", None),
        P("dp", None),
        P("tensor", "dp"),
        P("dp", "tensor"),
        P("dp", "tensor"),
        P("tensor", "dp"),
        P("dp"),
        P("dp"),
        P("dp"),
        P("dp"),
    )
    program = functools.partial(body, mesh.shape["tensor"], mesh.shape["dp"])
    return jax.shard_map(program, mesh=mesh, in_specs=in_specs, out_specs=out_specs, check_vma=False)
```

```python
import functools

import jax
import jax.numpy as jnp
from jax import lax
from jax.experimental import pallas as pl
from jax.experimental.pallas import tpu as pltpu
from jax.sharding import PartitionSpec as P

H = 8
KV = 4
HD = 256
L = 1024
PIECE = 256

EPS = 1e-06
CAP = 50.0
F32 = jnp.float32
BF16 = jnp.bfloat16
MESH = pl.DeviceIdType.MESH
ANY = pl.BlockSpec(memory_space=pl.ANY)
VM = pl.BlockSpec(memory_space=pltpu.VMEM)
SM = pl.BlockSpec(memory_space=pltpu.SMEM)
ROWS = 16
TILE = 256


def dot_nn(a, b):
    return lax.dot_general(a, b, (((1,), (0,)), ((), ())), preferred_element_type=F32)


def dot_nt(a, b):
    return lax.dot_general(a, b, (((1,), (1,)), ((), ())), preferred_element_type=F32)


def dot_tn(a, b):
    return lax.dot_general(a, b, (((0,), (0,)), ((), ())), preferred_element_type=F32)


def tile_of(width):
    return next(t for t in (256, 384, 128) if width % t == 0)


def loop(count, body):
    lax.fori_loop(0, count, lambda t, c: (body(t), c)[1], 0)


def block_at(i, n, s):
    m = jnp.minimum(i, n - 1 - i)
    near = i + jnp.where(s % 2 == 1, -((s + 1) // 2), s // 2)
    far = jnp.where(i * 2 < n, i + (s - m), i - (s - m))
    return jnp.where(s <= 2 * m, near, far)


def line_barrier(i, n, peers=()):
    barrier = pltpu.get_barrier_semaphore()

    @pl.when(i > 0)
    def _():
        pl.semaphore_signal(barrier, 1, device_id={"tensor": i - 1}, device_id_type=MESH)

    @pl.when(i < n - 1)
    def _():
        pl.semaphore_signal(barrier, 1, device_id={"tensor": i + 1}, device_id_type=MESH)

    for peer in peers:
        pl.semaphore_signal(barrier, 1, device_id={"dp": peer}, device_id_type=MESH)
    pl.semaphore_wait(barrier, len(peers) + jnp.minimum(i, 1) + jnp.minimum(n - 1 - i, 1))


def gather_line(i, n, held, send, recv, compute):
    def copy(block, way, s, to):
        return pltpu.make_async_remote_copy(
            held.at[block],
            held.at[block],
            send.at[way, s],
            recv.at[block],
            device_id={"tensor": to},
            device_id_type=MESH,
        )

    up, down = jnp.minimum(i + 1, n - 1), jnp.maximum(i - 1, 0)

    def step(s):
        low, high = i - s, i + s

        @pl.when((s > 0) & (low >= 0))
        def _():
            copy(low, 0, s, up).wait_recv()

        @pl.when((low >= 0) & (i < n - 1))
        def _():
            copy(low, 0, s, up).start()

        @pl.when((s > 0) & (high < n))
        def _():
            copy(high, 1, s, down).wait_recv()

        @pl.when((high < n) & (i > 0))
        def _():
            copy(high, 1, s, down).start()

        compute(s, block_at(i, n, s))

    loop(n, step)

    def finish(s):
        low, high = i - s, i + s

        @pl.when((low >= 0) & (i < n - 1))
        def _():
            copy(low, 0, s, up).wait_send()

        @pl.when((high < n) & (i > 0))
        def _():
            copy(high, 1, s, down).wait_send()

    loop(n, finish)


def scatter_steps(i, n, part, landed, send, recv, compute):
    rows = part.shape[1]

    def copy(block, way, t, to):
        slot = jnp.where(block == to, n, block) if way else block
        return pltpu.make_async_remote_copy(
            part.at[block],
            landed.at[slot],
            send.at[way, t],
            recv.at[slot],
            device_id={"tensor": to},
            device_id_type=MESH,
        )

    def arrived(slot):
        pltpu.make_async_remote_copy(
            landed.at[slot],
            landed.at[slot],
            send.at[0, 0],
            recv.at[slot],
            device_id={"tensor": i},
            device_id_type=MESH,
        ).wait_recv()

    def add(block):
        def chunk(c):
            r = pl.ds(c * ROWS, ROWS)
            total = part[block, r, :].astype(F32) + landed[block, r, :].astype(F32)
            part[block, r, :] = total.astype(BF16)

        loop(rows // ROWS, chunk)

    up, down = jnp.minimum(i + 1, n - 1), jnp.maximum(i - 1, 0)

    def step(k):
        t = k + 1
        compute(k, block_at(i, n, n - t))
        above, below = i + n - t, i - n + t

        @pl.when((above < n) & (i > 0))
        def _():
            arrived(above)
            add(above)

        @pl.when(above < n)
        def _():
            copy(above, 0, t, up).start()

        @pl.when((below >= 0) & (i < n - 1))
        def _():
            arrived(below)
            add(below)

        @pl.when(below >= 0)
        def _():
            copy(below, 1, t, down).start()

    def land():
        @pl.when(i > 0)
        def _():
            arrived(i)

        @pl.when(i < n - 1)
        def _():
            arrived(jnp.int32(n))

    def finish(k):
        t = k + 1

        @pl.when(i + n - t < n)
        def _():
            copy(i + n - t, 0, t, up).wait_send()

        @pl.when(i - n + t >= 0)
        def _():
            copy(i - n + t, 1, t, down).wait_send()

    return step, land, functools.partial(loop, n - 1, finish)


def scatter_line(i, n, part, landed, send, recv, compute, own):
    step, land, finish = scatter_steps(i, n, part, landed, send, recv, compute)
    loop(n - 1, step)
    own(n - 1)
    land()
    return finish


def summed_rows(i, n, mine, landed, r):
    zero = jnp.zeros((), F32)
    low = jnp.where(i > 0, landed[i, r, :].astype(F32), zero)
    high = jnp.where(i < n - 1, landed[n, r, :].astype(F32), zero)
    return mine[r, :] + low + high


def inverse_rms(v):
    return lax.rsqrt(jnp.mean(v * v, axis=-1, keepdims=True) + EPS)


def norm_back(e, v, r):
    unit = v * r
    return r * (e - unit * jnp.mean(e * unit, axis=-1, keepdims=True))


def fold_rows(v):
    return v.reshape(-1, 8, v.shape[-1]).sum(axis=0)


class Feed:
    def __init__(self, sources, slots, sems, which):
        self.sources, self.slots, self.sems, self.which = sources, slots, sems, which

    def copies(self, s):
        return [
            pltpu.make_async_copy(src.at[self.which(s)], slot.at[s % 2], self.sems.at[k, s % 2])
            for k, (src, slot) in enumerate(zip(self.sources, self.slots))
        ]

    def start(self, s):
        for c in self.copies(s):
            c.start()

    def wait(self, s):
        for c in self.copies(s):
            c.wait()

    def advance(self, s, count):
        self.wait(s)

        @pl.when(s + 1 < count)
        def _():
            self.start(s + 1)


class Drain:
    def __init__(self, targets, slots, sems, which):
        self.targets, self.slots, self.sems, self.which = targets, slots, sems, which

    def copies(self, s):
        return [
            pltpu.make_async_copy(slot.at[s % 2], dst.at[self.which(s)], self.sems.at[k, s % 2])
            for k, (dst, slot) in enumerate(zip(self.targets, self.slots))
        ]

    def free(self, s):
        @pl.when(s >= 2)
        def _():
            for c in self.copies(s - 2):
                c.wait()

    def start(self, s):
        for c in self.copies(s):
            c.start()

    def finish(self, count):
        for s in range(max(0, count - 2), count):
            for c in self.copies(jnp.int32(s)):
                c.wait()


class Spread:
    sems = 8

    def __init__(self, own, full, send, recv, local):
        me = lax.axis_index("dp")
        c, x, y = me % 2, (me // 2) % 2, me // 4
        self.own, self.full, self.send, self.recv, self.local = own, full, send, recv, local
        self.me = me
        self.core = me + 1 - 2 * c
        self.x = me + 2 - 4 * x
        self.y = me + 4 - 8 * y
        self.far = self.x + 4 - 8 * y
        self.flip = 1 - 2 * c

    def peers(self):
        return (self.core, self.x, self.y)

    def rows(self, part):
        count = self.full.shape[1]
        half = count // 2
        return pl.ds(*{0: (0, count), 1: (0, half), 2: (half, half)}[part])

    def copy(self, k, source, owner, part, to):
        r = self.rows(part)
        return pltpu.make_async_remote_copy(
            self.own.at[r] if source is None else self.full.at[source, r],
            self.full.at[owner, r],
            self.send.at[k],
            self.recv.at[k],
            device_id={"dp": to},
            device_id_type=MESH,
        )

    def sends(self):
        return (
            (0, None, self.me, 0, self.core),
            (1, None, self.me, 0, self.x),
            (2, None, self.me, 0, self.y),
            (3, self.x, self.x, 1, self.y),
            (4, self.y, self.y, 2, self.x),
            (5, self.x, self.x, 0, self.core),
            (6, self.y, self.y, 0, self.core),
            (7, self.far, self.far, 0, self.core),
        )

    def start(self, *which):
        for k in which:
            self.copy(*self.sends()[k]).start()

    def arrive(self, k):
        owner, part = {
            0: (self.core, 0),
            1: (self.x, 0),
            2: (self.y, 0),
            3: (self.far, 1),
            4: (self.far, 2),
            5: (self.x + self.flip, 0),
            6: (self.y + self.flip, 0),
            7: (self.far + self.flip, 0),
        }[k]
        self.copy(k, owner, owner, part, self.core).wait_recv()

    def keep(self):
        return pltpu.make_async_copy(self.own, self.full.at[self.me], self.local.at[0])

    def begin(self):
        self.keep().start()
        self.start(1, 2, 0)

    def middle(self):
        self.arrive(1)
        self.arrive(2)
        self.start(3, 4, 5, 6)

    def turn(self):
        self.arrive(3)
        self.arrive(4)
        self.start(7)

    def end(self):
        for k in (0, 5, 6, 7):
            self.arrive(k)
        self.keep().wait()
        for k in range(8):
            self.copy(*self.sends()[k]).wait_send()


def spread_scratch():
    return [pltpu.SemaphoreType.DMA((8,)), pltpu.SemaphoreType.DMA((8,)), pltpu.SemaphoreType.DMA((1,))]


def line_scratch(n):
    return [pltpu.SemaphoreType.DMA((2, n)), pltpu.SemaphoreType.DMA((n + 1,))]


def params(cid, mib):
    return pltpu.CompilerParams(
        collective_id=cid, has_side_effects=True, vmem_limit_bytes=mib << 20
    )


def cost(flops, moved):
    return pl.CostEstimate(flops=flops, bytes_accessed=moved, transcendentals=0)


def gains_kernel(m, mine, out, send, recv):
    me = lax.axis_index("dp")
    barrier = pltpu.get_barrier_semaphore()
    for k in range(1, m):
        pl.semaphore_signal(
            barrier, 1, device_id={"dp": lax.rem(me + k, m)}, device_id_type=MESH
        )
    pl.semaphore_wait(barrier, m - 1)

    def copy(owner, k):
        return pltpu.make_async_remote_copy(
            mine,
            out.at[owner],
            send.at[k],
            recv.at[k],
            device_id={"dp": lax.rem(me + k, m)},
            device_id_type=MESH,
        )

    for k in range(1, m):
        copy(me, k).start()
    out[me] = mine[...]
    for k in range(1, m):
        copy(lax.rem(me + m - k, m), k).wait_recv()
    for k in range(1, m):
        copy(me, k).wait_send()


def gather_gains(m, mine):
    return pl.pallas_call(
        functools.partial(gains_kernel, m),
        out_shape=jax.ShapeDtypeStruct((m,) + mine.shape, mine.dtype),
        in_specs=[VM],
        out_specs=VM,
        scratch_shapes=[pltpu.SemaphoreType.DMA((m,)), pltpu.SemaphoreType.DMA((m,))],
        compiler_params=params(0, 16),
        name="gains",
    )(mine)


def sum_gains_kernel(n, m, mine, out, landed, total, across, send, recv, send_two, recv_two):
    me, i = lax.axis_index("dp"), lax.axis_index("tensor")
    barrier = pltpu.get_barrier_semaphore()
    dp_peer = lambda k: {"dp": lax.rem(me + k, m)}
    line_peer = lambda k: {"tensor": lax.rem(i + k, n)}
    for k in range(1, m):
        pl.semaphore_signal(barrier, 1, device_id=dp_peer(k), device_id_type=MESH)
    for k in range(1, n):
        pl.semaphore_signal(barrier, 1, device_id=line_peer(k), device_id_type=MESH)
    pl.semaphore_wait(barrier, m + n - 2)

    def to_owner(k):
        return pltpu.make_async_remote_copy(
            mine.at[lax.rem(me + k, m)], landed.at[k], send.at[k], recv.at[k],
            device_id=dp_peer(k), device_id_type=MESH,
        )

    def along(k):
        return pltpu.make_async_remote_copy(
            total, across.at[k], send_two.at[k], recv_two.at[k],
            device_id=line_peer(k), device_id_type=MESH,
        )

    for k in range(1, m):
        to_owner(k).start()
    here = mine[me]
    for k in range(1, m):
        to_owner(k).wait_recv()
        here = here + landed[k]
    total[...] = here
    for k in range(1, n):
        along(k).start()
    for k in range(1, n):
        along(k).wait_recv()
        here = here + across[k]
    out[...] = here
    for k in range(1, m):
        to_owner(k).wait_send()
    for k in range(1, n):
        along(k).wait_send()


def sum_gains(n, m, mine):
    shape = mine.shape[1:]
    return pl.pallas_call(
        functools.partial(sum_gains_kernel, n, m),
        out_shape=jax.ShapeDtypeStruct(shape, F32),
        in_specs=[VM],
        out_specs=VM,
        scratch_shapes=[
            pltpu.VMEM((m,) + shape, F32),
            pltpu.VMEM(shape, F32),
            pltpu.VMEM((n,) + shape, F32),
        ]
        + [pltpu.SemaphoreType.DMA((m,))] * 2
        + [pltpu.SemaphoreType.DMA((n,))] * 2,
        compiler_params=params(6, 16),
        name="sum_gains",
    )(mine)


def first_kernel(n, spread, x, gains, *refs):
    i = lax.axis_index("tensor")
    rows = x.shape[0]
    if spread:
        shard, full, gathered, held, send, recv, out_sem, *sems = refs
        gather = Spread(shard, gathered, *sems)
        line_barrier(i, n, gather.peers())
        gather.begin()
    else:
        full, held, send, recv, out_sem = refs
        line_barrier(i, n)
    scale = 1.0 + gains[0:1, :]

    def chunk(c):
        r = pl.ds(c * ROWS, ROWS)
        v = x[r, :].astype(F32)
        held[i, r, :] = (v * inverse_rms(v) * scale).astype(BF16)

    loop(rows // ROWS, chunk)

    def keep(s, block):
        pltpu.make_async_copy(held.at[block], full.at[block], out_sem.at[s]).start()
        if spread:
            pl.when(s == min(1, n - 1))(gather.middle)
            pl.when(s == min(2, n - 1))(gather.turn)

    gather_line(i, n, held, send, recv, keep)

    def finish(s):
        block = block_at(i, n, s)
        pltpu.make_async_copy(held.at[block], full.at[block], out_sem.at[s]).wait()

    loop(n, finish)
    if spread:
        gather.end()


def first(n, m, x, gains, shard):
    rows, width = x.shape
    spread = shard is not None
    outs = [jax.ShapeDtypeStruct((n, rows, width), BF16)]
    if spread:
        outs += [jax.ShapeDtypeStruct((m,) + shard.shape, BF16)]
    out = pl.pallas_call(
        functools.partial(first_kernel, n, spread),
        out_shape=outs,
        in_specs=[VM, VM] + [ANY] * spread,
        out_specs=[ANY] + [ANY] * spread,
        scratch_shapes=[pltpu.VMEM((n, rows, width), BF16)]
        + line_scratch(n)
        + [pltpu.SemaphoreType.DMA((n,))]
        + (spread_scratch() if spread else []),
        compiler_params=params(1, 32),
        cost_estimate=cost(0, 300 << 20),
        name="first",
    )(x, gains, *([shard] if spread else []))
    return (out[0], out[1].reshape(-1, shard.shape[1])) if spread else (out[0], None)


def turn(u, cos, sin):
    half = HD // 2
    a, b = u[:, :half], u[:, half:]
    return jnp.concatenate([a * cos - b * sin, b * cos + a * sin], axis=-1)


def row_limit(starts, seq, first_row, rows):
    pos = first_row + lax.broadcasted_iota(jnp.int32, (rows, 1), 0)
    limit = pos + 1
    for piece in range(2):
        begin = starts[seq, piece]
        inside = (pos >= begin) & (pos < begin + PIECE)
        limit = jnp.maximum(limit, jnp.where(inside, begin + PIECE, 0))
    return limit


def key_span(first_row, rows):
    return min(L, first_row + rows + PIECE)


def weights_of(q, k, limit):
    bent = jnp.tanh(dot_nt(q, k) * (1.0 / CAP))
    seen = lax.broadcasted_iota(jnp.int32, (1, k.shape[0]), 1) < limit
    w = jnp.where(seen, jnp.exp(CAP * bent), 0.0)
    return w * pl.reciprocal(jnp.sum(w, axis=-1, keepdims=True)), bent


def attend_kernel(heads, kvs, starts, h1, w, cos, sin, q_out, k_out, v_out, o_out):
    tokens = h1.shape[0]
    fan = heads // kvs
    block = 256

    def project(b):
        r = pl.ds(pl.multiple_of(b * block, block), block)
        at = pl.ds(pl.multiple_of(lax.rem(b * block, L), block), block)
        c, s = cos[at, :], sin[at, :]
        x = h1[r, :]
        for h in range(heads):
            u = dot_nn(x, w[:, h * HD : (h + 1) * HD])
            q_out[h, r, :] = (turn(u, c, s) * (HD**-0.5)).astype(BF16)
        for g in range(kvs):
            u = dot_nn(x, w[:, (heads + g) * HD : (heads + g + 1) * HD])
            k_out[g, r, :] = turn(u, c, s).astype(BF16)
            u = dot_nn(x, w[:, (heads + kvs + g) * HD : (heads + kvs + g + 1) * HD])
            v_out[g, r, :] = u.astype(BF16)

    loop(tokens // block, project)
    for seq in range(tokens // L):
        base = seq * L
        for row in range(0, L, block):
            span = key_span(row, block)
            limit = row_limit(starts, seq, row, block)
            for h in range(heads):
                q = q_out[h, base + row : base + row + block, :]
                p, _ = weights_of(q, k_out[h // fan, base : base + span, :], limit)
                o = dot_nn(p.astype(BF16), v_out[h // fan, base : base + span, :])
                o_out[base + row : base + row + block, h * HD : (h + 1) * HD] = o.astype(BF16)


def attend(heads, kvs, starts, h1, w, cos, sin):
    tokens = h1.shape[0]
    return pl.pallas_call(
        functools.partial(attend_kernel, heads, kvs),
        out_shape=[
            jax.ShapeDtypeStruct((heads, tokens, HD), BF16),
            jax.ShapeDtypeStruct((kvs, tokens, HD), BF16),
            jax.ShapeDtypeStruct((kvs, tokens, HD), BF16),
            jax.ShapeDtypeStruct((tokens, heads * HD), BF16),
        ],
        in_specs=[SM, VM, VM, VM, VM],
        out_specs=[VM, VM, VM, VM],
        compiler_params=pltpu.CompilerParams(vmem_limit_bytes=48 << 20),
        cost_estimate=cost(20 << 30, 20 << 20),
        name="attend",
    )(starts, h1, w, cos, sin)


def attend_back_kernel(heads, kvs, starts, q_in, k_in, v_in, do_in, cos, sin, out, dk, dv):
    tokens = q_in.shape[1]
    fan = heads // kvs
    block = 256
    for seq in range(tokens // L):
        base = seq * L
        for g in range(kvs):
            dk[...] = jnp.zeros_like(dk)
            dv[...] = jnp.zeros_like(dv)
            for row in range(0, L, block):
                span = key_span(row, block)
                limit = row_limit(starts, seq, row, block)
                k = k_in[g, base : base + span, :]
                v = v_in[g, base : base + span, :]
                at = slice(base + row, base + row + block)
                for h in range(g * fan, (g + 1) * fan):
                    q = q_in[h, at, :]
                    do = do_in[at, h * HD : (h + 1) * HD]
                    p, bent = weights_of(q, k, limit)
                    dp = dot_nt(do, v)
                    delta = jnp.sum(p * dp, axis=-1, keepdims=True)
                    ds = (p * (dp - delta) * (1.0 - bent * bent)).astype(BF16)
                    dq = dot_nn(ds, k)
                    c, s = cos[row : row + block, :], sin[row : row + block, :]
                    out[at, h * HD : (h + 1) * HD] = (turn(dq, c, -s) * (HD**-0.5)).astype(BF16)
                    dk[:span, :] += dot_tn(ds, q)
                    dv[:span, :] += dot_tn(p.astype(BF16), do)

            def close(b, g=g, base=base):
                r = pl.ds(pl.multiple_of(b * block, block), block)
                to = pl.ds(pl.multiple_of(base + b * block, block), block)
                back = turn(dk[r, :], cos[r, :], -sin[r, :])
                out[to, (heads + g) * HD : (heads + g + 1) * HD] = back.astype(BF16)
                left = (heads + kvs + g) * HD
                out[to, left : left + HD] = dv[r, :].astype(BF16)

            loop(L // block, close)


def attend_back(heads, kvs, starts, q, k, v, do, cos, sin):
    tokens = q.shape[1]
    return pl.pallas_call(
        functools.partial(attend_back_kernel, heads, kvs),
        out_shape=jax.ShapeDtypeStruct((tokens, (heads + 2 * kvs) * HD), BF16),
        in_specs=[SM, VM, VM, VM, VM, VM, VM],
        out_specs=VM,
        scratch_shapes=[pltpu.VMEM((L, HD), F32), pltpu.VMEM((L, HD), F32)],
        compiler_params=pltpu.CompilerParams(vmem_limit_bytes=48 << 20),
        cost_estimate=cost(30 << 30, 20 << 20),
        name="attend_back",
    )(starts, q, k, v, do, cos, sin)


def into_feed_kernel(n, spread, x, gains, o_hbm, wo_hbm, wg_hbm, wu_hbm, *refs):
    attn_out, y_out, h3_full, hid_out, up_out, ge_out, *refs = refs
    if spread:
        wu_full, *refs = refs
        *refs, token, spread_send, spread_recv, spread_local = refs
    (
        o, wo, wg, wu, part, landed, mine, held, hid_s, up_s, ge_s,
        load, rs_send, rs_recv, ag_send, ag_recv, keep_sem, out_sem,
    ) = refs
    i = lax.axis_index("tensor")
    rows, width = x.shape
    pairs = [(o_hbm, o), (wo_hbm, wo), (wg_hbm, wg)] + ([] if spread else [(wu_hbm, wu)])
    loads = [pltpu.make_async_copy(src, dst, load.at[k]) for k, (src, dst) in enumerate(pairs)]
    for c in loads:
        c.start()
    if spread:
        gather = Spread(wu_hbm, wu_full, spread_send, spread_recv, spread_local)
        core = lax.axis_index("dp") % 2
        line_barrier(i, n, gather.peers())
        gather.begin()
    else:
        line_barrier(i, n)
    loads[0].wait()
    loads[1].wait()
    if spread:

        @pl.when(core == 1)
        def _():
            gather.middle()
            gather.turn()
            pl.semaphore_wait(token, 1)

    def compute(t, block):
        def tile(k):
            at = pl.ds(pl.multiple_of(k * TILE, TILE), TILE)
            part[block, :, at] = dot_nt(o[block], wo[at, :]).astype(BF16)

        loop(width // TILE, tile)

    def own(t):
        def tile(k):
            at = pl.ds(pl.multiple_of(k * TILE, TILE), TILE)
            mine[:, at] = dot_nt(o[i], wo[at, :])

        loop(width // TILE, tile)

    done = scatter_line(i, n, part, landed, rs_send, rs_recv, compute, own)
    if spread:

        @pl.when(core == 0)
        def _():
            pl.semaphore_signal(token, 1, device_id={"dp": gather.core}, device_id_type=MESH)
            gather.middle()

    scale_two, scale_three = 1.0 + gains[1:2, :], 1.0 + gains[2:3, :]

    def chunk(c):
        r = pl.ds(c * ROWS, ROWS)
        attn = summed_rows(i, n, mine, landed, r)
        attn_out[r, :] = attn
        y = x[r, :].astype(F32) + attn * inverse_rms(attn) * scale_two
        y_out[r, :] = y
        held[i, r, :] = (y * inverse_rms(y) * scale_three).astype(BF16)

    loop(rows // ROWS, chunk)
    done()
    if spread:
        pl.when(core == 0)(gather.turn)
        gather.end()
        size = wu_hbm.shape[0]
        loads += [
            pltpu.make_async_copy(wu_full.at[k], wu.at[pl.ds(k * size, size)], load.at[3 + k])
            for k in range(wu_full.shape[0])
        ]
        for c in loads[3:]:
            c.start()
    for c in loads[2:]:
        c.wait()
    drain = Drain(
        (hid_out, up_out, ge_out), (hid_s, up_s, ge_s), out_sem, lambda s: block_at(i, n, s)
    )

    def forward(s, block):
        pltpu.make_async_copy(held.at[block], h3_full.at[block], keep_sem.at[s]).start()
        drain.free(s)
        slot = s % 2
        span = tile_of(wg.shape[1])

        def tile(k):
            at = pl.ds(pl.multiple_of(k * span, span), span)
            u = dot_nn(held[block], wg[:, at])
            up = dot_nn(held[block], wu[:, at])
            c = 0.7978845608028654
            th = jnp.tanh(c * (u + 0.044715 * (u * u * u)))
            half = 0.5 * (1.0 + th)
            gelu = u * half
            slope = half + 0.5 * u * (1.0 - th * th) * (c * (1.0 + 0.134145 * (u * u)))
            hid_s[slot, :, at] = (gelu * up).astype(BF16)
            up_s[slot, :, at] = (up * slope).astype(BF16)
            ge_s[slot, :, at] = gelu.astype(BF16)

        loop(wg.shape[1] // span, tile)
        drain.start(s)

    gather_line(i, n, held, ag_send, ag_recv, forward)
    drain.finish(n)

    def finish(s):
        block = block_at(i, n, s)
        pltpu.make_async_copy(held.at[block], h3_full.at[block], keep_sem.at[s]).wait()

    loop(n, finish)


def into_feed(n, m, spread, x, gains, o, wo, wg, wu):
    rows, width = x.shape
    wide = wg.shape[1]
    blocks = lambda w: jax.ShapeDtypeStruct((n, rows, w), BF16)
    mine = jax.ShapeDtypeStruct((rows, width), F32)
    outs = [mine, mine, blocks(width), blocks(wide), blocks(wide), blocks(wide)]
    outs += [jax.ShapeDtypeStruct((m,) + wu.shape, BF16)] * spread
    return pl.pallas_call(
        functools.partial(into_feed_kernel, n, spread),
        out_shape=outs,
        in_specs=[VM, VM, ANY, ANY, ANY, ANY],
        out_specs=[VM, VM] + [ANY] * (len(outs) - 2),
        scratch_shapes=[
            pltpu.VMEM(o.shape, BF16),
            pltpu.VMEM(wo.shape, BF16),
            pltpu.VMEM(wg.shape, BF16),
            pltpu.VMEM(wg.shape, BF16),
            pltpu.VMEM((n, rows, width), BF16),
            pltpu.VMEM((n + 1, rows, width), BF16),
            pltpu.VMEM((rows, width), F32),
            pltpu.VMEM((n, rows, width), BF16),
        ]
        + [pltpu.VMEM((2, rows, wide), BF16)] * 3
        + [pltpu.SemaphoreType.DMA((3 + m,))]
        + line_scratch(n) * 2
        + [pltpu.SemaphoreType.DMA((n,)), pltpu.SemaphoreType.DMA((3, 2))]
        + ([pltpu.SemaphoreType.REGULAR] + spread_scratch() if spread else []),
        compiler_params=params(2, 62),
        cost_estimate=cost(0, 600 << 20),
        name="into_feed",
    )(x, gains, o, wo, wg, wu)


def turn_feed_kernel(
    n, y, dout, gains, hid_hbm, wd_hbm, up_hbm, ge_hbm,
    layer_out, gain_out, df_full, dgate_out, dup_out,
    wd, hid_s, part, landed, mine, held, up_s, ge_s, dg_s, du_s, fold,
    load, feed_sem, rs_send, rs_recv, ag_send, ag_recv, keep_sem, back_sem, out_sem,
):
    i = lax.axis_index("tensor")
    rows, width = y.shape
    whole = pltpu.make_async_copy(wd_hbm, wd, load.at[0])
    whole.start()
    feed = Feed((hid_hbm,), (hid_s,), feed_sem, lambda s: block_at(i, n, n - 1 - s))
    feed.start(jnp.int32(0))
    line_barrier(i, n)
    whole.wait()

    def compute(t, block):
        feed.advance(t, n)
        slot = t % 2

        def tile(k):
            at = pl.ds(pl.multiple_of(k * TILE, TILE), TILE)
            part[block, :, at] = dot_nt(hid_s[slot], wd[at, :]).astype(BF16)

        loop(width // TILE, tile)

    def own(t):
        t = jnp.int32(t)
        feed.advance(t, n)
        slot = t % 2

        def tile(k):
            at = pl.ds(pl.multiple_of(k * TILE, TILE), TILE)
            mine[:, at] = dot_nt(hid_s[slot], wd[at, :])

        loop(width // TILE, tile)

    done = scatter_line(i, n, part, landed, rs_send, rs_recv, compute, own)
    scale = 1.0 + gains[3:4, :]
    fold[...] = jnp.zeros_like(fold)

    def chunk(c):
        r = pl.ds(c * ROWS, ROWS)
        f = summed_rows(i, n, mine, landed, r)
        g = dout[r, :].astype(F32)
        inv = inverse_rms(f)
        layer_out[r, :] = (y[r, :] + f * inv * scale).astype(BF16)
        held[i, r, :] = norm_back(g * scale, f, inv).astype(BF16)
        fold[...] += fold_rows(g * (f * inv))

    loop(rows // ROWS, chunk)
    gain_out[...] = jnp.sum(fold[...], axis=0, keepdims=True)
    done()
    sides = Feed((up_hbm, ge_hbm), (up_s, ge_s), back_sem, lambda s: block_at(i, n, s))
    drain = Drain((dgate_out, dup_out), (dg_s, du_s), out_sem, lambda s: block_at(i, n, s))
    sides.start(jnp.int32(0))

    def backward(s, block):
        pltpu.make_async_copy(held.at[block], df_full.at[block], keep_sem.at[s]).start()
        sides.advance(s, n)
        drain.free(s)
        slot = s % 2
        span = tile_of(wd.shape[1])

        def tile(k):
            at = pl.ds(pl.multiple_of(k * span, span), span)
            dhid = dot_nn(held[block], wd[:, at])
            dg_s[slot, :, at] = (dhid * up_s[slot, :, at].astype(F32)).astype(BF16)
            du_s[slot, :, at] = (dhid * ge_s[slot, :, at].astype(F32)).astype(BF16)

        loop(wd.shape[1] // span, tile)
        drain.start(s)

    gather_line(i, n, held, ag_send, ag_recv, backward)
    drain.finish(n)

    def finish(s):
        block = block_at(i, n, s)
        pltpu.make_async_copy(held.at[block], df_full.at[block], keep_sem.at[s]).wait()

    loop(n, finish)


def turn_feed(n, y, dout, gains, hid, wd, up, ge):
    rows, width = y.shape
    wide = wd.shape[1]
    blocks = lambda w: jax.ShapeDtypeStruct((n, rows, w), BF16)
    return pl.pallas_call(
        functools.partial(turn_feed_kernel, n),
        out_shape=[
            jax.ShapeDtypeStruct((rows, width), BF16),
            jax.ShapeDtypeStruct((1, width), F32),
            blocks(width),
            blocks(wide),
            blocks(wide),
        ],
        in_specs=[VM, VM, VM, ANY, ANY, ANY, ANY],
        out_specs=[VM, VM, ANY, ANY, ANY],
        scratch_shapes=[
            pltpu.VMEM(wd.shape, BF16),
            pltpu.VMEM((2, rows, wide), BF16),
            pltpu.VMEM((n, rows, width), BF16),
            pltpu.VMEM((n + 1, rows, width), BF16),
            pltpu.VMEM((rows, width), F32),
            pltpu.VMEM((n, rows, width), BF16),
        ]
        + [pltpu.VMEM((2, rows, wide), BF16)] * 4
        + [pltpu.VMEM((8, width), F32)]
        + [pltpu.SemaphoreType.DMA((1,)), pltpu.SemaphoreType.DMA((1, 2))]
        + line_scratch(n) * 2
        + [
            pltpu.SemaphoreType.DMA((n,)),
            pltpu.SemaphoreType.DMA((2, 2)),
            pltpu.SemaphoreType.DMA((2, 2)),
        ],
        compiler_params=params(3, 62),
        cost_estimate=cost(0, 600 << 20),
        name="turn_feed",
    )(y, dout, gains, hid, wd, up, ge)


def out_of_feed_kernel(
    n, y, attn, dout, gains, dgate_hbm, dup_hbm, wg_hbm, wu_hbm, wo_hbm,
    dy_out, gain_out, dattn_full, do_out,
    wg, wu, wo, dg_s, du_s, part, landed, mine, held, do_s, fold,
    load, feed_sem, rs_send, rs_recv, ag_send, ag_recv, keep_sem, out_sem,
):
    i = lax.axis_index("tensor")
    rows, width = y.shape
    loads = [
        pltpu.make_async_copy(src, dst, load.at[k])
        for k, (src, dst) in enumerate(((wg_hbm, wg), (wu_hbm, wu), (wo_hbm, wo)))
    ]
    for c in loads:
        c.start()
    feed = Feed((dgate_hbm, dup_hbm), (dg_s, du_s), feed_sem, lambda s: block_at(i, n, n - 1 - s))
    feed.start(jnp.int32(0))
    line_barrier(i, n)
    loads[0].wait()
    loads[1].wait()

    def product(slot, at):
        return dot_nt(dg_s[slot], wg[at, :]) + dot_nt(du_s[slot], wu[at, :])

    def compute(t, block):
        feed.advance(t, n)
        slot = t % 2

        def tile(k):
            at = pl.ds(pl.multiple_of(k * TILE, TILE), TILE)
            part[block, :, at] = product(slot, at).astype(BF16)

        loop(width // TILE, tile)

    def own(t):
        t = jnp.int32(t)
        feed.advance(t, n)
        slot = t % 2

        def tile(k):
            at = pl.ds(pl.multiple_of(k * TILE, TILE), TILE)
            mine[:, at] = product(slot, at)

        loop(width // TILE, tile)

    done = scatter_line(i, n, part, landed, rs_send, rs_recv, compute, own)
    scale_two, scale_three = 1.0 + gains[1:2, :], 1.0 + gains[2:3, :]
    fold[...] = jnp.zeros_like(fold)

    def chunk(c):
        r = pl.ds(c * ROWS, ROWS)
        dh3 = summed_rows(i, n, mine, landed, r)
        v = y[r, :]
        inv = inverse_rms(v)
        dy = dout[r, :].astype(F32) + norm_back(dh3 * scale_three, v, inv)
        dy_out[r, :] = dy
        fold[1] += fold_rows(dh3 * (v * inv))
        a = attn[r, :]
        inv = inverse_rms(a)
        held[i, r, :] = norm_back(dy * scale_two, a, inv).astype(BF16)
        fold[0] += fold_rows(dy * (a * inv))

    loop(rows // ROWS, chunk)
    gain_out[0:1, :] = jnp.sum(fold[0], axis=0, keepdims=True)
    gain_out[1:2, :] = jnp.sum(fold[1], axis=0, keepdims=True)
    done()
    loads[2].wait()
    drain = Drain((do_out,), (do_s,), out_sem, lambda s: block_at(i, n, s))

    def backward(s, block):
        pltpu.make_async_copy(held.at[block], dattn_full.at[block], keep_sem.at[s]).start()
        drain.free(s)
        do_s[s % 2] = dot_nn(held[block], wo[...]).astype(BF16)
        drain.start(s)

    gather_line(i, n, held, ag_send, ag_recv, backward)
    drain.finish(n)

    def finish(s):
        block = block_at(i, n, s)
        pltpu.make_async_copy(held.at[block], dattn_full.at[block], keep_sem.at[s]).wait()

    loop(n, finish)


def out_of_feed(n, y, attn, dout, gains, dgate, dup, wg, wu, wo):
    rows, width = y.shape
    wide = wg.shape[1]
    narrow = wo.shape[1]
    return pl.pallas_call(
        functools.partial(out_of_feed_kernel, n),
        out_shape=[
            jax.ShapeDtypeStruct((rows, width), F32),
            jax.ShapeDtypeStruct((2, width), F32),
            jax.ShapeDtypeStruct((n, rows, width), BF16),
            jax.ShapeDtypeStruct((n, rows, narrow), BF16),
        ],
        in_specs=[VM, VM, VM, VM, ANY, ANY, ANY, ANY, ANY],
        out_specs=[VM, VM, ANY, ANY],
        scratch_shapes=[
            pltpu.VMEM(wg.shape, BF16),
            pltpu.VMEM(wu.shape, BF16),
            pltpu.VMEM(wo.shape, BF16),
            pltpu.VMEM((2, rows, wide), BF16),
            pltpu.VMEM((2, rows, wide), BF16),
            pltpu.VMEM((n, rows, width), BF16),
            pltpu.VMEM((n + 1, rows, width), BF16),
            pltpu.VMEM((rows, width), F32),
            pltpu.VMEM((n, rows, width), BF16),
            pltpu.VMEM((2, rows, narrow), BF16),
            pltpu.VMEM((2, 8, width), F32),
        ]
        + [pltpu.SemaphoreType.DMA((3,)), pltpu.SemaphoreType.DMA((2, 2))]
        + line_scratch(n) * 2
        + [pltpu.SemaphoreType.DMA((n,)), pltpu.SemaphoreType.DMA((1, 2))],
        compiler_params=params(4, 62),
        cost_estimate=cost(0, 600 << 20),
        name="out_of_feed",
    )(y, attn, dout, gains, dgate, dup, wg, wu, wo)


def last_kernel(
    n, x, dy, gains, d_hbm, w_hbm, in_grad, gain_out,
    d, w, part, landed, mine, fold, load, rs_send, rs_recv,
):
    i = lax.axis_index("tensor")
    rows, width = x.shape
    loads = [
        pltpu.make_async_copy(src, dst, load.at[k])
        for k, (src, dst) in enumerate(((d_hbm, d), (w_hbm, w)))
    ]
    for c in loads:
        c.start()
    line_barrier(i, n)
    for c in loads:
        c.wait()

    def compute(t, block):
        def tile(k):
            at = pl.ds(pl.multiple_of(k * TILE, TILE), TILE)
            part[block, :, at] = dot_nt(d[block], w[at, :]).astype(BF16)

        loop(width // TILE, tile)

    def own(t):
        def tile(k):
            at = pl.ds(pl.multiple_of(k * TILE, TILE), TILE)
            mine[:, at] = dot_nt(d[i], w[at, :])

        loop(width // TILE, tile)

    done = scatter_line(i, n, part, landed, rs_send, rs_recv, compute, own)
    scale = 1.0 + gains[0:1, :]
    fold[...] = jnp.zeros_like(fold)

    def chunk(c):
        r = pl.ds(c * ROWS, ROWS)
        dh1 = summed_rows(i, n, mine, landed, r)
        v = x[r, :].astype(F32)
        inv = inverse_rms(v)
        in_grad[r, :] = (dy[r, :] + norm_back(dh1 * scale, v, inv)).astype(BF16)
        fold[...] += fold_rows(dh1 * (v * inv))

    loop(rows // ROWS, chunk)
    gain_out[...] = jnp.sum(fold[...], axis=0, keepdims=True)
    done()


def last(n, x, dy, gains, d, w):
    rows, width = x.shape
    return pl.pallas_call(
        functools.partial(last_kernel, n),
        out_shape=[
            jax.ShapeDtypeStruct((rows, width), BF16),
            jax.ShapeDtypeStruct((1, width), F32),
        ],
        in_specs=[VM, VM, VM, ANY, ANY],
        out_specs=[VM, VM],
        scratch_shapes=[
            pltpu.VMEM(d.shape, BF16),
            pltpu.VMEM(w.shape, BF16),
            pltpu.VMEM((n, rows, width), BF16),
            pltpu.VMEM((n + 1, rows, width), BF16),
            pltpu.VMEM((rows, width), F32),
            pltpu.VMEM((8, width), F32),
            pltpu.SemaphoreType.DMA((2,)),
        ]
        + line_scratch(n),
        compiler_params=params(5, 48),
        cost_estimate=cost(0, 300 << 20),
        name="last",
    )(x, dy, gains, d, w)


class Reduce:
    def __init__(self, u, left, right, column, width, bufs, sems):
        me = lax.axis_index("dp")
        c, x, y = me % 2, (me // 2) % 2, me // 4
        self.me, self.set, self.third, self.fifth, self.width = me, u % 2, u % 3, u % 5, width
        self.left, self.right, self.column = left, right, column
        self.dx, self.dy, self.dc = 2 - 4 * x, 4 - 8 * y, 1 - 2 * c
        self.lefts, self.rights, self.pair, self.pair_in, self.sums, self.far_in, self.xy_in, self.own = bufs
        (
            self.left_sem, self.right_sem, self.pair_send, self.pair_recv,
            self.far_send, self.far_recv, self.xy_send, self.xy_recv,
        ) = sems
        self.rows = self.own.shape[1]
        self.cols = pl.ds(0, width)
        self.top = pl.ds(0, self.rows // 2)
        self.low = pl.ds(self.rows // 2, self.rows // 2)

    def owner(self, q):
        k = q % 4
        x = jnp.where(k <= 1, self.dx, 0)
        y = jnp.where(k % 2 == 0, self.dy, 0)
        return self.me + x + jnp.where(k == 3, 0, y) + jnp.where(q < 4, self.dc, 0)

    def left_copy(self, q):
        r = pl.ds(self.owner(q) * self.rows, self.rows)
        return pltpu.make_async_copy(self.left.at[r], self.lefts.at[q % 2], self.left_sem.at[q % 2])

    def right_copy(self):
        return pltpu.make_async_copy(
            self.right.at[:, pl.ds(self.column, self.width)],
            self.rights.at[self.set, :, self.cols],
            self.right_sem.at[self.set],
        )

    def remote(self, src, dst, send, recv, shift):
        return pltpu.make_async_remote_copy(
            src, dst, send, recv, device_id={"dp": self.me + shift}, device_id_type=MESH
        )

    def pair_copy(self, k):
        return self.remote(
            self.pair.at[self.set, k, :, self.cols],
            self.pair_in.at[self.set, k, :, self.cols],
            self.pair_send.at[self.set, k],
            self.pair_recv.at[self.set, k],
            self.dc,
        )

    def far_copy(self, way):
        return self.remote(
            self.sums.at[self.third, 0, (self.top, self.low)[way], self.cols],
            self.far_in.at[self.third, way, :, self.cols],
            self.far_send.at[self.third, way],
            self.far_recv.at[self.third, way],
            (self.dx, self.dy)[way],
        )

    def xy_copy(self, way, half):
        r = (self.top, self.low)[half]
        return self.remote(
            self.sums.at[self.third, 1 + way, r, self.cols],
            self.xy_in.at[self.fifth, way, r, self.cols],
            self.xy_send.at[self.third, way, half],
            self.xy_recv.at[self.fifth, way, half],
            (self.dx, self.dy)[way],
        )

    def product(self, q, put):
        self.left_copy(q).wait()
        if isinstance(q, int):
            if q < 7:
                self.left_copy(q + 1).start()
        else:
            self.left_copy(q + 1).start()
        tile = next(t for t in (384, 256, 128) if self.width % t == 0)

        def one(t):
            at = pl.ds(pl.multiple_of(t * tile, tile), tile)
            put(at, dot_nn(self.lefts[q % 2], self.rights[self.set, :, at]))

        loop(self.width // tile, one)

    def load(self):
        self.right_copy().start()

    def begin(self):
        self.left_copy(0).start()
        self.right_copy().wait()

        def chunk(k):
            def put(at, value):
                self.pair[self.set, k, :, at] = value.astype(BF16)

            self.product(k, put)
            self.pair_copy(k).start()

        loop(4, chunk)

    def middle(self):
        for k in range(4):
            arrived = []

            def put(at, value, k=k):
                total = value + self.pair_in[self.set, k, :, at].astype(F32)
                if k < 3:
                    self.sums[self.third, k, :, at] = total.astype(BF16)
                else:
                    self.own[self.third, :, at] = total

            self.pair_copy(k).wait_recv()
            self.product(4 + k, put)
            if k == 0:
                self.far_copy(0).start()
                self.far_copy(1).start()
            elif k == 1:
                self.xy_copy(0, 0).start()
            elif k == 2:
                self.xy_copy(1, 1).start()
        for k in range(4):
            self.pair_copy(k).wait_send()

    def turn(self):
        self.far_copy(0).wait_recv()
        self.far_copy(1).wait_recv()
        half = self.rows // 2

        def chunk(c):
            for way, first in ((0, 0), (1, half)):
                r = pl.ds(first + c * ROWS, ROWS)
                f = pl.ds(c * ROWS, ROWS)
                k = 2 - way
                total = self.sums[self.third, k, r, self.cols].astype(F32)
                total += self.far_in[self.third, way, f, self.cols].astype(F32)
                self.sums[self.third, k, r, self.cols] = total.astype(BF16)

        loop(half // ROWS, chunk)
        self.xy_copy(0, 1).start()
        self.xy_copy(1, 0).start()

    def end(self, put):
        for way in range(2):
            for half in range(2):
                self.xy_copy(way, half).wait_recv()

        def chunk(c):
            r = pl.ds(c * ROWS, ROWS)
            total = self.own[self.third, r, self.cols]
            for way in range(2):
                total += self.xy_in[self.fifth, way, r, self.cols].astype(F32)
            put(r, total)

        loop(self.rows // ROWS, chunk)
        for way in range(2):
            self.far_copy(way).wait_send()
            for half in range(2):
                self.xy_copy(way, half).wait_send()


def reduce_scratch(rows, tokens, widest):
    sem = pltpu.SemaphoreType.DMA
    bufs = [
        pltpu.VMEM((2, rows, tokens), BF16),
        pltpu.VMEM((2, tokens, widest), BF16),
        pltpu.VMEM((2, 4, rows, widest), BF16),
        pltpu.VMEM((2, 4, rows, widest), BF16),
        pltpu.VMEM((3, 3, rows, widest), BF16),
        pltpu.VMEM((3, 2, rows // 2, widest), BF16),
        pltpu.VMEM((5, 2, rows, widest), BF16),
        pltpu.VMEM((3, rows, widest), F32),
    ]
    sems = [
        sem((2,)), sem((2,)), sem((2, 4)), sem((2, 4)),
        sem((3, 2)), sem((3, 2)), sem((3, 2, 2)), sem((5, 2, 2)),
    ]
    return bufs, sems


def halves(width):
    return [(0, width)] if width <= 1280 else [(0, width // 2), (width // 2, width // 2)]


def tail_kernel(n, split, x, dy, gains, d_hbm, w_hbm, *refs):
    lefts, rights, refs = refs[:4], refs[4:9], refs[9:]
    in_grad, gain_out, *outs = refs[:7]
    kv_out, refs = refs[7], refs[8:]
    d, w, part, landed, mine, fold, stage, kv_stage = refs[:8]
    load, rs_send, rs_recv, out_sem, kv_sem, kv_send, kv_recv = refs[8:15]
    bufs, sems = refs[15:23], refs[23:31]
    h1_t, df_t, h3_t, da_t = lefts
    dqkv, hid, dgate, dup, o = rights
    i = lax.axis_index("tensor")
    rows, width = x.shape
    loads = [
        pltpu.make_async_copy(src, dst, load.at[k])
        for k, (src, dst) in enumerate(((d_hbm, d), (w_hbm, w)))
    ]
    for c in loads:
        c.start()

    pairs = [(h1_t, dqkv), (df_t, hid), (h3_t, dgate), (h3_t, dup), (da_t, o)]
    units, places = [], []
    for k, (left, right) in enumerate(pairs):
        for column, size in halves(right.shape[1]):
            units.append(Reduce(len(units), left, right, column, size, bufs, sems))
            places.append((k, column, size))
    units[0].load()
    me = units[0].me

    barrier = pltpu.get_barrier_semaphore()
    for shift in (units[0].dc, units[0].dx, units[0].dy):
        pl.semaphore_signal(barrier, 1, device_id={"dp": me + shift}, device_id_type=MESH)
    for k in range(1, n):
        peer = lax.rem(i + k, n)
        pl.semaphore_signal(barrier, 1, device_id={"tensor": peer}, device_id_type=MESH)
    pl.semaphore_wait(barrier, n + 2)
    for c in loads:
        c.wait()

    def compute(t, block):
        def tile(k):
            at = pl.ds(pl.multiple_of(k * TILE, TILE), TILE)
            part[block, :, at] = dot_nt(d[block], w[at, :]).astype(BF16)

        loop(width // TILE, tile)

    step, land, done = scatter_steps(i, n, part, landed, rs_send, rs_recv, compute)

    def input_rows():
        def tile(k):
            at = pl.ds(pl.multiple_of(k * TILE, TILE), TILE)
            mine[:, at] = dot_nt(d[i], w[at, :])

        loop(width // TILE, tile)

    def input_grad():
        land()
        scale = 1.0 + gains[0:1, :]
        fold[...] = jnp.zeros_like(fold)

        def chunk(c):
            r = pl.ds(c * ROWS, ROWS)
            dh1 = summed_rows(i, n, mine, landed, r)
            v = x[r, :].astype(F32)
            inv = inverse_rms(v)
            in_grad[r, :] = (dy[r, :] + norm_back(dh1 * scale, v, inv)).astype(BF16)
            fold[...] += fold_rows(dh1 * (v * inv))

        loop(rows // ROWS, chunk)
        gain_out[...] = jnp.sum(fold[...], axis=0, keepdims=True)
        done()

    def out_copy(u):
        k, column, size = places[u]
        return pltpu.make_async_copy(
            stage.at[u % 2, :, pl.ds(0, size)],
            outs[k].at[:, pl.ds(column, size)],
            out_sem.at[u % 2],
        )

    def kv_copy(k):
        return pltpu.make_async_remote_copy(
            kv_stage,
            kv_out.at[i],
            kv_send.at[k],
            kv_recv.at[k],
            device_id={"tensor": lax.rem(i + k, n)},
            device_id_type=MESH,
        )

    def kv_arrival(k):
        from_peer = lax.rem(i + n - k, n)
        return pltpu.make_async_remote_copy(
            kv_stage,
            kv_out.at[from_peer],
            kv_send.at[k],
            kv_recv.at[k],
            device_id={"tensor": from_peer},
            device_id_type=MESH,
        )

    kv_own = pltpu.make_async_copy(kv_stage, kv_out.at[i], kv_sem.at[0])

    def finish(u):
        if u >= 2:
            out_copy(u - 2).wait()
        size = places[u][2]

        def put(r, total):
            stage[u % 2, r, pl.ds(0, size)] = total
            if u == 0:
                kv_stage[r, :] = total[:, split:].astype(BF16)

        units[u].end(put)
        out_copy(u).start()
        if u == 0:
            for k in range(1, n):
                kv_copy(k).start()
            kv_own.start()

    count = len(units)
    line = [functools.partial(step, jnp.int32(k)) for k in range(n - 1)] + [input_rows, input_grad]
    for u in range(count + 2):
        if u < count:
            units[u].begin()
            if u + 1 < count:
                units[u + 1].load()
            units[u].middle()
        if 1 <= u <= count:
            units[u - 1].turn()
        if u >= 2:
            finish(u - 2)
        if u < len(line):
            line[u]()
    for u in range(count + 2, len(line)):
        line[u]()
    for u in range(max(0, count - 2), count):
        out_copy(u).wait()
    kv_own.wait()
    for k in range(1, n):
        kv_copy(k).wait_send()
        kv_arrival(k).wait_recv()


def tail(n, m, split, x, dy, gains, d, w, lefts, rights):
    rows, width = x.shape
    tokens = n * rows
    own_rows = width // m
    widest = max(size for right in rights for _, size in halves(right.shape[1]))
    bufs, sems = reduce_scratch(own_rows, tokens, widest)
    sem = pltpu.SemaphoreType.DMA
    kv_width = rights[0].shape[1] - split
    return pl.pallas_call(
        functools.partial(tail_kernel, n, split),
        out_shape=[
            jax.ShapeDtypeStruct((rows, width), BF16),
            jax.ShapeDtypeStruct((1, width), F32),
        ]
        + [jax.ShapeDtypeStruct((own_rows, right.shape[1]), F32) for right in rights]
        + [jax.ShapeDtypeStruct((n, own_rows, kv_width), BF16)],
        in_specs=[VM, VM, VM] + [ANY] * 11,
        out_specs=[VM, VM] + [ANY] * 6,
        scratch_shapes=[
            pltpu.VMEM(d.shape, BF16),
            pltpu.VMEM(w.shape, BF16),
            pltpu.VMEM((n, rows, width), BF16),
            pltpu.VMEM((n + 1, rows, width), BF16),
            pltpu.VMEM((rows, width), F32),
            pltpu.VMEM((8, width), F32),
            pltpu.VMEM((2, own_rows, widest), F32),
            pltpu.VMEM((own_rows, kv_width), BF16),
            sem((2,)),
        ]
        + line_scratch(n)
        + [sem((2,)), sem((1,)), sem((n,)), sem((n,))]
        + bufs
        + sems,
        compiler_params=params(7, 62),
        cost_estimate=cost(0, 600 << 20),
        name="tail",
    )(x, dy, gains, d, w, *lefts, *rights)


def rope_tables():
    positions = jnp.arange(L, dtype=jnp.int32).astype(F32)
    exponent = jnp.arange(HD // 2, dtype=jnp.int32).astype(F32) * (-2.0 / HD)
    angles = positions[:, None] * jnp.exp(exponent * jnp.log(F32(10000.0)))[None, :]
    return jnp.cos(angles), jnp.sin(angles)


def weight_grad(left, right):
    return dot_tn(left, right).astype(BF16)


def scatter_rows(grad):
    return lax.psum_scatter(grad, "dp", scatter_dimension=0, tiled=True)


def body(
    n,
    m,
    layer_in,
    out_grad,
    piece_starts,
    attn_gain,
    attn_out_gain,
    feed_gain,
    feed_out_gain,
    query_weight,
    key_weight,
    value_weight,
    out_weight,
    gate_weight,
    up_weight,
    down_weight,
):
    heads = query_weight.shape[1] // HD
    fan = H // KV
    kvs = max(1, heads // fan)
    rank = lax.axis_index("tensor")
    kv_at = (rank * heads // fan) * HD
    rows, width = layer_in.shape
    tokens = n * rows

    gathered = gather_gains(m, jnp.stack([attn_gain, attn_out_gain, feed_gain, feed_out_gain]))
    gains = gathered.transpose(1, 0, 2).reshape(4, width).astype(F32)

    def collect(shard):
        return lax.all_gather(shard, "dp", axis=0, tiled=True)

    wqkv = collect(
        jnp.concatenate(
            [
                query_weight,
                lax.dynamic_slice_in_dim(key_weight, kv_at, kvs * HD, 1),
                lax.dynamic_slice_in_dim(value_weight, kv_at, kvs * HD, 1),
            ],
            axis=1,
        )
    )
    wo = collect(out_weight.T)
    wd = collect(down_weight.T)
    cos, sin = rope_tables()

    spread = m == 8
    h1, wg = first(n, m, layer_in, gains, gate_weight if spread else None)
    if not spread:
        wg = collect(gate_weight)
    h1_flat = h1.reshape(tokens, width)
    q, k, v, o = attend(heads, kvs, piece_starts, h1_flat, wqkv, cos, sin)
    wu = up_weight if spread else collect(up_weight)
    attn, y, h3, hid, up, ge, *wu_full = into_feed(
        n, m, spread, layer_in, gains, o.reshape(n, rows, heads * HD), wo, wg, wu
    )
    if spread:
        wu = wu_full[0].reshape(wg.shape)
    layer_out, gain_four, df, dgate, dup = turn_feed(n, y, out_grad, gains, hid, wd, up, ge)
    flat = lambda a: a.reshape(tokens, a.shape[-1])
    split = heads * HD
    if spread and n * kvs == KV:
        dy, gain_mid, dattn, do = out_of_feed(n, y, attn, out_grad, gains, dgate, dup, wg, wu, wo)
        d = attend_back(heads, kvs, piece_starts, q, k, v, flat(do), cos, sin)
        lefts = [flat(a).T for a in (h1, df, h3, dattn)]
        rights = [d, flat(hid), flat(dgate), flat(dup), o]
        in_grad, gain_one, qkv_sum, down_sum, gate_sum, up_sum, out_sum, kv = tail(
            n, m, split, layer_in, dy, gains, d.reshape(n, rows, -1), wqkv, lefts, rights
        )
        own_rows = qkv_sum.shape[0]
        kv = kv.reshape(n, own_rows, 2, kvs * HD).transpose(2, 1, 0, 3).reshape(2, own_rows, KV * HD)
    else:
        tie = lax.optimization_barrier
        down_part = weight_grad(flat(df), flat(hid))
        gate_part = weight_grad(flat(h3), flat(dgate))
        up_part = weight_grad(flat(h3), flat(dup))
        dgate, dup, down_part, gate_part, up_part = tie((dgate, dup, down_part, gate_part, up_part))
        down_sum, gate_sum, up_sum = map(scatter_rows, (down_part, gate_part, up_part))
        dy, gain_mid, dattn, do = out_of_feed(n, y, attn, out_grad, gains, dgate, dup, wg, wu, wo)
        do, dattn, down_sum, gate_sum = tie((do, dattn, down_sum, gate_sum))
        out_part = weight_grad(flat(dattn), o)
        do, out_part = tie((do, out_part))
        d = attend_back(heads, kvs, piece_starts, q, k, v, flat(do), cos, sin)
        qkv_part = weight_grad(h1_flat, d)
        d, qkv_part, up_sum = tie((d, qkv_part, up_sum))
        out_sum, qkv_sum = scatter_rows(out_part), scatter_rows(qkv_part)
        in_grad, gain_one = last(n, layer_in, dy, gains, d.reshape(n, rows, -1), wqkv)

        own_rows = qkv_sum.shape[0]
        kv = qkv_sum[:, split:].reshape(own_rows, 2, kvs * HD).transpose(1, 0, 2)
        if n * kvs == KV:
            kv = lax.all_gather(kv, "tensor", axis=2, tiled=True)
        else:
            kv = lax.dynamic_update_slice_in_dim(jnp.zeros((2, own_rows, KV * HD), BF16), kv, kv_at, 2)
            kv = lax.psum(kv, "tensor")
    kv = kv.astype(F32)

    gain_grads = jnp.concatenate([gain_one, gain_mid, gain_four], axis=0)
    gain_grads = sum_gains(n, m, gain_grads.reshape(4, m, width // m).transpose(1, 0, 2))
    return (
        layer_out,
        in_grad,
        qkv_sum[:, :split].astype(F32),
        kv[0],
        kv[1],
        out_sum.astype(F32).T,
        gate_sum.astype(F32),
        up_sum.astype(F32),
        down_sum.astype(F32).T,
        gain_grads[0],
        gain_grads[1],
        gain_grads[2],
        gain_grads[3],
    )


def solution(mesh):
    in_specs = (
        P(("dp", "tensor"), None),
        P(("dp", "tensor"), None),
        P("dp", None),
        P("dp"),
        P("dp"),
        P("dp"),
        P("dp"),
        P("dp", "tensor"),
        P("dp", None),
        P("dp", None),
        P("tensor", "dp"),
        P("dp", "tensor"),
        P("dp", "tensor"),
        P("tensor", "dp"),
    )
    out_specs = (
        P(("dp", "tensor"), None),
        P(("dp", "tensor"), None),
        P("dp", "tensor"),
        P("dp", None),
        P("dp", None),
        P("tensor", "dp"),
        P("dp", "tensor"),
        P("dp", "tensor"),
        P("tensor", "dp"),
        P("dp"),
        P("dp"),
        P("dp"),
        P("dp"),
    )
    program = functools.partial(body, mesh.shape["tensor"], mesh.shape["dp"])
    return jax.shard_map(program, mesh=mesh, in_specs=in_specs, out_specs=out_specs, check_vma=False)
```

```python
import functools

import jax
import jax.numpy as jnp
from jax import lax
from jax.experimental import pallas as pl
from jax.experimental.pallas import tpu as pltpu
from jax.sharding import PartitionSpec as P

H = 8
KV = 4
HD = 256
L = 1024
PIECE = 256

EPS = 1e-06
CAP = 50.0
F32 = jnp.float32
BF16 = jnp.bfloat16
MESH = pl.DeviceIdType.MESH
ANY = pl.BlockSpec(memory_space=pl.ANY)
VM = pl.BlockSpec(memory_space=pltpu.VMEM)
SM = pl.BlockSpec(memory_space=pltpu.SMEM)
ROWS = 16
TILE = 256


def dot_nn(a, b):
    return lax.dot_general(a, b, (((1,), (0,)), ((), ())), preferred_element_type=F32)


def dot_nt(a, b):
    return lax.dot_general(a, b, (((1,), (1,)), ((), ())), preferred_element_type=F32)


def dot_tn(a, b):
    return lax.dot_general(a, b, (((0,), (0,)), ((), ())), preferred_element_type=F32)


def tile_of(width):
    return next(t for t in (256, 384, 128) if width % t == 0)


def strip_of(count):
    return next(t for t in (64, 48, 32, 16) if count % t == 0)


def wide_tile(width):
    return next(t for t in (1152, 1024, 768, 512, 384, 256, 128) if width % t == 0)


def loop(count, body):
    lax.fori_loop(0, count, lambda t, c: (body(t), c)[1], 0)


def block_at(i, n, s):
    m = jnp.minimum(i, n - 1 - i)
    near = i + jnp.where(s % 2 == 1, -((s + 1) // 2), s // 2)
    far = jnp.where(i * 2 < n, i + (s - m), i - (s - m))
    return jnp.where(s <= 2 * m, near, far)


def line_barrier(i, n, peers=()):
    barrier = pltpu.get_barrier_semaphore()

    @pl.when(i > 0)
    def _():
        pl.semaphore_signal(barrier, 1, device_id={"tensor": i - 1}, device_id_type=MESH)

    @pl.when(i < n - 1)
    def _():
        pl.semaphore_signal(barrier, 1, device_id={"tensor": i + 1}, device_id_type=MESH)

    for peer in peers:
        pl.semaphore_signal(barrier, 1, device_id={"dp": peer}, device_id_type=MESH)
    pl.semaphore_wait(barrier, len(peers) + jnp.minimum(i, 1) + jnp.minimum(n - 1 - i, 1))


def gather_steps(i, n, held, send, recv):
    def copy(block, way, s, to):
        return pltpu.make_async_remote_copy(
            held.at[block],
            held.at[block],
            send.at[way, s],
            recv.at[block],
            device_id={"tensor": to},
            device_id_type=MESH,
        )

    up, down = jnp.minimum(i + 1, n - 1), jnp.maximum(i - 1, 0)

    def pass_on(s):
        low, high = i - s, i + s

        @pl.when((s > 0) & (low >= 0))
        def _():
            copy(low, 0, s, up).wait_recv()

        @pl.when((low >= 0) & (i < n - 1))
        def _():
            copy(low, 0, s, up).start()

        @pl.when((s > 0) & (high < n))
        def _():
            copy(high, 1, s, down).wait_recv()

        @pl.when((high < n) & (i > 0))
        def _():
            copy(high, 1, s, down).start()

    def finish(s):
        low, high = i - s, i + s

        @pl.when((low >= 0) & (i < n - 1))
        def _():
            copy(low, 0, s, up).wait_send()

        @pl.when((high < n) & (i > 0))
        def _():
            copy(high, 1, s, down).wait_send()

    return pass_on, functools.partial(loop, n, finish)


def gather_line(i, n, held, send, recv, compute):
    pass_on, finish = gather_steps(i, n, held, send, recv)

    def step(s):
        pass_on(s)
        compute(s, block_at(i, n, s))

    loop(n, step)
    finish()


def scatter_steps(i, n, part, landed, send, recv, compute):
    rows = part.shape[1]

    def copy(block, way, t, to):
        slot = jnp.where(block == to, n, block) if way else block
        return pltpu.make_async_remote_copy(
            part.at[block],
            landed.at[slot],
            send.at[way, t],
            recv.at[slot],
            device_id={"tensor": to},
            device_id_type=MESH,
        )

    def arrived(slot):
        pltpu.make_async_remote_copy(
            landed.at[slot],
            landed.at[slot],
            send.at[0, 0],
            recv.at[slot],
            device_id={"tensor": i},
            device_id_type=MESH,
        ).wait_recv()

    def add(block):
        strip = strip_of(rows)

        def chunk(c):
            r = pl.ds(c * strip, strip)
            total = part[block, r, :].astype(F32) + landed[block, r, :].astype(F32)
            part[block, r, :] = total.astype(BF16)

        loop(rows // strip, chunk)

    up, down = jnp.minimum(i + 1, n - 1), jnp.maximum(i - 1, 0)

    def step(k):
        t = k + 1
        compute(k, block_at(i, n, n - t))
        above, below = i + n - t, i - n + t

        @pl.when((above < n) & (i > 0))
        def _():
            arrived(above)
            add(above)

        @pl.when(above < n)
        def _():
            copy(above, 0, t, up).start()

        @pl.when((below >= 0) & (i < n - 1))
        def _():
            arrived(below)
            add(below)

        @pl.when(below >= 0)
        def _():
            copy(below, 1, t, down).start()

    def land():
        @pl.when(i > 0)
        def _():
            arrived(i)

        @pl.when(i < n - 1)
        def _():
            arrived(jnp.int32(n))

    def finish(k):
        t = k + 1

        @pl.when(i + n - t < n)
        def _():
            copy(i + n - t, 0, t, up).wait_send()

        @pl.when(i - n + t >= 0)
        def _():
            copy(i - n + t, 1, t, down).wait_send()

    return step, land, functools.partial(loop, n - 1, finish)


def scatter_line(i, n, part, landed, send, recv, compute, own):
    step, land, finish = scatter_steps(i, n, part, landed, send, recv, compute)
    loop(n - 1, step)
    own(n - 1)
    land()
    return finish


def summed_rows(i, n, mine, landed, r):
    zero = jnp.zeros((), F32)
    low = jnp.where(i > 0, landed[i, r, :].astype(F32), zero)
    high = jnp.where(i < n - 1, landed[n, r, :].astype(F32), zero)
    return mine[r, :] + low + high


def inverse_rms(v):
    return lax.rsqrt(jnp.mean(v * v, axis=-1, keepdims=True) + EPS)


def norm_back(e, v, r):
    unit = v * r
    return r * (e - unit * jnp.mean(e * unit, axis=-1, keepdims=True))


def fold_rows(v):
    return v.reshape(-1, 8, v.shape[-1]).sum(axis=0)


class Feed:
    def __init__(self, sources, slots, sems, which):
        self.sources, self.slots, self.sems, self.which = sources, slots, sems, which

    def copies(self, s):
        return [
            pltpu.make_async_copy(src.at[self.which(s)], slot.at[s % 2], self.sems.at[k, s % 2])
            for k, (src, slot) in enumerate(zip(self.sources, self.slots))
        ]

    def start(self, s):
        for c in self.copies(s):
            c.start()

    def wait(self, s):
        for c in self.copies(s):
            c.wait()

    def advance(self, s, count):
        self.wait(s)

        @pl.when(s + 1 < count)
        def _():
            self.start(s + 1)


class Drain:
    def __init__(self, targets, slots, sems, which):
        self.targets, self.slots, self.sems, self.which = targets, slots, sems, which

    def copies(self, s):
        return [
            pltpu.make_async_copy(slot.at[s % 2], dst.at[self.which(s)], self.sems.at[k, s % 2])
            for k, (dst, slot) in enumerate(zip(self.targets, self.slots))
        ]

    def free(self, s):
        @pl.when(s >= 2)
        def _():
            for c in self.copies(s - 2):
                c.wait()

    def start(self, s):
        for c in self.copies(s):
            c.start()

    def finish(self, count):
        for s in range(max(0, count - 2), count):
            for c in self.copies(jnp.int32(s)):
                c.wait()


class Spread:
    def __init__(self, own, full, send, recv, local):
        me = lax.axis_index("dp")
        c, x, y = me % 2, (me // 2) % 2, me // 4
        self.own, self.full, self.send, self.recv, self.local = own, full, send, recv, local
        self.me = me
        self.core = me + 1 - 2 * c
        self.x = me + 2 - 4 * x
        self.y = me + 4 - 8 * y
        self.far = self.x + 4 - 8 * y
        self.flip = 1 - 2 * c

    def peers(self):
        return (self.core, self.x, self.y)

    def view(self, owner, part):
        count = self.own.shape[0]
        first, size = ((0, count), (0, count // 2), (count // 2, count // 2))[part]
        return self.full.at[pl.ds(pl.multiple_of(owner * count + first, ROWS), size)]

    def copy(self, k, source, owner, part, to):
        return pltpu.make_async_remote_copy(
            self.own if source is None else self.view(source, part),
            self.view(owner, part),
            self.send.at[k],
            self.recv.at[k],
            device_id={"dp": to},
            device_id_type=MESH,
        )

    def sends(self):
        return (
            (0, None, self.me, 0, self.core),
            (1, None, self.me, 0, self.x),
            (2, None, self.me, 0, self.y),
            (3, self.x, self.x, 1, self.y),
            (4, self.y, self.y, 2, self.x),
            (5, self.x, self.x, 0, self.core),
            (6, self.y, self.y, 0, self.core),
            (7, self.far, self.far, 0, self.core),
        )

    def start(self, *which):
        for k in which:
            self.copy(*self.sends()[k]).start()

    def arrive(self, k):
        owner, part = {
            0: (self.core, 0),
            1: (self.x, 0),
            2: (self.y, 0),
            3: (self.far, 1),
            4: (self.far, 2),
            5: (self.x + self.flip, 0),
            6: (self.y + self.flip, 0),
            7: (self.far + self.flip, 0),
        }[k]
        self.copy(k, owner, owner, part, self.core).wait_recv()

    def keep(self):
        return pltpu.make_async_copy(self.own, self.view(self.me, 0), self.local.at[0])

    def begin(self):
        self.keep().start()
        self.start(1, 2, 0)

    def middle(self):
        self.arrive(1)
        self.arrive(2)
        self.start(3, 4, 5, 6)

    def turn(self):
        self.arrive(3)
        self.arrive(4)
        self.start(7)

    def end(self):
        for k in (0, 5, 6, 7):
            self.arrive(k)
        self.keep().wait()
        for k in range(8):
            self.copy(*self.sends()[k]).wait_send()


def spread_scratch():
    return [pltpu.SemaphoreType.DMA((8,)), pltpu.SemaphoreType.DMA((8,)), pltpu.SemaphoreType.DMA((1,))]


def line_scratch(n):
    return [pltpu.SemaphoreType.DMA((2, n)), pltpu.SemaphoreType.DMA((n + 1,))]


def params(cid, mib):
    return pltpu.CompilerParams(
        collective_id=cid, has_side_effects=True, vmem_limit_bytes=mib << 20
    )


def cost(flops, moved):
    return pl.CostEstimate(flops=flops, bytes_accessed=moved, transcendentals=0)


def gains_kernel(m, mine, out, send, recv):
    me = lax.axis_index("dp")
    barrier = pltpu.get_barrier_semaphore()
    for k in range(1, m):
        pl.semaphore_signal(
            barrier, 1, device_id={"dp": lax.rem(me + k, m)}, device_id_type=MESH
        )
    pl.semaphore_wait(barrier, m - 1)

    def copy(owner, k):
        return pltpu.make_async_remote_copy(
            mine,
            out.at[owner],
            send.at[k],
            recv.at[k],
            device_id={"dp": lax.rem(me + k, m)},
            device_id_type=MESH,
        )

    for k in range(1, m):
        copy(me, k).start()
    out[me] = mine[...]
    for k in range(1, m):
        copy(lax.rem(me + m - k, m), k).wait_recv()
    for k in range(1, m):
        copy(me, k).wait_send()


def gather_gains(m, mine):
    return pl.pallas_call(
        functools.partial(gains_kernel, m),
        out_shape=jax.ShapeDtypeStruct((m,) + mine.shape, mine.dtype),
        in_specs=[VM],
        out_specs=VM,
        scratch_shapes=[pltpu.SemaphoreType.DMA((m,)), pltpu.SemaphoreType.DMA((m,))],
        compiler_params=params(0, 16),
        name="gains",
    )(mine)


def sum_gains_kernel(n, m, mine, out, landed, total, across, send, recv, send_two, recv_two):
    me, i = lax.axis_index("dp"), lax.axis_index("tensor")
    barrier = pltpu.get_barrier_semaphore()
    dp_peer = lambda k: {"dp": lax.rem(me + k, m)}
    line_peer = lambda k: {"tensor": lax.rem(i + k, n)}
    for k in range(1, m):
        pl.semaphore_signal(barrier, 1, device_id=dp_peer(k), device_id_type=MESH)
    for k in range(1, n):
        pl.semaphore_signal(barrier, 1, device_id=line_peer(k), device_id_type=MESH)
    pl.semaphore_wait(barrier, m + n - 2)

    def to_owner(k):
        return pltpu.make_async_remote_copy(
            mine.at[lax.rem(me + k, m)], landed.at[k], send.at[k], recv.at[k],
            device_id=dp_peer(k), device_id_type=MESH,
        )

    def along(k):
        return pltpu.make_async_remote_copy(
            total, across.at[k], send_two.at[k], recv_two.at[k],
            device_id=line_peer(k), device_id_type=MESH,
        )

    for k in range(1, m):
        to_owner(k).start()
    here = mine[me]
    for k in range(1, m):
        to_owner(k).wait_recv()
        here = here + landed[k]
    total[...] = here
    for k in range(1, n):
        along(k).start()
    for k in range(1, n):
        along(k).wait_recv()
        here = here + across[k]
    out[...] = here
    for k in range(1, m):
        to_owner(k).wait_send()
    for k in range(1, n):
        along(k).wait_send()


def sum_gains(n, m, mine):
    shape = mine.shape[1:]
    return pl.pallas_call(
        functools.partial(sum_gains_kernel, n, m),
        out_shape=jax.ShapeDtypeStruct(shape, F32),
        in_specs=[VM],
        out_specs=VM,
        scratch_shapes=[
            pltpu.VMEM((m,) + shape, F32),
            pltpu.VMEM(shape, F32),
            pltpu.VMEM((n,) + shape, F32),
        ]
        + [pltpu.SemaphoreType.DMA((m,))] * 2
        + [pltpu.SemaphoreType.DMA((n,))] * 2,
        compiler_params=params(6, 16),
        name="sum_gains",
    )(mine)


def first_kernel(n, spread, x, gains, *refs):
    i = lax.axis_index("tensor")
    rows = x.shape[0]
    if spread:
        shard, full, gathered, turned, held, send, recv, out_sem, turn, turn_sem, *sems = refs
        gather = Spread(shard, gathered, *sems)
        line_barrier(i, n, gather.peers())
        gather.begin()
    else:
        full, held, send, recv, out_sem = refs
        line_barrier(i, n)
    scale = 1.0 + gains[0:1, :]

    strip = strip_of(rows)

    def chunk(c):
        r = pl.ds(c * strip, strip)
        v = x[r, :].astype(F32)
        held[i, r, :] = (v * inverse_rms(v) * scale).astype(BF16)

    loop(rows // strip, chunk)

    def keep(s, block):
        pltpu.make_async_copy(held.at[block], full.at[block], out_sem.at[s]).start()
        if spread:
            flip_rows(held.at[block], turned, block * rows, turn, turn_sem)
            pl.when(s == min(1, n - 1))(gather.middle)
            pl.when(s == min(2, n - 1))(gather.turn)

    gather_line(i, n, held, send, recv, keep)

    def finish(s):
        block = block_at(i, n, s)
        pltpu.make_async_copy(held.at[block], full.at[block], out_sem.at[s]).wait()

    loop(n, finish)
    if spread:
        gather.end()


def flip_rows(block, target, column, stage, sem):
    rows, width = block.shape
    size = stage.shape[1]
    pieces = width // size

    def copy(k):
        return pltpu.make_async_copy(
            stage.at[k % 2],
            target.at[pl.ds(k * size, size), pl.ds(pl.multiple_of(column, 128), rows)],
            sem.at[k % 2],
        )

    for k in range(pieces):
        if k >= 2:
            copy(k - 2).wait()
        for j in range(size // 256):
            at = pl.ds(k * size + j * 256, 256)
            stage[k % 2, pl.ds(j * 256, 256), :] = block[:, at].T
        copy(k).start()
    for k in range(max(0, pieces - 2), pieces):
        copy(k).wait()


def first(n, m, x, gains, shard):
    rows, width = x.shape
    spread = shard is not None
    outs = [jax.ShapeDtypeStruct((n, rows, width), BF16)]
    if spread:
        outs += [jax.ShapeDtypeStruct((m * shard.shape[0], shard.shape[1]), BF16)]
        outs += [jax.ShapeDtypeStruct((width, n * rows), BF16)]
        turn = [pltpu.VMEM((2, 768, rows), BF16), pltpu.SemaphoreType.DMA((2,))]
    out = pl.pallas_call(
        functools.partial(first_kernel, n, spread),
        out_shape=outs,
        in_specs=[VM, VM] + [ANY] * spread,
        out_specs=[ANY] * len(outs),
        scratch_shapes=[pltpu.VMEM((n, rows, width), BF16)]
        + line_scratch(n)
        + [pltpu.SemaphoreType.DMA((n,))]
        + (turn + spread_scratch() if spread else []),
        compiler_params=params(1, 32),
        cost_estimate=cost(0, 300 << 20),
        name="first",
    )(x, gains, *([shard] if spread else []))
    return out if spread else (out[0], None, None)


def turn(u, cos, sin):
    half = HD // 2
    a, b = u[:, :half], u[:, half:]
    return jnp.concatenate([a * cos - b * sin, b * cos + a * sin], axis=-1)


def row_limit(starts, seq, first_row, rows):
    pos = first_row + lax.broadcasted_iota(jnp.int32, (rows, 1), 0)
    limit = pos + 1
    for piece in range(2):
        begin = starts[seq, piece]
        inside = (pos >= begin) & (pos < begin + PIECE)
        limit = jnp.maximum(limit, jnp.where(inside, begin + PIECE, 0))
    return limit


def key_span(first_row, rows):
    return min(L, first_row + rows + PIECE)


def weights_of(q, k, limit):
    bent = jnp.tanh(dot_nt(q, k) * (1.0 / CAP))
    seen = lax.broadcasted_iota(jnp.int32, (1, k.shape[0]), 1) < limit
    w = jnp.where(seen, jnp.exp(CAP * bent), 0.0)
    return w * pl.reciprocal(jnp.sum(w, axis=-1, keepdims=True)), bent


def attend_kernel(heads, kvs, starts, h1, w, cos, sin, q_out, k_out, v_out, o_out):
    tokens = h1.shape[0]
    fan = heads // kvs
    block = 256

    def project(b):
        r = pl.ds(pl.multiple_of(b * block, block), block)
        at = pl.ds(pl.multiple_of(lax.rem(b * block, L), block), block)
        c, s = cos[at, :], sin[at, :]
        x = h1[r, :]
        for h in range(heads):
            u = dot_nn(x, w[:, h * HD : (h + 1) * HD])
            q_out[h, r, :] = (turn(u, c, s) * (HD**-0.5)).astype(BF16)
        for g in range(kvs):
            u = dot_nn(x, w[:, (heads + g) * HD : (heads + g + 1) * HD])
            k_out[g, r, :] = turn(u, c, s).astype(BF16)
            u = dot_nn(x, w[:, (heads + kvs + g) * HD : (heads + kvs + g + 1) * HD])
            v_out[g, r, :] = u.astype(BF16)

    loop(tokens // block, project)
    for seq in range(tokens // L):
        base = seq * L
        for row in range(0, L, block):
            span = key_span(row, block)
            limit = row_limit(starts, seq, row, block)
            for h in range(heads):
                q = q_out[h, base + row : base + row + block, :]
                p, _ = weights_of(q, k_out[h // fan, base : base + span, :], limit)
                o = dot_nn(p.astype(BF16), v_out[h // fan, base : base + span, :])
                o_out[base + row : base + row + block, h * HD : (h + 1) * HD] = o.astype(BF16)


def attend(heads, kvs, starts, h1, w, cos, sin):
    tokens = h1.shape[0]
    return pl.pallas_call(
        functools.partial(attend_kernel, heads, kvs),
        out_shape=[
            jax.ShapeDtypeStruct((heads, tokens, HD), BF16),
            jax.ShapeDtypeStruct((kvs, tokens, HD), BF16),
            jax.ShapeDtypeStruct((kvs, tokens, HD), BF16),
            jax.ShapeDtypeStruct((tokens, heads * HD), BF16),
        ],
        in_specs=[SM, VM, VM, VM, VM],
        out_specs=[VM, VM, VM, VM],
        compiler_params=pltpu.CompilerParams(vmem_limit_bytes=48 << 20),
        cost_estimate=cost(20 << 30, 20 << 20),
        name="attend",
    )(starts, h1, w, cos, sin)


def attend_back_kernel(heads, kvs, starts, q_in, k_in, v_in, do_in, cos, sin, out, dk, dv):
    tokens = q_in.shape[1]
    fan = heads // kvs
    block = 256
    for seq in range(tokens // L):
        base = seq * L
        for g in range(kvs):
            dk[...] = jnp.zeros_like(dk)
            dv[...] = jnp.zeros_like(dv)
            for row in range(0, L, block):
                span = key_span(row, block)
                limit = row_limit(starts, seq, row, block)
                k = k_in[g, base : base + span, :]
                v = v_in[g, base : base + span, :]
                at = slice(base + row, base + row + block)
                for h in range(g * fan, (g + 1) * fan):
                    q = q_in[h, at, :]
                    do = do_in[at, h * HD : (h + 1) * HD]
                    p, bent = weights_of(q, k, limit)
                    dp = dot_nt(do, v)
                    delta = jnp.sum(p * dp, axis=-1, keepdims=True)
                    ds = (p * (dp - delta) * (1.0 - bent * bent)).astype(BF16)
                    dq = dot_nn(ds, k)
                    c, s = cos[row : row + block, :], sin[row : row + block, :]
                    out[at, h * HD : (h + 1) * HD] = (turn(dq, c, -s) * (HD**-0.5)).astype(BF16)
                    dk[:span, :] += dot_tn(ds, q)
                    dv[:span, :] += dot_tn(p.astype(BF16), do)

            def close(b, g=g, base=base):
                r = pl.ds(pl.multiple_of(b * block, block), block)
                to = pl.ds(pl.multiple_of(base + b * block, block), block)
                back = turn(dk[r, :], cos[r, :], -sin[r, :])
                out[to, (heads + g) * HD : (heads + g + 1) * HD] = back.astype(BF16)
                left = (heads + kvs + g) * HD
                out[to, left : left + HD] = dv[r, :].astype(BF16)

            loop(L // block, close)


def attend_back(heads, kvs, starts, q, k, v, do, cos, sin):
    tokens = q.shape[1]
    return pl.pallas_call(
        functools.partial(attend_back_kernel, heads, kvs),
        out_shape=jax.ShapeDtypeStruct((tokens, (heads + 2 * kvs) * HD), BF16),
        in_specs=[SM, VM, VM, VM, VM, VM, VM],
        out_specs=VM,
        scratch_shapes=[pltpu.VMEM((L, HD), F32), pltpu.VMEM((L, HD), F32)],
        compiler_params=pltpu.CompilerParams(vmem_limit_bytes=48 << 20),
        cost_estimate=cost(30 << 30, 20 << 20),
        name="attend_back",
    )(starts, q, k, v, do, cos, sin)


def into_feed_kernel(
    n, x, gains, o_hbm, wo_hbm, wg_hbm, wu_hbm,
    attn_out, y_out, h3_full, hid_out, up_out, ge_out,
    o, wo, wg, wu, part, landed, mine, held, hid_s, up_s, ge_s,
    load, rs_send, rs_recv, ag_send, ag_recv, keep_sem, out_sem,
):
    i = lax.axis_index("tensor")
    rows, width = x.shape
    loads = [
        pltpu.make_async_copy(src, dst, load.at[k])
        for k, (src, dst) in enumerate(((o_hbm, o), (wo_hbm, wo), (wg_hbm, wg), (wu_hbm, wu)))
    ]
    for c in loads:
        c.start()
    line_barrier(i, n)
    loads[0].wait()
    loads[1].wait()

    def compute(t, block):
        def tile(k):
            at = pl.ds(pl.multiple_of(k * TILE, TILE), TILE)
            part[block, :, at] = dot_nt(o[block], wo[at, :]).astype(BF16)

        loop(width // TILE, tile)

    def own(t):
        def tile(k):
            at = pl.ds(pl.multiple_of(k * TILE, TILE), TILE)
            mine[:, at] = dot_nt(o[i], wo[at, :])

        loop(width // TILE, tile)

    done = scatter_line(i, n, part, landed, rs_send, rs_recv, compute, own)
    scale_two, scale_three = 1.0 + gains[1:2, :], 1.0 + gains[2:3, :]

    def chunk(c):
        r = pl.ds(c * ROWS, ROWS)
        attn = summed_rows(i, n, mine, landed, r)
        attn_out[r, :] = attn
        y = x[r, :].astype(F32) + attn * inverse_rms(attn) * scale_two
        y_out[r, :] = y
        held[i, r, :] = (y * inverse_rms(y) * scale_three).astype(BF16)

    loop(rows // ROWS, chunk)
    done()
    loads[2].wait()
    loads[3].wait()
    drain = Drain(
        (hid_out, up_out, ge_out), (hid_s, up_s, ge_s), out_sem, lambda s: block_at(i, n, s)
    )

    def forward(s, block):
        pltpu.make_async_copy(held.at[block], h3_full.at[block], keep_sem.at[s]).start()
        drain.free(s)
        slot = s % 2
        span = tile_of(wg.shape[1])

        def tile(k):
            at = pl.ds(pl.multiple_of(k * span, span), span)
            u = dot_nn(held[block], wg[:, at])
            up = dot_nn(held[block], wu[:, at])
            c = 0.7978845608028654
            th = jnp.tanh(c * (u + 0.044715 * (u * u * u)))
            half = 0.5 * (1.0 + th)
            gelu = u * half
            slope = half + 0.5 * u * (1.0 - th * th) * (c * (1.0 + 0.134145 * (u * u)))
            hid_s[slot, :, at] = (gelu * up).astype(BF16)
            up_s[slot, :, at] = (up * slope).astype(BF16)
            ge_s[slot, :, at] = gelu.astype(BF16)

        loop(wg.shape[1] // span, tile)
        drain.start(s)

    gather_line(i, n, held, ag_send, ag_recv, forward)
    drain.finish(n)

    def finish(s):
        block = block_at(i, n, s)
        pltpu.make_async_copy(held.at[block], h3_full.at[block], keep_sem.at[s]).wait()

    loop(n, finish)


def into_feed(n, x, gains, o, wo, wg, wu):
    rows, width = x.shape
    wide = wg.shape[1]
    blocks = lambda w: jax.ShapeDtypeStruct((n, rows, w), BF16)
    mine = jax.ShapeDtypeStruct((rows, width), F32)
    return pl.pallas_call(
        functools.partial(into_feed_kernel, n),
        out_shape=[mine, mine, blocks(width), blocks(wide), blocks(wide), blocks(wide)],
        in_specs=[VM, VM, ANY, ANY, ANY, ANY],
        out_specs=[VM, VM, ANY, ANY, ANY, ANY],
        scratch_shapes=[
            pltpu.VMEM(o.shape, BF16),
            pltpu.VMEM(wo.shape, BF16),
            pltpu.VMEM(wg.shape, BF16),
            pltpu.VMEM(wu.shape, BF16),
            pltpu.VMEM((n, rows, width), BF16),
            pltpu.VMEM((n + 1, rows, width), BF16),
            pltpu.VMEM((rows, width), F32),
            pltpu.VMEM((n, rows, width), BF16),
        ]
        + [pltpu.VMEM((2, rows, wide), BF16)] * 3
        + [pltpu.SemaphoreType.DMA((4,))]
        + line_scratch(n) * 2
        + [pltpu.SemaphoreType.DMA((n,)), pltpu.SemaphoreType.DMA((3, 2))],
        compiler_params=params(2, 62),
        cost_estimate=cost(0, 600 << 20),
        name="into_feed",
    )(x, gains, o, wo, wg, wu)


def turn_feed_kernel(
    n, y, dout, gains, hid_hbm, wd_hbm, up_hbm, ge_hbm,
    layer_out, gain_out, df_full, dgate_out, dup_out,
    wd, hid_s, part, landed, mine, held, up_s, ge_s, dg_s, du_s, fold,
    load, feed_sem, rs_send, rs_recv, ag_send, ag_recv, keep_sem, back_sem, out_sem,
):
    i = lax.axis_index("tensor")
    rows, width = y.shape
    whole = pltpu.make_async_copy(wd_hbm, wd, load.at[0])
    whole.start()
    feed = Feed((hid_hbm,), (hid_s,), feed_sem, lambda s: block_at(i, n, n - 1 - s))
    feed.start(jnp.int32(0))
    line_barrier(i, n)
    whole.wait()

    def compute(t, block):
        feed.advance(t, n)
        slot = t % 2

        def tile(k):
            at = pl.ds(pl.multiple_of(k * TILE, TILE), TILE)
            part[block, :, at] = dot_nt(hid_s[slot], wd[at, :]).astype(BF16)

        loop(width // TILE, tile)

    def own(t):
        t = jnp.int32(t)
        feed.advance(t, n)
        slot = t % 2

        def tile(k):
            at = pl.ds(pl.multiple_of(k * TILE, TILE), TILE)
            mine[:, at] = dot_nt(hid_s[slot], wd[at, :])

        loop(width // TILE, tile)

    done = scatter_line(i, n, part, landed, rs_send, rs_recv, compute, own)
    scale = 1.0 + gains[3:4, :]
    fold[...] = jnp.zeros_like(fold)

    def chunk(c):
        r = pl.ds(c * ROWS, ROWS)
        f = summed_rows(i, n, mine, landed, r)
        g = dout[r, :].astype(F32)
        inv = inverse_rms(f)
        layer_out[r, :] = (y[r, :] + f * inv * scale).astype(BF16)
        held[i, r, :] = norm_back(g * scale, f, inv).astype(BF16)
        fold[...] += fold_rows(g * (f * inv))

    loop(rows // ROWS, chunk)
    gain_out[...] = jnp.sum(fold[...], axis=0, keepdims=True)
    done()
    sides = Feed((up_hbm, ge_hbm), (up_s, ge_s), back_sem, lambda s: block_at(i, n, s))
    drain = Drain((dgate_out, dup_out), (dg_s, du_s), out_sem, lambda s: block_at(i, n, s))
    sides.start(jnp.int32(0))

    def backward(s, block):
        pltpu.make_async_copy(held.at[block], df_full.at[block], keep_sem.at[s]).start()
        sides.advance(s, n)
        drain.free(s)
        slot = s % 2
        span = tile_of(wd.shape[1])

        def tile(k):
            at = pl.ds(pl.multiple_of(k * span, span), span)
            dhid = dot_nn(held[block], wd[:, at])
            dg_s[slot, :, at] = (dhid * up_s[slot, :, at].astype(F32)).astype(BF16)
            du_s[slot, :, at] = (dhid * ge_s[slot, :, at].astype(F32)).astype(BF16)

        loop(wd.shape[1] // span, tile)
        drain.start(s)

    gather_line(i, n, held, ag_send, ag_recv, backward)
    drain.finish(n)

    def finish(s):
        block = block_at(i, n, s)
        pltpu.make_async_copy(held.at[block], df_full.at[block], keep_sem.at[s]).wait()

    loop(n, finish)


def turn_feed(n, y, dout, gains, hid, wd, up, ge):
    rows, width = y.shape
    wide = wd.shape[1]
    blocks = lambda w: jax.ShapeDtypeStruct((n, rows, w), BF16)
    return pl.pallas_call(
        functools.partial(turn_feed_kernel, n),
        out_shape=[
            jax.ShapeDtypeStruct((rows, width), BF16),
            jax.ShapeDtypeStruct((1, width), F32),
            blocks(width),
            blocks(wide),
            blocks(wide),
        ],
        in_specs=[VM, VM, VM, ANY, ANY, ANY, ANY],
        out_specs=[VM, VM, ANY, ANY, ANY],
        scratch_shapes=[
            pltpu.VMEM(wd.shape, BF16),
            pltpu.VMEM((2, rows, wide), BF16),
            pltpu.VMEM((n, rows, width), BF16),
            pltpu.VMEM((n + 1, rows, width), BF16),
            pltpu.VMEM((rows, width), F32),
            pltpu.VMEM((n, rows, width), BF16),
        ]
        + [pltpu.VMEM((2, rows, wide), BF16)] * 4
        + [pltpu.VMEM((8, width), F32)]
        + [pltpu.SemaphoreType.DMA((1,)), pltpu.SemaphoreType.DMA((1, 2))]
        + line_scratch(n) * 2
        + [
            pltpu.SemaphoreType.DMA((n,)),
            pltpu.SemaphoreType.DMA((2, 2)),
            pltpu.SemaphoreType.DMA((2, 2)),
        ],
        compiler_params=params(3, 62),
        cost_estimate=cost(0, 600 << 20),
        name="turn_feed",
    )(y, dout, gains, hid, wd, up, ge)


def out_of_feed_kernel(
    n, y, attn, dout, gains, dgate_hbm, dup_hbm, wg_hbm, wu_hbm, wo_hbm,
    dy_out, gain_out, dattn_full, do_out,
    wg, wu, wo, dg_s, du_s, part, landed, mine, held, do_s, fold,
    load, feed_sem, rs_send, rs_recv, ag_send, ag_recv, keep_sem, out_sem,
):
    i = lax.axis_index("tensor")
    rows, width = y.shape
    loads = [
        pltpu.make_async_copy(src, dst, load.at[k])
        for k, (src, dst) in enumerate(((wg_hbm, wg), (wu_hbm, wu), (wo_hbm, wo)))
    ]
    for c in loads:
        c.start()
    feed = Feed((dgate_hbm, dup_hbm), (dg_s, du_s), feed_sem, lambda s: block_at(i, n, n - 1 - s))
    feed.start(jnp.int32(0))
    line_barrier(i, n)
    loads[0].wait()
    loads[1].wait()

    def product(slot, at):
        return dot_nt(dg_s[slot], wg[at, :]) + dot_nt(du_s[slot], wu[at, :])

    def compute(t, block):
        feed.advance(t, n)
        slot = t % 2

        def tile(k):
            at = pl.ds(pl.multiple_of(k * TILE, TILE), TILE)
            part[block, :, at] = product(slot, at).astype(BF16)

        loop(width // TILE, tile)

    def own(t):
        t = jnp.int32(t)
        feed.advance(t, n)
        slot = t % 2

        def tile(k):
            at = pl.ds(pl.multiple_of(k * TILE, TILE), TILE)
            mine[:, at] = product(slot, at)

        loop(width // TILE, tile)

    done = scatter_line(i, n, part, landed, rs_send, rs_recv, compute, own)
    scale_two, scale_three = 1.0 + gains[1:2, :], 1.0 + gains[2:3, :]
    fold[...] = jnp.zeros_like(fold)

    def chunk(c):
        r = pl.ds(c * ROWS, ROWS)
        dh3 = summed_rows(i, n, mine, landed, r)
        v = y[r, :]
        inv = inverse_rms(v)
        dy = dout[r, :].astype(F32) + norm_back(dh3 * scale_three, v, inv)
        dy_out[r, :] = dy
        fold[1] += fold_rows(dh3 * (v * inv))
        a = attn[r, :]
        inv = inverse_rms(a)
        held[i, r, :] = norm_back(dy * scale_two, a, inv).astype(BF16)
        fold[0] += fold_rows(dy * (a * inv))

    loop(rows // ROWS, chunk)
    gain_out[0:1, :] = jnp.sum(fold[0], axis=0, keepdims=True)
    gain_out[1:2, :] = jnp.sum(fold[1], axis=0, keepdims=True)
    done()
    loads[2].wait()
    drain = Drain((do_out,), (do_s,), out_sem, lambda s: block_at(i, n, s))

    def backward(s, block):
        pltpu.make_async_copy(held.at[block], dattn_full.at[block], keep_sem.at[s]).start()
        drain.free(s)
        do_s[s % 2] = dot_nn(held[block], wo[...]).astype(BF16)
        drain.start(s)

    gather_line(i, n, held, ag_send, ag_recv, backward)
    drain.finish(n)

    def finish(s):
        block = block_at(i, n, s)
        pltpu.make_async_copy(held.at[block], dattn_full.at[block], keep_sem.at[s]).wait()

    loop(n, finish)


def out_of_feed(n, y, attn, dout, gains, dgate, dup, wg, wu, wo):
    rows, width = y.shape
    wide = wg.shape[1]
    narrow = wo.shape[1]
    return pl.pallas_call(
        functools.partial(out_of_feed_kernel, n),
        out_shape=[
            jax.ShapeDtypeStruct((rows, width), F32),
            jax.ShapeDtypeStruct((2, width), F32),
            jax.ShapeDtypeStruct((n, rows, width), BF16),
            jax.ShapeDtypeStruct((n, rows, narrow), BF16),
        ],
        in_specs=[VM, VM, VM, VM, ANY, ANY, ANY, ANY, ANY],
        out_specs=[VM, VM, ANY, ANY],
        scratch_shapes=[
            pltpu.VMEM(wg.shape, BF16),
            pltpu.VMEM(wu.shape, BF16),
            pltpu.VMEM(wo.shape, BF16),
            pltpu.VMEM((2, rows, wide), BF16),
            pltpu.VMEM((2, rows, wide), BF16),
            pltpu.VMEM((n, rows, width), BF16),
            pltpu.VMEM((n + 1, rows, width), BF16),
            pltpu.VMEM((rows, width), F32),
            pltpu.VMEM((n, rows, width), BF16),
            pltpu.VMEM((2, rows, narrow), BF16),
            pltpu.VMEM((2, 8, width), F32),
        ]
        + [pltpu.SemaphoreType.DMA((3,)), pltpu.SemaphoreType.DMA((2, 2))]
        + line_scratch(n) * 2
        + [pltpu.SemaphoreType.DMA((n,)), pltpu.SemaphoreType.DMA((1, 2))],
        compiler_params=params(4, 62),
        cost_estimate=cost(0, 600 << 20),
        name="out_of_feed",
    )(y, attn, dout, gains, dgate, dup, wg, wu, wo)


class Slots:
    def __init__(self, arrays, pool, firsts, sems, view, width=None):
        self.arrays, self.pool, self.firsts, self.sems, self.view = arrays, pool, firsts, sems, view
        self.width = width or pool.shape[2]

    def copies(self, s, inward):
        for k, (array, first) in enumerate(zip(self.arrays, self.firsts)):
            slot = self.pool.at[first + s % 2, :, pl.ds(0, self.width)]
            block = self.view(array, s)
            pair = (block, slot) if inward else (slot, block)
            yield pltpu.make_async_copy(*pair, self.sems.at[k, s % 2])

    def fetch(self, s):
        for c in self.copies(s, True):
            c.start()

    def advance(self, s, count):
        for c in self.copies(s, True):
            c.wait()
        if s + 1 < count:
            self.fetch(s + 1)

    def free(self, s):
        if s >= 2:
            self.settle(s - 2)

    def settle(self, s):
        for c in self.copies(s, False):
            c.wait()

    def leave(self, s):
        for c in self.copies(s, False):
            c.start()

    def finish(self, count):
        for s in range(max(0, count - 2), count):
            self.settle(s)


def middle_kernel(
    n, x_hbm, dout_hbm, gains, o_hbm, wo_hbm, wg_hbm, wu_hbm, wd_hbm,
    layer_out, dy_out, gain_out, h3_t, hid_out, up_out, ge_out, df_t, dgate_out, dup_out,
    dattn_t, do_out,
    xs, dout, wo, wg, wu, wd, part, landed, held, y, attn, pool, fold, flip,
    load, rs_send, rs_recv, ag_send, ag_recv, flip_sem, in_sem, out_sem, last_sem,
    wu_send, wu_recv, wu_local, wd_send, wd_recv, wd_local,
):
    i = lax.axis_index("tensor")
    rows, width = xs.shape
    piece = rows // 2
    narrow = wo_hbm.shape[1]
    pairs = ((wo_hbm, wo), (x_hbm, xs), (wg_hbm, wg), (dout_hbm, dout))
    loads = [pltpu.make_async_copy(a, b, load.at[k]) for k, (a, b) in enumerate(pairs)]
    for c in loads:
        c.start()
    up_spread = Spread(wu_hbm, wu, wu_send, wu_recv, wu_local)
    down_spread = Spread(wd_hbm, wd, wd_send, wd_recv, wd_local)
    line_barrier(i, n, up_spread.peers())
    up_spread.begin()
    loads[0].wait()
    wide = wd.shape[1]
    over, across = min(768, wide_tile(width)), min(768, wide_tile(wide))
    scale_two, scale_three, scale_four = (1.0 + gains[k : k + 1, :] for k in (1, 2, 3))
    fold[...] = jnp.zeros_like(fold)

    def tiles(total, size, body):
        loop(total // size, lambda k: body(pl.ds(pl.multiple_of(k * size, size), size)))

    def place(c):
        return pl.ds(c * piece, piece)

    def forward_view(c):
        return lambda array, s: array.at[block_at(i, n, s), place(c)]

    def backward_view(c):
        return lambda array, s: array.at[block_at(i, n, n - 1 - s), place(c)]

    class Sum:
        def __init__(self, which, c, product, feed=None):
            at = 2 * which + c
            self.c, self.feed = c, feed
            self.part, self.landed = part.at[c], landed.at[c]

            def compute(t, block):
                if feed:
                    feed.advance(t, n)

                def tile(at):
                    self.part[block, :, at] = product(t, block, at).astype(BF16)

                tiles(width, over, tile)

            self.compute = compute
            self.step, self.land, self.done = scatter_steps(
                i, n, self.part, self.landed, rs_send.at[at], rs_recv.at[at], compute
            )

        def start(self):
            if self.feed:
                self.feed.fetch(0)
            self.step(0)

        def own(self):
            self.compute(n - 1, i)

        def rows(self, r):
            return summed_rows(i, n, self.part.at[i], self.landed, r)

    class Gather:
        def __init__(self, which, c, full, compute, drained):
            at = 2 * which + c
            self.c, self.full, self.compute, self.drained = c, full, compute, drained
            self.pass_on, self.sent = gather_steps(i, n, held.at[c], ag_send.at[at], ag_recv.at[at])

        def use(self, s):
            block = block_at(i, n, s)
            self.compute(s, block)
            column = block * rows + self.c * piece
            flip_rows(held.at[self.c, block], self.full, column, flip, flip_sem)

        def finish(self):
            self.use(n - 1)
            self.sent()
            self.drained(n)

    def chunks(c, body):
        strip = strip_of(piece)

        def one(k):
            body(pl.ds(k * strip, strip), pl.ds(c * piece + k * strip, strip))

        loop(piece // strip, one)


    def out_product(t, block, at):
        return dot_nt(pool[8 + t % 2, :, pl.ds(0, narrow)], wo[at, :])

    def down_product(t, block, at):
        return dot_nt(pool[6 + t % 2], wd[at, :])

    def in_product(t, block, at):
        return dot_nt(pool[6 + t % 2], wg[at, :]) + dot_nt(pool[10 + t % 2], wu[at, :])

    def sums(c):
        heads = Slots((o_hbm,), pool, (8,), in_sem.at[3, c], backward_view(c), narrow)
        hid = Slots((hid_out,), pool, (6,), in_sem.at[0, c], backward_view(c))
        both = Slots((dgate_out, dup_out), pool, (6, 10), in_sem.at[1, c], backward_view(c))
        return (
            Sum(0, c, out_product, heads),
            Sum(1, c, down_product, hid),
            Sum(2, c, in_product, both),
        )


    def after_attention(c, total):
        def body(r, g):
            a = total.rows(r)
            attn[g, :] = a.astype(BF16)
            v = xs[g, :].astype(F32) + a * inverse_rms(a) * scale_two
            y[g, :] = v
            held[c, i, r, :] = (v * inverse_rms(v) * scale_three).astype(BF16)

        chunks(c, body)

    def after_down(c, total):
        def body(r, g):
            f = total.rows(r)
            d = dout[g, :].astype(F32)
            inv = inverse_rms(f)
            xs[g, :] = (y[g, :] + f * inv * scale_four).astype(BF16)
            held[c, i, r, :] = norm_back(d * scale_four, f, inv).astype(BF16)
            fold[2] += fold_rows(d * (f * inv))

        chunks(c, body)

    def after_in(c, total):
        def body(r, g):
            dh3 = total.rows(r)
            v = y[g, :]
            inv = inverse_rms(v)
            dy = dout[g, :].astype(F32) + norm_back(dh3 * scale_three, v, inv)
            y[g, :] = dy
            fold[1] += fold_rows(dh3 * (v * inv))
            a = attn[g, :].astype(F32)
            inv = inverse_rms(a)
            held[c, i, r, :] = norm_back(dy * scale_two, a, inv).astype(BF16)
            fold[0] += fold_rows(dy * (a * inv))

        chunks(c, body)


    def gathers(c):
        ahead = Slots((hid_out, up_out, ge_out), pool, (0, 2, 4), out_sem.at[0, c], forward_view(c))
        sides = Slots((up_out, ge_out), pool, (0, 2), in_sem.at[2, c], forward_view(c))
        back = Slots((dgate_out, dup_out), pool, (4, 8), out_sem.at[1, c], forward_view(c))

        def into(s, block):
            if s == 0 and c == 0:
                up_spread.end()
                loads[2].wait()
            ahead.free(s)
            k = s % 2

            def tile(at):
                u = dot_nn(held[c, block], wg[:, at])
                up = dot_nn(held[c, block], wu[:, at])
                b = 0.7978845608028654
                th = jnp.tanh(b * (u + 0.044715 * (u * u * u)))
                half = 0.5 * (1.0 + th)
                gelu = u * half
                slope = half + 0.5 * u * (1.0 - th * th) * (b * (1.0 + 0.134145 * (u * u)))
                pool[0 + k, :, at] = (gelu * up).astype(BF16)
                pool[2 + k, :, at] = (up * slope).astype(BF16)
                pool[4 + k, :, at] = gelu.astype(BF16)

            tiles(wide, across, tile)
            ahead.leave(s)

        def turned(s, block):
            if s == 0:
                sides.fetch(0)
            sides.advance(s, n)
            back.free(s)
            k = s % 2

            def tile(at):
                dhid = dot_nn(held[c, block], wd[:, at])
                pool[4 + k, :, at] = (dhid * pool[0 + k, :, at].astype(F32)).astype(BF16)
                pool[8 + k, :, at] = (dhid * pool[2 + k, :, at].astype(F32)).astype(BF16)

            tiles(wide, across, tile)
            back.leave(s)

        heads = Slots((do_out,), pool, (0,), out_sem.at[2, c], forward_view(c), narrow)

        def out(s, block):
            heads.free(s)
            pool[s % 2, :, pl.ds(0, narrow)] = dot_nn(held[c, block], wo[...]).astype(BF16)
            heads.leave(s)

        return (
            Gather(0, c, h3_t, into, ahead.finish),
            Gather(1, c, df_t, turned, back.finish),
            Gather(2, c, dattn_t, out, heads.finish),
        )

    sum_of = (sums(0), sums(1))
    gather_of = (gathers(0), gathers(1))
    own_rows = (after_attention, after_down, after_in)

    first_sum = sum_of[0][0]
    first_sum.start()
    for k in range(1, n - 1):
        first_sum.step(k)
    first_sum.own()
    up_spread.middle()
    loads[1].wait()
    loads[3].wait()
    before = None
    for turn in range(6):
        which, c = turn // 2, turn % 2
        total = sum_of[c][which]
        later = (turn + 1) // 2
        following = sum_of[1 - c][later] if later < 3 else None
        gather = gather_of[c][which]
        total.land()
        own_rows[which](c, total)
        gather.pass_on(0)
        total.done()
        if turn == 0:
            up_spread.turn()
            down_spread.begin()
        if before:
            before.finish()
        if turn == 1:
            down_spread.end()
        if turn == 4:
            pltpu.make_async_copy(xs, layer_out, last_sem.at[0]).start()
        if following:
            following.start()
        for k in range(1, n):
            gather.pass_on(k)
            gather.use(k - 1)
            if following and k < n - 1:
                following.step(k)
            elif following:
                following.own()
        if turn == 0:
            down_spread.middle()
            down_spread.turn()
        before = gather
    before.finish()
    pltpu.make_async_copy(y, dy_out, last_sem.at[1]).start()
    for k in range(3):
        gain_out[k : k + 1, :] = jnp.sum(fold[k], axis=0, keepdims=True)
    pltpu.make_async_copy(xs, layer_out, last_sem.at[0]).wait()
    pltpu.make_async_copy(y, dy_out, last_sem.at[1]).wait()


def middle(n, x, dout, gains, o, wo, wg, wu, wd):
    rows, width = x.shape
    wide = wg.shape[1]
    piece = rows // 2
    sem = pltpu.SemaphoreType.DMA
    blocks = lambda w: jax.ShapeDtypeStruct((n, rows, w), BF16)
    turned = jax.ShapeDtypeStruct((width, n * rows), BF16)
    return pl.pallas_call(
        functools.partial(middle_kernel, n),
        out_shape=[
            jax.ShapeDtypeStruct((rows, width), BF16),
            jax.ShapeDtypeStruct((rows, width), F32),
            jax.ShapeDtypeStruct((3, width), F32),
            turned, blocks(wide), blocks(wide), blocks(wide),
            turned, blocks(wide), blocks(wide), turned, blocks(wo.shape[1]),
        ],
        in_specs=[ANY, ANY, VM] + [ANY] * 5,
        out_specs=[ANY, ANY, VM] + [ANY] * 9,
        scratch_shapes=[
            pltpu.VMEM(x.shape, BF16),
            pltpu.VMEM(x.shape, BF16),
            pltpu.VMEM(wo.shape, BF16),
            pltpu.VMEM(wg.shape, BF16),
            pltpu.VMEM(wg.shape, BF16),
            pltpu.VMEM((width, wide), BF16),
            pltpu.VMEM((2, n, piece, width), BF16),
            pltpu.VMEM((2, n + 1, piece, width), BF16),
            pltpu.VMEM((2, n, piece, width), BF16),
            pltpu.VMEM(x.shape, F32),
            pltpu.VMEM(x.shape, BF16),
            pltpu.VMEM((12, piece, wide), BF16),
            pltpu.VMEM((3, 8, width), F32),
            pltpu.VMEM((2, 768, piece), BF16),
            sem((4,)), sem((6, 2, n)), sem((6, n + 1)), sem((6, 2, n)), sem((6, n)),
            sem((2,)), sem((4, 2, 2, 2)), sem((3, 2, 3, 2)), sem((2,)),
        ]
        + spread_scratch() * 2,
        compiler_params=pltpu.CompilerParams(
            collective_id=8, has_side_effects=True, vmem_limit_bytes=(127 << 20) // 2
        ),
        cost_estimate=cost(0, 1200 << 20),
        name="middle",
    )(x, dout, gains, o, wo, wg, wu, wd)


def last_kernel(
    n, x, dy, gains, d_hbm, w_hbm, in_grad, gain_out,
    d, w, part, landed, mine, fold, load, rs_send, rs_recv,
):
    i = lax.axis_index("tensor")
    rows, width = x.shape
    loads = [
        pltpu.make_async_copy(src, dst, load.at[k])
        for k, (src, dst) in enumerate(((d_hbm, d), (w_hbm, w)))
    ]
    for c in loads:
        c.start()
    line_barrier(i, n)
    for c in loads:
        c.wait()

    def compute(t, block):
        def tile(k):
            at = pl.ds(pl.multiple_of(k * TILE, TILE), TILE)
            part[block, :, at] = dot_nt(d[block], w[at, :]).astype(BF16)

        loop(width // TILE, tile)

    def own(t):
        def tile(k):
            at = pl.ds(pl.multiple_of(k * TILE, TILE), TILE)
            mine[:, at] = dot_nt(d[i], w[at, :])

        loop(width // TILE, tile)

    done = scatter_line(i, n, part, landed, rs_send, rs_recv, compute, own)
    scale = 1.0 + gains[0:1, :]
    fold[...] = jnp.zeros_like(fold)

    def chunk(c):
        r = pl.ds(c * ROWS, ROWS)
        dh1 = summed_rows(i, n, mine, landed, r)
        v = x[r, :].astype(F32)
        inv = inverse_rms(v)
        in_grad[r, :] = (dy[r, :] + norm_back(dh1 * scale, v, inv)).astype(BF16)
        fold[...] += fold_rows(dh1 * (v * inv))

    loop(rows // ROWS, chunk)
    gain_out[...] = jnp.sum(fold[...], axis=0, keepdims=True)
    done()


def last(n, x, dy, gains, d, w):
    rows, width = x.shape
    return pl.pallas_call(
        functools.partial(last_kernel, n),
        out_shape=[
            jax.ShapeDtypeStruct((rows, width), BF16),
            jax.ShapeDtypeStruct((1, width), F32),
        ],
        in_specs=[VM, VM, VM, ANY, ANY],
        out_specs=[VM, VM],
        scratch_shapes=[
            pltpu.VMEM(d.shape, BF16),
            pltpu.VMEM(w.shape, BF16),
            pltpu.VMEM((n, rows, width), BF16),
            pltpu.VMEM((n + 1, rows, width), BF16),
            pltpu.VMEM((rows, width), F32),
            pltpu.VMEM((8, width), F32),
            pltpu.SemaphoreType.DMA((2,)),
        ]
        + line_scratch(n),
        compiler_params=params(5, 48),
        cost_estimate=cost(0, 300 << 20),
        name="last",
    )(x, dy, gains, d, w)


class Reduce:
    def __init__(self, u, left, right, column, width, bufs, sems):
        me = lax.axis_index("dp")
        c, x, y = me % 2, (me // 2) % 2, me // 4
        self.me, self.set, self.third, self.fifth, self.width = me, u % 2, u % 3, u % 5, width
        self.left, self.right, self.column = left, right, column
        self.dx, self.dy, self.dc = 2 - 4 * x, 4 - 8 * y, 1 - 2 * c
        self.lefts, self.rights, self.pair, self.pair_in, self.sums, self.far_in, self.xy_in, self.own = bufs
        (
            self.left_sem, self.right_sem, self.pair_send, self.pair_recv,
            self.far_send, self.far_recv, self.xy_send, self.xy_recv,
        ) = sems
        self.rows = self.own.shape[1]
        self.cols = pl.ds(0, width)
        self.top = pl.ds(0, self.rows // 2)
        self.low = pl.ds(self.rows // 2, self.rows // 2)

    def owner(self, q):
        k = q % 4
        x = jnp.where(k <= 1, self.dx, 0)
        y = jnp.where(k % 2 == 0, self.dy, 0)
        return self.me + x + jnp.where(k == 3, 0, y) + jnp.where(q < 4, self.dc, 0)

    def left_copy(self, q):
        r = pl.ds(self.owner(q) * self.rows, self.rows)
        return pltpu.make_async_copy(self.left.at[r], self.lefts.at[q % 2], self.left_sem.at[q % 2])

    def right_copy(self):
        return pltpu.make_async_copy(
            self.right.at[:, pl.ds(self.column, self.width)],
            self.rights.at[self.set, :, self.cols],
            self.right_sem.at[self.set],
        )

    def remote(self, src, dst, send, recv, shift):
        return pltpu.make_async_remote_copy(
            src, dst, send, recv, device_id={"dp": self.me + shift}, device_id_type=MESH
        )

    def pair_copy(self, k):
        return self.remote(
            self.pair.at[self.set, k, :, self.cols],
            self.pair_in.at[self.set, k, :, self.cols],
            self.pair_send.at[self.set, k],
            self.pair_recv.at[self.set, k],
            self.dc,
        )

    def far_copy(self, way):
        return self.remote(
            self.sums.at[self.third, 0, (self.top, self.low)[way], self.cols],
            self.far_in.at[self.third, way, :, self.cols],
            self.far_send.at[self.third, way],
            self.far_recv.at[self.third, way],
            (self.dx, self.dy)[way],
        )

    def xy_copy(self, way, half):
        r = (self.top, self.low)[half]
        return self.remote(
            self.sums.at[self.third, 1 + way, r, self.cols],
            self.xy_in.at[self.fifth, way, r, self.cols],
            self.xy_send.at[self.third, way, half],
            self.xy_recv.at[self.fifth, way, half],
            (self.dx, self.dy)[way],
        )

    def product(self, q, put):
        self.left_copy(q).wait()
        if isinstance(q, int):
            if q < 7:
                self.left_copy(q + 1).start()
        else:
            self.left_copy(q + 1).start()
        tile = wide_tile(self.width)

        def one(t):
            at = pl.ds(pl.multiple_of(t * tile, tile), tile)
            put(at, dot_nn(self.lefts[q % 2], self.rights[self.set, :, at]))

        loop(self.width // tile, one)

    def load(self):
        self.right_copy().start()

    def begin(self):
        self.left_copy(0).start()
        self.right_copy().wait()

        def chunk(k):
            def put(at, value):
                self.pair[self.set, k, :, at] = value.astype(BF16)

            self.product(k, put)
            self.pair_copy(k).start()

        loop(4, chunk)

    def middle(self):
        for k in range(4):
            arrived = []

            def put(at, value, k=k):
                total = value + self.pair_in[self.set, k, :, at].astype(F32)
                if k < 3:
                    self.sums[self.third, k, :, at] = total.astype(BF16)
                else:
                    self.own[self.third, :, at] = total

            self.pair_copy(k).wait_recv()
            self.product(4 + k, put)
            if k == 0:
                self.far_copy(0).start()
                self.far_copy(1).start()
            elif k == 1:
                self.xy_copy(0, 0).start()
            elif k == 2:
                self.xy_copy(1, 1).start()
        for k in range(4):
            self.pair_copy(k).wait_send()

    def turn(self):
        self.far_copy(0).wait_recv()
        self.far_copy(1).wait_recv()
        half = self.rows // 2

        strip = strip_of(half)

        def chunk(c):
            for way, first in ((0, 0), (1, half)):
                r = pl.ds(first + c * strip, strip)
                f = pl.ds(c * strip, strip)
                k = 2 - way
                total = self.sums[self.third, k, r, self.cols].astype(F32)
                total += self.far_in[self.third, way, f, self.cols].astype(F32)
                self.sums[self.third, k, r, self.cols] = total.astype(BF16)

        loop(half // strip, chunk)
        self.xy_copy(0, 1).start()
        self.xy_copy(1, 0).start()

    def end(self, put):
        for way in range(2):
            for half in range(2):
                self.xy_copy(way, half).wait_recv()

        strip = strip_of(self.rows)

        def chunk(c):
            r = pl.ds(c * strip, strip)
            total = self.own[self.third, r, self.cols]
            for way in range(2):
                total += self.xy_in[self.fifth, way, r, self.cols].astype(F32)
            put(r, total)

        loop(self.rows // strip, chunk)
        for way in range(2):
            self.far_copy(way).wait_send()
            for half in range(2):
                self.xy_copy(way, half).wait_send()


def reduce_scratch(rows, tokens, widest):
    sem = pltpu.SemaphoreType.DMA
    bufs = [
        pltpu.VMEM((2, rows, tokens), BF16),
        pltpu.VMEM((2, tokens, widest), BF16),
        pltpu.VMEM((2, 4, rows, widest), BF16),
        pltpu.VMEM((2, 4, rows, widest), BF16),
        pltpu.VMEM((3, 3, rows, widest), BF16),
        pltpu.VMEM((3, 2, rows // 2, widest), BF16),
        pltpu.VMEM((5, 2, rows, widest), BF16),
        pltpu.VMEM((3, rows, widest), F32),
    ]
    sems = [
        sem((2,)), sem((2,)), sem((2, 4)), sem((2, 4)),
        sem((3, 2)), sem((3, 2)), sem((3, 2, 2)), sem((5, 2, 2)),
    ]
    return bufs, sems


def halves(width):
    return [(0, width)] if width <= 1280 else [(0, width // 2), (width // 2, width // 2)]


def tail_kernel(n, split, x, dy, gains, d_hbm, w_hbm, *refs):
    lefts, rights, refs = refs[:4], refs[4:9], refs[9:]
    in_grad, gain_out, *outs = refs[:7]
    kv_out, refs = refs[7], refs[8:]
    d, w, part, landed, mine, fold, stage, kv_stage = refs[:8]
    load, rs_send, rs_recv, out_sem, kv_sem, kv_send, kv_recv = refs[8:15]
    bufs, sems = refs[15:23], refs[23:31]
    h1_t, df_t, h3_t, da_t = lefts
    dqkv, hid, dgate, dup, o = rights
    i = lax.axis_index("tensor")
    rows, width = x.shape
    over = min(768, wide_tile(width))
    loads = [
        pltpu.make_async_copy(src, dst, load.at[k])
        for k, (src, dst) in enumerate(((d_hbm, d), (w_hbm, w)))
    ]
    for c in loads:
        c.start()

    pairs = [(h1_t, dqkv), (df_t, hid), (h3_t, dgate), (h3_t, dup), (da_t, o)]
    units, places = [], []
    for k, (left, right) in enumerate(pairs):
        for column, size in halves(right.shape[1]):
            units.append(Reduce(len(units), left, right, column, size, bufs, sems))
            places.append((k, column, size))
    units[0].load()
    me = units[0].me

    barrier = pltpu.get_barrier_semaphore()
    for shift in (units[0].dc, units[0].dx, units[0].dy):
        pl.semaphore_signal(barrier, 1, device_id={"dp": me + shift}, device_id_type=MESH)
    for k in range(1, n):
        peer = lax.rem(i + k, n)
        pl.semaphore_signal(barrier, 1, device_id={"tensor": peer}, device_id_type=MESH)
    pl.semaphore_wait(barrier, n + 2)
    for c in loads:
        c.wait()

    def compute(t, block):
        def tile(k):
            at = pl.ds(pl.multiple_of(k * over, over), over)
            part[block, :, at] = dot_nt(d[block], w[at, :]).astype(BF16)

        loop(width // over, tile)

    step, land, done = scatter_steps(i, n, part, landed, rs_send, rs_recv, compute)

    def input_rows():
        def tile(k):
            at = pl.ds(pl.multiple_of(k * over, over), over)
            mine[:, at] = dot_nt(d[i], w[at, :])

        loop(width // over, tile)

    def input_grad():
        land()
        scale = 1.0 + gains[0:1, :]
        fold[...] = jnp.zeros_like(fold)

        strip = strip_of(rows)

        def chunk(c):
            r = pl.ds(c * strip, strip)
            dh1 = summed_rows(i, n, mine, landed, r)
            v = x[r, :].astype(F32)
            inv = inverse_rms(v)
            in_grad[r, :] = (dy[r, :] + norm_back(dh1 * scale, v, inv)).astype(BF16)
            fold[...] += fold_rows(dh1 * (v * inv))

        loop(rows // strip, chunk)
        gain_out[...] = jnp.sum(fold[...], axis=0, keepdims=True)
        done()

    def out_copy(u):
        k, column, size = places[u]
        return pltpu.make_async_copy(
            stage.at[u % 2, :, pl.ds(0, size)],
            outs[k].at[:, pl.ds(column, size)],
            out_sem.at[u % 2],
        )

    def kv_copy(k):
        return pltpu.make_async_remote_copy(
            kv_stage,
            kv_out.at[i],
            kv_send.at[k],
            kv_recv.at[k],
            device_id={"tensor": lax.rem(i + k, n)},
            device_id_type=MESH,
        )

    def kv_arrival(k):
        from_peer = lax.rem(i + n - k, n)
        return pltpu.make_async_remote_copy(
            kv_stage,
            kv_out.at[from_peer],
            kv_send.at[k],
            kv_recv.at[k],
            device_id={"tensor": from_peer},
            device_id_type=MESH,
        )

    kv_own = pltpu.make_async_copy(kv_stage, kv_out.at[i], kv_sem.at[0])

    def finish(u):
        if u >= 2:
            out_copy(u - 2).wait()
        size = places[u][2]

        def put(r, total):
            stage[u % 2, r, pl.ds(0, size)] = total
            if u == 0:
                kv_stage[r, :] = total[:, split:].astype(BF16)

        units[u].end(put)
        out_copy(u).start()
        if u == 0:
            for k in range(1, n):
                kv_copy(k).start()
            kv_own.start()

    count = len(units)
    line = [functools.partial(step, jnp.int32(k)) for k in range(n - 1)] + [input_rows, input_grad]
    for u in range(count + 2):
        if u < count:
            units[u].begin()
            if u + 1 < count:
                units[u + 1].load()
            units[u].middle()
        if 1 <= u <= count:
            units[u - 1].turn()
        if u >= 2:
            finish(u - 2)
        if u < len(line):
            line[u]()
    for u in range(count + 2, len(line)):
        line[u]()
    for u in range(max(0, count - 2), count):
        out_copy(u).wait()
    kv_own.wait()
    for k in range(1, n):
        kv_copy(k).wait_send()
        kv_arrival(k).wait_recv()


def tail(n, m, split, x, dy, gains, d, w, lefts, rights):
    rows, width = x.shape
    tokens = n * rows
    own_rows = width // m
    widest = max(size for right in rights for _, size in halves(right.shape[1]))
    bufs, sems = reduce_scratch(own_rows, tokens, widest)
    sem = pltpu.SemaphoreType.DMA
    kv_width = rights[0].shape[1] - split
    return pl.pallas_call(
        functools.partial(tail_kernel, n, split),
        out_shape=[
            jax.ShapeDtypeStruct((rows, width), BF16),
            jax.ShapeDtypeStruct((1, width), F32),
        ]
        + [jax.ShapeDtypeStruct((own_rows, right.shape[1]), F32) for right in rights]
        + [jax.ShapeDtypeStruct((n, own_rows, kv_width), BF16)],
        in_specs=[VM, VM, VM] + [ANY] * 11,
        out_specs=[VM, VM] + [ANY] * 6,
        scratch_shapes=[
            pltpu.VMEM(d.shape, BF16),
            pltpu.VMEM(w.shape, BF16),
            pltpu.VMEM((n, rows, width), BF16),
            pltpu.VMEM((n + 1, rows, width), BF16),
            pltpu.VMEM((rows, width), F32),
            pltpu.VMEM((8, width), F32),
            pltpu.VMEM((2, own_rows, widest), F32),
            pltpu.VMEM((own_rows, kv_width), BF16),
            sem((2,)),
        ]
        + line_scratch(n)
        + [sem((2,)), sem((1,)), sem((n,)), sem((n,))]
        + bufs
        + sems,
        compiler_params=params(7, 62),
        cost_estimate=cost(0, 600 << 20),
        name="tail",
    )(x, dy, gains, d, w, *lefts, *rights)


def rope_tables():
    positions = jnp.arange(L, dtype=jnp.int32).astype(F32)
    exponent = jnp.arange(HD // 2, dtype=jnp.int32).astype(F32) * (-2.0 / HD)
    angles = positions[:, None] * jnp.exp(exponent * jnp.log(F32(10000.0)))[None, :]
    return jnp.cos(angles), jnp.sin(angles)


def weight_grad(left, right):
    return dot_tn(left, right).astype(BF16)


def scatter_rows(grad):
    return lax.psum_scatter(grad, "dp", scatter_dimension=0, tiled=True)


def body(
    n,
    m,
    layer_in,
    out_grad,
    piece_starts,
    attn_gain,
    attn_out_gain,
    feed_gain,
    feed_out_gain,
    query_weight,
    key_weight,
    value_weight,
    out_weight,
    gate_weight,
    up_weight,
    down_weight,
):
    heads = query_weight.shape[1] // HD
    fan = H // KV
    kvs = max(1, heads // fan)
    rank = lax.axis_index("tensor")
    kv_at = (rank * heads // fan) * HD
    rows, width = layer_in.shape
    tokens = n * rows

    gathered = gather_gains(m, jnp.stack([attn_gain, attn_out_gain, feed_gain, feed_out_gain]))
    gains = gathered.transpose(1, 0, 2).reshape(4, width).astype(F32)

    def collect(shard):
        return lax.all_gather(shard, "dp", axis=0, tiled=True)

    wqkv = collect(
        jnp.concatenate(
            [
                query_weight,
                lax.dynamic_slice_in_dim(key_weight, kv_at, kvs * HD, 1),
                lax.dynamic_slice_in_dim(value_weight, kv_at, kvs * HD, 1),
            ],
            axis=1,
        )
    )
    wo = collect(out_weight.T)
    cos, sin = rope_tables()

    spread = m == 8 and n * kvs == KV
    h1, wg, h1_t = first(n, m, layer_in, gains, gate_weight if spread else None)
    if not spread:
        wg = collect(gate_weight)
    h1_flat = h1.reshape(tokens, width)
    q, k, v, o = attend(heads, kvs, piece_starts, h1_flat, wqkv, cos, sin)
    o_blocks = o.reshape(n, rows, heads * HD)
    if spread:
        layer_out, dy, gain_later, h3_t, hid, _, _, df_t, dgate, dup, dattn_t, do = middle(
            n, layer_in, out_grad, gains, o_blocks, wo, wg, up_weight, down_weight.T
        )
    else:
        wu, wd = collect(up_weight), collect(down_weight.T)
        attn, y, h3, hid, up, ge = into_feed(n, layer_in, gains, o_blocks, wo, wg, wu)
        layer_out, gain_four, df, dgate, dup = turn_feed(n, y, out_grad, gains, hid, wd, up, ge)
    flat = lambda a: a.reshape(tokens, a.shape[-1])
    split = heads * HD
    if spread:
        d = attend_back(heads, kvs, piece_starts, q, k, v, flat(do), cos, sin)
        lefts = [h1_t, df_t, h3_t, dattn_t]
        rights = [d, flat(hid), flat(dgate), flat(dup), o]
        in_grad, gain_one, qkv_sum, down_sum, gate_sum, up_sum, out_sum, kv = tail(
            n, m, split, layer_in, dy, gains, d.reshape(n, rows, -1), wqkv, lefts, rights
        )
        own_rows = qkv_sum.shape[0]
        kv = kv.reshape(n, own_rows, 2, kvs * HD).transpose(2, 1, 0, 3).reshape(2, own_rows, KV * HD)
    else:
        tie = lax.optimization_barrier
        down_part = weight_grad(flat(df), flat(hid))
        gate_part = weight_grad(flat(h3), flat(dgate))
        up_part = weight_grad(flat(h3), flat(dup))
        dgate, dup, down_part, gate_part, up_part = tie((dgate, dup, down_part, gate_part, up_part))
        down_sum, gate_sum, up_sum = map(scatter_rows, (down_part, gate_part, up_part))
        dy, gain_mid, dattn, do = out_of_feed(n, y, attn, out_grad, gains, dgate, dup, wg, wu, wo)
        do, dattn, down_sum, gate_sum = tie((do, dattn, down_sum, gate_sum))
        out_part = weight_grad(flat(dattn), o)
        do, out_part = tie((do, out_part))
        d = attend_back(heads, kvs, piece_starts, q, k, v, flat(do), cos, sin)
        qkv_part = weight_grad(h1_flat, d)
        d, qkv_part, up_sum = tie((d, qkv_part, up_sum))
        out_sum, qkv_sum = scatter_rows(out_part), scatter_rows(qkv_part)
        in_grad, gain_one = last(n, layer_in, dy, gains, d.reshape(n, rows, -1), wqkv)
        gain_later = jnp.concatenate([gain_mid, gain_four], axis=0)

        own_rows = qkv_sum.shape[0]
        kv = qkv_sum[:, split:].reshape(own_rows, 2, kvs * HD).transpose(1, 0, 2)
        if n * kvs == KV:
            kv = lax.all_gather(kv, "tensor", axis=2, tiled=True)
        else:
            kv = lax.dynamic_update_slice_in_dim(jnp.zeros((2, own_rows, KV * HD), BF16), kv, kv_at, 2)
            kv = lax.psum(kv, "tensor")
    kv = kv.astype(F32)

    gain_grads = jnp.concatenate([gain_one, gain_later], axis=0)
    gain_grads = sum_gains(n, m, gain_grads.reshape(4, m, width // m).transpose(1, 0, 2))
    return (
        layer_out,
        in_grad,
        qkv_sum[:, :split].astype(F32),
        kv[0],
        kv[1],
        out_sum.astype(F32).T,
        gate_sum.astype(F32),
        up_sum.astype(F32),
        down_sum.astype(F32).T,
        gain_grads[0],
        gain_grads[1],
        gain_grads[2],
        gain_grads[3],
    )


def solution(mesh):
    in_specs = (
        P(("dp", "tensor"), None),
        P(("dp", "tensor"), None),
        P("dp", None),
        P("dp"),
        P("dp"),
        P("dp"),
        P("dp"),
        P("dp", "tensor"),
        P("dp", None),
        P("dp", None),
        P("tensor", "dp"),
        P("dp", "tensor"),
        P("dp", "tensor"),
        P("tensor", "dp"),
    )
    out_specs = (
        P(("dp", "tensor"), None),
        P(("dp", "tensor"), None),
        P("dp", "tensor"),
        P("dp", None),
        P("dp", None),
        P("tensor", "dp"),
        P("dp", "tensor"),
        P("dp", "tensor"),
        P("tensor", "dp"),
        P("dp"),
        P("dp"),
        P("dp"),
        P("dp"),
    )
    program = functools.partial(body, mesh.shape["tensor"], mesh.shape["dp"])
    return jax.shard_map(program, mesh=mesh, in_specs=in_specs, out_specs=out_specs, check_vma=False)
```

```python
import functools

import jax
import jax.numpy as jnp
from jax import lax
from jax.experimental import pallas as pl
from jax.experimental.pallas import tpu as pltpu
from jax.sharding import PartitionSpec as P

H = 8
KV = 4
HD = 256
L = 1024
PIECE = 256

EPS = 1e-06
CAP = 50.0
F32 = jnp.float32
BF16 = jnp.bfloat16
MESH = pl.DeviceIdType.MESH
ANY = pl.BlockSpec(memory_space=pl.ANY)
VM = pl.BlockSpec(memory_space=pltpu.VMEM)
SM = pl.BlockSpec(memory_space=pltpu.SMEM)
ROWS = 16
TILE = 256


def dot_nn(a, b):
    return lax.dot_general(a, b, (((1,), (0,)), ((), ())), preferred_element_type=F32)


def dot_nt(a, b):
    return lax.dot_general(a, b, (((1,), (1,)), ((), ())), preferred_element_type=F32)


def dot_tn(a, b):
    return lax.dot_general(a, b, (((0,), (0,)), ((), ())), preferred_element_type=F32)


def tile_of(width):
    return next(t for t in (256, 384, 128) if width % t == 0)


def strip_of(count):
    return next(t for t in (64, 48, 32, 16) if count % t == 0)


def wide_tile(width):
    return next(t for t in (1152, 1024, 768, 512, 384, 256, 128) if width % t == 0)


def loop(count, body):
    lax.fori_loop(0, count, lambda t, c: (body(t), c)[1], 0)


def block_at(i, n, s):
    m = jnp.minimum(i, n - 1 - i)
    near = i + jnp.where(s % 2 == 1, -((s + 1) // 2), s // 2)
    far = jnp.where(i * 2 < n, i + (s - m), i - (s - m))
    return jnp.where(s <= 2 * m, near, far)


def line_barrier(i, n, peers=()):
    barrier = pltpu.get_barrier_semaphore()

    @pl.when(i > 0)
    def _():
        pl.semaphore_signal(barrier, 1, device_id={"tensor": i - 1}, device_id_type=MESH)

    @pl.when(i < n - 1)
    def _():
        pl.semaphore_signal(barrier, 1, device_id={"tensor": i + 1}, device_id_type=MESH)

    for peer in peers:
        pl.semaphore_signal(barrier, 1, device_id={"dp": peer}, device_id_type=MESH)
    pl.semaphore_wait(barrier, len(peers) + jnp.minimum(i, 1) + jnp.minimum(n - 1 - i, 1))


def gather_steps(i, n, held, send, recv):
    def copy(block, way, s, to):
        return pltpu.make_async_remote_copy(
            held.at[block],
            held.at[block],
            send.at[way, s],
            recv.at[block],
            device_id={"tensor": to},
            device_id_type=MESH,
        )

    up, down = jnp.minimum(i + 1, n - 1), jnp.maximum(i - 1, 0)

    def pass_on(s):
        low, high = i - s, i + s

        @pl.when((s > 0) & (low >= 0))
        def _():
            copy(low, 0, s, up).wait_recv()

        @pl.when((low >= 0) & (i < n - 1))
        def _():
            copy(low, 0, s, up).start()

        @pl.when((s > 0) & (high < n))
        def _():
            copy(high, 1, s, down).wait_recv()

        @pl.when((high < n) & (i > 0))
        def _():
            copy(high, 1, s, down).start()

    def finish(s):
        low, high = i - s, i + s

        @pl.when((low >= 0) & (i < n - 1))
        def _():
            copy(low, 0, s, up).wait_send()

        @pl.when((high < n) & (i > 0))
        def _():
            copy(high, 1, s, down).wait_send()

    return pass_on, functools.partial(loop, n, finish)


def gather_line(i, n, held, send, recv, compute):
    pass_on, finish = gather_steps(i, n, held, send, recv)

    def step(s):
        pass_on(s)
        compute(s, block_at(i, n, s))

    loop(n, step)
    finish()


def scatter_steps(i, n, part, landed, send, recv, compute):
    rows = part.shape[1]

    def copy(block, way, t, to):
        slot = jnp.where(block == to, n, block) if way else block
        return pltpu.make_async_remote_copy(
            part.at[block],
            landed.at[slot],
            send.at[way, t],
            recv.at[slot],
            device_id={"tensor": to},
            device_id_type=MESH,
        )

    def arrived(slot):
        pltpu.make_async_remote_copy(
            landed.at[slot],
            landed.at[slot],
            send.at[0, 0],
            recv.at[slot],
            device_id={"tensor": i},
            device_id_type=MESH,
        ).wait_recv()

    def add(block):
        strip = strip_of(rows)

        def chunk(c):
            r = pl.ds(c * strip, strip)
            total = part[block, r, :].astype(F32) + landed[block, r, :].astype(F32)
            part[block, r, :] = total.astype(BF16)

        loop(rows // strip, chunk)

    up, down = jnp.minimum(i + 1, n - 1), jnp.maximum(i - 1, 0)

    def step(k):
        t = k + 1
        compute(k, block_at(i, n, n - t))
        above, below = i + n - t, i - n + t

        @pl.when((above < n) & (i > 0))
        def _():
            arrived(above)
            add(above)

        @pl.when(above < n)
        def _():
            copy(above, 0, t, up).start()

        @pl.when((below >= 0) & (i < n - 1))
        def _():
            arrived(below)
            add(below)

        @pl.when(below >= 0)
        def _():
            copy(below, 1, t, down).start()

    def land():
        @pl.when(i > 0)
        def _():
            arrived(i)

        @pl.when(i < n - 1)
        def _():
            arrived(jnp.int32(n))

    def finish(k):
        t = k + 1

        @pl.when(i + n - t < n)
        def _():
            copy(i + n - t, 0, t, up).wait_send()

        @pl.when(i - n + t >= 0)
        def _():
            copy(i - n + t, 1, t, down).wait_send()

    return step, land, functools.partial(loop, n - 1, finish)


def scatter_line(i, n, part, landed, send, recv, compute, own):
    step, land, finish = scatter_steps(i, n, part, landed, send, recv, compute)
    loop(n - 1, step)
    own(n - 1)
    land()
    return finish


def summed_rows(i, n, mine, landed, r):
    zero = jnp.zeros((), F32)
    low = jnp.where(i > 0, landed[i, r, :].astype(F32), zero)
    high = jnp.where(i < n - 1, landed[n, r, :].astype(F32), zero)
    return mine[r, :] + low + high


def inverse_rms(v):
    return lax.rsqrt(jnp.mean(v * v, axis=-1, keepdims=True) + EPS)


def norm_back(e, v, r):
    unit = v * r
    return r * (e - unit * jnp.mean(e * unit, axis=-1, keepdims=True))


def fold_rows(v):
    return v.reshape(-1, 8, v.shape[-1]).sum(axis=0)


class Feed:
    def __init__(self, sources, slots, sems, which):
        self.sources, self.slots, self.sems, self.which = sources, slots, sems, which

    def copies(self, s):
        return [
            pltpu.make_async_copy(src.at[self.which(s)], slot.at[s % 2], self.sems.at[k, s % 2])
            for k, (src, slot) in enumerate(zip(self.sources, self.slots))
        ]

    def start(self, s):
        for c in self.copies(s):
            c.start()

    def wait(self, s):
        for c in self.copies(s):
            c.wait()

    def advance(self, s, count):
        self.wait(s)

        @pl.when(s + 1 < count)
        def _():
            self.start(s + 1)


class Drain:
    def __init__(self, targets, slots, sems, which):
        self.targets, self.slots, self.sems, self.which = targets, slots, sems, which

    def copies(self, s):
        return [
            pltpu.make_async_copy(slot.at[s % 2], dst.at[self.which(s)], self.sems.at[k, s % 2])
            for k, (dst, slot) in enumerate(zip(self.targets, self.slots))
        ]

    def free(self, s):
        @pl.when(s >= 2)
        def _():
            for c in self.copies(s - 2):
                c.wait()

    def start(self, s):
        for c in self.copies(s):
            c.start()

    def finish(self, count):
        for s in range(max(0, count - 2), count):
            for c in self.copies(jnp.int32(s)):
                c.wait()


class Spread:
    def __init__(self, own, full, send, recv, local):
        me = lax.axis_index("dp")
        c, x, y = me % 2, (me // 2) % 2, me // 4
        self.own, self.full, self.send, self.recv, self.local = own, full, send, recv, local
        self.me = me
        self.core = me + 1 - 2 * c
        self.x = me + 2 - 4 * x
        self.y = me + 4 - 8 * y
        self.far = self.x + 4 - 8 * y
        self.flip = 1 - 2 * c

    def peers(self):
        return (self.core, self.x, self.y)

    def view(self, owner, part):
        count = self.own.shape[0]
        first, size = ((0, count), (0, count // 2), (count // 2, count // 2))[part]
        return self.full.at[pl.ds(pl.multiple_of(owner * count + first, ROWS), size)]

    def copy(self, k, source, owner, part, to):
        return pltpu.make_async_remote_copy(
            self.own if source is None else self.view(source, part),
            self.view(owner, part),
            self.send.at[k],
            self.recv.at[k],
            device_id={"dp": to},
            device_id_type=MESH,
        )

    def sends(self):
        return (
            (0, None, self.me, 0, self.core),
            (1, None, self.me, 0, self.x),
            (2, None, self.me, 0, self.y),
            (3, self.x, self.x, 1, self.y),
            (4, self.y, self.y, 2, self.x),
            (5, self.x, self.x, 0, self.core),
            (6, self.y, self.y, 0, self.core),
            (7, self.far, self.far, 0, self.core),
        )

    def start(self, *which):
        for k in which:
            self.copy(*self.sends()[k]).start()

    def arrive(self, k):
        owner, part = {
            0: (self.core, 0),
            1: (self.x, 0),
            2: (self.y, 0),
            3: (self.far, 1),
            4: (self.far, 2),
            5: (self.x + self.flip, 0),
            6: (self.y + self.flip, 0),
            7: (self.far + self.flip, 0),
        }[k]
        self.copy(k, owner, owner, part, self.core).wait_recv()

    def keep(self):
        return pltpu.make_async_copy(self.own, self.view(self.me, 0), self.local.at[0])

    def begin(self):
        self.keep().start()
        self.start(1, 2, 0)

    def middle(self):
        self.arrive(1)
        self.arrive(2)
        self.start(3, 4, 5, 6)

    def turn(self):
        self.arrive(3)
        self.arrive(4)
        self.start(7)

    def end(self):
        for k in (0, 5, 6, 7):
            self.arrive(k)
        self.keep().wait()
        for k in range(8):
            self.copy(*self.sends()[k]).wait_send()


def spread_scratch():
    return [pltpu.SemaphoreType.DMA((8,)), pltpu.SemaphoreType.DMA((8,)), pltpu.SemaphoreType.DMA((1,))]


def line_scratch(n):
    return [pltpu.SemaphoreType.DMA((2, n)), pltpu.SemaphoreType.DMA((n + 1,))]


def params(cid, mib):
    return pltpu.CompilerParams(
        collective_id=cid, has_side_effects=True, vmem_limit_bytes=mib << 20
    )


def cost(flops, moved):
    return pl.CostEstimate(flops=flops, bytes_accessed=moved, transcendentals=0)


def gains_kernel(m, mine, out, send, recv):
    me = lax.axis_index("dp")
    barrier = pltpu.get_barrier_semaphore()
    for k in range(1, m):
        pl.semaphore_signal(
            barrier, 1, device_id={"dp": lax.rem(me + k, m)}, device_id_type=MESH
        )
    pl.semaphore_wait(barrier, m - 1)

    def copy(owner, k):
        return pltpu.make_async_remote_copy(
            mine,
            out.at[owner],
            send.at[k],
            recv.at[k],
            device_id={"dp": lax.rem(me + k, m)},
            device_id_type=MESH,
        )

    for k in range(1, m):
        copy(me, k).start()
    out[me] = mine[...]
    for k in range(1, m):
        copy(lax.rem(me + m - k, m), k).wait_recv()
    for k in range(1, m):
        copy(me, k).wait_send()


def gather_gains(m, mine):
    return pl.pallas_call(
        functools.partial(gains_kernel, m),
        out_shape=jax.ShapeDtypeStruct((m,) + mine.shape, mine.dtype),
        in_specs=[VM],
        out_specs=VM,
        scratch_shapes=[pltpu.SemaphoreType.DMA((m,)), pltpu.SemaphoreType.DMA((m,))],
        compiler_params=params(0, 16),
        name="gains",
    )(mine)


def sum_gains_kernel(n, m, mine, out, landed, total, across, send, recv, send_two, recv_two):
    me, i = lax.axis_index("dp"), lax.axis_index("tensor")
    barrier = pltpu.get_barrier_semaphore()
    dp_peer = lambda k: {"dp": lax.rem(me + k, m)}
    line_peer = lambda k: {"tensor": lax.rem(i + k, n)}
    for k in range(1, m):
        pl.semaphore_signal(barrier, 1, device_id=dp_peer(k), device_id_type=MESH)
    for k in range(1, n):
        pl.semaphore_signal(barrier, 1, device_id=line_peer(k), device_id_type=MESH)
    pl.semaphore_wait(barrier, m + n - 2)

    def to_owner(k):
        return pltpu.make_async_remote_copy(
            mine.at[lax.rem(me + k, m)], landed.at[k], send.at[k], recv.at[k],
            device_id=dp_peer(k), device_id_type=MESH,
        )

    def along(k):
        return pltpu.make_async_remote_copy(
            total, across.at[k], send_two.at[k], recv_two.at[k],
            device_id=line_peer(k), device_id_type=MESH,
        )

    for k in range(1, m):
        to_owner(k).start()
    here = mine[me]
    for k in range(1, m):
        to_owner(k).wait_recv()
        here = here + landed[k]
    total[...] = here
    for k in range(1, n):
        along(k).start()
    for k in range(1, n):
        along(k).wait_recv()
        here = here + across[k]
    out[...] = here
    for k in range(1, m):
        to_owner(k).wait_send()
    for k in range(1, n):
        along(k).wait_send()


def sum_gains(n, m, mine):
    shape = mine.shape[1:]
    return pl.pallas_call(
        functools.partial(sum_gains_kernel, n, m),
        out_shape=jax.ShapeDtypeStruct(shape, F32),
        in_specs=[VM],
        out_specs=VM,
        scratch_shapes=[
            pltpu.VMEM((m,) + shape, F32),
            pltpu.VMEM(shape, F32),
            pltpu.VMEM((n,) + shape, F32),
        ]
        + [pltpu.SemaphoreType.DMA((m,))] * 2
        + [pltpu.SemaphoreType.DMA((n,))] * 2,
        compiler_params=params(6, 16),
        name="sum_gains",
    )(mine)


def first_kernel(n, spread, x, gains, *refs):
    i = lax.axis_index("tensor")
    rows = x.shape[0]
    if spread:
        shard, full, gathered, turned, held, send, recv, out_sem, turn, turn_sem, *sems = refs
        gather = Spread(shard, gathered, *sems)
        line_barrier(i, n, gather.peers())
        gather.begin()
    else:
        full, held, send, recv, out_sem = refs
        line_barrier(i, n)
    scale = 1.0 + gains[0:1, :]

    strip = strip_of(rows)

    def chunk(c):
        r = pl.ds(c * strip, strip)
        v = x[r, :].astype(F32)
        held[i, r, :] = (v * inverse_rms(v) * scale).astype(BF16)

    loop(rows // strip, chunk)

    def keep(s, block):
        pltpu.make_async_copy(held.at[block], full.at[block], out_sem.at[s]).start()
        if spread:
            flip_rows(held.at[block], turned, block * rows, turn, turn_sem)
            pl.when(s == min(1, n - 1))(gather.middle)
            pl.when(s == min(2, n - 1))(gather.turn)

    gather_line(i, n, held, send, recv, keep)

    def finish(s):
        block = block_at(i, n, s)
        pltpu.make_async_copy(held.at[block], full.at[block], out_sem.at[s]).wait()

    loop(n, finish)
    if spread:
        gather.end()


def flip_rows(block, target, column, stage, sem):
    rows, width = block.shape
    size = stage.shape[1]
    pieces = width // size

    def copy(k):
        return pltpu.make_async_copy(
            stage.at[k % 2],
            target.at[pl.ds(k * size, size), pl.ds(pl.multiple_of(column, 128), rows)],
            sem.at[k % 2],
        )

    for k in range(pieces):
        if k >= 2:
            copy(k - 2).wait()
        for j in range(size // 256):
            at = pl.ds(k * size + j * 256, 256)
            stage[k % 2, pl.ds(j * 256, 256), :] = block[:, at].T
        copy(k).start()
    for k in range(max(0, pieces - 2), pieces):
        copy(k).wait()


def first(n, m, x, gains, shard):
    rows, width = x.shape
    spread = shard is not None
    outs = [jax.ShapeDtypeStruct((n, rows, width), BF16)]
    if spread:
        outs += [jax.ShapeDtypeStruct((m * shard.shape[0], shard.shape[1]), BF16)]
        outs += [jax.ShapeDtypeStruct((width, n * rows), BF16)]
        turn = [pltpu.VMEM((2, 768, rows), BF16), pltpu.SemaphoreType.DMA((2,))]
    out = pl.pallas_call(
        functools.partial(first_kernel, n, spread),
        out_shape=outs,
        in_specs=[VM, VM] + [ANY] * spread,
        out_specs=[ANY] * len(outs),
        scratch_shapes=[pltpu.VMEM((n, rows, width), BF16)]
        + line_scratch(n)
        + [pltpu.SemaphoreType.DMA((n,))]
        + (turn + spread_scratch() if spread else []),
        compiler_params=params(1, 62),
        cost_estimate=cost(0, 300 << 20),
        name="first",
    )(x, gains, *([shard] if spread else []))
    return out if spread else (out[0], None, None)


def turn(u, cos, sin):
    half = HD // 2
    a, b = u[:, :half], u[:, half:]
    return jnp.concatenate([a * cos - b * sin, b * cos + a * sin], axis=-1)


def row_limit(starts, seq, first_row, rows):
    pos = first_row + lax.broadcasted_iota(jnp.int32, (rows, 1), 0)
    limit = pos + 1
    for piece in range(2):
        begin = starts[seq, piece]
        inside = (pos >= begin) & (pos < begin + PIECE)
        limit = jnp.maximum(limit, jnp.where(inside, begin + PIECE, 0))
    return limit


def key_span(first_row, rows):
    return min(L, first_row + rows + PIECE)


def weights_of(q, k, limit):
    bent = jnp.tanh(dot_nt(q, k) * (1.0 / CAP))
    seen = lax.broadcasted_iota(jnp.int32, (1, k.shape[0]), 1) < limit
    w = jnp.where(seen, jnp.exp(CAP * bent), 0.0)
    return w * pl.reciprocal(jnp.sum(w, axis=-1, keepdims=True)), bent


def attend_kernel(heads, kvs, starts, h1, w, cos, sin, q_out, k_out, v_out, o_out):
    tokens = h1.shape[0]
    fan = heads // kvs
    block = 256

    def project(b):
        r = pl.ds(pl.multiple_of(b * block, block), block)
        at = pl.ds(pl.multiple_of(lax.rem(b * block, L), block), block)
        c, s = cos[at, :], sin[at, :]
        x = h1[r, :]
        for h in range(heads):
            u = dot_nn(x, w[:, h * HD : (h + 1) * HD])
            q_out[h, r, :] = (turn(u, c, s) * (HD**-0.5)).astype(BF16)
        for g in range(kvs):
            u = dot_nn(x, w[:, (heads + g) * HD : (heads + g + 1) * HD])
            k_out[g, r, :] = turn(u, c, s).astype(BF16)
            u = dot_nn(x, w[:, (heads + kvs + g) * HD : (heads + kvs + g + 1) * HD])
            v_out[g, r, :] = u.astype(BF16)

    loop(tokens // block, project)
    for seq in range(tokens // L):
        base = seq * L
        for row in range(0, L, block):
            span = key_span(row, block)
            limit = row_limit(starts, seq, row, block)
            for h in range(heads):
                q = q_out[h, base + row : base + row + block, :]
                p, _ = weights_of(q, k_out[h // fan, base : base + span, :], limit)
                o = dot_nn(p.astype(BF16), v_out[h // fan, base : base + span, :])
                o_out[base + row : base + row + block, h * HD : (h + 1) * HD] = o.astype(BF16)


def attend(heads, kvs, starts, h1, w, cos, sin):
    tokens = h1.shape[0]
    return pl.pallas_call(
        functools.partial(attend_kernel, heads, kvs),
        out_shape=[
            jax.ShapeDtypeStruct((heads, tokens, HD), BF16),
            jax.ShapeDtypeStruct((kvs, tokens, HD), BF16),
            jax.ShapeDtypeStruct((kvs, tokens, HD), BF16),
            jax.ShapeDtypeStruct((tokens, heads * HD), BF16),
        ],
        in_specs=[SM, VM, VM, VM, VM],
        out_specs=[VM, VM, VM, VM],
        compiler_params=pltpu.CompilerParams(vmem_limit_bytes=48 << 20),
        cost_estimate=cost(20 << 30, 20 << 20),
        name="attend",
    )(starts, h1, w, cos, sin)


def attend_back_kernel(heads, kvs, block, starts, q_in, k_in, v_in, do_in, cos, sin, out, dk, dv):
    tokens = q_in.shape[1]
    fan = heads // kvs
    for seq in range(tokens // L):
        base = seq * L
        for g in range(kvs):
            dk[...] = jnp.zeros_like(dk)
            dv[...] = jnp.zeros_like(dv)
            for row in range(0, L, block):
                span = key_span(row, block)
                limit = row_limit(starts, seq, row, block)
                k = k_in[g, base : base + span, :]
                v = v_in[g, base : base + span, :]
                at = slice(base + row, base + row + block)
                for h in range(g * fan, (g + 1) * fan):
                    q = q_in[h, at, :]
                    do = do_in[at, h * HD : (h + 1) * HD]
                    p, bent = weights_of(q, k, limit)
                    dp = dot_nt(do, v)
                    delta = jnp.sum(p * dp, axis=-1, keepdims=True)
                    ds = (p * (dp - delta) * (1.0 - bent * bent)).astype(BF16)
                    dq = dot_nn(ds, k)
                    c, s = cos[row : row + block, :], sin[row : row + block, :]
                    out[at, h * HD : (h + 1) * HD] = (turn(dq, c, -s) * (HD**-0.5)).astype(BF16)
                    dk[:span, :] += dot_tn(ds, q)
                    dv[:span, :] += dot_tn(p.astype(BF16), do)

            def close(b, g=g, base=base):
                r = pl.ds(pl.multiple_of(b * block, block), block)
                to = pl.ds(pl.multiple_of(base + b * block, block), block)
                back = turn(dk[r, :], cos[r, :], -sin[r, :])
                out[to, (heads + g) * HD : (heads + g + 1) * HD] = back.astype(BF16)
                left = (heads + kvs + g) * HD
                out[to, left : left + HD] = dv[r, :].astype(BF16)

            loop(L // block, close)


def attend_back(heads, kvs, starts, q, k, v, do, cos, sin):
    tokens = q.shape[1]
    return pl.pallas_call(
        functools.partial(attend_back_kernel, heads, kvs, 256),
        out_shape=jax.ShapeDtypeStruct((tokens, (heads + 2 * kvs) * HD), BF16),
        in_specs=[SM, VM, VM, VM, VM, VM, VM],
        out_specs=VM,
        scratch_shapes=[pltpu.VMEM((L, HD), F32), pltpu.VMEM((L, HD), F32)],
        compiler_params=pltpu.CompilerParams(vmem_limit_bytes=48 << 20),
        cost_estimate=cost(30 << 30, 20 << 20),
        name="attend_back",
    )(starts, q, k, v, do, cos, sin)


def into_feed_kernel(
    n, x, gains, o_hbm, wo_hbm, wg_hbm, wu_hbm,
    attn_out, y_out, h3_full, hid_out, up_out, ge_out,
    o, wo, wg, wu, part, landed, mine, held, hid_s, up_s, ge_s,
    load, rs_send, rs_recv, ag_send, ag_recv, keep_sem, out_sem,
):
    i = lax.axis_index("tensor")
    rows, width = x.shape
    loads = [
        pltpu.make_async_copy(src, dst, load.at[k])
        for k, (src, dst) in enumerate(((o_hbm, o), (wo_hbm, wo), (wg_hbm, wg), (wu_hbm, wu)))
    ]
    for c in loads:
        c.start()
    line_barrier(i, n)
    loads[0].wait()
    loads[1].wait()

    def compute(t, block):
        def tile(k):
            at = pl.ds(pl.multiple_of(k * TILE, TILE), TILE)
            part[block, :, at] = dot_nt(o[block], wo[at, :]).astype(BF16)

        loop(width // TILE, tile)

    def own(t):
        def tile(k):
            at = pl.ds(pl.multiple_of(k * TILE, TILE), TILE)
            mine[:, at] = dot_nt(o[i], wo[at, :])

        loop(width // TILE, tile)

    done = scatter_line(i, n, part, landed, rs_send, rs_recv, compute, own)
    scale_two, scale_three = 1.0 + gains[1:2, :], 1.0 + gains[2:3, :]

    def chunk(c):
        r = pl.ds(c * ROWS, ROWS)
        attn = summed_rows(i, n, mine, landed, r)
        attn_out[r, :] = attn
        y = x[r, :].astype(F32) + attn * inverse_rms(attn) * scale_two
        y_out[r, :] = y
        held[i, r, :] = (y * inverse_rms(y) * scale_three).astype(BF16)

    loop(rows // ROWS, chunk)
    done()
    loads[2].wait()
    loads[3].wait()
    drain = Drain(
        (hid_out, up_out, ge_out), (hid_s, up_s, ge_s), out_sem, lambda s: block_at(i, n, s)
    )

    def forward(s, block):
        pltpu.make_async_copy(held.at[block], h3_full.at[block], keep_sem.at[s]).start()
        drain.free(s)
        slot = s % 2
        span = tile_of(wg.shape[1])

        def tile(k):
            at = pl.ds(pl.multiple_of(k * span, span), span)
            u = dot_nn(held[block], wg[:, at])
            up = dot_nn(held[block], wu[:, at])
            c = 0.7978845608028654
            th = jnp.tanh(c * (u + 0.044715 * (u * u * u)))
            half = 0.5 * (1.0 + th)
            gelu = u * half
            slope = half + 0.5 * u * (1.0 - th * th) * (c * (1.0 + 0.134145 * (u * u)))
            hid_s[slot, :, at] = (gelu * up).astype(BF16)
            up_s[slot, :, at] = (up * slope).astype(BF16)
            ge_s[slot, :, at] = gelu.astype(BF16)

        loop(wg.shape[1] // span, tile)
        drain.start(s)

    gather_line(i, n, held, ag_send, ag_recv, forward)
    drain.finish(n)

    def finish(s):
        block = block_at(i, n, s)
        pltpu.make_async_copy(held.at[block], h3_full.at[block], keep_sem.at[s]).wait()

    loop(n, finish)


def into_feed(n, x, gains, o, wo, wg, wu):
    rows, width = x.shape
    wide = wg.shape[1]
    blocks = lambda w: jax.ShapeDtypeStruct((n, rows, w), BF16)
    mine = jax.ShapeDtypeStruct((rows, width), F32)
    return pl.pallas_call(
        functools.partial(into_feed_kernel, n),
        out_shape=[mine, mine, blocks(width), blocks(wide), blocks(wide), blocks(wide)],
        in_specs=[VM, VM, ANY, ANY, ANY, ANY],
        out_specs=[VM, VM, ANY, ANY, ANY, ANY],
        scratch_shapes=[
            pltpu.VMEM(o.shape, BF16),
            pltpu.VMEM(wo.shape, BF16),
            pltpu.VMEM(wg.shape, BF16),
            pltpu.VMEM(wu.shape, BF16),
            pltpu.VMEM((n, rows, width), BF16),
            pltpu.VMEM((n + 1, rows, width), BF16),
            pltpu.VMEM((rows, width), F32),
            pltpu.VMEM((n, rows, width), BF16),
        ]
        + [pltpu.VMEM((2, rows, wide), BF16)] * 3
        + [pltpu.SemaphoreType.DMA((4,))]
        + line_scratch(n) * 2
        + [pltpu.SemaphoreType.DMA((n,)), pltpu.SemaphoreType.DMA((3, 2))],
        compiler_params=params(2, 62),
        cost_estimate=cost(0, 600 << 20),
        name="into_feed",
    )(x, gains, o, wo, wg, wu)


def turn_feed_kernel(
    n, y, dout, gains, hid_hbm, wd_hbm, up_hbm, ge_hbm,
    layer_out, gain_out, df_full, dgate_out, dup_out,
    wd, hid_s, part, landed, mine, held, up_s, ge_s, dg_s, du_s, fold,
    load, feed_sem, rs_send, rs_recv, ag_send, ag_recv, keep_sem, back_sem, out_sem,
):
    i = lax.axis_index("tensor")
    rows, width = y.shape
    whole = pltpu.make_async_copy(wd_hbm, wd, load.at[0])
    whole.start()
    feed = Feed((hid_hbm,), (hid_s,), feed_sem, lambda s: block_at(i, n, n - 1 - s))
    feed.start(jnp.int32(0))
    line_barrier(i, n)
    whole.wait()

    def compute(t, block):
        feed.advance(t, n)
        slot = t % 2

        def tile(k):
            at = pl.ds(pl.multiple_of(k * TILE, TILE), TILE)
            part[block, :, at] = dot_nt(hid_s[slot], wd[at, :]).astype(BF16)

        loop(width // TILE, tile)

    def own(t):
        t = jnp.int32(t)
        feed.advance(t, n)
        slot = t % 2

        def tile(k):
            at = pl.ds(pl.multiple_of(k * TILE, TILE), TILE)
            mine[:, at] = dot_nt(hid_s[slot], wd[at, :])

        loop(width // TILE, tile)

    done = scatter_line(i, n, part, landed, rs_send, rs_recv, compute, own)
    scale = 1.0 + gains[3:4, :]
    fold[...] = jnp.zeros_like(fold)

    def chunk(c):
        r = pl.ds(c * ROWS, ROWS)
        f = summed_rows(i, n, mine, landed, r)
        g = dout[r, :].astype(F32)
        inv = inverse_rms(f)
        layer_out[r, :] = (y[r, :] + f * inv * scale).astype(BF16)
        held[i, r, :] = norm_back(g * scale, f, inv).astype(BF16)
        fold[...] += fold_rows(g * (f * inv))

    loop(rows // ROWS, chunk)
    gain_out[...] = jnp.sum(fold[...], axis=0, keepdims=True)
    done()
    sides = Feed((up_hbm, ge_hbm), (up_s, ge_s), back_sem, lambda s: block_at(i, n, s))
    drain = Drain((dgate_out, dup_out), (dg_s, du_s), out_sem, lambda s: block_at(i, n, s))
    sides.start(jnp.int32(0))

    def backward(s, block):
        pltpu.make_async_copy(held.at[block], df_full.at[block], keep_sem.at[s]).start()
        sides.advance(s, n)
        drain.free(s)
        slot = s % 2
        span = tile_of(wd.shape[1])

        def tile(k):
            at = pl.ds(pl.multiple_of(k * span, span), span)
            dhid = dot_nn(held[block], wd[:, at])
            dg_s[slot, :, at] = (dhid * up_s[slot, :, at].astype(F32)).astype(BF16)
            du_s[slot, :, at] = (dhid * ge_s[slot, :, at].astype(F32)).astype(BF16)

        loop(wd.shape[1] // span, tile)
        drain.start(s)

    gather_line(i, n, held, ag_send, ag_recv, backward)
    drain.finish(n)

    def finish(s):
        block = block_at(i, n, s)
        pltpu.make_async_copy(held.at[block], df_full.at[block], keep_sem.at[s]).wait()

    loop(n, finish)


def turn_feed(n, y, dout, gains, hid, wd, up, ge):
    rows, width = y.shape
    wide = wd.shape[1]
    blocks = lambda w: jax.ShapeDtypeStruct((n, rows, w), BF16)
    return pl.pallas_call(
        functools.partial(turn_feed_kernel, n),
        out_shape=[
            jax.ShapeDtypeStruct((rows, width), BF16),
            jax.ShapeDtypeStruct((1, width), F32),
            blocks(width),
            blocks(wide),
            blocks(wide),
        ],
        in_specs=[VM, VM, VM, ANY, ANY, ANY, ANY],
        out_specs=[VM, VM, ANY, ANY, ANY],
        scratch_shapes=[
            pltpu.VMEM(wd.shape, BF16),
            pltpu.VMEM((2, rows, wide), BF16),
            pltpu.VMEM((n, rows, width), BF16),
            pltpu.VMEM((n + 1, rows, width), BF16),
            pltpu.VMEM((rows, width), F32),
            pltpu.VMEM((n, rows, width), BF16),
        ]
        + [pltpu.VMEM((2, rows, wide), BF16)] * 4
        + [pltpu.VMEM((8, width), F32)]
        + [pltpu.SemaphoreType.DMA((1,)), pltpu.SemaphoreType.DMA((1, 2))]
        + line_scratch(n) * 2
        + [
            pltpu.SemaphoreType.DMA((n,)),
            pltpu.SemaphoreType.DMA((2, 2)),
            pltpu.SemaphoreType.DMA((2, 2)),
        ],
        compiler_params=params(3, 62),
        cost_estimate=cost(0, 600 << 20),
        name="turn_feed",
    )(y, dout, gains, hid, wd, up, ge)


def out_of_feed_kernel(
    n, y, attn, dout, gains, dgate_hbm, dup_hbm, wg_hbm, wu_hbm, wo_hbm,
    dy_out, gain_out, dattn_full, do_out,
    wg, wu, wo, dg_s, du_s, part, landed, mine, held, do_s, fold,
    load, feed_sem, rs_send, rs_recv, ag_send, ag_recv, keep_sem, out_sem,
):
    i = lax.axis_index("tensor")
    rows, width = y.shape
    loads = [
        pltpu.make_async_copy(src, dst, load.at[k])
        for k, (src, dst) in enumerate(((wg_hbm, wg), (wu_hbm, wu), (wo_hbm, wo)))
    ]
    for c in loads:
        c.start()
    feed = Feed((dgate_hbm, dup_hbm), (dg_s, du_s), feed_sem, lambda s: block_at(i, n, n - 1 - s))
    feed.start(jnp.int32(0))
    line_barrier(i, n)
    loads[0].wait()
    loads[1].wait()

    def product(slot, at):
        return dot_nt(dg_s[slot], wg[at, :]) + dot_nt(du_s[slot], wu[at, :])

    def compute(t, block):
        feed.advance(t, n)
        slot = t % 2

        def tile(k):
            at = pl.ds(pl.multiple_of(k * TILE, TILE), TILE)
            part[block, :, at] = product(slot, at).astype(BF16)

        loop(width // TILE, tile)

    def own(t):
        t = jnp.int32(t)
        feed.advance(t, n)
        slot = t % 2

        def tile(k):
            at = pl.ds(pl.multiple_of(k * TILE, TILE), TILE)
            mine[:, at] = product(slot, at)

        loop(width // TILE, tile)

    done = scatter_line(i, n, part, landed, rs_send, rs_recv, compute, own)
    scale_two, scale_three = 1.0 + gains[1:2, :], 1.0 + gains[2:3, :]
    fold[...] = jnp.zeros_like(fold)

    def chunk(c):
        r = pl.ds(c * ROWS, ROWS)
        dh3 = summed_rows(i, n, mine, landed, r)
        v = y[r, :]
        inv = inverse_rms(v)
        dy = dout[r, :].astype(F32) + norm_back(dh3 * scale_three, v, inv)
        dy_out[r, :] = dy
        fold[1] += fold_rows(dh3 * (v * inv))
        a = attn[r, :]
        inv = inverse_rms(a)
        held[i, r, :] = norm_back(dy * scale_two, a, inv).astype(BF16)
        fold[0] += fold_rows(dy * (a * inv))

    loop(rows // ROWS, chunk)
    gain_out[0:1, :] = jnp.sum(fold[0], axis=0, keepdims=True)
    gain_out[1:2, :] = jnp.sum(fold[1], axis=0, keepdims=True)
    done()
    loads[2].wait()
    drain = Drain((do_out,), (do_s,), out_sem, lambda s: block_at(i, n, s))

    def backward(s, block):
        pltpu.make_async_copy(held.at[block], dattn_full.at[block], keep_sem.at[s]).start()
        drain.free(s)
        do_s[s % 2] = dot_nn(held[block], wo[...]).astype(BF16)
        drain.start(s)

    gather_line(i, n, held, ag_send, ag_recv, backward)
    drain.finish(n)

    def finish(s):
        block = block_at(i, n, s)
        pltpu.make_async_copy(held.at[block], dattn_full.at[block], keep_sem.at[s]).wait()

    loop(n, finish)


def out_of_feed(n, y, attn, dout, gains, dgate, dup, wg, wu, wo):
    rows, width = y.shape
    wide = wg.shape[1]
    narrow = wo.shape[1]
    return pl.pallas_call(
        functools.partial(out_of_feed_kernel, n),
        out_shape=[
            jax.ShapeDtypeStruct((rows, width), F32),
            jax.ShapeDtypeStruct((2, width), F32),
            jax.ShapeDtypeStruct((n, rows, width), BF16),
            jax.ShapeDtypeStruct((n, rows, narrow), BF16),
        ],
        in_specs=[VM, VM, VM, VM, ANY, ANY, ANY, ANY, ANY],
        out_specs=[VM, VM, ANY, ANY],
        scratch_shapes=[
            pltpu.VMEM(wg.shape, BF16),
            pltpu.VMEM(wu.shape, BF16),
            pltpu.VMEM(wo.shape, BF16),
            pltpu.VMEM((2, rows, wide), BF16),
            pltpu.VMEM((2, rows, wide), BF16),
            pltpu.VMEM((n, rows, width), BF16),
            pltpu.VMEM((n + 1, rows, width), BF16),
            pltpu.VMEM((rows, width), F32),
            pltpu.VMEM((n, rows, width), BF16),
            pltpu.VMEM((2, rows, narrow), BF16),
            pltpu.VMEM((2, 8, width), F32),
        ]
        + [pltpu.SemaphoreType.DMA((3,)), pltpu.SemaphoreType.DMA((2, 2))]
        + line_scratch(n) * 2
        + [pltpu.SemaphoreType.DMA((n,)), pltpu.SemaphoreType.DMA((1, 2))],
        compiler_params=params(4, 62),
        cost_estimate=cost(0, 600 << 20),
        name="out_of_feed",
    )(y, attn, dout, gains, dgate, dup, wg, wu, wo)


class Slots:
    def __init__(self, arrays, pool, firsts, sems, view, width=None):
        self.arrays, self.pool, self.firsts, self.sems, self.view = arrays, pool, firsts, sems, view
        self.width = width or pool.shape[2]

    def copies(self, s, inward):
        for k, (array, first) in enumerate(zip(self.arrays, self.firsts)):
            slot = self.pool.at[first + s % 2, :, pl.ds(0, self.width)]
            block = self.view(array, s)
            pair = (block, slot) if inward else (slot, block)
            yield pltpu.make_async_copy(*pair, self.sems.at[k, s % 2])

    def fetch(self, s):
        for c in self.copies(s, True):
            c.start()

    def advance(self, s, count):
        for c in self.copies(s, True):
            c.wait()
        if s + 1 < count:
            self.fetch(s + 1)

    def free(self, s):
        if s >= 2:
            self.settle(s - 2)

    def settle(self, s):
        for c in self.copies(s, False):
            c.wait()

    def leave(self, s):
        for c in self.copies(s, False):
            c.start()

    def finish(self, count):
        for s in range(max(0, count - 2), count):
            self.settle(s)


def middle_kernel(
    n, x_hbm, dout_hbm, gains, o_hbm, wo_hbm, wg_hbm, wu_hbm, wd_hbm,
    layer_out, dy_out, gain_out, h3_t, hid_out, up_out, ge_out, df_t, dgate_out, dup_out,
    dattn_t, do_out, dattn_own,
    xs, dout, wo, wg, wu, wd, part, landed, held, y, attn, pool, fold, flip,
    load, rs_send, rs_recv, ag_send, ag_recv, flip_sem, in_sem, out_sem, last_sem,
    wu_send, wu_recv, wu_local, wd_send, wd_recv, wd_local,
):
    i = lax.axis_index("tensor")
    rows, width = xs.shape
    piece = rows // 2
    narrow = wo_hbm.shape[1]
    pairs = ((wo_hbm, wo), (x_hbm, xs), (wg_hbm, wg), (dout_hbm, dout))
    loads = [pltpu.make_async_copy(a, b, load.at[k]) for k, (a, b) in enumerate(pairs)]
    for c in loads:
        c.start()
    up_spread = Spread(wu_hbm, wu, wu_send, wu_recv, wu_local)
    down_spread = Spread(wd_hbm, wd, wd_send, wd_recv, wd_local)
    line_barrier(i, n, up_spread.peers())
    up_spread.begin()
    loads[0].wait()
    wide = wd.shape[1]
    over, across = min(768, wide_tile(width)), min(768, wide_tile(wide))
    scale_two, scale_three, scale_four = (1.0 + gains[k : k + 1, :] for k in (1, 2, 3))
    fold[...] = jnp.zeros_like(fold)

    def tiles(total, size, body):
        loop(total // size, lambda k: body(pl.ds(pl.multiple_of(k * size, size), size)))

    def place(c):
        return pl.ds(c * piece, piece)

    def forward_view(c):
        return lambda array, s: array.at[block_at(i, n, s), place(c)]

    def backward_view(c):
        return lambda array, s: array.at[block_at(i, n, n - 1 - s), place(c)]

    class Sum:
        def __init__(self, which, c, product, feed=None):
            at = 2 * which + c
            self.c, self.feed = c, feed
            self.part, self.landed = part.at[c], landed.at[c]

            def compute(t, block):
                if feed:
                    feed.advance(t, n)

                def tile(at):
                    self.part[block, :, at] = product(t, block, at).astype(BF16)

                tiles(width, over, tile)

            self.compute = compute
            self.step, self.land, self.done = scatter_steps(
                i, n, self.part, self.landed, rs_send.at[at], rs_recv.at[at], compute
            )

        def start(self):
            if self.feed:
                self.feed.fetch(0)
            self.step(0)

        def own(self):
            self.compute(n - 1, i)

        def rows(self, r):
            return summed_rows(i, n, self.part.at[i], self.landed, r)

    class Gather:
        def __init__(self, which, c, full, compute, drained):
            at = 2 * which + c
            self.c, self.full, self.compute, self.drained = c, full, compute, drained
            self.pass_on, self.sent = gather_steps(i, n, held.at[c], ag_send.at[at], ag_recv.at[at])

        def use(self, s):
            block = block_at(i, n, s)
            self.compute(s, block)
            column = block * rows + self.c * piece
            flip_rows(held.at[self.c, block], self.full, column, flip, flip_sem)

        def finish(self):
            self.use(n - 1)
            self.sent()
            self.drained(n)

    def chunks(c, body):
        strip = strip_of(piece)

        def one(k):
            body(pl.ds(k * strip, strip), pl.ds(c * piece + k * strip, strip))

        loop(piece // strip, one)


    def out_product(t, block, at):
        return dot_nt(pool[8 + t % 2, :, pl.ds(0, narrow)], wo[at, :])

    def down_product(t, block, at):
        return dot_nt(pool[6 + t % 2], wd[at, :])

    def in_product(t, block, at):
        return dot_nt(pool[6 + t % 2], wg[at, :]) + dot_nt(pool[10 + t % 2], wu[at, :])

    def sums(c):
        heads = Slots((o_hbm,), pool, (8,), in_sem.at[3, c], backward_view(c), narrow)
        hid = Slots((hid_out,), pool, (6,), in_sem.at[0, c], backward_view(c))
        both = Slots((dgate_out, dup_out), pool, (6, 10), in_sem.at[1, c], backward_view(c))
        return (
            Sum(0, c, out_product, heads),
            Sum(1, c, down_product, hid),
            Sum(2, c, in_product, both),
        )


    def after_attention(c, total):
        def body(r, g):
            a = total.rows(r)
            attn[g, :] = a.astype(BF16)
            v = xs[g, :].astype(F32) + a * inverse_rms(a) * scale_two
            y[g, :] = v
            held[c, i, r, :] = (v * inverse_rms(v) * scale_three).astype(BF16)

        chunks(c, body)

    def after_down(c, total):
        def body(r, g):
            f = total.rows(r)
            d = dout[g, :].astype(F32)
            inv = inverse_rms(f)
            xs[g, :] = (y[g, :] + f * inv * scale_four).astype(BF16)
            held[c, i, r, :] = norm_back(d * scale_four, f, inv).astype(BF16)
            fold[2] += fold_rows(d * (f * inv))

        chunks(c, body)

    def after_in(c, total):
        def body(r, g):
            dh3 = total.rows(r)
            v = y[g, :]
            inv = inverse_rms(v)
            dy = dout[g, :].astype(F32) + norm_back(dh3 * scale_three, v, inv)
            y[g, :] = dy
            fold[1] += fold_rows(dh3 * (v * inv))
            a = attn[g, :].astype(F32)
            inv = inverse_rms(a)
            held[c, i, r, :] = norm_back(dy * scale_two, a, inv).astype(BF16)
            fold[0] += fold_rows(dy * (a * inv))

        chunks(c, body)


    def gathers(c):
        ahead = Slots((hid_out, up_out, ge_out), pool, (0, 2, 4), out_sem.at[0, c], forward_view(c))
        sides = Slots((up_out, ge_out), pool, (0, 2), in_sem.at[2, c], forward_view(c))
        back = Slots((dgate_out, dup_out), pool, (4, 8), out_sem.at[1, c], forward_view(c))

        def into(s, block):
            if s == 0 and c == 0:
                up_spread.end()
                loads[2].wait()
            ahead.free(s)
            k = s % 2

            def tile(at):
                u = dot_nn(held[c, block], wg[:, at])
                up = dot_nn(held[c, block], wu[:, at])
                b = 0.7978845608028654
                th = jnp.tanh(b * (u + 0.044715 * (u * u * u)))
                half = 0.5 * (1.0 + th)
                gelu = u * half
                slope = half + 0.5 * u * (1.0 - th * th) * (b * (1.0 + 0.134145 * (u * u)))
                pool[0 + k, :, at] = (gelu * up).astype(BF16)
                pool[2 + k, :, at] = (up * slope).astype(BF16)
                pool[4 + k, :, at] = gelu.astype(BF16)

            tiles(wide, across, tile)
            ahead.leave(s)

        def turned(s, block):
            if s == 0:
                sides.fetch(0)
            sides.advance(s, n)
            back.free(s)
            k = s % 2

            def tile(at):
                dhid = dot_nn(held[c, block], wd[:, at])
                pool[4 + k, :, at] = (dhid * pool[0 + k, :, at].astype(F32)).astype(BF16)
                pool[8 + k, :, at] = (dhid * pool[2 + k, :, at].astype(F32)).astype(BF16)

            tiles(wide, across, tile)
            back.leave(s)

        heads = Slots((do_out,), pool, (0,), out_sem.at[2, c], forward_view(c), narrow)

        def out(s, block):
            heads.free(s)
            pool[s % 2, :, pl.ds(0, narrow)] = dot_nn(held[c, block], wo[...]).astype(BF16)
            heads.leave(s)

        return (
            Gather(0, c, h3_t, into, ahead.finish),
            Gather(1, c, df_t, turned, back.finish),
            Gather(2, c, dattn_t, out, heads.finish),
        )

    sum_of = (sums(0), sums(1))
    gather_of = (gathers(0), gathers(1))
    own_rows = (after_attention, after_down, after_in)

    first_sum = sum_of[0][0]
    first_sum.start()
    for k in range(1, n - 1):
        first_sum.step(k)
    first_sum.own()
    up_spread.middle()
    loads[1].wait()
    loads[3].wait()
    before = None
    for turn in range(5):
        which, c = turn // 2, turn % 2
        total = sum_of[c][which]
        later = (turn + 1) // 2
        following = sum_of[1 - c][later] if later < 3 else None
        gather = gather_of[c][which]
        total.land()
        own_rows[which](c, total)
        gather.pass_on(0)
        total.done()
        if turn == 0:
            up_spread.turn()
            down_spread.begin()
        if before:
            before.finish()
        if turn == 1:
            down_spread.end()
        if turn == 4:
            pltpu.make_async_copy(xs, layer_out, last_sem.at[0]).start()
        if following:
            following.start()
        for k in range(1, n):
            gather.pass_on(k)
            gather.use(k - 1)
            if following and k < n - 1:
                following.step(k)
            elif following:
                following.own()
        if turn == 0:
            down_spread.middle()
            down_spread.turn()
        before = gather
    total = sum_of[1][2]
    total.land()
    own_rows[2](1, total)
    own_out = pltpu.make_async_copy(held.at[1, i], dattn_own, last_sem.at[2])
    own_out.start()
    total.done()
    before.finish()
    pltpu.make_async_copy(y, dy_out, last_sem.at[1]).start()
    for k in range(3):
        gain_out[k : k + 1, :] = jnp.sum(fold[k], axis=0, keepdims=True)
    pltpu.make_async_copy(xs, layer_out, last_sem.at[0]).wait()
    pltpu.make_async_copy(y, dy_out, last_sem.at[1]).wait()
    own_out.wait()


def middle(n, x, dout, gains, o, wo, wg, wu, wd):
    rows, width = x.shape
    wide = wg.shape[1]
    piece = rows // 2
    sem = pltpu.SemaphoreType.DMA
    blocks = lambda w: jax.ShapeDtypeStruct((n, rows, w), BF16)
    turned = jax.ShapeDtypeStruct((width, n * rows), BF16)
    return pl.pallas_call(
        functools.partial(middle_kernel, n),
        out_shape=[
            jax.ShapeDtypeStruct((rows, width), BF16),
            jax.ShapeDtypeStruct((rows, width), F32),
            jax.ShapeDtypeStruct((3, width), F32),
            turned, blocks(wide), blocks(wide), blocks(wide),
            turned, blocks(wide), blocks(wide), turned, blocks(wo.shape[1]),
            jax.ShapeDtypeStruct((piece, width), BF16),
        ],
        in_specs=[ANY, ANY, VM] + [ANY] * 5,
        out_specs=[ANY, ANY, VM] + [ANY] * 10,
        scratch_shapes=[
            pltpu.VMEM(x.shape, BF16),
            pltpu.VMEM(x.shape, BF16),
            pltpu.VMEM(wo.shape, BF16),
            pltpu.VMEM(wg.shape, BF16),
            pltpu.VMEM(wg.shape, BF16),
            pltpu.VMEM((width, wide), BF16),
            pltpu.VMEM((2, n, piece, width), BF16),
            pltpu.VMEM((2, n + 1, piece, width), BF16),
            pltpu.VMEM((2, n, piece, width), BF16),
            pltpu.VMEM(x.shape, F32),
            pltpu.VMEM(x.shape, BF16),
            pltpu.VMEM((12, piece, wide), BF16),
            pltpu.VMEM((3, 8, width), F32),
            pltpu.VMEM((2, 768, piece), BF16),
            sem((4,)), sem((6, 2, n)), sem((6, n + 1)), sem((6, 2, n)), sem((6, n)),
            sem((2,)), sem((4, 2, 2, 2)), sem((3, 2, 3, 2)), sem((3,)),
        ]
        + spread_scratch() * 2,
        compiler_params=pltpu.CompilerParams(
            collective_id=8, has_side_effects=True, vmem_limit_bytes=(127 << 20) // 2
        ),
        cost_estimate=cost(0, 1200 << 20),
        name="middle",
    )(x, dout, gains, o, wo, wg, wu, wd)


def last_kernel(
    n, x, dy, gains, d_hbm, w_hbm, in_grad, gain_out,
    d, w, part, landed, mine, fold, load, rs_send, rs_recv,
):
    i = lax.axis_index("tensor")
    rows, width = x.shape
    loads = [
        pltpu.make_async_copy(src, dst, load.at[k])
        for k, (src, dst) in enumerate(((d_hbm, d), (w_hbm, w)))
    ]
    for c in loads:
        c.start()
    line_barrier(i, n)
    for c in loads:
        c.wait()

    def compute(t, block):
        def tile(k):
            at = pl.ds(pl.multiple_of(k * TILE, TILE), TILE)
            part[block, :, at] = dot_nt(d[block], w[at, :]).astype(BF16)

        loop(width // TILE, tile)

    def own(t):
        def tile(k):
            at = pl.ds(pl.multiple_of(k * TILE, TILE), TILE)
            mine[:, at] = dot_nt(d[i], w[at, :])

        loop(width // TILE, tile)

    done = scatter_line(i, n, part, landed, rs_send, rs_recv, compute, own)
    scale = 1.0 + gains[0:1, :]
    fold[...] = jnp.zeros_like(fold)

    def chunk(c):
        r = pl.ds(c * ROWS, ROWS)
        dh1 = summed_rows(i, n, mine, landed, r)
        v = x[r, :].astype(F32)
        inv = inverse_rms(v)
        in_grad[r, :] = (dy[r, :] + norm_back(dh1 * scale, v, inv)).astype(BF16)
        fold[...] += fold_rows(dh1 * (v * inv))

    loop(rows // ROWS, chunk)
    gain_out[...] = jnp.sum(fold[...], axis=0, keepdims=True)
    done()


def last(n, x, dy, gains, d, w):
    rows, width = x.shape
    return pl.pallas_call(
        functools.partial(last_kernel, n),
        out_shape=[
            jax.ShapeDtypeStruct((rows, width), BF16),
            jax.ShapeDtypeStruct((1, width), F32),
        ],
        in_specs=[VM, VM, VM, ANY, ANY],
        out_specs=[VM, VM],
        scratch_shapes=[
            pltpu.VMEM(d.shape, BF16),
            pltpu.VMEM(w.shape, BF16),
            pltpu.VMEM((n, rows, width), BF16),
            pltpu.VMEM((n + 1, rows, width), BF16),
            pltpu.VMEM((rows, width), F32),
            pltpu.VMEM((8, width), F32),
            pltpu.SemaphoreType.DMA((2,)),
        ]
        + line_scratch(n),
        compiler_params=params(5, 48),
        cost_estimate=cost(0, 300 << 20),
        name="last",
    )(x, dy, gains, d, w)


class Reduce:
    def __init__(self, u, left, right, column, width, bufs, sems):
        me = lax.axis_index("dp")
        c, x, y = me % 2, (me // 2) % 2, me // 4
        self.me, self.set, self.third, self.fifth, self.width = me, u % 2, u % 3, u % 5, width
        self.left, self.right, self.column = left, right, column
        self.dx, self.dy, self.dc = 2 - 4 * x, 4 - 8 * y, 1 - 2 * c
        self.lefts, self.rights, self.pair, self.pair_in, self.sums, self.far_in, self.xy_in, self.own = bufs
        (
            self.left_sem, self.right_sem, self.pair_send, self.pair_recv,
            self.far_send, self.far_recv, self.xy_send, self.xy_recv,
        ) = sems
        self.rows = self.own.shape[1]
        self.cols = pl.ds(0, width)
        self.top = pl.ds(0, self.rows // 2)
        self.low = pl.ds(self.rows // 2, self.rows // 2)

    def owner(self, q):
        k = q % 4
        x = jnp.where(k <= 1, self.dx, 0)
        y = jnp.where(k % 2 == 0, self.dy, 0)
        return self.me + x + jnp.where(k == 3, 0, y) + jnp.where(q < 4, self.dc, 0)

    def left_copy(self, q):
        r = pl.ds(self.owner(q) * self.rows, self.rows)
        return pltpu.make_async_copy(self.left.at[r], self.lefts.at[q % 2], self.left_sem.at[q % 2])

    def right_copy(self):
        return pltpu.make_async_copy(
            self.right.at[:, pl.ds(self.column, self.width)],
            self.rights.at[self.set, :, self.cols],
            self.right_sem.at[self.set],
        )

    def remote(self, src, dst, send, recv, shift):
        return pltpu.make_async_remote_copy(
            src, dst, send, recv, device_id={"dp": self.me + shift}, device_id_type=MESH
        )

    def pair_copy(self, k):
        return self.remote(
            self.pair.at[self.set, k, :, self.cols],
            self.pair_in.at[self.set, k, :, self.cols],
            self.pair_send.at[self.set, k],
            self.pair_recv.at[self.set, k],
            self.dc,
        )

    def far_copy(self, way):
        return self.remote(
            self.sums.at[self.third, 0, (self.top, self.low)[way], self.cols],
            self.far_in.at[self.third, way, :, self.cols],
            self.far_send.at[self.third, way],
            self.far_recv.at[self.third, way],
            (self.dx, self.dy)[way],
        )

    def xy_copy(self, way, half):
        r = (self.top, self.low)[half]
        return self.remote(
            self.sums.at[self.third, 1 + way, r, self.cols],
            self.xy_in.at[self.fifth, way, r, self.cols],
            self.xy_send.at[self.third, way, half],
            self.xy_recv.at[self.fifth, way, half],
            (self.dx, self.dy)[way],
        )

    def product(self, q, put):
        self.left_copy(q).wait()
        if isinstance(q, int):
            if q < 7:
                self.left_copy(q + 1).start()
        else:
            self.left_copy(q + 1).start()
        tile = wide_tile(self.width)

        def one(t):
            at = pl.ds(pl.multiple_of(t * tile, tile), tile)
            put(at, dot_nn(self.lefts[q % 2], self.rights[self.set, :, at]))

        loop(self.width // tile, one)

    def load(self):
        self.right_copy().start()

    def begin(self):
        self.left_copy(0).start()
        self.right_copy().wait()

        def chunk(k):
            def put(at, value):
                self.pair[self.set, k, :, at] = value.astype(BF16)

            self.product(k, put)
            self.pair_copy(k).start()

        loop(4, chunk)

    def middle(self):
        for k in range(4):
            arrived = []

            def put(at, value, k=k):
                total = value + self.pair_in[self.set, k, :, at].astype(F32)
                if k < 3:
                    self.sums[self.third, k, :, at] = total.astype(BF16)
                else:
                    self.own[self.third, :, at] = total

            self.pair_copy(k).wait_recv()
            self.product(4 + k, put)
            if k == 0:
                self.far_copy(0).start()
                self.far_copy(1).start()
            elif k == 1:
                self.xy_copy(0, 0).start()
            elif k == 2:
                self.xy_copy(1, 1).start()
        for k in range(4):
            self.pair_copy(k).wait_send()

    def turn(self):
        self.far_copy(0).wait_recv()
        self.far_copy(1).wait_recv()
        half = self.rows // 2

        strip = strip_of(half)

        def chunk(c):
            for way, first in ((0, 0), (1, half)):
                r = pl.ds(first + c * strip, strip)
                f = pl.ds(c * strip, strip)
                k = 2 - way
                total = self.sums[self.third, k, r, self.cols].astype(F32)
                total += self.far_in[self.third, way, f, self.cols].astype(F32)
                self.sums[self.third, k, r, self.cols] = total.astype(BF16)

        loop(half // strip, chunk)
        self.xy_copy(0, 1).start()
        self.xy_copy(1, 0).start()

    def end(self, put):
        for way in range(2):
            for half in range(2):
                self.xy_copy(way, half).wait_recv()

        strip = strip_of(self.rows)

        def chunk(c):
            r = pl.ds(c * strip, strip)
            total = self.own[self.third, r, self.cols]
            for way in range(2):
                total += self.xy_in[self.fifth, way, r, self.cols].astype(F32)
            put(r, total)

        loop(self.rows // strip, chunk)
        for way in range(2):
            self.far_copy(way).wait_send()
            for half in range(2):
                self.xy_copy(way, half).wait_send()


def reduce_scratch(rows, tokens, widest):
    sem = pltpu.SemaphoreType.DMA
    bufs = [
        pltpu.VMEM((2, rows, tokens), BF16),
        pltpu.VMEM((2, tokens, widest), BF16),
        pltpu.VMEM((2, 4, rows, widest), BF16),
        pltpu.VMEM((2, 4, rows, widest), BF16),
        pltpu.VMEM((3, 3, rows, widest), BF16),
        pltpu.VMEM((3, 2, rows // 2, widest), BF16),
        pltpu.VMEM((5, 2, rows, widest), BF16),
        pltpu.VMEM((3, rows, widest), F32),
    ]
    sems = [
        sem((2,)), sem((2,)), sem((2, 4)), sem((2, 4)),
        sem((3, 2)), sem((3, 2)), sem((3, 2, 2)), sem((5, 2, 2)),
    ]
    return bufs, sems


def finish_kernel(
    n, heads, kvs, units_of, starts, x_hbm, dy_hbm, gains, own_hbm, do_hbm, q_hbm, k_hbm, v_hbm,
    cos_hbm, sin_hbm, wo_hbm, w_hbm, dattn_in, h1_t, df_t, h3_t, hid, dgate, dup, o_hbm,
    in_grad, gain_out, out_qkv, out_down, out_gate, out_up, out_out, kv_out, dattn_t,
    x, dy, held, do, q, k, v, cos, sin, wo, w, d, dk, dv, part, landed, fold, flip, stage, kv_stage,
    load, do_load, ag_send, ag_recv, rs_send, rs_recv, flip_sem, out_sem, last_sem, kv_sem, kv_send,
    kv_recv, *reduce_refs,
):
    i = lax.axis_index("tensor")
    rows, width = x.shape
    piece = rows // 2
    over = min(768, wide_tile(width))
    split = heads * HD
    pairs = (
        (own_hbm, held.at[i]), (wo_hbm, wo), (q_hbm, q), (k_hbm, k), (v_hbm, v), (cos_hbm, cos),
        (sin_hbm, sin), (w_hbm, w), (x_hbm, x), (dy_hbm, dy),
    )
    loads = [pltpu.make_async_copy(a, b, load.at[j]) for j, (a, b) in enumerate(pairs)]
    for c in loads:
        c.start()
    half_loads = [
        pltpu.make_async_copy(
            do_hbm.at[j, pl.ds(0, piece)], do.at[pl.ds(j * rows, piece)], do_load.at[j]
        )
        for j in range(n)
    ]
    for c in half_loads:
        c.start()

    lefts = dict(qkv=h1_t, down=df_t, gate=h3_t, up=h3_t, out=dattn_t)
    rights = dict(qkv=d, down=hid, gate=dgate, up=dup, out=o_hbm)
    outs = dict(qkv=out_qkv, down=out_down, gate=out_gate, up=out_up, out=out_out)
    units = [
        Reduce(u, lefts[name], rights[name], column, size, reduce_refs[:8], reduce_refs[8:])
        for u, (name, column, size) in enumerate(units_of)
    ]
    count = len(units)
    units[0].load()
    me = units[0].me

    barrier = pltpu.get_barrier_semaphore()
    for shift in (units[0].dc, units[0].dx, units[0].dy):
        pl.semaphore_signal(barrier, 1, device_id={"dp": me + shift}, device_id_type=MESH)
    for j in range(1, n):
        peer = lax.rem(i + j, n)
        pl.semaphore_signal(barrier, 1, device_id={"tensor": peer}, device_id_type=MESH)
    pl.semaphore_wait(barrier, n + 2)


    pass_on, sent = gather_steps(i, n, held, ag_send, ag_recv)

    def use(s):
        block = block_at(i, n, s)
        at = pl.ds(pl.multiple_of(block * rows + piece, piece), piece)
        do[at, :] = dot_nn(held[block], wo[...]).astype(BF16)
        flip_rows(held.at[block], dattn_t, block * rows + piece, flip, flip_sem)

    def attention():
        use(n - 1)
        sent()
        for c in half_loads + loads[2:7]:
            c.wait()
        attend_back_kernel(heads, kvs, 128, starts, q, k, v, do, cos, sin, d, dk, dv)


    def compute(t, block):
        mine = d[pl.ds(pl.multiple_of(block * rows, rows), rows), :]

        def tile(j):
            at = pl.ds(pl.multiple_of(j * over, over), over)
            part[block, :, at] = dot_nt(mine, w[at, :]).astype(BF16)

        loop(width // over, tile)

    step, land, done = scatter_steps(i, n, part, landed, rs_send, rs_recv, compute)

    def begin_line():
        for c in loads[7:]:
            c.wait()
        step(0)

    def input_grad():
        land()
        scale = 1.0 + gains[0:1, :]
        fold[...] = jnp.zeros_like(fold)
        strip = strip_of(rows)

        def chunk(c):
            r = pl.ds(c * strip, strip)
            dh1 = summed_rows(i, n, part.at[i], landed, r)
            a = x[r, :].astype(F32)
            inv = inverse_rms(a)
            x[r, :] = (dy[r, :] + norm_back(dh1 * scale, a, inv)).astype(BF16)
            fold[...] += fold_rows(dh1 * (a * inv))

        loop(rows // strip, chunk)
        gain_out[...] = jnp.sum(fold[...], axis=0, keepdims=True)
        pltpu.make_async_copy(x, in_grad, last_sem.at[0]).start()
        done()


    def out_copy(u):
        name, column, size = units_of[u]
        return pltpu.make_async_copy(
            stage.at[u % 2, :, pl.ds(0, size)],
            outs[name].at[:, pl.ds(column, size)],
            out_sem.at[u % 2],
        )

    def kv_copy(j, owner, peer):
        return pltpu.make_async_remote_copy(
            kv_stage, kv_out.at[owner], kv_send.at[j], kv_recv.at[j],
            device_id={"tensor": peer}, device_id_type=MESH,
        )

    kv_own = pltpu.make_async_copy(kv_stage, kv_out.at[i], kv_sem.at[0])

    def finish(u):
        if u >= 2:
            out_copy(u - 2).wait()
        name, column, size = units_of[u]
        keys = name == "qkv" and column == split

        def put(r, total):
            stage[u % 2, r, pl.ds(0, size)] = total
            if keys:
                kv_stage[r, :] = total.astype(BF16)

        units[u].end(put)
        out_copy(u).start()
        if keys:
            for j in range(1, n):
                kv_copy(j, i, lax.rem(i + j, n)).start()
            kv_own.start()

    def passing(s):
        pass_on(s)
        use(s - 1)

    line = [[functools.partial(passing, s)] for s in range(1, n)]
    line[-1] += [attention, begin_line]
    for t in range(1, n - 1):
        line += [[], [functools.partial(step, t)]]
    line += [[lambda: compute(n - 1, i)], [input_grad]]

    loads[0].wait()
    loads[1].wait()
    pass_on(0)
    for u in range(max(count + 2, len(line))):
        if u < count:
            units[u].begin()
            if u + 1 < count:
                units[u + 1].load()
            units[u].middle()
        if 1 <= u <= count:
            units[u - 1].turn()
        if 2 <= u < count + 2:
            finish(u - 2)
        for action in line[u] if u < len(line) else ():
            action()
    for u in range(max(0, count - 2), count):
        out_copy(u).wait()
    pltpu.make_async_copy(x, in_grad, last_sem.at[0]).wait()
    kv_own.wait()
    for j in range(1, n):
        kv_copy(j, i, lax.rem(i + j, n)).wait_send()
        peer = lax.rem(i + n - j, n)
        kv_copy(j, peer, peer).wait_recv()


def pieces(name, width, most=768):
    count = next(c for c in range(1, width) if width % (c * 128) == 0 and width // c <= most)
    return [(name, k * (width // count), width // count) for k in range(count)]


def finish(n, m, heads, kvs, starts, x, dy, gains, own, do, q, k, v, cos, sin, wo, w, turned, rights, o):
    rows, width = x.shape
    tokens = n * rows
    own_rows = width // m
    split, across = heads * HD, w.shape[1]
    down, gate, up = (pieces(s, r.shape[1]) for s, r in zip(("down", "gate", "up"), rights))
    early = (down + gate)[: n + 1]
    late = (down + gate)[n + 1 :] + up + pieces("out", o.shape[1])
    units = early + [("qkv", split, across - split), ("qkv", 0, split)] + late
    widest = max(size for _, _, size in units)
    bufs, sems = reduce_scratch(own_rows, tokens, widest)
    sem = pltpu.SemaphoreType.DMA
    shape = lambda a, b, t=F32: jax.ShapeDtypeStruct((a, b), t)
    return pl.pallas_call(
        functools.partial(finish_kernel, n, heads, kvs, units),
        out_shape=[shape(rows, width, BF16), shape(1, width), shape(own_rows, across)]
        + [shape(own_rows, r.shape[1]) for r in (*rights, o)]
        + [jax.ShapeDtypeStruct((n, own_rows, across - split), BF16), shape(width, tokens, BF16)],
        in_specs=[SM, ANY, ANY, VM] + [ANY] * 17,
        out_specs=[ANY, VM] + [ANY] * 7,
        scratch_shapes=[
            pltpu.VMEM(x.shape, BF16),
            pltpu.VMEM(x.shape, F32),
            pltpu.VMEM((n, rows // 2, width), BF16),
            pltpu.VMEM((tokens, split), BF16),
            pltpu.VMEM(q.shape, BF16),
            pltpu.VMEM(k.shape, BF16),
            pltpu.VMEM(v.shape, BF16),
            pltpu.VMEM(cos.shape, F32),
            pltpu.VMEM(sin.shape, F32),
            pltpu.VMEM(wo.shape, BF16),
            pltpu.VMEM(w.shape, BF16),
            pltpu.VMEM((tokens, across), BF16),
            pltpu.VMEM((L, HD), F32),
            pltpu.VMEM((L, HD), F32),
            pltpu.VMEM((n, rows, width), BF16),
            pltpu.VMEM((n + 1, rows, width), BF16),
            pltpu.VMEM((8, width), F32),
            pltpu.VMEM((2, 768, rows // 2), BF16),
            pltpu.VMEM((2, own_rows, widest), F32),
            pltpu.VMEM((own_rows, across - split), BF16),
            sem((10,)), sem((n,)),
        ]
        + line_scratch(n) * 2
        + [sem((2,)), sem((2,)), sem((1,)), sem((1,)), sem((n,)), sem((n,))]
        + bufs
        + sems,
        input_output_aliases={13: 8},
        compiler_params=pltpu.CompilerParams(
            collective_id=7, has_side_effects=True, vmem_limit_bytes=(127 << 20) // 2
        ),
        cost_estimate=cost(0, 600 << 20),
        name="finish",
    )(starts, x, dy, gains, own, do, q, k, v, cos, sin, wo, w, turned[3], *turned[:3], *rights, o)


def deliver_kernel(count, *refs):
    sources, qkv, kv_hbm = refs[:count], refs[count], refs[count + 1]
    targets, k_out, v_out = refs[count + 2 : 2 * count + 3], *refs[2 * count + 3 : 2 * count + 5]
    stages = refs[2 * count + 5 : 3 * count + 6]
    kv, k_s, v_s, load, store = refs[3 * count + 6 :]
    n, rows, across = kv.shape
    split = targets[-1].shape[1]
    sources = (*sources, qkv.at[:, pl.ds(0, split)])
    first = pltpu.make_async_copy(kv_hbm, kv, load.at[count + 1])
    first.start()
    loads = [pltpu.make_async_copy(a, b, load.at[j]) for j, (a, b) in enumerate(zip(sources, stages))]
    for c in loads:
        c.start()
    stores = [
        pltpu.make_async_copy(a, b, store.at[j])
        for j, (a, b) in enumerate(zip((*stages, k_s, v_s), (*targets, k_out, v_out)))
    ]
    first.wait()
    half = across // 2
    for j in range(n):
        k_s[:, j * half : (j + 1) * half] = kv[j, :, :half].astype(F32)
        v_s[:, j * half : (j + 1) * half] = kv[j, :, half:].astype(F32)
    stores[-2].start()
    stores[-1].start()
    for a, b in zip(loads, stores):
        a.wait()
        b.start()
    for c in stores:
        c.wait()


def deliver(split, sources, qkv, kv):
    n, rows, across = kv.shape
    shape = lambda a: jax.ShapeDtypeStruct(a.shape, a.dtype)
    wide = jax.ShapeDtypeStruct((rows, n * across // 2), F32)
    count = len(sources)
    return pl.pallas_call(
        functools.partial(deliver_kernel, count),
        out_shape=[shape(a) for a in sources] + [jax.ShapeDtypeStruct((rows, split), F32), wide, wide],
        in_specs=[ANY] * (count + 2),
        out_specs=[ANY] * (count + 3),
        scratch_shapes=[pltpu.VMEM(a.shape, a.dtype) for a in sources]
        + [
            pltpu.VMEM((rows, split), F32),
            pltpu.VMEM(kv.shape, BF16),
            pltpu.VMEM(wide.shape, F32),
            pltpu.VMEM(wide.shape, F32),
            pltpu.SemaphoreType.DMA((count + 2,)),
            pltpu.SemaphoreType.DMA((count + 3,)),
        ],
        compiler_params=pltpu.CompilerParams(vmem_limit_bytes=62 << 20),
        cost_estimate=cost(0, 40 << 20),
        name="deliver",
    )(*sources, qkv, kv)


def rope_tables():
    positions = jnp.arange(L, dtype=jnp.int32).astype(F32)
    exponent = jnp.arange(HD // 2, dtype=jnp.int32).astype(F32) * (-2.0 / HD)
    angles = positions[:, None] * jnp.exp(exponent * jnp.log(F32(10000.0)))[None, :]
    return jnp.cos(angles), jnp.sin(angles)


def weight_grad(left, right):
    return dot_tn(left, right).astype(BF16)


def scatter_rows(grad):
    return lax.psum_scatter(grad, "dp", scatter_dimension=0, tiled=True)


def body(
    n,
    m,
    layer_in,
    out_grad,
    piece_starts,
    attn_gain,
    attn_out_gain,
    feed_gain,
    feed_out_gain,
    query_weight,
    key_weight,
    value_weight,
    out_weight,
    gate_weight,
    up_weight,
    down_weight,
):
    heads = query_weight.shape[1] // HD
    fan = H // KV
    kvs = max(1, heads // fan)
    rank = lax.axis_index("tensor")
    kv_at = (rank * heads // fan) * HD
    rows, width = layer_in.shape
    tokens = n * rows

    gathered = gather_gains(m, jnp.stack([attn_gain, attn_out_gain, feed_gain, feed_out_gain]))
    gains = gathered.transpose(1, 0, 2).reshape(4, width).astype(F32)

    def collect(shard):
        return lax.all_gather(shard, "dp", axis=0, tiled=True)

    wqkv = collect(
        jnp.concatenate(
            [
                query_weight,
                lax.dynamic_slice_in_dim(key_weight, kv_at, kvs * HD, 1),
                lax.dynamic_slice_in_dim(value_weight, kv_at, kvs * HD, 1),
            ],
            axis=1,
        )
    )
    wo = collect(out_weight.T)
    cos, sin = rope_tables()

    spread = m == 8 and n * kvs == KV
    h1, wg, h1_t = first(n, m, layer_in, gains, gate_weight if spread else None)
    if not spread:
        wg = collect(gate_weight)
    h1_flat = h1.reshape(tokens, width)
    q, k, v, o = attend(heads, kvs, piece_starts, h1_flat, wqkv, cos, sin)
    o_blocks = o.reshape(n, rows, heads * HD)
    if spread:
        layer_out, dy, gain_later, h3_t, hid, _, _, df_t, dgate, dup, dattn_t, do, own = middle(
            n, layer_in, out_grad, gains, o_blocks, wo, wg, up_weight, down_weight.T
        )
    else:
        wu, wd = collect(up_weight), collect(down_weight.T)
        attn, y, h3, hid, up, ge = into_feed(n, layer_in, gains, o_blocks, wo, wg, wu)
        layer_out, gain_four, df, dgate, dup = turn_feed(n, y, out_grad, gains, hid, wd, up, ge)
    flat = lambda a: a.reshape(tokens, a.shape[-1])
    split = heads * HD
    if spread:
        in_grad, gain_one, qkv_sum, down_sum, gate_sum, up_sum, out_sum, kv, _ = finish(
            n, m, heads, kvs, piece_starts, layer_in, dy, gains, own, do, q, k, v, cos, sin, wo, wqkv,
            (h1_t, df_t, h3_t, dattn_t), (flat(hid), flat(dgate), flat(dup)), o,
        )
    else:
        tie = lax.optimization_barrier
        down_part = weight_grad(flat(df), flat(hid))
        gate_part = weight_grad(flat(h3), flat(dgate))
        up_part = weight_grad(flat(h3), flat(dup))
        dgate, dup, down_part, gate_part, up_part = tie((dgate, dup, down_part, gate_part, up_part))
        down_sum, gate_sum, up_sum = map(scatter_rows, (down_part, gate_part, up_part))
        dy, gain_mid, dattn, do = out_of_feed(n, y, attn, out_grad, gains, dgate, dup, wg, wu, wo)
        do, dattn, down_sum, gate_sum = tie((do, dattn, down_sum, gate_sum))
        out_part = weight_grad(flat(dattn), o)
        do, out_part = tie((do, out_part))
        d = attend_back(heads, kvs, piece_starts, q, k, v, flat(do), cos, sin)
        qkv_part = weight_grad(h1_flat, d)
        d, qkv_part, up_sum = tie((d, qkv_part, up_sum))
        out_sum, qkv_sum = scatter_rows(out_part), scatter_rows(qkv_part)
        in_grad, gain_one = last(n, layer_in, dy, gains, d.reshape(n, rows, -1), wqkv)
        gain_later = jnp.concatenate([gain_mid, gain_four], axis=0)

        own_rows = qkv_sum.shape[0]
        kv = qkv_sum[:, split:].reshape(own_rows, 2, kvs * HD).transpose(1, 0, 2)
        if n * kvs == KV:
            kv = lax.all_gather(kv, "tensor", axis=2, tiled=True)
        else:
            kv = lax.dynamic_update_slice_in_dim(jnp.zeros((2, own_rows, KV * HD), BF16), kv, kv_at, 2)
            kv = lax.psum(kv, "tensor")
    gain_grads = jnp.concatenate([gain_one, gain_later], axis=0)
    gain_grads = sum_gains(n, m, gain_grads.reshape(4, m, width // m).transpose(1, 0, 2))
    if spread:
        layer_out, in_grad, down_sum, gate_sum, up_sum, out_sum, q_sum, k_sum, v_sum = deliver(
            split, (layer_out, in_grad, down_sum, gate_sum, up_sum, out_sum), qkv_sum, kv
        )
    else:
        q_sum, k_sum, v_sum = qkv_sum[:, :split].astype(F32), kv[0].astype(F32), kv[1].astype(F32)
    return (
        layer_out,
        in_grad,
        q_sum,
        k_sum,
        v_sum,
        out_sum.astype(F32).T,
        gate_sum.astype(F32),
        up_sum.astype(F32),
        down_sum.astype(F32).T,
        gain_grads[0],
        gain_grads[1],
        gain_grads[2],
        gain_grads[3],
    )


def solution(mesh):
    in_specs = (
        P(("dp", "tensor"), None),
        P(("dp", "tensor"), None),
        P("dp", None),
        P("dp"),
        P("dp"),
        P("dp"),
        P("dp"),
        P("dp", "tensor"),
        P("dp", None),
        P("dp", None),
        P("tensor", "dp"),
        P("dp", "tensor"),
        P("dp", "tensor"),
        P("tensor", "dp"),
    )
    out_specs = (
        P(("dp", "tensor"), None),
        P(("dp", "tensor"), None),
        P("dp", "tensor"),
        P("dp", None),
        P("dp", None),
        P("tensor", "dp"),
        P("dp", "tensor"),
        P("dp", "tensor"),
        P("tensor", "dp"),
        P("dp"),
        P("dp"),
        P("dp"),
        P("dp"),
    )
    program = functools.partial(body, mesh.shape["tensor"], mesh.shape["dp"])
    return jax.shard_map(program, mesh=mesh, in_specs=in_specs, out_specs=out_specs, check_vma=False)
```

```python
import functools

import jax
import jax.numpy as jnp
import numpy as np
from jax import lax
from jax.experimental import pallas as pl
from jax.experimental.pallas import tpu as pltpu
from jax.sharding import PartitionSpec as P

H = 8
KV = 4
HD = 256
L = 1024
PIECE = 256

EPS = 1e-06
CAP = 50.0
F32 = jnp.float32
BF16 = jnp.bfloat16
MESH = pl.DeviceIdType.MESH
ANY = pl.BlockSpec(memory_space=pl.ANY)
VM = pl.BlockSpec(memory_space=pltpu.VMEM)
SM = pl.BlockSpec(memory_space=pltpu.SMEM)
ROWS = 16
TILE = 256
AHEAD = 4


def dot_nn(a, b):
    return lax.dot_general(a, b, (((1,), (0,)), ((), ())), preferred_element_type=F32)


def dot_nt(a, b):
    return lax.dot_general(a, b, (((1,), (1,)), ((), ())), preferred_element_type=F32)


def dot_tn(a, b):
    return lax.dot_general(a, b, (((0,), (0,)), ((), ())), preferred_element_type=F32)


def tile_of(width):
    return next(t for t in (256, 384, 128) if width % t == 0)


def strip_of(count):
    return next(t for t in (64, 48, 32, 16) if count % t == 0)


def wide_tile(width):
    return next(t for t in (1152, 1024, 768, 512, 384, 256, 128) if width % t == 0)


def loop(count, body):
    lax.fori_loop(0, count, lambda t, c: (body(t), c)[1], 0)


def block_at(i, n, s):
    m = jnp.minimum(i, n - 1 - i)
    near = i + jnp.where(s % 2 == 1, -((s + 1) // 2), s // 2)
    far = jnp.where(i * 2 < n, i + (s - m), i - (s - m))
    return jnp.where(s <= 2 * m, near, far)


def line_barrier(i, n, peers=()):
    barrier = pltpu.get_barrier_semaphore()

    @pl.when(i > 0)
    def _():
        pl.semaphore_signal(barrier, 1, device_id={"tensor": i - 1}, device_id_type=MESH)

    @pl.when(i < n - 1)
    def _():
        pl.semaphore_signal(barrier, 1, device_id={"tensor": i + 1}, device_id_type=MESH)

    for peer in peers:
        pl.semaphore_signal(barrier, 1, device_id={"dp": peer}, device_id_type=MESH)
    pl.semaphore_wait(barrier, len(peers) + jnp.minimum(i, 1) + jnp.minimum(n - 1 - i, 1))


def gather_steps(i, n, held, send, recv):
    def copy(block, way, s, to):
        return pltpu.make_async_remote_copy(
            held.at[block],
            held.at[block],
            send.at[way, s],
            recv.at[block],
            device_id={"tensor": to},
            device_id_type=MESH,
        )

    up, down = jnp.minimum(i + 1, n - 1), jnp.maximum(i - 1, 0)

    def pass_on(s):
        low, high = i - s, i + s

        @pl.when((s > 0) & (low >= 0))
        def _():
            copy(low, 0, s, up).wait_recv()

        @pl.when((low >= 0) & (i < n - 1))
        def _():
            copy(low, 0, s, up).start()

        @pl.when((s > 0) & (high < n))
        def _():
            copy(high, 1, s, down).wait_recv()

        @pl.when((high < n) & (i > 0))
        def _():
            copy(high, 1, s, down).start()

    def finish(s):
        low, high = i - s, i + s

        @pl.when((low >= 0) & (i < n - 1))
        def _():
            copy(low, 0, s, up).wait_send()

        @pl.when((high < n) & (i > 0))
        def _():
            copy(high, 1, s, down).wait_send()

    return pass_on, functools.partial(loop, n, finish)


def gather_line(i, n, held, send, recv, compute):
    pass_on, finish = gather_steps(i, n, held, send, recv)

    def step(s):
        pass_on(s)
        compute(s, block_at(i, n, s))

    loop(n, step)
    finish()


def scatter_steps(i, n, part, landed, send, recv, compute):
    rows = part.shape[1]

    def copy(block, way, t, to):
        slot = jnp.where(block == to, n, block) if way else block
        return pltpu.make_async_remote_copy(
            part.at[block],
            landed.at[slot],
            send.at[way, t],
            recv.at[slot],
            device_id={"tensor": to},
            device_id_type=MESH,
        )

    def arrived(slot):
        pltpu.make_async_remote_copy(
            landed.at[slot],
            landed.at[slot],
            send.at[0, 0],
            recv.at[slot],
            device_id={"tensor": i},
            device_id_type=MESH,
        ).wait_recv()

    def add(block):
        strip = strip_of(rows)

        def chunk(c):
            r = pl.ds(c * strip, strip)
            total = part[block, r, :].astype(F32) + landed[block, r, :].astype(F32)
            part[block, r, :] = total.astype(BF16)

        loop(rows // strip, chunk)

    up, down = jnp.minimum(i + 1, n - 1), jnp.maximum(i - 1, 0)

    def step(k):
        t = k + 1
        compute(k, block_at(i, n, n - t))
        above, below = i + n - t, i - n + t

        @pl.when((above < n) & (i > 0))
        def _():
            arrived(above)
            add(above)

        @pl.when(above < n)
        def _():
            copy(above, 0, t, up).start()

        @pl.when((below >= 0) & (i < n - 1))
        def _():
            arrived(below)
            add(below)

        @pl.when(below >= 0)
        def _():
            copy(below, 1, t, down).start()

    def land():
        @pl.when(i > 0)
        def _():
            arrived(i)

        @pl.when(i < n - 1)
        def _():
            arrived(jnp.int32(n))

    def finish(k):
        t = k + 1

        @pl.when(i + n - t < n)
        def _():
            copy(i + n - t, 0, t, up).wait_send()

        @pl.when(i - n + t >= 0)
        def _():
            copy(i - n + t, 1, t, down).wait_send()

    return step, land, functools.partial(loop, n - 1, finish)


def scatter_line(i, n, part, landed, send, recv, compute, own):
    step, land, finish = scatter_steps(i, n, part, landed, send, recv, compute)
    loop(n - 1, step)
    own(n - 1)
    land()
    return finish


def summed_rows(i, n, mine, landed, r):
    zero = jnp.zeros((), F32)
    low = jnp.where(i > 0, landed[i, r, :].astype(F32), zero)
    high = jnp.where(i < n - 1, landed[n, r, :].astype(F32), zero)
    return mine[r, :] + low + high


def inverse_rms(v):
    return lax.rsqrt(jnp.mean(v * v, axis=-1, keepdims=True) + EPS)


def norm_back(e, v, r):
    unit = v * r
    return r * (e - unit * jnp.mean(e * unit, axis=-1, keepdims=True))


def fold_rows(v):
    return v.reshape(-1, 8, v.shape[-1]).sum(axis=0)


class Feed:
    def __init__(self, sources, slots, sems, which):
        self.sources, self.slots, self.sems, self.which = sources, slots, sems, which

    def copies(self, s):
        return [
            pltpu.make_async_copy(src.at[self.which(s)], slot.at[s % 2], self.sems.at[k, s % 2])
            for k, (src, slot) in enumerate(zip(self.sources, self.slots))
        ]

    def start(self, s):
        for c in self.copies(s):
            c.start()

    def wait(self, s):
        for c in self.copies(s):
            c.wait()

    def advance(self, s, count):
        self.wait(s)

        @pl.when(s + 1 < count)
        def _():
            self.start(s + 1)


class Drain:
    def __init__(self, targets, slots, sems, which):
        self.targets, self.slots, self.sems, self.which = targets, slots, sems, which

    def copies(self, s):
        return [
            pltpu.make_async_copy(slot.at[s % 2], dst.at[self.which(s)], self.sems.at[k, s % 2])
            for k, (dst, slot) in enumerate(zip(self.targets, self.slots))
        ]

    def free(self, s):
        @pl.when(s >= 2)
        def _():
            for c in self.copies(s - 2):
                c.wait()

    def start(self, s):
        for c in self.copies(s):
            c.start()

    def finish(self, count):
        for s in range(max(0, count - 2), count):
            for c in self.copies(jnp.int32(s)):
                c.wait()


class Spread:
    def __init__(self, own, full, send, recv, local):
        me = lax.axis_index("dp")
        c, x, y = me % 2, (me // 2) % 2, me // 4
        self.own, self.full, self.send, self.recv, self.local = own, full, send, recv, local
        self.me = me
        self.core = me + 1 - 2 * c
        self.x = me + 2 - 4 * x
        self.y = me + 4 - 8 * y
        self.far = self.x + 4 - 8 * y
        self.flip = 1 - 2 * c

    def peers(self):
        return (self.core, self.x, self.y)

    def view(self, owner, part):
        count = self.own.shape[0]
        first, size = ((0, count), (0, count // 2), (count // 2, count // 2))[part]
        return self.full.at[pl.ds(pl.multiple_of(owner * count + first, ROWS), size)]

    def copy(self, k, source, owner, part, to):
        return pltpu.make_async_remote_copy(
            self.own if source is None else self.view(source, part),
            self.view(owner, part),
            self.send.at[k],
            self.recv.at[k],
            device_id={"dp": to},
            device_id_type=MESH,
        )

    def sends(self):
        return (
            (0, None, self.me, 0, self.core),
            (1, None, self.me, 0, self.x),
            (2, None, self.me, 0, self.y),
            (3, self.x, self.x, 1, self.y),
            (4, self.y, self.y, 2, self.x),
            (5, self.x, self.x, 0, self.core),
            (6, self.y, self.y, 0, self.core),
            (7, self.far, self.far, 0, self.core),
        )

    def start(self, *which):
        for k in which:
            self.copy(*self.sends()[k]).start()

    def arrive(self, k):
        owner, part = {
            0: (self.core, 0),
            1: (self.x, 0),
            2: (self.y, 0),
            3: (self.far, 1),
            4: (self.far, 2),
            5: (self.x + self.flip, 0),
            6: (self.y + self.flip, 0),
            7: (self.far + self.flip, 0),
        }[k]
        self.copy(k, owner, owner, part, self.core).wait_recv()

    def keep(self):
        return pltpu.make_async_copy(self.own, self.view(self.me, 0), self.local.at[0])

    def begin(self):
        self.keep().start()
        self.start(1, 2, 0)

    def middle(self):
        self.arrive(1)
        self.arrive(2)
        self.start(3, 4, 5, 6)

    def turn(self):
        self.arrive(3)
        self.arrive(4)
        self.start(7)

    def end(self):
        for k in (0, 5, 6, 7):
            self.arrive(k)
        self.keep().wait()
        for k in range(8):
            self.copy(*self.sends()[k]).wait_send()


def spread_scratch():
    return [pltpu.SemaphoreType.DMA((8,)), pltpu.SemaphoreType.DMA((8,)), pltpu.SemaphoreType.DMA((1,))]


def line_scratch(n):
    return [pltpu.SemaphoreType.DMA((2, n)), pltpu.SemaphoreType.DMA((n + 1,))]


def params(cid, mib):
    return pltpu.CompilerParams(
        collective_id=cid, has_side_effects=True, vmem_limit_bytes=mib << 20
    )


def cost(flops, moved):
    return pl.CostEstimate(flops=flops, bytes_accessed=moved, transcendentals=0)


def gains_kernel(m, mine, out, send, recv):
    me = lax.axis_index("dp")
    barrier = pltpu.get_barrier_semaphore()
    for k in range(1, m):
        pl.semaphore_signal(
            barrier, 1, device_id={"dp": lax.rem(me + k, m)}, device_id_type=MESH
        )
    pl.semaphore_wait(barrier, m - 1)

    def copy(owner, k):
        return pltpu.make_async_remote_copy(
            mine,
            out.at[owner],
            send.at[k],
            recv.at[k],
            device_id={"dp": lax.rem(me + k, m)},
            device_id_type=MESH,
        )

    for k in range(1, m):
        copy(me, k).start()
    out[me] = mine[...]
    for k in range(1, m):
        copy(lax.rem(me + m - k, m), k).wait_recv()
    for k in range(1, m):
        copy(me, k).wait_send()


def gather_gains(m, mine):
    return pl.pallas_call(
        functools.partial(gains_kernel, m),
        out_shape=jax.ShapeDtypeStruct((m,) + mine.shape, mine.dtype),
        in_specs=[VM],
        out_specs=VM,
        scratch_shapes=[pltpu.SemaphoreType.DMA((m,)), pltpu.SemaphoreType.DMA((m,))],
        compiler_params=params(0, 16),
        name="gains",
    )(mine)


def sum_gains_kernel(n, m, mine, out, landed, total, across, send, recv, send_two, recv_two):
    me, i = lax.axis_index("dp"), lax.axis_index("tensor")
    barrier = pltpu.get_barrier_semaphore()
    dp_peer = lambda k: {"dp": lax.rem(me + k, m)}
    line_peer = lambda k: {"tensor": lax.rem(i + k, n)}
    for k in range(1, m):
        pl.semaphore_signal(barrier, 1, device_id=dp_peer(k), device_id_type=MESH)
    for k in range(1, n):
        pl.semaphore_signal(barrier, 1, device_id=line_peer(k), device_id_type=MESH)
    pl.semaphore_wait(barrier, m + n - 2)

    def to_owner(k):
        return pltpu.make_async_remote_copy(
            mine.at[lax.rem(me + k, m)], landed.at[k], send.at[k], recv.at[k],
            device_id=dp_peer(k), device_id_type=MESH,
        )

    def along(k):
        return pltpu.make_async_remote_copy(
            total, across.at[k], send_two.at[k], recv_two.at[k],
            device_id=line_peer(k), device_id_type=MESH,
        )

    for k in range(1, m):
        to_owner(k).start()
    here = mine[me]
    for k in range(1, m):
        to_owner(k).wait_recv()
        here = here + landed[k]
    total[...] = here
    for k in range(1, n):
        along(k).start()
    for k in range(1, n):
        along(k).wait_recv()
        here = here + across[k]
    out[...] = here
    for k in range(1, m):
        to_owner(k).wait_send()
    for k in range(1, n):
        along(k).wait_send()


def sum_gains(n, m, mine):
    shape = mine.shape[1:]
    return pl.pallas_call(
        functools.partial(sum_gains_kernel, n, m),
        out_shape=jax.ShapeDtypeStruct(shape, F32),
        in_specs=[VM],
        out_specs=VM,
        scratch_shapes=[
            pltpu.VMEM((m,) + shape, F32),
            pltpu.VMEM(shape, F32),
            pltpu.VMEM((n,) + shape, F32),
        ]
        + [pltpu.SemaphoreType.DMA((m,))] * 2
        + [pltpu.SemaphoreType.DMA((n,))] * 2,
        compiler_params=params(6, 16),
        name="sum_gains",
    )(mine)


def first_kernel(n, spread, x, gains, *refs):
    i = lax.axis_index("tensor")
    rows = x.shape[0]
    if spread:
        shard, full, gathered, turned, held, send, recv, out_sem, turn, turn_sem, *sems = refs
        gather = Spread(shard, gathered, *sems)
        line_barrier(i, n, gather.peers())
        gather.begin()
    else:
        full, held, send, recv, out_sem = refs
        line_barrier(i, n)
    scale = 1.0 + gains[0:1, :]

    strip = strip_of(rows)

    def chunk(c):
        r = pl.ds(c * strip, strip)
        v = x[r, :].astype(F32)
        held[i, r, :] = (v * inverse_rms(v) * scale).astype(BF16)

    loop(rows // strip, chunk)

    def keep(s, block):
        pltpu.make_async_copy(held.at[block], full.at[block], out_sem.at[s]).start()
        if spread:
            flip_rows(held.at[block], turned, block * rows, turn, turn_sem, s == 0)
            pl.when(s == min(1, n - 1))(gather.middle)
            pl.when(s == min(2, n - 1))(gather.turn)

    gather_line(i, n, held, send, recv, keep)

    def finish(s):
        block = block_at(i, n, s)
        pltpu.make_async_copy(held.at[block], full.at[block], out_sem.at[s]).wait()

    loop(n, finish)
    if spread:
        flip_end(turned, turn, turn_sem)
        gather.end()


def flip_rows(block, target, column, stage, sem, fresh):
    rows, width = block.shape
    size = stage.shape[1]

    def copy(k):
        return pltpu.make_async_copy(
            stage.at[k % 2],
            target.at[pl.ds(k * size, size), pl.ds(pl.multiple_of(column, 128), rows)],
            sem.at[k % 2],
        )

    for k in range(width // size):
        if k >= 2:
            copy(k - 2).wait()
        elif fresh is False:
            copy(k).wait()
        elif fresh is not True:
            pl.when(jnp.logical_not(fresh))(lambda k=k: copy(k).wait())
        for j in range(size // 256):
            at = pl.ds(k * size + j * 256, 256)
            stage[k % 2, pl.ds(j * 256, 256), :] = block[:, at].T
        copy(k).start()


def flip_end(target, stage, sem):
    size, rows = stage.shape[1:]
    for k in range(2):
        pltpu.make_async_copy(
            stage.at[k], target.at[pl.ds(k * size, size), pl.ds(0, rows)], sem.at[k]
        ).wait()


def first(n, m, x, gains, shard):
    rows, width = x.shape
    spread = shard is not None
    outs = [jax.ShapeDtypeStruct((n, rows, width), BF16)]
    if spread:
        outs += [jax.ShapeDtypeStruct((m * shard.shape[0], shard.shape[1]), BF16)]
        outs += [jax.ShapeDtypeStruct((width, n * rows), BF16)]
        turn = [pltpu.VMEM((2, 768, rows), BF16), pltpu.SemaphoreType.DMA((2,))]
    out = pl.pallas_call(
        functools.partial(first_kernel, n, spread),
        out_shape=outs,
        in_specs=[VM, VM] + [ANY] * spread,
        out_specs=[ANY] * len(outs),
        scratch_shapes=[pltpu.VMEM((n, rows, width), BF16)]
        + line_scratch(n)
        + [pltpu.SemaphoreType.DMA((n,))]
        + (turn + spread_scratch() if spread else []),
        compiler_params=params(1, 62),
        cost_estimate=cost(0, 300 << 20),
        name="first",
    )(x, gains, *([shard] if spread else []))
    return out if spread else (out[0], None, None)


def turn(u, cos, sin):
    half = HD // 2
    a, b = u[:, :half], u[:, half:]
    return jnp.concatenate([a * cos - b * sin, b * cos + a * sin], axis=-1)


def row_limit(starts, seq, first_row, rows):
    pos = first_row + lax.broadcasted_iota(jnp.int32, (rows, 1), 0)
    limit = pos + 1
    for piece in range(2):
        begin = starts[seq, piece]
        inside = (pos >= begin) & (pos < begin + PIECE)
        limit = jnp.maximum(limit, jnp.where(inside, begin + PIECE, 0))
    return limit


def key_span(first_row, rows):
    return min(L, first_row + rows + PIECE)


def weights_of(q, k, limit):
    bent = jnp.tanh(dot_nt(q, k) * (1.0 / CAP))
    seen = lax.broadcasted_iota(jnp.int32, (1, k.shape[0]), 1) < limit
    w = jnp.where(seen, jnp.exp(CAP * bent), 0.0)
    return w * pl.reciprocal(jnp.sum(w, axis=-1, keepdims=True)), bent


def attend_kernel(
    heads, kvs, starts, h1_hbm, w_hbm, cos_hbm, sin_hbm, q_hbm, k_hbm, v_hbm, o_hbm,
    h1, w, cos, sin, q_out, k_out, v_out, o_out, load, h1_load, store, o_store,
):
    tokens = h1.shape[0]
    fan = heads // kvs
    block = 256
    pairs = ((w_hbm, w), (cos_hbm, cos), (sin_hbm, sin))
    loads = [pltpu.make_async_copy(a, b, load.at[j]) for j, (a, b) in enumerate(pairs)]
    outs = ((q_out, q_hbm), (k_out, k_hbm), (v_out, v_hbm))
    stores = [pltpu.make_async_copy(a, b, store.at[j]) for j, (a, b) in enumerate(outs)]

    def rows_of(b):
        return pl.ds(pl.multiple_of(b * block, block), block)

    def h1_copy(b):
        return pltpu.make_async_copy(h1_hbm.at[rows_of(b)], h1.at[rows_of(b)], h1_load.at[b])

    def o_copy(b):
        return pltpu.make_async_copy(o_out.at[rows_of(b)], o_hbm.at[rows_of(b)], o_store.at[b])

    for c in loads:
        c.start()
    for b in range(tokens // block):
        h1_copy(b).start()
    for c in loads:
        c.wait()

    def project(b):
        h1_copy(b).wait()
        r = rows_of(b)
        at = pl.ds(pl.multiple_of(lax.rem(b * block, L), block), block)
        c, s = cos[at, :], sin[at, :]
        x = h1[r, :]
        for h in range(heads):
            u = dot_nn(x, w[:, h * HD : (h + 1) * HD])
            q_out[h, r, :] = (turn(u, c, s) * (HD**-0.5)).astype(BF16)
        for g in range(kvs):
            u = dot_nn(x, w[:, (heads + g) * HD : (heads + g + 1) * HD])
            k_out[g, r, :] = turn(u, c, s).astype(BF16)
            u = dot_nn(x, w[:, (heads + kvs + g) * HD : (heads + kvs + g + 1) * HD])
            v_out[g, r, :] = u.astype(BF16)

    loop(tokens // block, project)
    for c in stores:
        c.start()
    for seq in range(tokens // L):
        base = seq * L
        for row in range(0, L, block):
            span = key_span(row, block)
            limit = row_limit(starts, seq, row, block)
            for h in range(heads):
                q = q_out[h, base + row : base + row + block, :]
                p, _ = weights_of(q, k_out[h // fan, base : base + span, :], limit)
                o = dot_nn(p.astype(BF16), v_out[h // fan, base : base + span, :])
                o_out[base + row : base + row + block, h * HD : (h + 1) * HD] = o.astype(BF16)
            o_copy((base + row) // block).start()
    for c in stores:
        c.wait()
    for b in range(tokens // block):
        o_copy(b).wait()


def attend(heads, kvs, starts, h1, w, cos, sin):
    tokens = h1.shape[0]
    outs = [(heads, tokens, HD), (kvs, tokens, HD), (kvs, tokens, HD), (tokens, heads * HD)]
    sem = pltpu.SemaphoreType.DMA
    return pl.pallas_call(
        functools.partial(attend_kernel, heads, kvs),
        out_shape=[jax.ShapeDtypeStruct(o, BF16) for o in outs],
        in_specs=[SM, ANY, ANY, ANY, ANY],
        out_specs=[ANY] * 4,
        scratch_shapes=[pltpu.VMEM(a.shape, a.dtype) for a in (h1, w, cos, sin)]
        + [pltpu.VMEM(o, BF16) for o in outs]
        + [sem((3,)), sem((tokens // 256,)), sem((3,)), sem((tokens // 256,))],
        compiler_params=pltpu.CompilerParams(vmem_limit_bytes=62 << 20),
        cost_estimate=cost(20 << 30, 20 << 20),
        name="attend",
    )(starts, h1, w, cos, sin)


def attend_back_kernel(heads, kvs, block, starts, q_in, k_in, v_in, do_in, cos, sin, out, dk, dv):
    tokens = q_in.shape[1]
    fan = heads // kvs
    for seq in range(tokens // L):
        base = seq * L
        for g in range(kvs):
            dk[...] = jnp.zeros_like(dk)
            dv[...] = jnp.zeros_like(dv)
            for row in range(0, L, block):
                span = key_span(row, block)
                limit = row_limit(starts, seq, row, block)
                k = k_in[g, base : base + span, :]
                v = v_in[g, base : base + span, :]
                at = slice(base + row, base + row + block)
                for h in range(g * fan, (g + 1) * fan):
                    q = q_in[h, at, :]
                    do = do_in[at, h * HD : (h + 1) * HD]
                    p, bent = weights_of(q, k, limit)
                    dp = dot_nt(do, v)
                    delta = jnp.sum(p * dp, axis=-1, keepdims=True)
                    ds = (p * (dp - delta) * (1.0 - bent * bent)).astype(BF16)
                    dq = dot_nn(ds, k)
                    c, s = cos[row : row + block, :], sin[row : row + block, :]
                    out[at, h * HD : (h + 1) * HD] = (turn(dq, c, -s) * (HD**-0.5)).astype(BF16)
                    dk[:span, :] += dot_tn(ds, q)
                    dv[:span, :] += dot_tn(p.astype(BF16), do)

            def close(b, g=g, base=base):
                r = pl.ds(pl.multiple_of(b * block, block), block)
                to = pl.ds(pl.multiple_of(base + b * block, block), block)
                back = turn(dk[r, :], cos[r, :], -sin[r, :])
                out[to, (heads + g) * HD : (heads + g + 1) * HD] = back.astype(BF16)
                left = (heads + kvs + g) * HD
                out[to, left : left + HD] = dv[r, :].astype(BF16)

            loop(L // block, close)


def attend_back(heads, kvs, starts, q, k, v, do, cos, sin):
    tokens = q.shape[1]
    return pl.pallas_call(
        functools.partial(attend_back_kernel, heads, kvs, 256),
        out_shape=jax.ShapeDtypeStruct((tokens, (heads + 2 * kvs) * HD), BF16),
        in_specs=[SM, VM, VM, VM, VM, VM, VM],
        out_specs=VM,
        scratch_shapes=[pltpu.VMEM((L, HD), F32), pltpu.VMEM((L, HD), F32)],
        compiler_params=pltpu.CompilerParams(vmem_limit_bytes=48 << 20),
        cost_estimate=cost(30 << 30, 20 << 20),
        name="attend_back",
    )(starts, q, k, v, do, cos, sin)


def into_feed_kernel(
    n, x, gains, o_hbm, wo_hbm, wg_hbm, wu_hbm,
    attn_out, y_out, h3_full, hid_out, up_out, ge_out,
    o, wo, wg, wu, part, landed, mine, held, hid_s, up_s, ge_s,
    load, rs_send, rs_recv, ag_send, ag_recv, keep_sem, out_sem,
):
    i = lax.axis_index("tensor")
    rows, width = x.shape
    loads = [
        pltpu.make_async_copy(src, dst, load.at[k])
        for k, (src, dst) in enumerate(((o_hbm, o), (wo_hbm, wo), (wg_hbm, wg), (wu_hbm, wu)))
    ]
    for c in loads:
        c.start()
    line_barrier(i, n)
    loads[0].wait()
    loads[1].wait()

    def compute(t, block):
        def tile(k):
            at = pl.ds(pl.multiple_of(k * TILE, TILE), TILE)
            part[block, :, at] = dot_nt(o[block], wo[at, :]).astype(BF16)

        loop(width // TILE, tile)

    def own(t):
        def tile(k):
            at = pl.ds(pl.multiple_of(k * TILE, TILE), TILE)
            mine[:, at] = dot_nt(o[i], wo[at, :])

        loop(width // TILE, tile)

    done = scatter_line(i, n, part, landed, rs_send, rs_recv, compute, own)
    scale_two, scale_three = 1.0 + gains[1:2, :], 1.0 + gains[2:3, :]

    def chunk(c):
        r = pl.ds(c * ROWS, ROWS)
        attn = summed_rows(i, n, mine, landed, r)
        attn_out[r, :] = attn
        y = x[r, :].astype(F32) + attn * inverse_rms(attn) * scale_two
        y_out[r, :] = y
        held[i, r, :] = (y * inverse_rms(y) * scale_three).astype(BF16)

    loop(rows // ROWS, chunk)
    done()
    loads[2].wait()
    loads[3].wait()
    drain = Drain(
        (hid_out, up_out, ge_out), (hid_s, up_s, ge_s), out_sem, lambda s: block_at(i, n, s)
    )

    def forward(s, block):
        pltpu.make_async_copy(held.at[block], h3_full.at[block], keep_sem.at[s]).start()
        drain.free(s)
        slot = s % 2
        span = tile_of(wg.shape[1])

        def tile(k):
            at = pl.ds(pl.multiple_of(k * span, span), span)
            u = dot_nn(held[block], wg[:, at])
            up = dot_nn(held[block], wu[:, at])
            c = 0.7978845608028654
            th = jnp.tanh(c * (u + 0.044715 * (u * u * u)))
            half = 0.5 * (1.0 + th)
            gelu = u * half
            slope = half + 0.5 * u * (1.0 - th * th) * (c * (1.0 + 0.134145 * (u * u)))
            hid_s[slot, :, at] = (gelu * up).astype(BF16)
            up_s[slot, :, at] = (up * slope).astype(BF16)
            ge_s[slot, :, at] = gelu.astype(BF16)

        loop(wg.shape[1] // span, tile)
        drain.start(s)

    gather_line(i, n, held, ag_send, ag_recv, forward)
    drain.finish(n)

    def finish(s):
        block = block_at(i, n, s)
        pltpu.make_async_copy(held.at[block], h3_full.at[block], keep_sem.at[s]).wait()

    loop(n, finish)


def into_feed(n, x, gains, o, wo, wg, wu):
    rows, width = x.shape
    wide = wg.shape[1]
    blocks = lambda w: jax.ShapeDtypeStruct((n, rows, w), BF16)
    mine = jax.ShapeDtypeStruct((rows, width), F32)
    return pl.pallas_call(
        functools.partial(into_feed_kernel, n),
        out_shape=[mine, mine, blocks(width), blocks(wide), blocks(wide), blocks(wide)],
        in_specs=[VM, VM, ANY, ANY, ANY, ANY],
        out_specs=[VM, VM, ANY, ANY, ANY, ANY],
        scratch_shapes=[
            pltpu.VMEM(o.shape, BF16),
            pltpu.VMEM(wo.shape, BF16),
            pltpu.VMEM(wg.shape, BF16),
            pltpu.VMEM(wu.shape, BF16),
            pltpu.VMEM((n, rows, width), BF16),
            pltpu.VMEM((n + 1, rows, width), BF16),
            pltpu.VMEM((rows, width), F32),
            pltpu.VMEM((n, rows, width), BF16),
        ]
        + [pltpu.VMEM((2, rows, wide), BF16)] * 3
        + [pltpu.SemaphoreType.DMA((4,))]
        + line_scratch(n) * 2
        + [pltpu.SemaphoreType.DMA((n,)), pltpu.SemaphoreType.DMA((3, 2))],
        compiler_params=params(2, 62),
        cost_estimate=cost(0, 600 << 20),
        name="into_feed",
    )(x, gains, o, wo, wg, wu)


def turn_feed_kernel(
    n, y, dout, gains, hid_hbm, wd_hbm, up_hbm, ge_hbm,
    layer_out, gain_out, df_full, dgate_out, dup_out,
    wd, hid_s, part, landed, mine, held, up_s, ge_s, dg_s, du_s, fold,
    load, feed_sem, rs_send, rs_recv, ag_send, ag_recv, keep_sem, back_sem, out_sem,
):
    i = lax.axis_index("tensor")
    rows, width = y.shape
    whole = pltpu.make_async_copy(wd_hbm, wd, load.at[0])
    whole.start()
    feed = Feed((hid_hbm,), (hid_s,), feed_sem, lambda s: block_at(i, n, n - 1 - s))
    feed.start(jnp.int32(0))
    line_barrier(i, n)
    whole.wait()

    def compute(t, block):
        feed.advance(t, n)
        slot = t % 2

        def tile(k):
            at = pl.ds(pl.multiple_of(k * TILE, TILE), TILE)
            part[block, :, at] = dot_nt(hid_s[slot], wd[at, :]).astype(BF16)

        loop(width // TILE, tile)

    def own(t):
        t = jnp.int32(t)
        feed.advance(t, n)
        slot = t % 2

        def tile(k):
            at = pl.ds(pl.multiple_of(k * TILE, TILE), TILE)
            mine[:, at] = dot_nt(hid_s[slot], wd[at, :])

        loop(width // TILE, tile)

    done = scatter_line(i, n, part, landed, rs_send, rs_recv, compute, own)
    scale = 1.0 + gains[3:4, :]
    fold[...] = jnp.zeros_like(fold)

    def chunk(c):
        r = pl.ds(c * ROWS, ROWS)
        f = summed_rows(i, n, mine, landed, r)
        g = dout[r, :].astype(F32)
        inv = inverse_rms(f)
        layer_out[r, :] = (y[r, :] + f * inv * scale).astype(BF16)
        held[i, r, :] = norm_back(g * scale, f, inv).astype(BF16)
        fold[...] += fold_rows(g * (f * inv))

    loop(rows // ROWS, chunk)
    gain_out[...] = jnp.sum(fold[...], axis=0, keepdims=True)
    done()
    sides = Feed((up_hbm, ge_hbm), (up_s, ge_s), back_sem, lambda s: block_at(i, n, s))
    drain = Drain((dgate_out, dup_out), (dg_s, du_s), out_sem, lambda s: block_at(i, n, s))
    sides.start(jnp.int32(0))

    def backward(s, block):
        pltpu.make_async_copy(held.at[block], df_full.at[block], keep_sem.at[s]).start()
        sides.advance(s, n)
        drain.free(s)
        slot = s % 2
        span = tile_of(wd.shape[1])

        def tile(k):
            at = pl.ds(pl.multiple_of(k * span, span), span)
            dhid = dot_nn(held[block], wd[:, at])
            dg_s[slot, :, at] = (dhid * up_s[slot, :, at].astype(F32)).astype(BF16)
            du_s[slot, :, at] = (dhid * ge_s[slot, :, at].astype(F32)).astype(BF16)

        loop(wd.shape[1] // span, tile)
        drain.start(s)

    gather_line(i, n, held, ag_send, ag_recv, backward)
    drain.finish(n)

    def finish(s):
        block = block_at(i, n, s)
        pltpu.make_async_copy(held.at[block], df_full.at[block], keep_sem.at[s]).wait()

    loop(n, finish)


def turn_feed(n, y, dout, gains, hid, wd, up, ge):
    rows, width = y.shape
    wide = wd.shape[1]
    blocks = lambda w: jax.ShapeDtypeStruct((n, rows, w), BF16)
    return pl.pallas_call(
        functools.partial(turn_feed_kernel, n),
        out_shape=[
            jax.ShapeDtypeStruct((rows, width), BF16),
            jax.ShapeDtypeStruct((1, width), F32),
            blocks(width),
            blocks(wide),
            blocks(wide),
        ],
        in_specs=[VM, VM, VM, ANY, ANY, ANY, ANY],
        out_specs=[VM, VM, ANY, ANY, ANY],
        scratch_shapes=[
            pltpu.VMEM(wd.shape, BF16),
            pltpu.VMEM((2, rows, wide), BF16),
            pltpu.VMEM((n, rows, width), BF16),
            pltpu.VMEM((n + 1, rows, width), BF16),
            pltpu.VMEM((rows, width), F32),
            pltpu.VMEM((n, rows, width), BF16),
        ]
        + [pltpu.VMEM((2, rows, wide), BF16)] * 4
        + [pltpu.VMEM((8, width), F32)]
        + [pltpu.SemaphoreType.DMA((1,)), pltpu.SemaphoreType.DMA((1, 2))]
        + line_scratch(n) * 2
        + [
            pltpu.SemaphoreType.DMA((n,)),
            pltpu.SemaphoreType.DMA((2, 2)),
            pltpu.SemaphoreType.DMA((2, 2)),
        ],
        compiler_params=params(3, 62),
        cost_estimate=cost(0, 600 << 20),
        name="turn_feed",
    )(y, dout, gains, hid, wd, up, ge)


def out_of_feed_kernel(
    n, y, attn, dout, gains, dgate_hbm, dup_hbm, wg_hbm, wu_hbm, wo_hbm,
    dy_out, gain_out, dattn_full, do_out,
    wg, wu, wo, dg_s, du_s, part, landed, mine, held, do_s, fold,
    load, feed_sem, rs_send, rs_recv, ag_send, ag_recv, keep_sem, out_sem,
):
    i = lax.axis_index("tensor")
    rows, width = y.shape
    loads = [
        pltpu.make_async_copy(src, dst, load.at[k])
        for k, (src, dst) in enumerate(((wg_hbm, wg), (wu_hbm, wu), (wo_hbm, wo)))
    ]
    for c in loads:
        c.start()
    feed = Feed((dgate_hbm, dup_hbm), (dg_s, du_s), feed_sem, lambda s: block_at(i, n, n - 1 - s))
    feed.start(jnp.int32(0))
    line_barrier(i, n)
    loads[0].wait()
    loads[1].wait()

    def product(slot, at):
        return dot_nt(dg_s[slot], wg[at, :]) + dot_nt(du_s[slot], wu[at, :])

    def compute(t, block):
        feed.advance(t, n)
        slot = t % 2

        def tile(k):
            at = pl.ds(pl.multiple_of(k * TILE, TILE), TILE)
            part[block, :, at] = product(slot, at).astype(BF16)

        loop(width // TILE, tile)

    def own(t):
        t = jnp.int32(t)
        feed.advance(t, n)
        slot = t % 2

        def tile(k):
            at = pl.ds(pl.multiple_of(k * TILE, TILE), TILE)
            mine[:, at] = product(slot, at)

        loop(width // TILE, tile)

    done = scatter_line(i, n, part, landed, rs_send, rs_recv, compute, own)
    scale_two, scale_three = 1.0 + gains[1:2, :], 1.0 + gains[2:3, :]
    fold[...] = jnp.zeros_like(fold)

    def chunk(c):
        r = pl.ds(c * ROWS, ROWS)
        dh3 = summed_rows(i, n, mine, landed, r)
        v = y[r, :]
        inv = inverse_rms(v)
        dy = dout[r, :].astype(F32) + norm_back(dh3 * scale_three, v, inv)
        dy_out[r, :] = dy
        fold[1] += fold_rows(dh3 * (v * inv))
        a = attn[r, :]
        inv = inverse_rms(a)
        held[i, r, :] = norm_back(dy * scale_two, a, inv).astype(BF16)
        fold[0] += fold_rows(dy * (a * inv))

    loop(rows // ROWS, chunk)
    gain_out[0:1, :] = jnp.sum(fold[0], axis=0, keepdims=True)
    gain_out[1:2, :] = jnp.sum(fold[1], axis=0, keepdims=True)
    done()
    loads[2].wait()
    drain = Drain((do_out,), (do_s,), out_sem, lambda s: block_at(i, n, s))

    def backward(s, block):
        pltpu.make_async_copy(held.at[block], dattn_full.at[block], keep_sem.at[s]).start()
        drain.free(s)
        do_s[s % 2] = dot_nn(held[block], wo[...]).astype(BF16)
        drain.start(s)

    gather_line(i, n, held, ag_send, ag_recv, backward)
    drain.finish(n)

    def finish(s):
        block = block_at(i, n, s)
        pltpu.make_async_copy(held.at[block], dattn_full.at[block], keep_sem.at[s]).wait()

    loop(n, finish)


def out_of_feed(n, y, attn, dout, gains, dgate, dup, wg, wu, wo):
    rows, width = y.shape
    wide = wg.shape[1]
    narrow = wo.shape[1]
    return pl.pallas_call(
        functools.partial(out_of_feed_kernel, n),
        out_shape=[
            jax.ShapeDtypeStruct((rows, width), F32),
            jax.ShapeDtypeStruct((2, width), F32),
            jax.ShapeDtypeStruct((n, rows, width), BF16),
            jax.ShapeDtypeStruct((n, rows, narrow), BF16),
        ],
        in_specs=[VM, VM, VM, VM, ANY, ANY, ANY, ANY, ANY],
        out_specs=[VM, VM, ANY, ANY],
        scratch_shapes=[
            pltpu.VMEM(wg.shape, BF16),
            pltpu.VMEM(wu.shape, BF16),
            pltpu.VMEM(wo.shape, BF16),
            pltpu.VMEM((2, rows, wide), BF16),
            pltpu.VMEM((2, rows, wide), BF16),
            pltpu.VMEM((n, rows, width), BF16),
            pltpu.VMEM((n + 1, rows, width), BF16),
            pltpu.VMEM((rows, width), F32),
            pltpu.VMEM((n, rows, width), BF16),
            pltpu.VMEM((2, rows, narrow), BF16),
            pltpu.VMEM((2, 8, width), F32),
        ]
        + [pltpu.SemaphoreType.DMA((3,)), pltpu.SemaphoreType.DMA((2, 2))]
        + line_scratch(n) * 2
        + [pltpu.SemaphoreType.DMA((n,)), pltpu.SemaphoreType.DMA((1, 2))],
        compiler_params=params(4, 62),
        cost_estimate=cost(0, 600 << 20),
        name="out_of_feed",
    )(y, attn, dout, gains, dgate, dup, wg, wu, wo)


class Slots:
    def __init__(self, arrays, pool, firsts, sems, view, width=None):
        self.arrays, self.pool, self.firsts, self.sems, self.view = arrays, pool, firsts, sems, view
        self.width = width or pool.shape[2]

    def copies(self, s, inward):
        for k, (array, first) in enumerate(zip(self.arrays, self.firsts)):
            slot = self.pool.at[first + s % 2, :, pl.ds(0, self.width)]
            block = self.view(array, s)
            pair = (block, slot) if inward else (slot, block)
            yield pltpu.make_async_copy(*pair, self.sems.at[k, s % 2])

    def fetch(self, s):
        for c in self.copies(s, True):
            c.start()

    def advance(self, s, count):
        for c in self.copies(s, True):
            c.wait()
        if s + 1 < count:
            self.fetch(s + 1)

    def free(self, s):
        if s >= 2:
            self.settle(s - 2)

    def settle(self, s):
        for c in self.copies(s, False):
            c.wait()

    def leave(self, s):
        for c in self.copies(s, False):
            c.start()

    def finish(self, count):
        for s in range(max(0, count - 2), count):
            self.settle(s)


def middle_kernel(
    n, x_hbm, dout_hbm, gains, o_hbm, wo_hbm, wg_hbm, wu_hbm, wd_hbm,
    layer_out, dy_out, gain_out, h3_t, hid_out, up_out, ge_out, df_t, dgate_out, dup_out,
    dattn_t, do_out, dattn_own,
    xs, dout, wo, wg, wu, wd, part, landed, held, y, attn, pool, fold, flip,
    load, rs_send, rs_recv, ag_send, ag_recv, flip_sem, in_sem, out_sem, last_sem,
    wu_send, wu_recv, wu_local, wd_send, wd_recv, wd_local,
):
    i = lax.axis_index("tensor")
    rows, width = xs.shape
    piece = rows // 2
    narrow = wo_hbm.shape[1]
    pairs = ((wo_hbm, wo), (x_hbm, xs), (wg_hbm, wg), (dout_hbm, dout))
    loads = [pltpu.make_async_copy(a, b, load.at[k]) for k, (a, b) in enumerate(pairs)]
    for c in loads:
        c.start()
    up_spread = Spread(wu_hbm, wu, wu_send, wu_recv, wu_local)
    down_spread = Spread(wd_hbm, wd, wd_send, wd_recv, wd_local)
    line_barrier(i, n, up_spread.peers())
    up_spread.begin()
    loads[0].wait()
    wide = wd.shape[1]
    over, across = min(768, wide_tile(width)), min(768, wide_tile(wide))
    scale_two, scale_three, scale_four = (1.0 + gains[k : k + 1, :] for k in (1, 2, 3))
    fold[...] = jnp.zeros_like(fold)

    def tiles(total, size, body):
        loop(total // size, lambda k: body(pl.ds(pl.multiple_of(k * size, size), size)))

    def place(c):
        return pl.ds(c * piece, piece)

    def forward_view(c):
        return lambda array, s: array.at[block_at(i, n, s), place(c)]

    def backward_view(c):
        return lambda array, s: array.at[block_at(i, n, n - 1 - s), place(c)]

    class Sum:
        def __init__(self, which, c, product, feed=None):
            at = 2 * which + c
            self.c, self.feed = c, feed
            self.part, self.landed = part.at[c], landed.at[c]

            def compute(t, block):
                if feed:
                    feed.advance(t, n)

                def tile(at):
                    self.part[block, :, at] = product(t, block, at).astype(BF16)

                tiles(width, over, tile)

            self.compute = compute
            self.step, self.land, self.done = scatter_steps(
                i, n, self.part, self.landed, rs_send.at[at], rs_recv.at[at], compute
            )

        def start(self):
            if self.feed:
                self.feed.fetch(0)
            self.step(0)

        def own(self):
            self.compute(n - 1, i)

        def rows(self, r):
            return summed_rows(i, n, self.part.at[i], self.landed, r)

    class Gather:
        def __init__(self, which, c, full, compute, drained):
            at = 2 * which + c
            self.c, self.full, self.compute, self.drained = c, full, compute, drained
            self.pass_on, self.sent = gather_steps(i, n, held.at[c], ag_send.at[at], ag_recv.at[at])

        def use(self, s):
            block = block_at(i, n, s)
            self.compute(s, block)
            column = block * rows + self.c * piece
            flip_rows(held.at[self.c, block], self.full, column, flip, flip_sem, True)
            flip_end(self.full, flip, flip_sem)

        def finish(self):
            self.use(n - 1)
            self.sent()
            self.drained(n)

    def chunks(c, body):
        strip = strip_of(piece)

        def one(k):
            body(pl.ds(k * strip, strip), pl.ds(c * piece + k * strip, strip))

        loop(piece // strip, one)


    def out_product(t, block, at):
        return dot_nt(pool[8 + t % 2, :, pl.ds(0, narrow)], wo[at, :])

    def down_product(t, block, at):
        return dot_nt(pool[6 + t % 2], wd[at, :])

    def in_product(t, block, at):
        return dot_nt(pool[6 + t % 2], wg[at, :]) + dot_nt(pool[10 + t % 2], wu[at, :])

    def sums(c):
        heads = Slots((o_hbm,), pool, (8,), in_sem.at[3, c], backward_view(c), narrow)
        hid = Slots((hid_out,), pool, (6,), in_sem.at[0, c], backward_view(c))
        both = Slots((dgate_out, dup_out), pool, (6, 10), in_sem.at[1, c], backward_view(c))
        return (
            Sum(0, c, out_product, heads),
            Sum(1, c, down_product, hid),
            Sum(2, c, in_product, both),
        )


    def after_attention(c, total):
        def body(r, g):
            a = total.rows(r)
            attn[g, :] = a.astype(BF16)
            v = xs[g, :].astype(F32) + a * inverse_rms(a) * scale_two
            y[g, :] = v
            held[c, i, r, :] = (v * inverse_rms(v) * scale_three).astype(BF16)

        chunks(c, body)

    def after_down(c, total):
        def body(r, g):
            f = total.rows(r)
            d = dout[g, :].astype(F32)
            inv = inverse_rms(f)
            xs[g, :] = (y[g, :] + f * inv * scale_four).astype(BF16)
            held[c, i, r, :] = norm_back(d * scale_four, f, inv).astype(BF16)
            fold[2] += fold_rows(d * (f * inv))

        chunks(c, body)

    def after_in(c, total):
        def body(r, g):
            dh3 = total.rows(r)
            v = y[g, :]
            inv = inverse_rms(v)
            dy = dout[g, :].astype(F32) + norm_back(dh3 * scale_three, v, inv)
            y[g, :] = dy
            fold[1] += fold_rows(dh3 * (v * inv))
            a = attn[g, :].astype(F32)
            inv = inverse_rms(a)
            held[c, i, r, :] = norm_back(dy * scale_two, a, inv).astype(BF16)
            fold[0] += fold_rows(dy * (a * inv))

        chunks(c, body)


    def gathers(c):
        ahead = Slots((hid_out, up_out, ge_out), pool, (0, 2, 4), out_sem.at[0, c], forward_view(c))
        sides = Slots((up_out, ge_out), pool, (0, 2), in_sem.at[2, c], forward_view(c))
        back = Slots((dgate_out, dup_out), pool, (4, 8), out_sem.at[1, c], forward_view(c))

        def into(s, block):
            if s == 0 and c == 0:
                up_spread.end()
                loads[2].wait()
            ahead.free(s)
            k = s % 2

            def tile(at):
                u = dot_nn(held[c, block], wg[:, at])
                up = dot_nn(held[c, block], wu[:, at])
                b = 0.7978845608028654
                th = jnp.tanh(b * (u + 0.044715 * (u * u * u)))
                half = 0.5 * (1.0 + th)
                gelu = u * half
                slope = half + 0.5 * u * (1.0 - th * th) * (b * (1.0 + 0.134145 * (u * u)))
                pool[0 + k, :, at] = (gelu * up).astype(BF16)
                pool[2 + k, :, at] = (up * slope).astype(BF16)
                pool[4 + k, :, at] = gelu.astype(BF16)

            tiles(wide, across, tile)
            ahead.leave(s)

        def turned(s, block):
            if s == 0:
                sides.fetch(0)
            sides.advance(s, n)
            back.free(s)
            k = s % 2

            def tile(at):
                dhid = dot_nn(held[c, block], wd[:, at])
                pool[4 + k, :, at] = (dhid * pool[0 + k, :, at].astype(F32)).astype(BF16)
                pool[8 + k, :, at] = (dhid * pool[2 + k, :, at].astype(F32)).astype(BF16)

            tiles(wide, across, tile)
            back.leave(s)

        heads = Slots((do_out,), pool, (0,), out_sem.at[2, c], forward_view(c), narrow)

        def out(s, block):
            heads.free(s)
            pool[s % 2, :, pl.ds(0, narrow)] = dot_nn(held[c, block], wo[...]).astype(BF16)
            heads.leave(s)

        return (
            Gather(0, c, h3_t, into, ahead.finish),
            Gather(1, c, df_t, turned, back.finish),
            Gather(2, c, dattn_t, out, heads.finish),
        )

    sum_of = (sums(0), sums(1))
    gather_of = (gathers(0), gathers(1))
    own_rows = (after_attention, after_down, after_in)

    first_sum = sum_of[0][0]
    first_sum.start()
    for k in range(1, n - 1):
        first_sum.step(k)
    first_sum.own()
    up_spread.middle()
    loads[1].wait()
    loads[3].wait()
    before = None
    for turn in range(5):
        which, c = turn // 2, turn % 2
        total = sum_of[c][which]
        later = (turn + 1) // 2
        following = sum_of[1 - c][later] if later < 3 else None
        gather = gather_of[c][which]
        total.land()
        own_rows[which](c, total)
        gather.pass_on(0)
        total.done()
        if turn == 0:
            up_spread.turn()
            down_spread.begin()
        if before:
            before.finish()
        if turn == 1:
            down_spread.end()
        if turn == 4:
            pltpu.make_async_copy(xs, layer_out, last_sem.at[0]).start()
        if following:
            following.start()
        for k in range(1, n):
            gather.pass_on(k)
            gather.use(k - 1)
            if following and k < n - 1:
                following.step(k)
            elif following:
                following.own()
        if turn == 0:
            down_spread.middle()
            down_spread.turn()
        before = gather
    total = sum_of[1][2]
    total.land()
    own_rows[2](1, total)
    own_out = pltpu.make_async_copy(held.at[1, i], dattn_own, last_sem.at[2])
    own_out.start()
    total.done()
    before.finish()
    pltpu.make_async_copy(y, dy_out, last_sem.at[1]).start()
    for k in range(3):
        gain_out[k : k + 1, :] = jnp.sum(fold[k], axis=0, keepdims=True)
    pltpu.make_async_copy(xs, layer_out, last_sem.at[0]).wait()
    pltpu.make_async_copy(y, dy_out, last_sem.at[1]).wait()
    own_out.wait()


def middle(n, x, dout, gains, o, wo, wg, wu, wd):
    rows, width = x.shape
    wide = wg.shape[1]
    piece = rows // 2
    sem = pltpu.SemaphoreType.DMA
    blocks = lambda w: jax.ShapeDtypeStruct((n, rows, w), BF16)
    turned = jax.ShapeDtypeStruct((width, n * rows), BF16)
    return pl.pallas_call(
        functools.partial(middle_kernel, n),
        out_shape=[
            jax.ShapeDtypeStruct((rows, width), BF16),
            jax.ShapeDtypeStruct((rows, width), F32),
            jax.ShapeDtypeStruct((3, width), F32),
            turned, blocks(wide), blocks(wide), blocks(wide),
            turned, blocks(wide), blocks(wide), turned, blocks(wo.shape[1]),
            jax.ShapeDtypeStruct((piece, width), BF16),
        ],
        in_specs=[ANY, ANY, VM] + [ANY] * 5,
        out_specs=[ANY, ANY, VM] + [ANY] * 10,
        scratch_shapes=[
            pltpu.VMEM(x.shape, BF16),
            pltpu.VMEM(x.shape, BF16),
            pltpu.VMEM(wo.shape, BF16),
            pltpu.VMEM(wg.shape, BF16),
            pltpu.VMEM(wg.shape, BF16),
            pltpu.VMEM((width, wide), BF16),
            pltpu.VMEM((2, n, piece, width), BF16),
            pltpu.VMEM((2, n + 1, piece, width), BF16),
            pltpu.VMEM((2, n, piece, width), BF16),
            pltpu.VMEM(x.shape, F32),
            pltpu.VMEM(x.shape, BF16),
            pltpu.VMEM((12, piece, wide), BF16),
            pltpu.VMEM((3, 8, width), F32),
            pltpu.VMEM((2, 768, piece), BF16),
            sem((4,)), sem((6, 2, n)), sem((6, n + 1)), sem((6, 2, n)), sem((6, n)),
            sem((2,)), sem((4, 2, 2, 2)), sem((3, 2, 3, 2)), sem((3,)),
        ]
        + spread_scratch() * 2,
        compiler_params=pltpu.CompilerParams(
            collective_id=8, has_side_effects=True, vmem_limit_bytes=(127 << 20) // 2
        ),
        cost_estimate=cost(0, 1200 << 20),
        name="middle",
    )(x, dout, gains, o, wo, wg, wu, wd)


def last_kernel(
    n, x, dy, gains, d_hbm, w_hbm, in_grad, gain_out,
    d, w, part, landed, mine, fold, load, rs_send, rs_recv,
):
    i = lax.axis_index("tensor")
    rows, width = x.shape
    loads = [
        pltpu.make_async_copy(src, dst, load.at[k])
        for k, (src, dst) in enumerate(((d_hbm, d), (w_hbm, w)))
    ]
    for c in loads:
        c.start()
    line_barrier(i, n)
    for c in loads:
        c.wait()

    def compute(t, block):
        def tile(k):
            at = pl.ds(pl.multiple_of(k * TILE, TILE), TILE)
            part[block, :, at] = dot_nt(d[block], w[at, :]).astype(BF16)

        loop(width // TILE, tile)

    def own(t):
        def tile(k):
            at = pl.ds(pl.multiple_of(k * TILE, TILE), TILE)
            mine[:, at] = dot_nt(d[i], w[at, :])

        loop(width // TILE, tile)

    done = scatter_line(i, n, part, landed, rs_send, rs_recv, compute, own)
    scale = 1.0 + gains[0:1, :]
    fold[...] = jnp.zeros_like(fold)

    def chunk(c):
        r = pl.ds(c * ROWS, ROWS)
        dh1 = summed_rows(i, n, mine, landed, r)
        v = x[r, :].astype(F32)
        inv = inverse_rms(v)
        in_grad[r, :] = (dy[r, :] + norm_back(dh1 * scale, v, inv)).astype(BF16)
        fold[...] += fold_rows(dh1 * (v * inv))

    loop(rows // ROWS, chunk)
    gain_out[...] = jnp.sum(fold[...], axis=0, keepdims=True)
    done()


def last(n, x, dy, gains, d, w):
    rows, width = x.shape
    return pl.pallas_call(
        functools.partial(last_kernel, n),
        out_shape=[
            jax.ShapeDtypeStruct((rows, width), BF16),
            jax.ShapeDtypeStruct((1, width), F32),
        ],
        in_specs=[VM, VM, VM, ANY, ANY],
        out_specs=[VM, VM],
        scratch_shapes=[
            pltpu.VMEM(d.shape, BF16),
            pltpu.VMEM(w.shape, BF16),
            pltpu.VMEM((n, rows, width), BF16),
            pltpu.VMEM((n + 1, rows, width), BF16),
            pltpu.VMEM((rows, width), F32),
            pltpu.VMEM((8, width), F32),
            pltpu.SemaphoreType.DMA((2,)),
        ]
        + line_scratch(n),
        compiler_params=params(5, 48),
        cost_estimate=cost(0, 300 << 20),
        name="last",
    )(x, dy, gains, d, w)


class Reduce:
    def __init__(self, u, left, right, column, width, bufs, sems):
        me = lax.axis_index("dp")
        c, x, y = me % 2, (me // 2) % 2, me // 4
        self.me, self.set, self.third, self.fifth, self.width = me, u % 2, u % 3, u % 5, width
        self.left, self.right, self.column, self.next = left, right, column, None
        self.dx, self.dy, self.dc = 2 - 4 * x, 4 - 8 * y, 1 - 2 * c
        self.lefts, self.rights, self.pair, self.pair_in, self.sums, self.far_in, self.xy_in, self.own = bufs
        (
            self.left_sem, self.right_sem, self.pair_send, self.pair_recv,
            self.far_send, self.far_recv, self.xy_send, self.xy_recv,
        ) = sems
        self.rows = self.own.shape[1]
        self.cols = pl.ds(0, width)
        self.top = pl.ds(0, self.rows // 2)
        self.low = pl.ds(self.rows // 2, self.rows // 2)

    def owner(self, q):
        k = q % 4
        x = jnp.where(k <= 1, self.dx, 0)
        y = jnp.where(k % 2 == 0, self.dy, 0)
        return self.me + x + jnp.where(k == 3, 0, y) + jnp.where(q < 4, self.dc, 0)

    def left_copy(self, q):
        r = pl.ds(self.owner(q) * self.rows, self.rows)
        return pltpu.make_async_copy(self.left.at[r], self.lefts.at[q % AHEAD], self.left_sem.at[q % AHEAD])

    def right_copy(self):
        return pltpu.make_async_copy(
            self.right.at[:, pl.ds(self.column, self.width)],
            self.rights.at[self.set, :, self.cols],
            self.right_sem.at[self.set],
        )

    def remote(self, src, dst, send, recv, shift):
        return pltpu.make_async_remote_copy(
            src, dst, send, recv, device_id={"dp": self.me + shift}, device_id_type=MESH
        )

    def pair_copy(self, k):
        return self.remote(
            self.pair.at[self.set, k, :, self.cols],
            self.pair_in.at[self.set, k, :, self.cols],
            self.pair_send.at[self.set, k],
            self.pair_recv.at[self.set, k],
            self.dc,
        )

    def far_copy(self, way):
        return self.remote(
            self.sums.at[self.third, 0, (self.top, self.low)[way], self.cols],
            self.far_in.at[self.third, way, :, self.cols],
            self.far_send.at[self.third, way],
            self.far_recv.at[self.third, way],
            (self.dx, self.dy)[way],
        )

    def xy_copy(self, way, half):
        r = (self.top, self.low)[half]
        return self.remote(
            self.sums.at[self.third, 1 + way, r, self.cols],
            self.xy_in.at[self.fifth, way, r, self.cols],
            self.xy_send.at[self.third, way, half],
            self.xy_recv.at[self.fifth, way, half],
            (self.dx, self.dy)[way],
        )

    def product(self, q, put):
        self.left_copy(q).wait()
        later = q + AHEAD - 1
        if not isinstance(q, int) or later < 8:
            self.left_copy(later).start()
        elif self.next:
            self.next.left_copy(later - 8).start()
        tile = wide_tile(self.width)

        def one(t):
            at = pl.ds(pl.multiple_of(t * tile, tile), tile)
            put(at, dot_nn(self.lefts[q % AHEAD], self.rights[self.set, :, at]))

        loop(self.width // tile, one)

    def load(self, first=False):
        self.right_copy().start()
        if first:
            for q in range(AHEAD - 1):
                self.left_copy(q).start()

    def begin(self):
        self.right_copy().wait()

        def chunk(k):
            def put(at, value):
                self.pair[self.set, k, :, at] = value.astype(BF16)

            self.product(k, put)
            self.pair_copy(k).start()

        loop(4, chunk)

    def middle(self):
        for k in range(4):
            arrived = []

            def put(at, value, k=k):
                total = value + self.pair_in[self.set, k, :, at].astype(F32)
                if k < 3:
                    self.sums[self.third, k, :, at] = total.astype(BF16)
                else:
                    self.own[self.third, :, at] = total

            self.pair_copy(k).wait_recv()
            self.product(4 + k, put)
            if k == 0:
                self.far_copy(0).start()
                self.far_copy(1).start()
            elif k == 1:
                self.xy_copy(0, 0).start()
            elif k == 2:
                self.xy_copy(1, 1).start()
        for k in range(4):
            self.pair_copy(k).wait_send()

    def turn(self):
        self.far_copy(0).wait_recv()
        self.far_copy(1).wait_recv()
        half = self.rows // 2

        strip = strip_of(half)

        def chunk(c):
            for way, first in ((0, 0), (1, half)):
                r = pl.ds(first + c * strip, strip)
                f = pl.ds(c * strip, strip)
                k = 2 - way
                total = self.sums[self.third, k, r, self.cols].astype(F32)
                total += self.far_in[self.third, way, f, self.cols].astype(F32)
                self.sums[self.third, k, r, self.cols] = total.astype(BF16)

        loop(half // strip, chunk)
        self.xy_copy(0, 1).start()
        self.xy_copy(1, 0).start()

    def end(self, put):
        for way in range(2):
            for half in range(2):
                self.xy_copy(way, half).wait_recv()

        strip = strip_of(self.rows)

        def chunk(c):
            r = pl.ds(c * strip, strip)
            total = self.own[self.third, r, self.cols]
            for way in range(2):
                total += self.xy_in[self.fifth, way, r, self.cols].astype(F32)
            put(r, total)

        loop(self.rows // strip, chunk)
        for way in range(2):
            self.far_copy(way).wait_send()
            for half in range(2):
                self.xy_copy(way, half).wait_send()


def reduce_scratch(rows, tokens, widest):
    sem = pltpu.SemaphoreType.DMA
    bufs = [
        pltpu.VMEM((AHEAD, rows, tokens), BF16),
        pltpu.VMEM((2, tokens, widest), BF16),
        pltpu.VMEM((2, 4, rows, widest), BF16),
        pltpu.VMEM((2, 4, rows, widest), BF16),
        pltpu.VMEM((3, 3, rows, widest), BF16),
        pltpu.VMEM((3, 2, rows // 2, widest), BF16),
        pltpu.VMEM((5, 2, rows, widest), BF16),
        pltpu.VMEM((3, rows, widest), F32),
    ]
    sems = [
        sem((AHEAD,)), sem((2,)), sem((2, 4)), sem((2, 4)),
        sem((3, 2)), sem((3, 2)), sem((3, 2, 2)), sem((5, 2, 2)),
    ]
    return bufs, sems


def finish_kernel(
    n, m, heads, kvs, units_of, starts, x_hbm, dy_hbm, gains, own_hbm, do_hbm, q_hbm, k_hbm, v_hbm,
    cos_hbm, sin_hbm, wo_hbm, w_hbm, dattn_in, h1_t, df_t, h3_t, hid, dgate, dup, o_hbm,
    later_gains,
    in_grad, gain_out, out_qkv, out_down, out_gate, out_up, out_out, kv_out, dattn_t,
    x, dy, total_gains, line_gains, dp_gains, held, do, q, k, v, cos, sin, wo, w, d, dk, dv, part, landed, fold, flip, stage, kv_stage,
    load, do_load, ag_send, ag_recv, rs_send, rs_recv, flip_sem, out_sem, last_sem, kv_sem, kv_send,
    kv_recv, gain_send, gain_recv, *reduce_refs,
):
    i = lax.axis_index("tensor")
    rows, width = x.shape
    piece = rows // 2
    over = min(768, wide_tile(width))
    split = heads * HD
    pairs = (
        (own_hbm, held.at[i]), (wo_hbm, wo), (q_hbm, q), (k_hbm, k), (v_hbm, v), (cos_hbm, cos),
        (sin_hbm, sin), (w_hbm, w), (x_hbm, x), (dy_hbm, dy),
    )
    loads = [pltpu.make_async_copy(a, b, load.at[j]) for j, (a, b) in enumerate(pairs)]
    for c in loads:
        c.start()
    half_loads = [
        pltpu.make_async_copy(
            do_hbm.at[j, pl.ds(0, piece)], do.at[pl.ds(j * rows, piece)], do_load.at[j]
        )
        for j in range(n)
    ]
    for c in half_loads:
        c.start()

    lefts = dict(qkv=h1_t, down=df_t, gate=h3_t, up=h3_t, out=dattn_t)
    rights = dict(qkv=d, down=hid, gate=dgate, up=dup, out=o_hbm)
    outs = dict(qkv=out_qkv, down=out_down, gate=out_gate, up=out_up, out=out_out)
    units = [
        Reduce(u, lefts[name], rights[name], column, size, reduce_refs[:8], reduce_refs[8:])
        for u, (name, column, size) in enumerate(units_of)
    ]
    count = len(units)
    for a, b in zip(units, units[1:]):
        a.next = b
    units[0].load(True)
    me = units[0].me

    barrier = pltpu.get_barrier_semaphore()
    for j in range(1, m):
        peer = lax.rem(me + j, m)
        pl.semaphore_signal(barrier, 1, device_id={"dp": peer}, device_id_type=MESH)
    for j in range(1, n):
        peer = lax.rem(i + j, n)
        pl.semaphore_signal(barrier, 1, device_id={"tensor": peer}, device_id_type=MESH)
    pl.semaphore_wait(barrier, m + n - 2)


    pass_on, sent = gather_steps(i, n, held, ag_send, ag_recv)

    def use(s):
        block = block_at(i, n, s)
        at = pl.ds(pl.multiple_of(block * rows + piece, piece), piece)
        do[at, :] = dot_nn(held[block], wo[...]).astype(BF16)
        flip_rows(held.at[block], dattn_t, block * rows + piece, flip, flip_sem, s == 0)

    def attention():
        use(n - 1)
        flip_end(dattn_t, flip, flip_sem)
        sent()
        for c in half_loads + loads[2:7]:
            c.wait()
        attend_back_kernel(heads, kvs, 128, starts, q, k, v, do, cos, sin, d, dk, dv)


    def compute(t, block):
        mine = d[pl.ds(pl.multiple_of(block * rows, rows), rows), :]

        def tile(j):
            at = pl.ds(pl.multiple_of(j * over, over), over)
            part[block, :, at] = dot_nt(mine, w[at, :]).astype(BF16)

        loop(width // over, tile)

    step, land, done = scatter_steps(i, n, part, landed, rs_send, rs_recv, compute)

    def begin_line():
        for c in loads[7:]:
            c.wait()
        step(0)

    def input_grad():
        land()
        scale = 1.0 + gains[0:1, :]
        fold[...] = jnp.zeros_like(fold)
        strip = strip_of(rows)

        def chunk(c):
            r = pl.ds(c * strip, strip)
            dh1 = summed_rows(i, n, part.at[i], landed, r)
            a = x[r, :].astype(F32)
            inv = inverse_rms(a)
            x[r, :] = (dy[r, :] + norm_back(dh1 * scale, a, inv)).astype(BF16)
            fold[...] += fold_rows(dh1 * (a * inv))

        loop(rows // strip, chunk)
        total_gains[0:1, :] = jnp.sum(fold[...], axis=0, keepdims=True)
        total_gains[1:4, :] = later_gains[...]
        for j in range(1, n):
            gain_copy(0, j).start()
        pltpu.make_async_copy(x, in_grad, last_sem.at[0]).start()
        done()


    def gain_copy(way, j):
        peer = {"dp": lax.rem(me + j, m)} if way else {"tensor": lax.rem(i + j, n)}
        return pltpu.make_async_remote_copy(
            gain_out if way else total_gains,
            (dp_gains if way else line_gains).at[j - 1],
            gain_send.at[way, j],
            gain_recv.at[way, j],
            device_id=peer,
            device_id_type=MESH,
        )

    def gains_over_line():
        total = total_gains[...]
        for j in range(1, n):
            gain_copy(0, j).wait_recv()
            total += line_gains[j - 1]
        gain_out[...] = total
        for j in range(1, m):
            gain_copy(1, j).start()

    def gains_over_dp():
        total = gain_out[...]
        for j in range(1, m):
            gain_copy(1, j).wait_recv()
            total += dp_gains[j - 1]
        for j in range(1, n):
            gain_copy(0, j).wait_send()
        for j in range(1, m):
            gain_copy(1, j).wait_send()
        gain_out[...] = total


    def out_copy(u):
        name, column, size = units_of[u]
        return pltpu.make_async_copy(
            stage.at[u % 2, :, pl.ds(0, size)],
            outs[name].at[:, pl.ds(column, size)],
            out_sem.at[u % 2],
        )

    def kv_copy(j, owner, peer):
        return pltpu.make_async_remote_copy(
            kv_stage, kv_out.at[owner], kv_send.at[j], kv_recv.at[j],
            device_id={"tensor": peer}, device_id_type=MESH,
        )

    kv_own = pltpu.make_async_copy(kv_stage, kv_out.at[i], kv_sem.at[0])

    def finish(u):
        if u >= 2:
            out_copy(u - 2).wait()
        name, column, size = units_of[u]
        keys = name == "qkv" and column == split

        def put(r, total):
            stage[u % 2, r, pl.ds(0, size)] = total
            if keys:
                kv_stage[r, :] = total.astype(BF16)

        units[u].end(put)
        out_copy(u).start()
        if keys:
            for j in range(1, n):
                kv_copy(j, i, lax.rem(i + j, n)).start()
            kv_own.start()

    def passing(s):
        pass_on(s)
        use(s - 1)

    line = [[functools.partial(passing, s)] for s in range(1, n)]
    line[-1] += [attention]
    line += [[begin_line]]
    for t in range(1, n - 1):
        line += [[], [], [functools.partial(step, t)]]
    line += [[lambda: compute(n - 1, i), input_grad], [gains_over_line], [], [gains_over_dp]]

    loads[0].wait()
    loads[1].wait()
    pass_on(0)
    for u in range(max(count + 2, len(line))):
        if u < count:
            units[u].begin()
            if u + 1 < count:
                units[u + 1].load()
            units[u].middle()
        if 1 <= u <= count:
            units[u - 1].turn()
        for action in line[u] if u < len(line) else ():
            action()
        if 2 <= u < count + 2:
            finish(u - 2)
    for u in range(max(0, count - 2), count):
        out_copy(u).wait()
    pltpu.make_async_copy(x, in_grad, last_sem.at[0]).wait()
    kv_own.wait()
    for j in range(1, n):
        kv_copy(j, i, lax.rem(i + j, n)).wait_send()
        peer = lax.rem(i + n - j, n)
        kv_copy(j, peer, peer).wait_recv()


def pieces(name, width, most=768):
    count = next(c for c in range(1, width) if width % (c * 128) == 0 and width // c <= most)
    return [(name, k * (width // count), width // count) for k in range(count)]


def finish(
    n, m, heads, kvs, starts, x, dy, gains, own, do, q, k, v, cos, sin, wo, w, turned, rights, o, later
):
    rows, width = x.shape
    tokens = n * rows
    own_rows = width // m
    split, across = heads * HD, w.shape[1]
    down, gate, up = (pieces(s, r.shape[1]) for s, r in zip(("down", "gate", "up"), rights))
    early = (down + gate)[: n + 1]
    late = (down + gate)[n + 1 :] + up + pieces("out", o.shape[1])
    units = early + [("qkv", split, across - split), ("qkv", 0, split)] + late
    widest = max(size for _, _, size in units)
    bufs, sems = reduce_scratch(own_rows, tokens, widest)
    sem = pltpu.SemaphoreType.DMA
    shape = lambda a, b, t=F32: jax.ShapeDtypeStruct((a, b), t)
    return pl.pallas_call(
        functools.partial(finish_kernel, n, m, heads, kvs, units),
        out_shape=[shape(rows, width, BF16), shape(4, width), shape(own_rows, across)]
        + [shape(own_rows, r.shape[1]) for r in (*rights, o)]
        + [jax.ShapeDtypeStruct((n, own_rows, across - split), BF16), shape(width, tokens, BF16)],
        in_specs=[SM, ANY, ANY, VM] + [ANY] * 17 + [VM],
        out_specs=[ANY, VM] + [ANY] * 7,
        scratch_shapes=[
            pltpu.VMEM(x.shape, BF16),
            pltpu.VMEM(x.shape, F32),
            pltpu.VMEM((4, width), F32),
            pltpu.VMEM((n - 1, 4, width), F32),
            pltpu.VMEM((m - 1, 4, width), F32),
            pltpu.VMEM((n, rows // 2, width), BF16),
            pltpu.VMEM((tokens, split), BF16),
            pltpu.VMEM(q.shape, BF16),
            pltpu.VMEM(k.shape, BF16),
            pltpu.VMEM(v.shape, BF16),
            pltpu.VMEM(cos.shape, F32),
            pltpu.VMEM(sin.shape, F32),
            pltpu.VMEM(wo.shape, BF16),
            pltpu.VMEM(w.shape, BF16),
            pltpu.VMEM((tokens, across), BF16),
            pltpu.VMEM((L, HD), F32),
            pltpu.VMEM((L, HD), F32),
            pltpu.VMEM((n, rows, width), BF16),
            pltpu.VMEM((n + 1, rows, width), BF16),
            pltpu.VMEM((8, width), F32),
            pltpu.VMEM((2, 768, rows // 2), BF16),
            pltpu.VMEM((2, own_rows, widest), F32),
            pltpu.VMEM((own_rows, across - split), BF16),
            sem((10,)), sem((n,)),
        ]
        + line_scratch(n) * 2
        + [sem((2,)), sem((2,)), sem((1,)), sem((1,)), sem((n,)), sem((n,)), sem((2, m)), sem((2, m))]
        + bufs
        + sems,
        input_output_aliases={13: 8},
        compiler_params=pltpu.CompilerParams(
            collective_id=7, has_side_effects=True, vmem_limit_bytes=(127 << 20) // 2
        ),
        cost_estimate=cost(0, 600 << 20),
        name="finish",
    )(starts, x, dy, gains, own, do, q, k, v, cos, sin, wo, w, turned[3], *turned[:3], *rights, o, later)


def deliver_kernel(count, *refs):
    sources, qkv, kv_hbm = refs[:count], refs[count], refs[count + 1]
    targets, k_out, v_out = refs[count + 2 : 2 * count + 3], *refs[2 * count + 3 : 2 * count + 5]
    stages = refs[2 * count + 5 : 3 * count + 6]
    kv, k_s, v_s, load, store = refs[3 * count + 6 :]
    n, rows, across = kv.shape
    split = targets[-1].shape[1]
    sources = (*sources, qkv.at[:, pl.ds(0, split)])
    first = pltpu.make_async_copy(kv_hbm, kv, load.at[count + 1])
    first.start()
    loads = [pltpu.make_async_copy(a, b, load.at[j]) for j, (a, b) in enumerate(zip(sources, stages))]
    for c in loads:
        c.start()
    stores = [
        pltpu.make_async_copy(a, b, store.at[j])
        for j, (a, b) in enumerate(zip((*stages, k_s, v_s), (*targets, k_out, v_out)))
    ]
    first.wait()
    half = across // 2
    for j in range(n):
        k_s[:, j * half : (j + 1) * half] = kv[j, :, :half].astype(F32)
        v_s[:, j * half : (j + 1) * half] = kv[j, :, half:].astype(F32)
    stores[-2].start()
    stores[-1].start()
    for a, b in zip(loads, stores):
        a.wait()
        b.start()
    for c in stores:
        c.wait()


def deliver(split, sources, qkv, kv):
    n, rows, across = kv.shape
    shape = lambda a: jax.ShapeDtypeStruct(a.shape, a.dtype)
    wide = jax.ShapeDtypeStruct((rows, n * across // 2), F32)
    count = len(sources)
    return pl.pallas_call(
        functools.partial(deliver_kernel, count),
        out_shape=[shape(a) for a in sources] + [jax.ShapeDtypeStruct((rows, split), F32), wide, wide],
        in_specs=[ANY] * (count + 2),
        out_specs=[ANY] * (count + 3),
        scratch_shapes=[pltpu.VMEM(a.shape, a.dtype) for a in sources]
        + [
            pltpu.VMEM((rows, split), F32),
            pltpu.VMEM(kv.shape, BF16),
            pltpu.VMEM(wide.shape, F32),
            pltpu.VMEM(wide.shape, F32),
            pltpu.SemaphoreType.DMA((count + 2,)),
            pltpu.SemaphoreType.DMA((count + 3,)),
        ],
        compiler_params=pltpu.CompilerParams(vmem_limit_bytes=62 << 20),
        cost_estimate=cost(0, 40 << 20),
        name="deliver",
    )(*sources, qkv, kv)


def rope_tables():
    positions = np.arange(L, dtype=np.float32)
    exponent = np.arange(HD // 2, dtype=np.float32) * np.float32(-2.0 / HD)
    angles = positions[:, None] * np.exp(exponent * np.log(np.float32(10000.0)))[None, :]
    angles = angles.astype(np.float64)
    return jnp.asarray(np.cos(angles), F32), jnp.asarray(np.sin(angles), F32)


def weight_grad(left, right):
    return dot_tn(left, right).astype(BF16)


def scatter_rows(grad):
    return lax.psum_scatter(grad, "dp", scatter_dimension=0, tiled=True)


def body(
    n,
    m,
    layer_in,
    out_grad,
    piece_starts,
    attn_gain,
    attn_out_gain,
    feed_gain,
    feed_out_gain,
    query_weight,
    key_weight,
    value_weight,
    out_weight,
    gate_weight,
    up_weight,
    down_weight,
):
    heads = query_weight.shape[1] // HD
    fan = H // KV
    kvs = max(1, heads // fan)
    rank = lax.axis_index("tensor")
    kv_at = (rank * heads // fan) * HD
    rows, width = layer_in.shape
    tokens = n * rows

    gathered = gather_gains(m, jnp.stack([attn_gain, attn_out_gain, feed_gain, feed_out_gain]))
    gains = gathered.transpose(1, 0, 2).reshape(4, width).astype(F32)

    def collect(shard):
        return lax.all_gather(shard, "dp", axis=0, tiled=True)

    wqkv = collect(
        jnp.concatenate(
            [
                query_weight,
                lax.dynamic_slice_in_dim(key_weight, kv_at, kvs * HD, 1),
                lax.dynamic_slice_in_dim(value_weight, kv_at, kvs * HD, 1),
            ],
            axis=1,
        )
    )
    wo = collect(out_weight.T)
    cos, sin = rope_tables()

    spread = m == 8 and n * kvs == KV
    h1, wg, h1_t = first(n, m, layer_in, gains, gate_weight if spread else None)
    if not spread:
        wg = collect(gate_weight)
    h1_flat = h1.reshape(tokens, width)
    q, k, v, o = attend(heads, kvs, piece_starts, h1_flat, wqkv, cos, sin)
    o_blocks = o.reshape(n, rows, heads * HD)
    if spread:
        layer_out, dy, gain_later, h3_t, hid, _, _, df_t, dgate, dup, dattn_t, do, own = middle(
            n, layer_in, out_grad, gains, o_blocks, wo, wg, up_weight, down_weight.T
        )
    else:
        wu, wd = collect(up_weight), collect(down_weight.T)
        attn, y, h3, hid, up, ge = into_feed(n, layer_in, gains, o_blocks, wo, wg, wu)
        layer_out, gain_four, df, dgate, dup = turn_feed(n, y, out_grad, gains, hid, wd, up, ge)
    flat = lambda a: a.reshape(tokens, a.shape[-1])
    split = heads * HD
    if spread:
        in_grad, gain_grads, qkv_sum, down_sum, gate_sum, up_sum, out_sum, kv, _ = finish(
            n, m, heads, kvs, piece_starts, layer_in, dy, gains, own, do, q, k, v, cos, sin, wo, wqkv,
            (h1_t, df_t, h3_t, dattn_t), (flat(hid), flat(dgate), flat(dup)), o, gain_later,
        )
    else:
        tie = lax.optimization_barrier
        down_part = weight_grad(flat(df), flat(hid))
        gate_part = weight_grad(flat(h3), flat(dgate))
        up_part = weight_grad(flat(h3), flat(dup))
        dgate, dup, down_part, gate_part, up_part = tie((dgate, dup, down_part, gate_part, up_part))
        down_sum, gate_sum, up_sum = map(scatter_rows, (down_part, gate_part, up_part))
        dy, gain_mid, dattn, do = out_of_feed(n, y, attn, out_grad, gains, dgate, dup, wg, wu, wo)
        do, dattn, down_sum, gate_sum = tie((do, dattn, down_sum, gate_sum))
        out_part = weight_grad(flat(dattn), o)
        do, out_part = tie((do, out_part))
        d = attend_back(heads, kvs, piece_starts, q, k, v, flat(do), cos, sin)
        qkv_part = weight_grad(h1_flat, d)
        d, qkv_part, up_sum = tie((d, qkv_part, up_sum))
        out_sum, qkv_sum = scatter_rows(out_part), scatter_rows(qkv_part)
        in_grad, gain_one = last(n, layer_in, dy, gains, d.reshape(n, rows, -1), wqkv)
        gain_later = jnp.concatenate([gain_mid, gain_four], axis=0)

        own_rows = qkv_sum.shape[0]
        kv = qkv_sum[:, split:].reshape(own_rows, 2, kvs * HD).transpose(1, 0, 2)
        if n * kvs == KV:
            kv = lax.all_gather(kv, "tensor", axis=2, tiled=True)
        else:
            kv = lax.dynamic_update_slice_in_dim(jnp.zeros((2, own_rows, KV * HD), BF16), kv, kv_at, 2)
            kv = lax.psum(kv, "tensor")
    if spread:
        own_at = lax.axis_index("dp") * (width // m)
        gain_grads = lax.dynamic_slice_in_dim(gain_grads, own_at, width // m, 1)
    else:
        gain_grads = jnp.concatenate([gain_one, gain_later], axis=0)
        gain_grads = sum_gains(n, m, gain_grads.reshape(4, m, width // m).transpose(1, 0, 2))
    if spread:
        layer_out, in_grad, down_sum, gate_sum, up_sum, out_sum, q_sum, k_sum, v_sum = deliver(
            split, (layer_out, in_grad, down_sum, gate_sum, up_sum, out_sum), qkv_sum, kv
        )
    else:
        q_sum, k_sum, v_sum = qkv_sum[:, :split].astype(F32), kv[0].astype(F32), kv[1].astype(F32)
    return (
        layer_out,
        in_grad,
        q_sum,
        k_sum,
        v_sum,
        out_sum.astype(F32).T,
        gate_sum.astype(F32),
        up_sum.astype(F32),
        down_sum.astype(F32).T,
        gain_grads[0],
        gain_grads[1],
        gain_grads[2],
        gain_grads[3],
    )


def solution(mesh):
    in_specs = (
        P(("dp", "tensor"), None),
        P(("dp", "tensor"), None),
        P("dp", None),
        P("dp"),
        P("dp"),
        P("dp"),
        P("dp"),
        P("dp", "tensor"),
        P("dp", None),
        P("dp", None),
        P("tensor", "dp"),
        P("dp", "tensor"),
        P("dp", "tensor"),
        P("tensor", "dp"),
    )
    out_specs = (
        P(("dp", "tensor"), None),
        P(("dp", "tensor"), None),
        P("dp", "tensor"),
        P("dp", None),
        P("dp", None),
        P("tensor", "dp"),
        P("dp", "tensor"),
        P("dp", "tensor"),
        P("tensor", "dp"),
        P("dp"),
        P("dp"),
        P("dp"),
        P("dp"),
    )
    program = functools.partial(body, mesh.shape["tensor"], mesh.shape["dp"])
    return jax.shard_map(program, mesh=mesh, in_specs=in_specs, out_specs=out_specs, check_vma=False)
```

```python
import functools

import jax
import jax.numpy as jnp
import numpy as np
from jax import lax
from jax.experimental import pallas as pl
from jax.experimental.pallas import tpu as pltpu
from jax.sharding import PartitionSpec as P

H = 8
KV = 4
HD = 256
L = 1024
PIECE = 256

EPS = 1e-06
CAP = 50.0
F32 = jnp.float32
BF16 = jnp.bfloat16
MESH = pl.DeviceIdType.MESH
ANY = pl.BlockSpec(memory_space=pl.ANY)
VM = pl.BlockSpec(memory_space=pltpu.VMEM)
SM = pl.BlockSpec(memory_space=pltpu.SMEM)
ROWS = 16
TILE = 256
AHEAD = 4


def dot_nn(a, b):
    return lax.dot_general(a, b, (((1,), (0,)), ((), ())), preferred_element_type=F32)


def dot_nt(a, b):
    return lax.dot_general(a, b, (((1,), (1,)), ((), ())), preferred_element_type=F32)


def dot_tn(a, b):
    return lax.dot_general(a, b, (((0,), (0,)), ((), ())), preferred_element_type=F32)


def tile_of(width):
    return next(t for t in (256, 384, 128) if width % t == 0)


def strip_of(count):
    return next(t for t in (64, 48, 32, 16) if count % t == 0)


def wide_tile(width):
    return next(t for t in (1152, 1024, 768, 512, 384, 256, 128) if width % t == 0)


def loop(count, body):
    lax.fori_loop(0, count, lambda t, c: (body(t), c)[1], 0)


def block_at(i, n, s):
    m = jnp.minimum(i, n - 1 - i)
    near = i + jnp.where(s % 2 == 1, -((s + 1) // 2), s // 2)
    far = jnp.where(i * 2 < n, i + (s - m), i - (s - m))
    return jnp.where(s <= 2 * m, near, far)


def line_barrier(i, n, peers=()):
    barrier = pltpu.get_barrier_semaphore()

    @pl.when(i > 0)
    def _():
        pl.semaphore_signal(barrier, 1, device_id={"tensor": i - 1}, device_id_type=MESH)

    @pl.when(i < n - 1)
    def _():
        pl.semaphore_signal(barrier, 1, device_id={"tensor": i + 1}, device_id_type=MESH)

    for peer in peers:
        pl.semaphore_signal(barrier, 1, device_id={"dp": peer}, device_id_type=MESH)
    pl.semaphore_wait(barrier, len(peers) + jnp.minimum(i, 1) + jnp.minimum(n - 1 - i, 1))


def gather_steps(i, n, held, send, recv):
    def copy(block, way, s, to):
        return pltpu.make_async_remote_copy(
            held.at[block],
            held.at[block],
            send.at[way, s],
            recv.at[block],
            device_id={"tensor": to},
            device_id_type=MESH,
        )

    up, down = jnp.minimum(i + 1, n - 1), jnp.maximum(i - 1, 0)

    def pass_on(s):
        low, high = i - s, i + s

        @pl.when((s > 0) & (low >= 0))
        def _():
            copy(low, 0, s, up).wait_recv()

        @pl.when((low >= 0) & (i < n - 1))
        def _():
            copy(low, 0, s, up).start()

        @pl.when((s > 0) & (high < n))
        def _():
            copy(high, 1, s, down).wait_recv()

        @pl.when((high < n) & (i > 0))
        def _():
            copy(high, 1, s, down).start()

    def finish(s):
        low, high = i - s, i + s

        @pl.when((low >= 0) & (i < n - 1))
        def _():
            copy(low, 0, s, up).wait_send()

        @pl.when((high < n) & (i > 0))
        def _():
            copy(high, 1, s, down).wait_send()

    return pass_on, functools.partial(loop, n, finish)


def gather_line(i, n, held, send, recv, compute):
    pass_on, finish = gather_steps(i, n, held, send, recv)

    def step(s):
        pass_on(s)
        compute(s, block_at(i, n, s))

    loop(n, step)
    finish()


def scatter_steps(i, n, part, landed, send, recv, compute):
    rows = part.shape[1]

    def copy(block, way, t, to):
        slot = jnp.where(block == to, n, block) if way else block
        return pltpu.make_async_remote_copy(
            part.at[block],
            landed.at[slot],
            send.at[way, t],
            recv.at[slot],
            device_id={"tensor": to},
            device_id_type=MESH,
        )

    def arrived(slot):
        pltpu.make_async_remote_copy(
            landed.at[slot],
            landed.at[slot],
            send.at[0, 0],
            recv.at[slot],
            device_id={"tensor": i},
            device_id_type=MESH,
        ).wait_recv()

    def add(block):
        strip = strip_of(rows)

        def chunk(c):
            r = pl.ds(c * strip, strip)
            total = part[block, r, :].astype(F32) + landed[block, r, :].astype(F32)
            part[block, r, :] = total.astype(BF16)

        loop(rows // strip, chunk)

    up, down = jnp.minimum(i + 1, n - 1), jnp.maximum(i - 1, 0)

    def step(k):
        t = k + 1
        compute(k, block_at(i, n, n - t))
        above, below = i + n - t, i - n + t

        @pl.when((above < n) & (i > 0))
        def _():
            arrived(above)
            add(above)

        @pl.when(above < n)
        def _():
            copy(above, 0, t, up).start()

        @pl.when((below >= 0) & (i < n - 1))
        def _():
            arrived(below)
            add(below)

        @pl.when(below >= 0)
        def _():
            copy(below, 1, t, down).start()

    def land():
        @pl.when(i > 0)
        def _():
            arrived(i)

        @pl.when(i < n - 1)
        def _():
            arrived(jnp.int32(n))

    def finish(k):
        t = k + 1

        @pl.when(i + n - t < n)
        def _():
            copy(i + n - t, 0, t, up).wait_send()

        @pl.when(i - n + t >= 0)
        def _():
            copy(i - n + t, 1, t, down).wait_send()

    return step, land, functools.partial(loop, n - 1, finish)


def scatter_line(i, n, part, landed, send, recv, compute, own):
    step, land, finish = scatter_steps(i, n, part, landed, send, recv, compute)
    loop(n - 1, step)
    own(n - 1)
    land()
    return finish


def summed_rows(i, n, mine, landed, r):
    zero = jnp.zeros((), F32)
    low = jnp.where(i > 0, landed[i, r, :].astype(F32), zero)
    high = jnp.where(i < n - 1, landed[n, r, :].astype(F32), zero)
    return mine[r, :] + low + high


def inverse_rms(v):
    return lax.rsqrt(jnp.mean(v * v, axis=-1, keepdims=True) + EPS)


def norm_back(e, v, r):
    unit = v * r
    return r * (e - unit * jnp.mean(e * unit, axis=-1, keepdims=True))


def fold_rows(v):
    return v.reshape(-1, 8, v.shape[-1]).sum(axis=0)


class Feed:
    def __init__(self, sources, slots, sems, which):
        self.sources, self.slots, self.sems, self.which = sources, slots, sems, which

    def copies(self, s):
        return [
            pltpu.make_async_copy(src.at[self.which(s)], slot.at[s % 2], self.sems.at[k, s % 2])
            for k, (src, slot) in enumerate(zip(self.sources, self.slots))
        ]

    def start(self, s):
        for c in self.copies(s):
            c.start()

    def wait(self, s):
        for c in self.copies(s):
            c.wait()

    def advance(self, s, count):
        self.wait(s)

        @pl.when(s + 1 < count)
        def _():
            self.start(s + 1)


class Drain:
    def __init__(self, targets, slots, sems, which):
        self.targets, self.slots, self.sems, self.which = targets, slots, sems, which

    def copies(self, s):
        return [
            pltpu.make_async_copy(slot.at[s % 2], dst.at[self.which(s)], self.sems.at[k, s % 2])
            for k, (dst, slot) in enumerate(zip(self.targets, self.slots))
        ]

    def free(self, s):
        @pl.when(s >= 2)
        def _():
            for c in self.copies(s - 2):
                c.wait()

    def start(self, s):
        for c in self.copies(s):
            c.start()

    def finish(self, count):
        for s in range(max(0, count - 2), count):
            for c in self.copies(jnp.int32(s)):
                c.wait()


class Spread:
    def __init__(self, own, full, send, recv, local):
        me = lax.axis_index("dp")
        c, x, y = me % 2, (me // 2) % 2, me // 4
        self.own, self.full, self.send, self.recv, self.local = own, full, send, recv, local
        self.me = me
        self.core = me + 1 - 2 * c
        self.x = me + 2 - 4 * x
        self.y = me + 4 - 8 * y
        self.far = self.x + 4 - 8 * y
        self.flip = 1 - 2 * c

    def peers(self):
        return (self.core, self.x, self.y)

    def view(self, owner, part):
        count = self.own.shape[0]
        first, size = ((0, count), (0, count // 2), (count // 2, count // 2))[part]
        return self.full.at[pl.ds(pl.multiple_of(owner * count + first, ROWS), size)]

    def copy(self, k, source, owner, part, to):
        return pltpu.make_async_remote_copy(
            self.own if source is None else self.view(source, part),
            self.view(owner, part),
            self.send.at[k],
            self.recv.at[k],
            device_id={"dp": to},
            device_id_type=MESH,
        )

    def sends(self):
        return (
            (0, None, self.me, 0, self.core),
            (1, None, self.me, 0, self.x),
            (2, None, self.me, 0, self.y),
            (3, self.x, self.x, 1, self.y),
            (4, self.y, self.y, 2, self.x),
            (5, self.x, self.x, 0, self.core),
            (6, self.y, self.y, 0, self.core),
            (7, self.far, self.far, 0, self.core),
        )

    def start(self, *which):
        for k in which:
            self.copy(*self.sends()[k]).start()

    def arrive(self, k):
        owner, part = {
            0: (self.core, 0),
            1: (self.x, 0),
            2: (self.y, 0),
            3: (self.far, 1),
            4: (self.far, 2),
            5: (self.x + self.flip, 0),
            6: (self.y + self.flip, 0),
            7: (self.far + self.flip, 0),
        }[k]
        self.copy(k, owner, owner, part, self.core).wait_recv()

    def keep(self):
        return pltpu.make_async_copy(self.own, self.view(self.me, 0), self.local.at[0])

    def begin(self):
        self.keep().start()
        self.start(1, 2, 0)

    def middle(self):
        self.arrive(1)
        self.arrive(2)
        self.start(3, 4, 5, 6)

    def turn(self):
        self.arrive(3)
        self.arrive(4)
        self.start(7)

    def end(self):
        for k in (0, 5, 6, 7):
            self.arrive(k)
        self.keep().wait()
        for k in range(8):
            self.copy(*self.sends()[k]).wait_send()


def spread_scratch():
    return [pltpu.SemaphoreType.DMA((8,)), pltpu.SemaphoreType.DMA((8,)), pltpu.SemaphoreType.DMA((1,))]


def line_scratch(n):
    return [pltpu.SemaphoreType.DMA((2, n)), pltpu.SemaphoreType.DMA((n + 1,))]


def params(cid, mib):
    return pltpu.CompilerParams(
        collective_id=cid, has_side_effects=True, vmem_limit_bytes=mib << 20
    )


def cost(flops, moved):
    return pl.CostEstimate(flops=flops, bytes_accessed=moved, transcendentals=0)


def gains_kernel(m, mine, out, send, recv):
    me = lax.axis_index("dp")
    barrier = pltpu.get_barrier_semaphore()
    for k in range(1, m):
        pl.semaphore_signal(
            barrier, 1, device_id={"dp": lax.rem(me + k, m)}, device_id_type=MESH
        )
    pl.semaphore_wait(barrier, m - 1)

    def copy(owner, k):
        return pltpu.make_async_remote_copy(
            mine,
            out.at[owner],
            send.at[k],
            recv.at[k],
            device_id={"dp": lax.rem(me + k, m)},
            device_id_type=MESH,
        )

    for k in range(1, m):
        copy(me, k).start()
    out[me] = mine[...]
    for k in range(1, m):
        copy(lax.rem(me + m - k, m), k).wait_recv()
    for k in range(1, m):
        copy(me, k).wait_send()


def gather_gains(m, mine):
    return pl.pallas_call(
        functools.partial(gains_kernel, m),
        out_shape=jax.ShapeDtypeStruct((m,) + mine.shape, mine.dtype),
        in_specs=[VM],
        out_specs=VM,
        scratch_shapes=[pltpu.SemaphoreType.DMA((m,)), pltpu.SemaphoreType.DMA((m,))],
        compiler_params=params(0, 16),
        name="gains",
    )(mine)


def sum_gains_kernel(n, m, mine, out, landed, total, across, send, recv, send_two, recv_two):
    me, i = lax.axis_index("dp"), lax.axis_index("tensor")
    barrier = pltpu.get_barrier_semaphore()
    dp_peer = lambda k: {"dp": lax.rem(me + k, m)}
    line_peer = lambda k: {"tensor": lax.rem(i + k, n)}
    for k in range(1, m):
        pl.semaphore_signal(barrier, 1, device_id=dp_peer(k), device_id_type=MESH)
    for k in range(1, n):
        pl.semaphore_signal(barrier, 1, device_id=line_peer(k), device_id_type=MESH)
    pl.semaphore_wait(barrier, m + n - 2)

    def to_owner(k):
        return pltpu.make_async_remote_copy(
            mine.at[lax.rem(me + k, m)], landed.at[k], send.at[k], recv.at[k],
            device_id=dp_peer(k), device_id_type=MESH,
        )

    def along(k):
        return pltpu.make_async_remote_copy(
            total, across.at[k], send_two.at[k], recv_two.at[k],
            device_id=line_peer(k), device_id_type=MESH,
        )

    for k in range(1, m):
        to_owner(k).start()
    here = mine[me]
    for k in range(1, m):
        to_owner(k).wait_recv()
        here = here + landed[k]
    total[...] = here
    for k in range(1, n):
        along(k).start()
    for k in range(1, n):
        along(k).wait_recv()
        here = here + across[k]
    out[...] = here
    for k in range(1, m):
        to_owner(k).wait_send()
    for k in range(1, n):
        along(k).wait_send()


def sum_gains(n, m, mine):
    shape = mine.shape[1:]
    return pl.pallas_call(
        functools.partial(sum_gains_kernel, n, m),
        out_shape=jax.ShapeDtypeStruct(shape, F32),
        in_specs=[VM],
        out_specs=VM,
        scratch_shapes=[
            pltpu.VMEM((m,) + shape, F32),
            pltpu.VMEM(shape, F32),
            pltpu.VMEM((n,) + shape, F32),
        ]
        + [pltpu.SemaphoreType.DMA((m,))] * 2
        + [pltpu.SemaphoreType.DMA((n,))] * 2,
        compiler_params=params(6, 16),
        name="sum_gains",
    )(mine)


def first_kernel(n, spread, x, gains, *refs):
    i = lax.axis_index("tensor")
    rows = x.shape[0]
    if spread:
        shard, full, gathered, turned, held, send, recv, out_sem, turn, turn_sem, *sems = refs
        gather = Spread(shard, gathered, *sems)
        line_barrier(i, n, gather.peers())
        gather.begin()
    else:
        full, held, send, recv, out_sem = refs
        line_barrier(i, n)
    scale = 1.0 + gains[0:1, :]

    strip = strip_of(rows)

    def chunk(c):
        r = pl.ds(c * strip, strip)
        v = x[r, :].astype(F32)
        held[i, r, :] = (v * inverse_rms(v) * scale).astype(BF16)

    loop(rows // strip, chunk)

    def keep(s, block):
        pltpu.make_async_copy(held.at[block], full.at[block], out_sem.at[s]).start()
        if spread:
            flip_rows(held.at[block], turned, block * rows, turn, turn_sem, s == 0)
            pl.when(s == min(1, n - 1))(gather.middle)
            pl.when(s == min(2, n - 1))(gather.turn)

    gather_line(i, n, held, send, recv, keep)

    def finish(s):
        block = block_at(i, n, s)
        pltpu.make_async_copy(held.at[block], full.at[block], out_sem.at[s]).wait()

    loop(n, finish)
    if spread:
        flip_end(turned, turn, turn_sem)
        gather.end()


def flip_rows(block, target, column, stage, sem, fresh):
    rows, width = block.shape
    size = stage.shape[1]

    def copy(k):
        return pltpu.make_async_copy(
            stage.at[k % 2],
            target.at[pl.ds(k * size, size), pl.ds(pl.multiple_of(column, 128), rows)],
            sem.at[k % 2],
        )

    for k in range(width // size):
        if k >= 2:
            copy(k - 2).wait()
        elif fresh is False:
            copy(k).wait()
        elif fresh is not True:
            pl.when(jnp.logical_not(fresh))(lambda k=k: copy(k).wait())
        for j in range(size // 256):
            at = pl.ds(k * size + j * 256, 256)
            stage[k % 2, pl.ds(j * 256, 256), :] = block[:, at].T
        copy(k).start()


def flip_end(target, stage, sem):
    size, rows = stage.shape[1:]
    for k in range(2):
        pltpu.make_async_copy(
            stage.at[k], target.at[pl.ds(k * size, size), pl.ds(0, rows)], sem.at[k]
        ).wait()


def first(n, m, x, gains, shard):
    rows, width = x.shape
    spread = shard is not None
    outs = [jax.ShapeDtypeStruct((n, rows, width), BF16)]
    if spread:
        outs += [jax.ShapeDtypeStruct((m * shard.shape[0], shard.shape[1]), BF16)]
        outs += [jax.ShapeDtypeStruct((width, n * rows), BF16)]
        turn = [pltpu.VMEM((2, 768, rows), BF16), pltpu.SemaphoreType.DMA((2,))]
    out = pl.pallas_call(
        functools.partial(first_kernel, n, spread),
        out_shape=outs,
        in_specs=[VM, VM] + [ANY] * spread,
        out_specs=[ANY] * len(outs),
        scratch_shapes=[pltpu.VMEM((n, rows, width), BF16)]
        + line_scratch(n)
        + [pltpu.SemaphoreType.DMA((n,))]
        + (turn + spread_scratch() if spread else []),
        compiler_params=params(1, 62),
        cost_estimate=cost(0, 300 << 20),
        name="first",
    )(x, gains, *([shard] if spread else []))
    return out if spread else (out[0], None, None)


def turn(u, cos, sin):
    half = HD // 2
    a, b = u[:, :half], u[:, half:]
    return jnp.concatenate([a * cos - b * sin, b * cos + a * sin], axis=-1)


def row_limit(starts, seq, first_row, rows):
    pos = first_row + lax.broadcasted_iota(jnp.int32, (rows, 1), 0)
    limit = pos + 1
    for piece in range(2):
        begin = starts[seq, piece]
        inside = (pos >= begin) & (pos < begin + PIECE)
        limit = jnp.maximum(limit, jnp.where(inside, begin + PIECE, 0))
    return limit


def key_span(first_row, rows):
    return min(L, first_row + rows + PIECE)


def weights_of(q, k, limit):
    bent = jnp.tanh(dot_nt(q, k) * (1.0 / CAP))
    seen = lax.broadcasted_iota(jnp.int32, (1, k.shape[0]), 1) < limit
    w = jnp.where(seen, jnp.exp(CAP * bent), 0.0)
    return w * pl.reciprocal(jnp.sum(w, axis=-1, keepdims=True)), bent


def attend_kernel(
    heads, kvs, starts, h1_hbm, w_hbm, cos_hbm, sin_hbm, q_hbm, k_hbm, v_hbm, o_hbm,
    h1, w, cos, sin, q_out, k_out, v_out, o_out, load, h1_load, store, o_store,
):
    tokens = h1.shape[0]
    fan = heads // kvs
    block = 256
    pairs = ((w_hbm, w), (cos_hbm, cos), (sin_hbm, sin))
    loads = [pltpu.make_async_copy(a, b, load.at[j]) for j, (a, b) in enumerate(pairs)]
    outs = ((q_out, q_hbm), (k_out, k_hbm), (v_out, v_hbm))
    stores = [pltpu.make_async_copy(a, b, store.at[j]) for j, (a, b) in enumerate(outs)]

    def rows_of(b):
        return pl.ds(pl.multiple_of(b * block, block), block)

    def h1_copy(b):
        return pltpu.make_async_copy(h1_hbm.at[rows_of(b)], h1.at[rows_of(b)], h1_load.at[b])

    def o_copy(b):
        return pltpu.make_async_copy(o_out.at[rows_of(b)], o_hbm.at[rows_of(b)], o_store.at[b])

    for c in loads:
        c.start()
    for b in range(tokens // block):
        h1_copy(b).start()
    for c in loads:
        c.wait()

    def project(b):
        h1_copy(b).wait()
        r = rows_of(b)
        at = pl.ds(pl.multiple_of(lax.rem(b * block, L), block), block)
        c, s = cos[at, :], sin[at, :]
        x = h1[r, :]
        for h in range(heads):
            u = dot_nn(x, w[:, h * HD : (h + 1) * HD])
            q_out[h, r, :] = (turn(u, c, s) * (HD**-0.5)).astype(BF16)
        for g in range(kvs):
            u = dot_nn(x, w[:, (heads + g) * HD : (heads + g + 1) * HD])
            k_out[g, r, :] = turn(u, c, s).astype(BF16)
            u = dot_nn(x, w[:, (heads + kvs + g) * HD : (heads + kvs + g + 1) * HD])
            v_out[g, r, :] = u.astype(BF16)

    loop(tokens // block, project)
    for c in stores:
        c.start()
    for seq in range(tokens // L):
        base = seq * L
        for row in range(0, L, block):
            span = key_span(row, block)
            limit = row_limit(starts, seq, row, block)
            for h in range(heads):
                q = q_out[h, base + row : base + row + block, :]
                p, _ = weights_of(q, k_out[h // fan, base : base + span, :], limit)
                o = dot_nn(p.astype(BF16), v_out[h // fan, base : base + span, :])
                o_out[base + row : base + row + block, h * HD : (h + 1) * HD] = o.astype(BF16)
            o_copy((base + row) // block).start()
    for c in stores:
        c.wait()
    for b in range(tokens // block):
        o_copy(b).wait()


def attend(heads, kvs, starts, h1, w, cos, sin):
    tokens = h1.shape[0]
    outs = [(heads, tokens, HD), (kvs, tokens, HD), (kvs, tokens, HD), (tokens, heads * HD)]
    sem = pltpu.SemaphoreType.DMA
    return pl.pallas_call(
        functools.partial(attend_kernel, heads, kvs),
        out_shape=[jax.ShapeDtypeStruct(o, BF16) for o in outs],
        in_specs=[SM, ANY, ANY, ANY, ANY],
        out_specs=[ANY] * 4,
        scratch_shapes=[pltpu.VMEM(a.shape, a.dtype) for a in (h1, w, cos, sin)]
        + [pltpu.VMEM(o, BF16) for o in outs]
        + [sem((3,)), sem((tokens // 256,)), sem((3,)), sem((tokens // 256,))],
        compiler_params=pltpu.CompilerParams(vmem_limit_bytes=62 << 20),
        cost_estimate=cost(20 << 30, 20 << 20),
        name="attend",
    )(starts, h1, w, cos, sin)


def attend_back_kernel(heads, kvs, block, starts, q_in, k_in, v_in, do_in, cos, sin, out, dk, dv):
    tokens = q_in.shape[1]
    fan = heads // kvs
    for seq in range(tokens // L):
        base = seq * L
        for g in range(kvs):
            dk[...] = jnp.zeros_like(dk)
            dv[...] = jnp.zeros_like(dv)
            for row in range(0, L, block):
                span = key_span(row, block)
                limit = row_limit(starts, seq, row, block)
                k = k_in[g, base : base + span, :]
                v = v_in[g, base : base + span, :]
                at = slice(base + row, base + row + block)
                for h in range(g * fan, (g + 1) * fan):
                    q = q_in[h, at, :]
                    do = do_in[at, h * HD : (h + 1) * HD]
                    p, bent = weights_of(q, k, limit)
                    dp = dot_nt(do, v)
                    delta = jnp.sum(p * dp, axis=-1, keepdims=True)
                    ds = (p * (dp - delta) * (1.0 - bent * bent)).astype(BF16)
                    dq = dot_nn(ds, k)
                    c, s = cos[row : row + block, :], sin[row : row + block, :]
                    out[at, h * HD : (h + 1) * HD] = (turn(dq, c, -s) * (HD**-0.5)).astype(BF16)
                    dk[:span, :] += dot_tn(ds, q)
                    dv[:span, :] += dot_tn(p.astype(BF16), do)

            def close(b, g=g, base=base):
                r = pl.ds(pl.multiple_of(b * block, block), block)
                to = pl.ds(pl.multiple_of(base + b * block, block), block)
                back = turn(dk[r, :], cos[r, :], -sin[r, :])
                out[to, (heads + g) * HD : (heads + g + 1) * HD] = back.astype(BF16)
                left = (heads + kvs + g) * HD
                out[to, left : left + HD] = dv[r, :].astype(BF16)

            loop(L // block, close)


def attend_back(heads, kvs, starts, q, k, v, do, cos, sin):
    tokens = q.shape[1]
    return pl.pallas_call(
        functools.partial(attend_back_kernel, heads, kvs, 256),
        out_shape=jax.ShapeDtypeStruct((tokens, (heads + 2 * kvs) * HD), BF16),
        in_specs=[SM, VM, VM, VM, VM, VM, VM],
        out_specs=VM,
        scratch_shapes=[pltpu.VMEM((L, HD), F32), pltpu.VMEM((L, HD), F32)],
        compiler_params=pltpu.CompilerParams(vmem_limit_bytes=48 << 20),
        cost_estimate=cost(30 << 30, 20 << 20),
        name="attend_back",
    )(starts, q, k, v, do, cos, sin)


def into_feed_kernel(
    n, x, gains, o_hbm, wo_hbm, wg_hbm, wu_hbm,
    attn_out, y_out, h3_full, hid_out, up_out, ge_out,
    o, wo, wg, wu, part, landed, mine, held, hid_s, up_s, ge_s,
    load, rs_send, rs_recv, ag_send, ag_recv, keep_sem, out_sem,
):
    i = lax.axis_index("tensor")
    rows, width = x.shape
    loads = [
        pltpu.make_async_copy(src, dst, load.at[k])
        for k, (src, dst) in enumerate(((o_hbm, o), (wo_hbm, wo), (wg_hbm, wg), (wu_hbm, wu)))
    ]
    for c in loads:
        c.start()
    line_barrier(i, n)
    loads[0].wait()
    loads[1].wait()

    def compute(t, block):
        def tile(k):
            at = pl.ds(pl.multiple_of(k * TILE, TILE), TILE)
            part[block, :, at] = dot_nt(o[block], wo[at, :]).astype(BF16)

        loop(width // TILE, tile)

    def own(t):
        def tile(k):
            at = pl.ds(pl.multiple_of(k * TILE, TILE), TILE)
            mine[:, at] = dot_nt(o[i], wo[at, :])

        loop(width // TILE, tile)

    done = scatter_line(i, n, part, landed, rs_send, rs_recv, compute, own)
    scale_two, scale_three = 1.0 + gains[1:2, :], 1.0 + gains[2:3, :]

    def chunk(c):
        r = pl.ds(c * ROWS, ROWS)
        attn = summed_rows(i, n, mine, landed, r)
        attn_out[r, :] = attn
        y = x[r, :].astype(F32) + attn * inverse_rms(attn) * scale_two
        y_out[r, :] = y
        held[i, r, :] = (y * inverse_rms(y) * scale_three).astype(BF16)

    loop(rows // ROWS, chunk)
    done()
    loads[2].wait()
    loads[3].wait()
    drain = Drain(
        (hid_out, up_out, ge_out), (hid_s, up_s, ge_s), out_sem, lambda s: block_at(i, n, s)
    )

    def forward(s, block):
        pltpu.make_async_copy(held.at[block], h3_full.at[block], keep_sem.at[s]).start()
        drain.free(s)
        slot = s % 2
        span = tile_of(wg.shape[1])

        def tile(k):
            at = pl.ds(pl.multiple_of(k * span, span), span)
            u = dot_nn(held[block], wg[:, at])
            up = dot_nn(held[block], wu[:, at])
            c = 0.7978845608028654
            th = jnp.tanh(c * (u + 0.044715 * (u * u * u)))
            half = 0.5 * (1.0 + th)
            gelu = u * half
            slope = half + 0.5 * u * (1.0 - th * th) * (c * (1.0 + 0.134145 * (u * u)))
            hid_s[slot, :, at] = (gelu * up).astype(BF16)
            up_s[slot, :, at] = (up * slope).astype(BF16)
            ge_s[slot, :, at] = gelu.astype(BF16)

        loop(wg.shape[1] // span, tile)
        drain.start(s)

    gather_line(i, n, held, ag_send, ag_recv, forward)
    drain.finish(n)

    def finish(s):
        block = block_at(i, n, s)
        pltpu.make_async_copy(held.at[block], h3_full.at[block], keep_sem.at[s]).wait()

    loop(n, finish)


def into_feed(n, x, gains, o, wo, wg, wu):
    rows, width = x.shape
    wide = wg.shape[1]
    blocks = lambda w: jax.ShapeDtypeStruct((n, rows, w), BF16)
    mine = jax.ShapeDtypeStruct((rows, width), F32)
    return pl.pallas_call(
        functools.partial(into_feed_kernel, n),
        out_shape=[mine, mine, blocks(width), blocks(wide), blocks(wide), blocks(wide)],
        in_specs=[VM, VM, ANY, ANY, ANY, ANY],
        out_specs=[VM, VM, ANY, ANY, ANY, ANY],
        scratch_shapes=[
            pltpu.VMEM(o.shape, BF16),
            pltpu.VMEM(wo.shape, BF16),
            pltpu.VMEM(wg.shape, BF16),
            pltpu.VMEM(wu.shape, BF16),
            pltpu.VMEM((n, rows, width), BF16),
            pltpu.VMEM((n + 1, rows, width), BF16),
            pltpu.VMEM((rows, width), F32),
            pltpu.VMEM((n, rows, width), BF16),
        ]
        + [pltpu.VMEM((2, rows, wide), BF16)] * 3
        + [pltpu.SemaphoreType.DMA((4,))]
        + line_scratch(n) * 2
        + [pltpu.SemaphoreType.DMA((n,)), pltpu.SemaphoreType.DMA((3, 2))],
        compiler_params=params(2, 62),
        cost_estimate=cost(0, 600 << 20),
        name="into_feed",
    )(x, gains, o, wo, wg, wu)


def turn_feed_kernel(
    n, y, dout, gains, hid_hbm, wd_hbm, up_hbm, ge_hbm,
    layer_out, gain_out, df_full, dgate_out, dup_out,
    wd, hid_s, part, landed, mine, held, up_s, ge_s, dg_s, du_s, fold,
    load, feed_sem, rs_send, rs_recv, ag_send, ag_recv, keep_sem, back_sem, out_sem,
):
    i = lax.axis_index("tensor")
    rows, width = y.shape
    whole = pltpu.make_async_copy(wd_hbm, wd, load.at[0])
    whole.start()
    feed = Feed((hid_hbm,), (hid_s,), feed_sem, lambda s: block_at(i, n, n - 1 - s))
    feed.start(jnp.int32(0))
    line_barrier(i, n)
    whole.wait()

    def compute(t, block):
        feed.advance(t, n)
        slot = t % 2

        def tile(k):
            at = pl.ds(pl.multiple_of(k * TILE, TILE), TILE)
            part[block, :, at] = dot_nt(hid_s[slot], wd[at, :]).astype(BF16)

        loop(width // TILE, tile)

    def own(t):
        t = jnp.int32(t)
        feed.advance(t, n)
        slot = t % 2

        def tile(k):
            at = pl.ds(pl.multiple_of(k * TILE, TILE), TILE)
            mine[:, at] = dot_nt(hid_s[slot], wd[at, :])

        loop(width // TILE, tile)

    done = scatter_line(i, n, part, landed, rs_send, rs_recv, compute, own)
    scale = 1.0 + gains[3:4, :]
    fold[...] = jnp.zeros_like(fold)

    def chunk(c):
        r = pl.ds(c * ROWS, ROWS)
        f = summed_rows(i, n, mine, landed, r)
        g = dout[r, :].astype(F32)
        inv = inverse_rms(f)
        layer_out[r, :] = (y[r, :] + f * inv * scale).astype(BF16)
        held[i, r, :] = norm_back(g * scale, f, inv).astype(BF16)
        fold[...] += fold_rows(g * (f * inv))

    loop(rows // ROWS, chunk)
    gain_out[...] = jnp.sum(fold[...], axis=0, keepdims=True)
    done()
    sides = Feed((up_hbm, ge_hbm), (up_s, ge_s), back_sem, lambda s: block_at(i, n, s))
    drain = Drain((dgate_out, dup_out), (dg_s, du_s), out_sem, lambda s: block_at(i, n, s))
    sides.start(jnp.int32(0))

    def backward(s, block):
        pltpu.make_async_copy(held.at[block], df_full.at[block], keep_sem.at[s]).start()
        sides.advance(s, n)
        drain.free(s)
        slot = s % 2
        span = tile_of(wd.shape[1])

        def tile(k):
            at = pl.ds(pl.multiple_of(k * span, span), span)
            dhid = dot_nn(held[block], wd[:, at])
            dg_s[slot, :, at] = (dhid * up_s[slot, :, at].astype(F32)).astype(BF16)
            du_s[slot, :, at] = (dhid * ge_s[slot, :, at].astype(F32)).astype(BF16)

        loop(wd.shape[1] // span, tile)
        drain.start(s)

    gather_line(i, n, held, ag_send, ag_recv, backward)
    drain.finish(n)

    def finish(s):
        block = block_at(i, n, s)
        pltpu.make_async_copy(held.at[block], df_full.at[block], keep_sem.at[s]).wait()

    loop(n, finish)


def turn_feed(n, y, dout, gains, hid, wd, up, ge):
    rows, width = y.shape
    wide = wd.shape[1]
    blocks = lambda w: jax.ShapeDtypeStruct((n, rows, w), BF16)
    return pl.pallas_call(
        functools.partial(turn_feed_kernel, n),
        out_shape=[
            jax.ShapeDtypeStruct((rows, width), BF16),
            jax.ShapeDtypeStruct((1, width), F32),
            blocks(width),
            blocks(wide),
            blocks(wide),
        ],
        in_specs=[VM, VM, VM, ANY, ANY, ANY, ANY],
        out_specs=[VM, VM, ANY, ANY, ANY],
        scratch_shapes=[
            pltpu.VMEM(wd.shape, BF16),
            pltpu.VMEM((2, rows, wide), BF16),
            pltpu.VMEM((n, rows, width), BF16),
            pltpu.VMEM((n + 1, rows, width), BF16),
            pltpu.VMEM((rows, width), F32),
            pltpu.VMEM((n, rows, width), BF16),
        ]
        + [pltpu.VMEM((2, rows, wide), BF16)] * 4
        + [pltpu.VMEM((8, width), F32)]
        + [pltpu.SemaphoreType.DMA((1,)), pltpu.SemaphoreType.DMA((1, 2))]
        + line_scratch(n) * 2
        + [
            pltpu.SemaphoreType.DMA((n,)),
            pltpu.SemaphoreType.DMA((2, 2)),
            pltpu.SemaphoreType.DMA((2, 2)),
        ],
        compiler_params=params(3, 62),
        cost_estimate=cost(0, 600 << 20),
        name="turn_feed",
    )(y, dout, gains, hid, wd, up, ge)


def out_of_feed_kernel(
    n, y, attn, dout, gains, dgate_hbm, dup_hbm, wg_hbm, wu_hbm, wo_hbm,
    dy_out, gain_out, dattn_full, do_out,
    wg, wu, wo, dg_s, du_s, part, landed, mine, held, do_s, fold,
    load, feed_sem, rs_send, rs_recv, ag_send, ag_recv, keep_sem, out_sem,
):
    i = lax.axis_index("tensor")
    rows, width = y.shape
    loads = [
        pltpu.make_async_copy(src, dst, load.at[k])
        for k, (src, dst) in enumerate(((wg_hbm, wg), (wu_hbm, wu), (wo_hbm, wo)))
    ]
    for c in loads:
        c.start()
    feed = Feed((dgate_hbm, dup_hbm), (dg_s, du_s), feed_sem, lambda s: block_at(i, n, n - 1 - s))
    feed.start(jnp.int32(0))
    line_barrier(i, n)
    loads[0].wait()
    loads[1].wait()

    def product(slot, at):
        return dot_nt(dg_s[slot], wg[at, :]) + dot_nt(du_s[slot], wu[at, :])

    def compute(t, block):
        feed.advance(t, n)
        slot = t % 2

        def tile(k):
            at = pl.ds(pl.multiple_of(k * TILE, TILE), TILE)
            part[block, :, at] = product(slot, at).astype(BF16)

        loop(width // TILE, tile)

    def own(t):
        t = jnp.int32(t)
        feed.advance(t, n)
        slot = t % 2

        def tile(k):
            at = pl.ds(pl.multiple_of(k * TILE, TILE), TILE)
            mine[:, at] = product(slot, at)

        loop(width // TILE, tile)

    done = scatter_line(i, n, part, landed, rs_send, rs_recv, compute, own)
    scale_two, scale_three = 1.0 + gains[1:2, :], 1.0 + gains[2:3, :]
    fold[...] = jnp.zeros_like(fold)

    def chunk(c):
        r = pl.ds(c * ROWS, ROWS)
        dh3 = summed_rows(i, n, mine, landed, r)
        v = y[r, :]
        inv = inverse_rms(v)
        dy = dout[r, :].astype(F32) + norm_back(dh3 * scale_three, v, inv)
        dy_out[r, :] = dy
        fold[1] += fold_rows(dh3 * (v * inv))
        a = attn[r, :]
        inv = inverse_rms(a)
        held[i, r, :] = norm_back(dy * scale_two, a, inv).astype(BF16)
        fold[0] += fold_rows(dy * (a * inv))

    loop(rows // ROWS, chunk)
    gain_out[0:1, :] = jnp.sum(fold[0], axis=0, keepdims=True)
    gain_out[1:2, :] = jnp.sum(fold[1], axis=0, keepdims=True)
    done()
    loads[2].wait()
    drain = Drain((do_out,), (do_s,), out_sem, lambda s: block_at(i, n, s))

    def backward(s, block):
        pltpu.make_async_copy(held.at[block], dattn_full.at[block], keep_sem.at[s]).start()
        drain.free(s)
        do_s[s % 2] = dot_nn(held[block], wo[...]).astype(BF16)
        drain.start(s)

    gather_line(i, n, held, ag_send, ag_recv, backward)
    drain.finish(n)

    def finish(s):
        block = block_at(i, n, s)
        pltpu.make_async_copy(held.at[block], dattn_full.at[block], keep_sem.at[s]).wait()

    loop(n, finish)


def out_of_feed(n, y, attn, dout, gains, dgate, dup, wg, wu, wo):
    rows, width = y.shape
    wide = wg.shape[1]
    narrow = wo.shape[1]
    return pl.pallas_call(
        functools.partial(out_of_feed_kernel, n),
        out_shape=[
            jax.ShapeDtypeStruct((rows, width), F32),
            jax.ShapeDtypeStruct((2, width), F32),
            jax.ShapeDtypeStruct((n, rows, width), BF16),
            jax.ShapeDtypeStruct((n, rows, narrow), BF16),
        ],
        in_specs=[VM, VM, VM, VM, ANY, ANY, ANY, ANY, ANY],
        out_specs=[VM, VM, ANY, ANY],
        scratch_shapes=[
            pltpu.VMEM(wg.shape, BF16),
            pltpu.VMEM(wu.shape, BF16),
            pltpu.VMEM(wo.shape, BF16),
            pltpu.VMEM((2, rows, wide), BF16),
            pltpu.VMEM((2, rows, wide), BF16),
            pltpu.VMEM((n, rows, width), BF16),
            pltpu.VMEM((n + 1, rows, width), BF16),
            pltpu.VMEM((rows, width), F32),
            pltpu.VMEM((n, rows, width), BF16),
            pltpu.VMEM((2, rows, narrow), BF16),
            pltpu.VMEM((2, 8, width), F32),
        ]
        + [pltpu.SemaphoreType.DMA((3,)), pltpu.SemaphoreType.DMA((2, 2))]
        + line_scratch(n) * 2
        + [pltpu.SemaphoreType.DMA((n,)), pltpu.SemaphoreType.DMA((1, 2))],
        compiler_params=params(4, 62),
        cost_estimate=cost(0, 600 << 20),
        name="out_of_feed",
    )(y, attn, dout, gains, dgate, dup, wg, wu, wo)


class Slots:
    def __init__(self, arrays, pool, firsts, sems, view, width=None):
        self.arrays, self.pool, self.firsts, self.sems, self.view = arrays, pool, firsts, sems, view
        self.width = width or pool.shape[2]

    def copies(self, s, inward):
        for k, (array, first) in enumerate(zip(self.arrays, self.firsts)):
            slot = self.pool.at[first + s % 2, :, pl.ds(0, self.width)]
            block = self.view(array, s)
            pair = (block, slot) if inward else (slot, block)
            yield pltpu.make_async_copy(*pair, self.sems.at[k, s % 2])

    def fetch(self, s):
        for c in self.copies(s, True):
            c.start()

    def advance(self, s, count):
        for c in self.copies(s, True):
            c.wait()
        if s + 1 < count:
            self.fetch(s + 1)

    def free(self, s):
        if s >= 2:
            self.settle(s - 2)

    def settle(self, s):
        for c in self.copies(s, False):
            c.wait()

    def leave(self, s):
        for c in self.copies(s, False):
            c.start()

    def finish(self, count):
        for s in range(max(0, count - 2), count):
            self.settle(s)


def middle_kernel(
    n, x_hbm, dout_hbm, gains, o_hbm, wo_hbm, wg_hbm, wu_hbm, wd_hbm,
    layer_out, dy_out, gain_out, h3_t, hid_out, up_out, ge_out, df_t, dgate_out, dup_out,
    dattn_t, do_out, dattn_own,
    xs, dout, wo, wg, wu, wd, part, landed, held, y, attn, pool, fold, flip,
    load, rs_send, rs_recv, ag_send, ag_recv, flip_sem, in_sem, out_sem, last_sem,
    wu_send, wu_recv, wu_local, wd_send, wd_recv, wd_local,
):
    i = lax.axis_index("tensor")
    rows, width = xs.shape
    piece = rows // 2
    narrow = wo_hbm.shape[1]
    pairs = ((wo_hbm, wo), (x_hbm, xs), (wg_hbm, wg), (dout_hbm, dout))
    loads = [pltpu.make_async_copy(a, b, load.at[k]) for k, (a, b) in enumerate(pairs)]
    for c in loads:
        c.start()
    up_spread = Spread(wu_hbm, wu, wu_send, wu_recv, wu_local)
    down_spread = Spread(wd_hbm, wd, wd_send, wd_recv, wd_local)
    line_barrier(i, n, up_spread.peers())
    up_spread.begin()
    loads[0].wait()
    wide = wd.shape[1]
    over, across = min(768, wide_tile(width)), min(768, wide_tile(wide))
    scale_two, scale_three, scale_four = (1.0 + gains[k : k + 1, :] for k in (1, 2, 3))
    fold[...] = jnp.zeros_like(fold)

    def tiles(total, size, body):
        loop(total // size, lambda k: body(pl.ds(pl.multiple_of(k * size, size), size)))

    def place(c):
        return pl.ds(c * piece, piece)

    def forward_view(c):
        return lambda array, s: array.at[block_at(i, n, s), place(c)]

    def backward_view(c):
        return lambda array, s: array.at[block_at(i, n, n - 1 - s), place(c)]

    class Sum:
        def __init__(self, which, c, product, feed=None):
            at = 2 * which + c
            self.c, self.feed = c, feed
            self.part, self.landed = part.at[c], landed.at[c]

            def compute(t, block):
                if feed:
                    feed.advance(t, n)

                def tile(at):
                    self.part[block, :, at] = product(t, block, at).astype(BF16)

                tiles(width, over, tile)

            self.compute = compute
            self.step, self.land, self.done = scatter_steps(
                i, n, self.part, self.landed, rs_send.at[at], rs_recv.at[at], compute
            )

        def start(self):
            if self.feed:
                self.feed.fetch(0)
            self.step(0)

        def own(self):
            self.compute(n - 1, i)

        def rows(self, r):
            return summed_rows(i, n, self.part.at[i], self.landed, r)

    class Gather:
        def __init__(self, which, c, full, compute, drained):
            at = 2 * which + c
            self.c, self.full, self.compute, self.drained = c, full, compute, drained
            self.pass_on, self.sent = gather_steps(i, n, held.at[c], ag_send.at[at], ag_recv.at[at])

        def use(self, s):
            block = block_at(i, n, s)
            self.compute(s, block)
            column = block * rows + self.c * piece
            flip_rows(held.at[self.c, block], self.full, column, flip, flip_sem, True)
            flip_end(self.full, flip, flip_sem)

        def finish(self):
            self.use(n - 1)
            self.sent()
            self.drained(n)

    def chunks(c, body):
        strip = strip_of(piece)

        def one(k):
            body(pl.ds(k * strip, strip), pl.ds(c * piece + k * strip, strip))

        loop(piece // strip, one)


    def out_product(t, block, at):
        return dot_nt(pool[8 + t % 2, :, pl.ds(0, narrow)], wo[at, :])

    def down_product(t, block, at):
        return dot_nt(pool[6 + t % 2], wd[at, :])

    def in_product(t, block, at):
        return dot_nt(pool[6 + t % 2], wg[at, :]) + dot_nt(pool[10 + t % 2], wu[at, :])

    def sums(c):
        heads = Slots((o_hbm,), pool, (8,), in_sem.at[3, c], backward_view(c), narrow)
        hid = Slots((hid_out,), pool, (6,), in_sem.at[0, c], backward_view(c))
        both = Slots((dgate_out, dup_out), pool, (6, 10), in_sem.at[1, c], backward_view(c))
        return (
            Sum(0, c, out_product, heads),
            Sum(1, c, down_product, hid),
            Sum(2, c, in_product, both),
        )


    def after_attention(c, total):
        def body(r, g):
            a = total.rows(r)
            attn[g, :] = a.astype(BF16)
            v = xs[g, :].astype(F32) + a * inverse_rms(a) * scale_two
            y[g, :] = v
            held[c, i, r, :] = (v * inverse_rms(v) * scale_three).astype(BF16)

        chunks(c, body)

    def after_down(c, total):
        def body(r, g):
            f = total.rows(r)
            d = dout[g, :].astype(F32)
            inv = inverse_rms(f)
            xs[g, :] = (y[g, :] + f * inv * scale_four).astype(BF16)
            held[c, i, r, :] = norm_back(d * scale_four, f, inv).astype(BF16)
            fold[2] += fold_rows(d * (f * inv))

        chunks(c, body)

    def after_in(c, total):
        def body(r, g):
            dh3 = total.rows(r)
            v = y[g, :]
            inv = inverse_rms(v)
            dy = dout[g, :].astype(F32) + norm_back(dh3 * scale_three, v, inv)
            y[g, :] = dy
            fold[1] += fold_rows(dh3 * (v * inv))
            a = attn[g, :].astype(F32)
            inv = inverse_rms(a)
            held[c, i, r, :] = norm_back(dy * scale_two, a, inv).astype(BF16)
            fold[0] += fold_rows(dy * (a * inv))

        chunks(c, body)


    def gathers(c):
        ahead = Slots((hid_out, up_out, ge_out), pool, (0, 2, 4), out_sem.at[0, c], forward_view(c))
        sides = Slots((up_out, ge_out), pool, (0, 2), in_sem.at[2, c], forward_view(c))
        back = Slots((dgate_out, dup_out), pool, (4, 8), out_sem.at[1, c], forward_view(c))

        def into(s, block):
            if s == 0 and c == 0:
                up_spread.end()
                loads[2].wait()
            ahead.free(s)
            k = s % 2

            def tile(at):
                u = dot_nn(held[c, block], wg[:, at])
                up = dot_nn(held[c, block], wu[:, at])
                b = 0.7978845608028654
                th = jnp.tanh(b * (u + 0.044715 * (u * u * u)))
                half = 0.5 * (1.0 + th)
                gelu = u * half
                slope = half + 0.5 * u * (1.0 - th * th) * (b * (1.0 + 0.134145 * (u * u)))
                pool[0 + k, :, at] = (gelu * up).astype(BF16)
                pool[2 + k, :, at] = (up * slope).astype(BF16)
                pool[4 + k, :, at] = gelu.astype(BF16)

            tiles(wide, across, tile)
            ahead.leave(s)

        def turned(s, block):
            if s == 0:
                sides.fetch(0)
            sides.advance(s, n)
            back.free(s)
            k = s % 2

            def tile(at):
                dhid = dot_nn(held[c, block], wd[:, at])
                pool[4 + k, :, at] = (dhid * pool[0 + k, :, at].astype(F32)).astype(BF16)
                pool[8 + k, :, at] = (dhid * pool[2 + k, :, at].astype(F32)).astype(BF16)

            tiles(wide, across, tile)
            back.leave(s)

        heads = Slots((do_out,), pool, (0,), out_sem.at[2, c], forward_view(c), narrow)

        def out(s, block):
            heads.free(s)
            pool[s % 2, :, pl.ds(0, narrow)] = dot_nn(held[c, block], wo[...]).astype(BF16)
            heads.leave(s)

        return (
            Gather(0, c, h3_t, into, ahead.finish),
            Gather(1, c, df_t, turned, back.finish),
            Gather(2, c, dattn_t, out, heads.finish),
        )

    sum_of = (sums(0), sums(1))
    gather_of = (gathers(0), gathers(1))
    own_rows = (after_attention, after_down, after_in)

    first_sum = sum_of[0][0]
    first_sum.start()
    for k in range(1, n - 1):
        first_sum.step(k)
    first_sum.own()
    up_spread.middle()
    loads[1].wait()
    loads[3].wait()
    before = None
    for turn in range(5):
        which, c = turn // 2, turn % 2
        total = sum_of[c][which]
        later = (turn + 1) // 2
        following = sum_of[1 - c][later] if later < 3 else None
        gather = gather_of[c][which]
        total.land()
        own_rows[which](c, total)
        gather.pass_on(0)
        total.done()
        if turn == 0:
            up_spread.turn()
            down_spread.begin()
        if before:
            before.finish()
        if turn == 1:
            down_spread.end()
        if turn == 4:
            pltpu.make_async_copy(xs, layer_out, last_sem.at[0]).start()
        if following:
            following.start()
        for k in range(1, n):
            gather.pass_on(k)
            gather.use(k - 1)
            if following and k < n - 1:
                following.step(k)
            elif following:
                following.own()
        if turn == 0:
            down_spread.middle()
            down_spread.turn()
        before = gather
    total = sum_of[1][2]
    total.land()
    own_rows[2](1, total)
    own_out = pltpu.make_async_copy(held.at[1, i], dattn_own, last_sem.at[2])
    own_out.start()
    total.done()
    before.finish()
    pltpu.make_async_copy(y, dy_out, last_sem.at[1]).start()
    for k in range(3):
        gain_out[k : k + 1, :] = jnp.sum(fold[k], axis=0, keepdims=True)
    pltpu.make_async_copy(xs, layer_out, last_sem.at[0]).wait()
    pltpu.make_async_copy(y, dy_out, last_sem.at[1]).wait()
    own_out.wait()


def middle(n, x, dout, gains, o, wo, wg, wu, wd):
    rows, width = x.shape
    wide = wg.shape[1]
    piece = rows // 2
    sem = pltpu.SemaphoreType.DMA
    blocks = lambda w: jax.ShapeDtypeStruct((n, rows, w), BF16)
    turned = jax.ShapeDtypeStruct((width, n * rows), BF16)
    return pl.pallas_call(
        functools.partial(middle_kernel, n),
        out_shape=[
            jax.ShapeDtypeStruct((rows, width), BF16),
            jax.ShapeDtypeStruct((rows, width), F32),
            jax.ShapeDtypeStruct((3, width), F32),
            turned, blocks(wide), blocks(wide), blocks(wide),
            turned, blocks(wide), blocks(wide), turned, blocks(wo.shape[1]),
            jax.ShapeDtypeStruct((piece, width), BF16),
        ],
        in_specs=[ANY, ANY, VM] + [ANY] * 5,
        out_specs=[ANY, ANY, VM] + [ANY] * 10,
        scratch_shapes=[
            pltpu.VMEM(x.shape, BF16),
            pltpu.VMEM(x.shape, BF16),
            pltpu.VMEM(wo.shape, BF16),
            pltpu.VMEM(wg.shape, BF16),
            pltpu.VMEM(wg.shape, BF16),
            pltpu.VMEM((width, wide), BF16),
            pltpu.VMEM((2, n, piece, width), BF16),
            pltpu.VMEM((2, n + 1, piece, width), BF16),
            pltpu.VMEM((2, n, piece, width), BF16),
            pltpu.VMEM(x.shape, F32),
            pltpu.VMEM(x.shape, BF16),
            pltpu.VMEM((12, piece, wide), BF16),
            pltpu.VMEM((3, 8, width), F32),
            pltpu.VMEM((2, 768, piece), BF16),
            sem((4,)), sem((6, 2, n)), sem((6, n + 1)), sem((6, 2, n)), sem((6, n)),
            sem((2,)), sem((4, 2, 2, 2)), sem((3, 2, 3, 2)), sem((3,)),
        ]
        + spread_scratch() * 2,
        compiler_params=pltpu.CompilerParams(
            collective_id=8, has_side_effects=True, vmem_limit_bytes=(127 << 20) // 2
        ),
        cost_estimate=cost(0, 1200 << 20),
        name="middle",
    )(x, dout, gains, o, wo, wg, wu, wd)


def last_kernel(
    n, x, dy, gains, d_hbm, w_hbm, in_grad, gain_out,
    d, w, part, landed, mine, fold, load, rs_send, rs_recv,
):
    i = lax.axis_index("tensor")
    rows, width = x.shape
    loads = [
        pltpu.make_async_copy(src, dst, load.at[k])
        for k, (src, dst) in enumerate(((d_hbm, d), (w_hbm, w)))
    ]
    for c in loads:
        c.start()
    line_barrier(i, n)
    for c in loads:
        c.wait()

    def compute(t, block):
        def tile(k):
            at = pl.ds(pl.multiple_of(k * TILE, TILE), TILE)
            part[block, :, at] = dot_nt(d[block], w[at, :]).astype(BF16)

        loop(width // TILE, tile)

    def own(t):
        def tile(k):
            at = pl.ds(pl.multiple_of(k * TILE, TILE), TILE)
            mine[:, at] = dot_nt(d[i], w[at, :])

        loop(width // TILE, tile)

    done = scatter_line(i, n, part, landed, rs_send, rs_recv, compute, own)
    scale = 1.0 + gains[0:1, :]
    fold[...] = jnp.zeros_like(fold)

    def chunk(c):
        r = pl.ds(c * ROWS, ROWS)
        dh1 = summed_rows(i, n, mine, landed, r)
        v = x[r, :].astype(F32)
        inv = inverse_rms(v)
        in_grad[r, :] = (dy[r, :] + norm_back(dh1 * scale, v, inv)).astype(BF16)
        fold[...] += fold_rows(dh1 * (v * inv))

    loop(rows // ROWS, chunk)
    gain_out[...] = jnp.sum(fold[...], axis=0, keepdims=True)
    done()


def last(n, x, dy, gains, d, w):
    rows, width = x.shape
    return pl.pallas_call(
        functools.partial(last_kernel, n),
        out_shape=[
            jax.ShapeDtypeStruct((rows, width), BF16),
            jax.ShapeDtypeStruct((1, width), F32),
        ],
        in_specs=[VM, VM, VM, ANY, ANY],
        out_specs=[VM, VM],
        scratch_shapes=[
            pltpu.VMEM(d.shape, BF16),
            pltpu.VMEM(w.shape, BF16),
            pltpu.VMEM((n, rows, width), BF16),
            pltpu.VMEM((n + 1, rows, width), BF16),
            pltpu.VMEM((rows, width), F32),
            pltpu.VMEM((8, width), F32),
            pltpu.SemaphoreType.DMA((2,)),
        ]
        + line_scratch(n),
        compiler_params=params(5, 48),
        cost_estimate=cost(0, 300 << 20),
        name="last",
    )(x, dy, gains, d, w)


class Reduce:
    def __init__(self, u, left, right, column, width, bufs, sems):
        me = lax.axis_index("dp")
        c, x, y = me % 2, (me // 2) % 2, me // 4
        self.me, self.set, self.third, self.fifth, self.width = me, u % 2, u % 3, u % 5, width
        self.left, self.right, self.column, self.next = left, right, column, None
        self.dx, self.dy, self.dc = 2 - 4 * x, 4 - 8 * y, 1 - 2 * c
        self.lefts, self.rights, self.pair, self.pair_in, self.sums, self.far_in, self.xy_in, self.own = bufs
        (
            self.left_sem, self.right_sem, self.pair_send, self.pair_recv,
            self.far_send, self.far_recv, self.xy_send, self.xy_recv,
        ) = sems
        self.rows = self.own.shape[1]
        self.cols = pl.ds(0, width)
        self.top = pl.ds(0, self.rows // 2)
        self.low = pl.ds(self.rows // 2, self.rows // 2)

    def owner(self, q):
        k = q % 4
        x = jnp.where(k <= 1, self.dx, 0)
        y = jnp.where(k % 2 == 0, self.dy, 0)
        return self.me + x + jnp.where(k == 3, 0, y) + jnp.where(q < 4, self.dc, 0)

    def left_copy(self, q):
        r = pl.ds(self.owner(q) * self.rows, self.rows)
        return pltpu.make_async_copy(self.left.at[r], self.lefts.at[q % AHEAD], self.left_sem.at[q % AHEAD])

    def right_copy(self):
        return pltpu.make_async_copy(
            self.right.at[:, pl.ds(self.column, self.width)],
            self.rights.at[self.set, :, self.cols],
            self.right_sem.at[self.set],
        )

    def remote(self, src, dst, send, recv, shift):
        return pltpu.make_async_remote_copy(
            src, dst, send, recv, device_id={"dp": self.me + shift}, device_id_type=MESH
        )

    def pair_copy(self, k):
        return self.remote(
            self.pair.at[self.set, k, :, self.cols],
            self.pair_in.at[self.set, k, :, self.cols],
            self.pair_send.at[self.set, k],
            self.pair_recv.at[self.set, k],
            self.dc,
        )

    def far_copy(self, way):
        return self.remote(
            self.sums.at[self.third, 0, (self.top, self.low)[way], self.cols],
            self.far_in.at[self.third, way, :, self.cols],
            self.far_send.at[self.third, way],
            self.far_recv.at[self.third, way],
            (self.dx, self.dy)[way],
        )

    def xy_copy(self, way, half):
        r = (self.top, self.low)[half]
        return self.remote(
            self.sums.at[self.third, 1 + way, r, self.cols],
            self.xy_in.at[self.fifth, way, r, self.cols],
            self.xy_send.at[self.third, way, half],
            self.xy_recv.at[self.fifth, way, half],
            (self.dx, self.dy)[way],
        )

    def product(self, q, put):
        self.left_copy(q).wait()
        later = q + AHEAD - 1
        if not isinstance(q, int) or later < 8:
            self.left_copy(later).start()
        elif self.next:
            self.next.left_copy(later - 8).start()
        tile = wide_tile(self.width)

        def one(t):
            at = pl.ds(pl.multiple_of(t * tile, tile), tile)
            put(at, dot_nn(self.lefts[q % AHEAD], self.rights[self.set, :, at]))

        loop(self.width // tile, one)

    def load(self, first=False):
        self.right_copy().start()
        if first:
            for q in range(AHEAD - 1):
                self.left_copy(q).start()

    def begin(self):
        self.right_copy().wait()

        def chunk(k):
            def put(at, value):
                self.pair[self.set, k, :, at] = value.astype(BF16)

            self.product(k, put)
            self.pair_copy(k).start()

        loop(4, chunk)

    def middle(self):
        for k in range(4):
            arrived = []

            def put(at, value, k=k):
                total = value + self.pair_in[self.set, k, :, at].astype(F32)
                if k < 3:
                    self.sums[self.third, k, :, at] = total.astype(BF16)
                else:
                    self.own[self.third, :, at] = total

            self.pair_copy(k).wait_recv()
            self.product(4 + k, put)
            if k == 0:
                self.far_copy(0).start()
                self.far_copy(1).start()
            elif k == 1:
                self.xy_copy(0, 0).start()
            elif k == 2:
                self.xy_copy(1, 1).start()
        for k in range(4):
            self.pair_copy(k).wait_send()

    def turn(self):
        self.far_copy(0).wait_recv()
        self.far_copy(1).wait_recv()
        half = self.rows // 2

        strip = strip_of(half)

        def chunk(c):
            for way, first in ((0, 0), (1, half)):
                r = pl.ds(first + c * strip, strip)
                f = pl.ds(c * strip, strip)
                k = 2 - way
                total = self.sums[self.third, k, r, self.cols].astype(F32)
                total += self.far_in[self.third, way, f, self.cols].astype(F32)
                self.sums[self.third, k, r, self.cols] = total.astype(BF16)

        loop(half // strip, chunk)
        self.xy_copy(0, 1).start()
        self.xy_copy(1, 0).start()

    def end(self, put):
        for way in range(2):
            for half in range(2):
                self.xy_copy(way, half).wait_recv()

        strip = strip_of(self.rows)

        def chunk(c):
            r = pl.ds(c * strip, strip)
            total = self.own[self.third, r, self.cols]
            for way in range(2):
                total += self.xy_in[self.fifth, way, r, self.cols].astype(F32)
            put(r, total)

        loop(self.rows // strip, chunk)
        for way in range(2):
            self.far_copy(way).wait_send()
            for half in range(2):
                self.xy_copy(way, half).wait_send()


def reduce_scratch(rows, tokens, widest):
    sem = pltpu.SemaphoreType.DMA
    bufs = [
        pltpu.VMEM((AHEAD, rows, tokens), BF16),
        pltpu.VMEM((2, tokens, widest), BF16),
        pltpu.VMEM((2, 4, rows, widest), BF16),
        pltpu.VMEM((2, 4, rows, widest), BF16),
        pltpu.VMEM((3, 3, rows, widest), BF16),
        pltpu.VMEM((3, 2, rows // 2, widest), BF16),
        pltpu.VMEM((5, 2, rows, widest), BF16),
        pltpu.VMEM((3, rows, widest), F32),
    ]
    sems = [
        sem((AHEAD,)), sem((2,)), sem((2, 4)), sem((2, 4)),
        sem((3, 2)), sem((3, 2)), sem((3, 2, 2)), sem((5, 2, 2)),
    ]
    return bufs, sems


def finish_kernel(
    n, m, heads, kvs, units_of, starts, x_hbm, dy_hbm, gains, own_hbm, do_hbm, q_hbm, k_hbm, v_hbm,
    cos_hbm, sin_hbm, wo_hbm, w_hbm, dattn_in, h1_t, df_t, h3_t, hid, dgate, dup, o_hbm,
    later_gains,
    in_grad, gain_out, out_qkv, out_down, out_gate, out_up, out_out, kv_out, dattn_t,
    x, dy, total_gains, line_gains, dp_gains, held, do, q, k, v, cos, sin, wo, w, d, dk, dv, part, landed, fold, flip, stage, kv_stage,
    load, do_load, ag_send, ag_recv, rs_send, rs_recv, flip_sem, out_sem, last_sem, kv_sem, kv_send,
    kv_recv, gain_send, gain_recv, *reduce_refs,
):
    i = lax.axis_index("tensor")
    rows, width = x.shape
    piece = rows // 2
    over = min(768, wide_tile(width))
    split = heads * HD
    pairs = (
        (own_hbm, held.at[i]), (wo_hbm, wo), (q_hbm, q), (k_hbm, k), (v_hbm, v), (cos_hbm, cos),
        (sin_hbm, sin), (w_hbm, w), (x_hbm, x), (dy_hbm, dy),
    )
    loads = [pltpu.make_async_copy(a, b, load.at[j]) for j, (a, b) in enumerate(pairs)]
    for c in loads:
        c.start()
    half_loads = [
        pltpu.make_async_copy(
            do_hbm.at[j, pl.ds(0, piece)], do.at[pl.ds(j * rows, piece)], do_load.at[j]
        )
        for j in range(n)
    ]
    for c in half_loads:
        c.start()

    lefts = dict(qkv=h1_t, down=df_t, gate=h3_t, up=h3_t, out=dattn_t)
    rights = dict(qkv=d, down=hid, gate=dgate, up=dup, out=o_hbm)
    outs = dict(qkv=out_qkv, down=out_down, gate=out_gate, up=out_up, out=out_out)
    units = [
        Reduce(u, lefts[name], rights[name], column, size, reduce_refs[:8], reduce_refs[8:])
        for u, (name, column, size) in enumerate(units_of)
    ]
    count = len(units)
    for a, b in zip(units, units[1:]):
        a.next = b
    units[0].load(True)
    me = units[0].me

    barrier = pltpu.get_barrier_semaphore()
    for j in range(1, m):
        peer = lax.rem(me + j, m)
        pl.semaphore_signal(barrier, 1, device_id={"dp": peer}, device_id_type=MESH)
    for j in range(1, n):
        peer = lax.rem(i + j, n)
        pl.semaphore_signal(barrier, 1, device_id={"tensor": peer}, device_id_type=MESH)
    pl.semaphore_wait(barrier, m + n - 2)


    pass_on, sent = gather_steps(i, n, held, ag_send, ag_recv)

    def use(s):
        block = block_at(i, n, s)
        at = pl.ds(pl.multiple_of(block * rows + piece, piece), piece)
        do[at, :] = dot_nn(held[block], wo[...]).astype(BF16)
        flip_rows(held.at[block], dattn_t, block * rows + piece, flip, flip_sem, s == 0)

    def attention():
        use(n - 1)
        flip_end(dattn_t, flip, flip_sem)
        sent()
        for c in half_loads + loads[2:7]:
            c.wait()
        attend_back_kernel(heads, kvs, 256, starts, q, k, v, do, cos, sin, d, dk, dv)


    def compute(t, block):
        mine = d[pl.ds(pl.multiple_of(block * rows, rows), rows), :]

        def tile(j):
            at = pl.ds(pl.multiple_of(j * over, over), over)
            part[block, :, at] = dot_nt(mine, w[at, :]).astype(BF16)

        loop(width // over, tile)

    step, land, done = scatter_steps(i, n, part, landed, rs_send, rs_recv, compute)

    def begin_line():
        for c in loads[7:]:
            c.wait()
        step(0)

    def input_grad():
        land()
        scale = 1.0 + gains[0:1, :]
        fold[...] = jnp.zeros_like(fold)
        strip = strip_of(rows)

        def chunk(c):
            r = pl.ds(c * strip, strip)
            dh1 = summed_rows(i, n, part.at[i], landed, r)
            a = x[r, :].astype(F32)
            inv = inverse_rms(a)
            x[r, :] = (dy[r, :] + norm_back(dh1 * scale, a, inv)).astype(BF16)
            fold[...] += fold_rows(dh1 * (a * inv))

        loop(rows // strip, chunk)
        total_gains[0:1, :] = jnp.sum(fold[...], axis=0, keepdims=True)
        total_gains[1:4, :] = later_gains[...]
        for j in range(1, n):
            gain_copy(0, j).start()
        pltpu.make_async_copy(x, in_grad, last_sem.at[0]).start()
        done()


    def gain_copy(way, j):
        peer = {"dp": lax.rem(me + j, m)} if way else {"tensor": lax.rem(i + j, n)}
        return pltpu.make_async_remote_copy(
            gain_out if way else total_gains,
            (dp_gains if way else line_gains).at[j - 1],
            gain_send.at[way, j],
            gain_recv.at[way, j],
            device_id=peer,
            device_id_type=MESH,
        )

    def gains_over_line():
        total = total_gains[...]
        for j in range(1, n):
            gain_copy(0, j).wait_recv()
            total += line_gains[j - 1]
        gain_out[...] = total
        for j in range(1, m):
            gain_copy(1, j).start()

    def gains_over_dp():
        total = gain_out[...]
        for j in range(1, m):
            gain_copy(1, j).wait_recv()
            total += dp_gains[j - 1]
        for j in range(1, n):
            gain_copy(0, j).wait_send()
        for j in range(1, m):
            gain_copy(1, j).wait_send()
        gain_out[...] = total


    def out_copy(u):
        name, column, size = units_of[u]
        return pltpu.make_async_copy(
            stage.at[u % 2, :, pl.ds(0, size)],
            outs[name].at[:, pl.ds(column, size)],
            out_sem.at[u % 2],
        )

    def kv_copy(j, owner, peer):
        return pltpu.make_async_remote_copy(
            kv_stage, kv_out.at[owner], kv_send.at[j], kv_recv.at[j],
            device_id={"tensor": peer}, device_id_type=MESH,
        )

    kv_own = pltpu.make_async_copy(kv_stage, kv_out.at[i], kv_sem.at[0])

    def finish(u):
        if u >= 2:
            out_copy(u - 2).wait()
        name, column, size = units_of[u]
        keys = name == "qkv" and column == split

        def put(r, total):
            stage[u % 2, r, pl.ds(0, size)] = total
            if keys:
                kv_stage[r, :] = total.astype(BF16)

        units[u].end(put)
        out_copy(u).start()
        if keys:
            for j in range(1, n):
                kv_copy(j, i, lax.rem(i + j, n)).start()
            kv_own.start()

    def passing(s):
        pass_on(s)
        use(s - 1)

    line = [[functools.partial(passing, s)] for s in range(1, n)]
    line[-1] += [attention]
    line += [[begin_line]]
    for t in range(1, n - 1):
        line += [[], [], [functools.partial(step, t)]]
    line += [[lambda: compute(n - 1, i), input_grad], [gains_over_line], [], [gains_over_dp]]

    loads[0].wait()
    loads[1].wait()
    pass_on(0)
    for u in range(max(count + 2, len(line))):
        if u < count:
            units[u].begin()
            if u + 1 < count:
                units[u + 1].load()
            units[u].middle()
        if 1 <= u <= count:
            units[u - 1].turn()
        for action in line[u] if u < len(line) else ():
            action()
        if 2 <= u < count + 2:
            finish(u - 2)
    for u in range(max(0, count - 2), count):
        out_copy(u).wait()
    pltpu.make_async_copy(x, in_grad, last_sem.at[0]).wait()
    kv_own.wait()
    for j in range(1, n):
        kv_copy(j, i, lax.rem(i + j, n)).wait_send()
        peer = lax.rem(i + n - j, n)
        kv_copy(j, peer, peer).wait_recv()


def pieces(name, width, most=768):
    count = next(c for c in range(1, width) if width % (c * 128) == 0 and width // c <= most)
    return [(name, k * (width // count), width // count) for k in range(count)]


def finish(
    n, m, heads, kvs, starts, x, dy, gains, own, do, q, k, v, cos, sin, wo, w, turned, rights, o, later
):
    rows, width = x.shape
    tokens = n * rows
    own_rows = width // m
    split, across = heads * HD, w.shape[1]
    down, gate, up = (pieces(s, r.shape[1]) for s, r in zip(("down", "gate", "up"), rights))
    early = (down + gate)[: n + 1]
    late = (down + gate)[n + 1 :] + up + pieces("out", o.shape[1])
    units = early + [("qkv", split, across - split), ("qkv", 0, split)] + late
    widest = max(size for _, _, size in units)
    bufs, sems = reduce_scratch(own_rows, tokens, widest)
    sem = pltpu.SemaphoreType.DMA
    shape = lambda a, b, t=F32: jax.ShapeDtypeStruct((a, b), t)
    return pl.pallas_call(
        functools.partial(finish_kernel, n, m, heads, kvs, units),
        out_shape=[shape(rows, width, BF16), shape(4, width), shape(own_rows, across)]
        + [shape(own_rows, r.shape[1]) for r in (*rights, o)]
        + [jax.ShapeDtypeStruct((n, own_rows, across - split), BF16), shape(width, tokens, BF16)],
        in_specs=[SM, ANY, ANY, VM] + [ANY] * 17 + [VM],
        out_specs=[ANY, VM] + [ANY] * 7,
        scratch_shapes=[
            pltpu.VMEM(x.shape, BF16),
            pltpu.VMEM(x.shape, F32),
            pltpu.VMEM((4, width), F32),
            pltpu.VMEM((n - 1, 4, width), F32),
            pltpu.VMEM((m - 1, 4, width), F32),
            pltpu.VMEM((n, rows // 2, width), BF16),
            pltpu.VMEM((tokens, split), BF16),
            pltpu.VMEM(q.shape, BF16),
            pltpu.VMEM(k.shape, BF16),
            pltpu.VMEM(v.shape, BF16),
            pltpu.VMEM(cos.shape, F32),
            pltpu.VMEM(sin.shape, F32),
            pltpu.VMEM(wo.shape, BF16),
            pltpu.VMEM(w.shape, BF16),
            pltpu.VMEM((tokens, across), BF16),
            pltpu.VMEM((L, HD), F32),
            pltpu.VMEM((L, HD), F32),
            pltpu.VMEM((n, rows, width), BF16),
            pltpu.VMEM((n + 1, rows, width), BF16),
            pltpu.VMEM((8, width), F32),
            pltpu.VMEM((2, 768, rows // 2), BF16),
            pltpu.VMEM((2, own_rows, widest), F32),
            pltpu.VMEM((own_rows, across - split), BF16),
            sem((10,)), sem((n,)),
        ]
        + line_scratch(n) * 2
        + [sem((2,)), sem((2,)), sem((1,)), sem((1,)), sem((n,)), sem((n,)), sem((2, m)), sem((2, m))]
        + bufs
        + sems,
        input_output_aliases={13: 8},
        compiler_params=pltpu.CompilerParams(
            collective_id=7, has_side_effects=True, vmem_limit_bytes=(127 << 20) // 2
        ),
        cost_estimate=cost(0, 600 << 20),
        name="finish",
    )(starts, x, dy, gains, own, do, q, k, v, cos, sin, wo, w, turned[3], *turned[:3], *rights, o, later)


def deliver_kernel(count, *refs):
    sources, qkv, kv_hbm = refs[:count], refs[count], refs[count + 1]
    targets, k_out, v_out = refs[count + 2 : 2 * count + 3], *refs[2 * count + 3 : 2 * count + 5]
    stages = refs[2 * count + 5 : 3 * count + 6]
    kv, k_s, v_s, load, store = refs[3 * count + 6 :]
    n, rows, across = kv.shape
    split = targets[-1].shape[1]
    sources = (*sources, qkv.at[:, pl.ds(0, split)])
    first = pltpu.make_async_copy(kv_hbm, kv, load.at[count + 1])
    first.start()
    loads = [pltpu.make_async_copy(a, b, load.at[j]) for j, (a, b) in enumerate(zip(sources, stages))]
    for c in loads:
        c.start()
    stores = [
        pltpu.make_async_copy(a, b, store.at[j])
        for j, (a, b) in enumerate(zip((*stages, k_s, v_s), (*targets, k_out, v_out)))
    ]
    first.wait()
    half = across // 2
    for j in range(n):
        k_s[:, j * half : (j + 1) * half] = kv[j, :, :half].astype(F32)
        v_s[:, j * half : (j + 1) * half] = kv[j, :, half:].astype(F32)
    stores[-2].start()
    stores[-1].start()
    for a, b in zip(loads, stores):
        a.wait()
        b.start()
    for c in stores:
        c.wait()


def deliver(split, sources, qkv, kv):
    n, rows, across = kv.shape
    shape = lambda a: jax.ShapeDtypeStruct(a.shape, a.dtype)
    wide = jax.ShapeDtypeStruct((rows, n * across // 2), F32)
    count = len(sources)
    return pl.pallas_call(
        functools.partial(deliver_kernel, count),
        out_shape=[shape(a) for a in sources] + [jax.ShapeDtypeStruct((rows, split), F32), wide, wide],
        in_specs=[ANY] * (count + 2),
        out_specs=[ANY] * (count + 3),
        scratch_shapes=[pltpu.VMEM(a.shape, a.dtype) for a in sources]
        + [
            pltpu.VMEM((rows, split), F32),
            pltpu.VMEM(kv.shape, BF16),
            pltpu.VMEM(wide.shape, F32),
            pltpu.VMEM(wide.shape, F32),
            pltpu.SemaphoreType.DMA((count + 2,)),
            pltpu.SemaphoreType.DMA((count + 3,)),
        ],
        compiler_params=pltpu.CompilerParams(vmem_limit_bytes=62 << 20),
        cost_estimate=cost(0, 40 << 20),
        name="deliver",
    )(*sources, qkv, kv)


def rope_tables():
    positions = np.arange(L, dtype=np.float32)
    exponent = np.arange(HD // 2, dtype=np.float32) * np.float32(-2.0 / HD)
    angles = positions[:, None] * np.exp(exponent * np.log(np.float32(10000.0)))[None, :]
    angles = angles.astype(np.float64)
    return jnp.asarray(np.cos(angles), F32), jnp.asarray(np.sin(angles), F32)


def weight_grad(left, right):
    return dot_tn(left, right).astype(BF16)


def scatter_rows(grad):
    return lax.psum_scatter(grad, "dp", scatter_dimension=0, tiled=True)


def body(
    n,
    m,
    layer_in,
    out_grad,
    piece_starts,
    attn_gain,
    attn_out_gain,
    feed_gain,
    feed_out_gain,
    query_weight,
    key_weight,
    value_weight,
    out_weight,
    gate_weight,
    up_weight,
    down_weight,
):
    heads = query_weight.shape[1] // HD
    fan = H // KV
    kvs = max(1, heads // fan)
    rank = lax.axis_index("tensor")
    kv_at = (rank * heads // fan) * HD
    rows, width = layer_in.shape
    tokens = n * rows

    gathered = gather_gains(m, jnp.stack([attn_gain, attn_out_gain, feed_gain, feed_out_gain]))
    gains = gathered.transpose(1, 0, 2).reshape(4, width).astype(F32)

    def collect(shard):
        return lax.all_gather(shard, "dp", axis=0, tiled=True)

    wqkv = collect(
        jnp.concatenate(
            [
                query_weight,
                lax.dynamic_slice_in_dim(key_weight, kv_at, kvs * HD, 1),
                lax.dynamic_slice_in_dim(value_weight, kv_at, kvs * HD, 1),
            ],
            axis=1,
        )
    )
    wo = collect(out_weight.T)
    cos, sin = rope_tables()

    spread = m == 8 and n * kvs == KV
    h1, wg, h1_t = first(n, m, layer_in, gains, gate_weight if spread else None)
    if not spread:
        wg = collect(gate_weight)
    h1_flat = h1.reshape(tokens, width)
    q, k, v, o = attend(heads, kvs, piece_starts, h1_flat, wqkv, cos, sin)
    o_blocks = o.reshape(n, rows, heads * HD)
    if spread:
        layer_out, dy, gain_later, h3_t, hid, _, _, df_t, dgate, dup, dattn_t, do, own = middle(
            n, layer_in, out_grad, gains, o_blocks, wo, wg, up_weight, down_weight.T
        )
    else:
        wu, wd = collect(up_weight), collect(down_weight.T)
        attn, y, h3, hid, up, ge = into_feed(n, layer_in, gains, o_blocks, wo, wg, wu)
        layer_out, gain_four, df, dgate, dup = turn_feed(n, y, out_grad, gains, hid, wd, up, ge)
    flat = lambda a: a.reshape(tokens, a.shape[-1])
    split = heads * HD
    if spread:
        in_grad, gain_grads, qkv_sum, down_sum, gate_sum, up_sum, out_sum, kv, _ = finish(
            n, m, heads, kvs, piece_starts, layer_in, dy, gains, own, do, q, k, v, cos, sin, wo, wqkv,
            (h1_t, df_t, h3_t, dattn_t), (flat(hid), flat(dgate), flat(dup)), o, gain_later,
        )
    else:
        tie = lax.optimization_barrier
        down_part = weight_grad(flat(df), flat(hid))
        gate_part = weight_grad(flat(h3), flat(dgate))
        up_part = weight_grad(flat(h3), flat(dup))
        dgate, dup, down_part, gate_part, up_part = tie((dgate, dup, down_part, gate_part, up_part))
        down_sum, gate_sum, up_sum = map(scatter_rows, (down_part, gate_part, up_part))
        dy, gain_mid, dattn, do = out_of_feed(n, y, attn, out_grad, gains, dgate, dup, wg, wu, wo)
        do, dattn, down_sum, gate_sum = tie((do, dattn, down_sum, gate_sum))
        out_part = weight_grad(flat(dattn), o)
        do, out_part = tie((do, out_part))
        d = attend_back(heads, kvs, piece_starts, q, k, v, flat(do), cos, sin)
        qkv_part = weight_grad(h1_flat, d)
        d, qkv_part, up_sum = tie((d, qkv_part, up_sum))
        out_sum, qkv_sum = scatter_rows(out_part), scatter_rows(qkv_part)
        in_grad, gain_one = last(n, layer_in, dy, gains, d.reshape(n, rows, -1), wqkv)
        gain_later = jnp.concatenate([gain_mid, gain_four], axis=0)

        own_rows = qkv_sum.shape[0]
        kv = qkv_sum[:, split:].reshape(own_rows, 2, kvs * HD).transpose(1, 0, 2)
        if n * kvs == KV:
            kv = lax.all_gather(kv, "tensor", axis=2, tiled=True)
        else:
            kv = lax.dynamic_update_slice_in_dim(jnp.zeros((2, own_rows, KV * HD), BF16), kv, kv_at, 2)
            kv = lax.psum(kv, "tensor")
    if spread:
        own_at = lax.axis_index("dp") * (width // m)
        gain_grads = lax.dynamic_slice_in_dim(gain_grads, own_at, width // m, 1)
    else:
        gain_grads = jnp.concatenate([gain_one, gain_later], axis=0)
        gain_grads = sum_gains(n, m, gain_grads.reshape(4, m, width // m).transpose(1, 0, 2))
    if spread:
        layer_out, in_grad, down_sum, gate_sum, up_sum, out_sum, q_sum, k_sum, v_sum = deliver(
            split, (layer_out, in_grad, down_sum, gate_sum, up_sum, out_sum), qkv_sum, kv
        )
    else:
        q_sum, k_sum, v_sum = qkv_sum[:, :split].astype(F32), kv[0].astype(F32), kv[1].astype(F32)
    return (
        layer_out,
        in_grad,
        q_sum,
        k_sum,
        v_sum,
        out_sum.astype(F32).T,
        gate_sum.astype(F32),
        up_sum.astype(F32),
        down_sum.astype(F32).T,
        gain_grads[0],
        gain_grads[1],
        gain_grads[2],
        gain_grads[3],
    )


def solution(mesh):
    in_specs = (
        P(("dp", "tensor"), None),
        P(("dp", "tensor"), None),
        P("dp", None),
        P("dp"),
        P("dp"),
        P("dp"),
        P("dp"),
        P("dp", "tensor"),
        P("dp", None),
        P("dp", None),
        P("tensor", "dp"),
        P("dp", "tensor"),
        P("dp", "tensor"),
        P("tensor", "dp"),
    )
    out_specs = (
        P(("dp", "tensor"), None),
        P(("dp", "tensor"), None),
        P("dp", "tensor"),
        P("dp", None),
        P("dp", None),
        P("tensor", "dp"),
        P("dp", "tensor"),
        P("dp", "tensor"),
        P("tensor", "dp"),
        P("dp"),
        P("dp"),
        P("dp"),
        P("dp"),
    )
    program = functools.partial(body, mesh.shape["tensor"], mesh.shape["dp"])
    return jax.shard_map(program, mesh=mesh, in_specs=in_specs, out_specs=out_specs, check_vma=False)
```
